32 devices in a mesh: fsdp: 2 (over x), seq: 16 (over z, y, core).
Axes of the slice: x: 2, y: 2, z: 4, core: 2. Of those that a mesh axis runs over, the one named last changes fastest.
Arguments:
- activations: bfloat16 [2, 2048, 2048], P('fsdp', 'seq'), may hold values from -6 to 6
- cotangent: bfloat16 [2, 2048, 2048], P('fsdp', 'seq'), may hold values from -6 to 6
- segments: int32 [2, 2048], P('fsdp'), may hold values from 0 to 3, as said below
- routing: int32 [2, 2048, 8], P('fsdp', 'seq'), may hold values from 0 to 15, all different within a row
- attn_gain: bfloat16 [2048], P('fsdp'), may hold values from 0.5 to 1.5
- mlp_gain: bfloat16 [2048], P('fsdp'), may hold values from 0.5 to 1.5
- query_gain: bfloat16 [128], P('fsdp'), may hold values from 0.5 to 1.5
- key_gain: bfloat16 [128], P('fsdp'), may hold values from 0.5 to 1.5
- w_query: bfloat16 [2048, 4096], P('fsdp'), may hold values from -0.125 to 0.125
- key_weight: bfloat16 [2048, 512], P('fsdp'), may hold values from -0.125 to 0.125
- value_weight: bfloat16 [2048, 512], P('fsdp'), may hold values from -0.125 to 0.125
- w_out: bfloat16 [4096, 2048], P('fsdp'), may hold values from -3 to 3
- w_router: bfloat16 [2048, 16], P('fsdp'), may hold values from -0.0625 to 0.0625
- w_gate: bfloat16 [16, 2048, 768], P('seq', 'fsdp'), may hold values from -0.125 to 0.125
- w_up: bfloat16 [16, 2048, 768], P('seq', 'fsdp'), may hold values from -0.125 to 0.125
- w_down: bfloat16 [16, 768, 2048], P('seq', None, 'fsdp'), may hold values from -0.875 to 0.875
Outputs:
- mixed: bfloat16 [2, 2048, 2048], P('fsdp', 'seq')
- input_grad: float32 [2, 2048, 2048], P('fsdp', 'seq')
- attn_gain_grad: float32 [2048], P('fsdp')
- mlp_gain_grad: float32 [2048], P('fsdp')
- query_gain_grad: float32 [128], P('fsdp')
- key_gain_grad: float32 [128], P('fsdp')
- w_query_grad: float32 [2048, 4096], P('fsdp')
- w_key_grad: float32 [2048, 512], P('fsdp')
- w_value_grad: float32 [2048, 512], P('fsdp')
- w_out_grad: float32 [4096, 2048], P('fsdp')
- w_router_grad: float32 [2048, 16], P('fsdp')
- w_gate_grad: float32 [16, 2048, 768], P('seq', 'fsdp')
- w_up_grad: float32 [16, 2048, 768], P('seq', 'fsdp')
- w_down_grad: float32 [16, 768, 2048], P('seq', None, 'fsdp')
The draws below stay inside these ranges and needn't reach their ends.
Inputs may be any that keep to these rules, and one draw needn't show every extreme that they name: `segments`: in each sequence id 0 marks padding, which fills the last 1 to 63 positions; before it the ids never fall, and the document that starts within the first 64 positions ends within the last 128 positions. `routing`: each token names 8 different experts.
All inputs are finite; a program needn't handle non-finite values.
Results may differ from the reference program's by a relative error of at most 0.024.
Values may be sent and summed in bfloat16 or wider, within the bound.
A program may use at most 320 MiB of HBM per device.

```python
import functools
import math
import jax
import jax.numpy as jnp
import numpy as np
from jax import lax

MODEL_DIM = 2048
QUERY_HEADS = 32
KEY_HEADS = 4
HEAD_DIM = 128
FFE = 768
TOPK = 8
TOK_DEV = 128
QUERY_GROUPS = 16
EXPERTS = 16
LENGTH = 2048
SEQS = 2
CAP = 72


def draw_segments(key, part):
    key = jax.random.fold_in(key, 7)
    pad_key, open_key, close_key = jax.random.split(key, 3)
    padding = jax.random.randint(pad_key, (SEQS, 1), 1, max(2, TOK_DEV // 2))
    opening = jax.random.randint(open_key, (SEQS, 1), 0, max(1, TOK_DEV // 2))
    closing = jax.random.randint(close_key, (SEQS, 1), 1, max(2, TOK_DEV // 4))
    position = jnp.arange(LENGTH, dtype=jnp.int32)[None, :]
    live_end = LENGTH - padding
    long_end = live_end - closing
    labels = 1 + (position >= opening).astype(jnp.int32) + (position >= long_end).astype(jnp.int32)
    return jnp.where(position < live_end, labels, 0).astype(jnp.int32)


def steps_of(own_key, extent, cuts, least, largest):
    loudness = 1.0
    for dim, blocks in cuts:
        heights = jax.random.uniform(jax.random.fold_in(jax.random.fold_in(own_key, 6), dim), (blocks,), jnp.float32, least / len(cuts), largest / len(cuts))
        loudness = loudness * jnp.repeat(jnp.exp(heights), extent[dim] // blocks).reshape((-1,) + (1,) * (len(extent) - 1 - dim))
    return loudness


def picks_of(rng, rows, count, top, lift):
    ranking = jax.random.permutation(jax.random.fold_in(rng, 1), count)
    boost = ranking
    for power in range(3):
        boost = boost * boost // count
    boost = boost * lift // count
    chance = jax.random.randint(jax.random.fold_in(rng, 2), (rows, count), 0, 4096) + boost
    sure = jax.random.permutation(jax.random.fold_in(rng, 3), rows)[jnp.arange(count) % rows]
    chance = jnp.where(jnp.arange(rows)[:, None] == sure[None, :], 1 << 14, chance)
    priority = chance * count + jnp.arange(count)
    return lax.top_k(priority.astype(jnp.int32), top)[1].astype(jnp.int32)


def normal_values(key, shape, deviation, reach, pieces=(), held_as=jnp.bfloat16):
    result = deviation * jax.random.normal(key, shape, jnp.float32)
    if pieces:
        result = result * steps_of(key, shape, pieces, -0.22, 0.18)
    return jnp.clip(result, -reach, reach).astype(held_as)


def setup_inputs(seed: int = 0) -> dict:
    key_list = jax.random.split(jax.random.key(seed), 17)
    return {
        "activations": normal_values(key_list[0], (SEQS, LENGTH, MODEL_DIM), 1.0, 6.0, ((0, 2), (1, 16))),
        "cotangent": normal_values(key_list[1], (SEQS, LENGTH, MODEL_DIM), 1.0, 6.0, ((0, 2), (1, 16))),
        "segments": draw_segments(jax.random.fold_in(key_list[16], 71), 0),
        "routing": picks_of(key_list[3], SEQS * LENGTH, EXPERTS, TOPK, 4096).reshape((SEQS, LENGTH, TOPK)),
        "attn_gain": jnp.clip(1.0 + 0.1 * jax.random.normal(key_list[4], (MODEL_DIM,), jnp.float32), 0.5, 1.5).astype(jnp.bfloat16),
        "mlp_gain": jnp.clip(1.0 + 0.1 * jax.random.normal(key_list[5], (MODEL_DIM,), jnp.float32), 0.5, 1.5).astype(jnp.bfloat16),
        "query_gain": jnp.clip(1.0 + 0.1 * jax.random.normal(key_list[6], (HEAD_DIM,), jnp.float32), 0.5, 1.5).astype(jnp.bfloat16),
        "key_gain": jnp.clip(1.0 + 0.1 * jax.random.normal(key_list[7], (HEAD_DIM,), jnp.float32), 0.5, 1.5).astype(jnp.bfloat16),
        "w_query": normal_values(key_list[8], (MODEL_DIM, QUERY_HEADS * HEAD_DIM), MODEL_DIM ** -0.5, 0.125, ((0, 2),)),
        "key_weight": normal_values(key_list[9], (MODEL_DIM, KEY_HEADS * HEAD_DIM), MODEL_DIM ** -0.5, 0.125, ((0, 2),)),
        "value_weight": normal_values(key_list[10], (MODEL_DIM, KEY_HEADS * HEAD_DIM), MODEL_DIM ** -0.5, 0.125, ((0, 2),)),
        "w_out": normal_values(key_list[11], (QUERY_HEADS * HEAD_DIM, MODEL_DIM), (max(1, 2 * QUERY_HEADS * HEAD_DIM // LENGTH)) ** -0.5, 3.0, ((0, 2),)),
        "w_router": normal_values(key_list[12], (MODEL_DIM, EXPERTS), (4 * MODEL_DIM) ** -0.5, 0.0625, ((0, 2),)),
        "w_gate": normal_values(key_list[13], (EXPERTS, MODEL_DIM, FFE), MODEL_DIM ** -0.5, 0.125, ((0, 16), (1, 2))),
        "w_up": normal_values(key_list[14], (EXPERTS, MODEL_DIM, FFE), MODEL_DIM ** -0.5, 0.125, ((0, 16), (1, 2))),
        "w_down": normal_values(key_list[15], (EXPERTS, FFE, MODEL_DIM), (FFE // 16) ** -0.5, 0.875, ((0, 16), (2, 2))),
    }


@jax.custom_vjp
def lower_bound(v):
    return lax.optimization_barrier(v.astype(jnp.bfloat16)).astype(jnp.float32)

@jax.custom_vjp
def lower_bound_back(v):
    return v

def low_keep(v):
    return (lower_bound(v), None)

def low_pass(kept, grad):
    return (grad,)

def back_keep(v):
    return (v, None)

def back_low(kept, grad):
    return (lower_bound(grad),)
lower_bound.defvjp(low_keep, low_pass)
lower_bound_back.defvjp(back_keep, back_low)
EPSILON = 1e-06
THETA = 1000000.0
MASKED = -1e+30
HIGHEST = lax.Precision.HIGHEST

def score_product(first_operand, second_operand):
    return jnp.dot(first_operand, second_operand, precision=HIGHEST)

def norm_rows(values, scaling):
    return values * lax.rsqrt(lax.optimization_barrier(jnp.mean(values * values, axis=-1, keepdims=True)) + EPSILON) * scaling

def rotate(values, cosine, sine_table):
    half_width = values.shape[-1] // 2
    first_half = values[..., :half_width]
    second_half = values[..., half_width:]
    return jnp.concatenate([first_half * cosine - second_half * sine_table, second_half * cosine + first_half * sine_table], axis=-1)

def angles(segment, head_size):
    span_length = segment.shape[0]
    position = jnp.arange(span_length, dtype=jnp.int32)
    starts = jnp.concatenate([jnp.ones((1,), dtype=bool), segment[1:] != segment[:-1]])
    doc_start = lax.cummax(jnp.where(starts, position, jnp.zeros_like(position)), axis=0)
    offset = (position - doc_start).astype(jnp.float32)
    frequency = jnp.exp(jnp.arange(head_size // 2, dtype=jnp.float32) * (-2.0 * math.log(THETA) / head_size))
    phases = offset[:, None] * frequency[None, :]
    return (jnp.cos(phases), jnp.sin(phases))

def allowed(segment, first_row, block_rows):
    query_doc = lax.dynamic_slice_in_dim(segment, first_row, block_rows)
    query_pos = first_row + jnp.arange(block_rows, dtype=jnp.int32)
    key_pos = jnp.arange(segment.shape[0], dtype=jnp.int32)
    same_doc = query_doc[:, None] == segment[None, :]
    causal = key_pos[None, :] <= query_pos[:, None]
    live_key = (segment[None, :] > 0) | (key_pos[None, :] == query_pos[:, None])
    return same_doc & causal & live_key

def slot_rank(routes, experts):
    named = lax.optimization_barrier(jnp.sum((routes[:, :, None] == jnp.arange(experts, dtype=jnp.int32)[None, None, :]).astype(jnp.int32), axis=1, dtype=jnp.int32))
    earlier = jnp.cumsum(named, axis=0, dtype=jnp.int32) - named
    return jnp.take_along_axis(earlier, routes, axis=1)

def layer(tokens, segment, routes, attn_gain, mlp_gain, query_gain, key_gain, w_query, key_weight, value_weight, w_out, w_router, w_gate, w_up, w_down):
    span_length = tokens.shape[0]
    heads_per_group = QUERY_HEADS // QUERY_GROUPS
    key_head_index = np.arange(QUERY_GROUPS) * heads_per_group // (QUERY_HEADS // KEY_HEADS)
    hidden_input = lower_bound(norm_rows(tokens, attn_gain))
    queries = lower_bound_back(lower_bound(score_product(hidden_input, w_query))).reshape(span_length, QUERY_GROUPS, heads_per_group, HEAD_DIM)
    keys_gathered = lower_bound(lower_bound_back(score_product(hidden_input, key_weight))).reshape(span_length, KEY_HEADS, HEAD_DIM)
    values_gathered = lower_bound(lower_bound_back(score_product(hidden_input, value_weight))).reshape(span_length, KEY_HEADS, HEAD_DIM)
    key_groups = lower_bound_back(keys_gathered[:, key_head_index])
    value_groups = lower_bound_back(values_gathered[:, key_head_index])
    cosine, sine_table = angles(segment, HEAD_DIM)
    query_ready = lower_bound(rotate(norm_rows(queries, query_gain), cosine[:, None, None], sine_table[:, None, None]))
    key_ready = lower_bound(rotate(norm_rows(key_groups, key_gain), cosine[:, None], sine_table[:, None]))
    block_rows = min(512, span_length)
    score_scale = HEAD_DIM ** (-0.5)

    def attend(block_index):
        first_row = block_index * block_rows
        query_block = lax.dynamic_slice_in_dim(query_ready, first_row, block_rows, 0)
        scores = lower_bound_back(jnp.einsum('qsph,ksh->spqk', query_block, key_ready, precision=HIGHEST) * score_scale)
        masked = jnp.where(allowed(segment, first_row, block_rows)[None, None], scores, MASKED)
        probability = lower_bound(jax.nn.softmax(masked, axis=-1))
        return jnp.einsum('spqk,ksh->qsph', probability, value_groups, precision=HIGHEST)
    attended = lax.map(jax.checkpoint(attend), jnp.arange(span_length // block_rows, dtype=jnp.int32))
    attended = lower_bound_back(lower_bound(attended.reshape(span_length, QUERY_HEADS * HEAD_DIM)))
    resid = tokens + lower_bound_back(score_product(attended, w_out))
    hidden_mid = lower_bound(norm_rows(resid, mlp_gain))
    logits = lower_bound_back(score_product(hidden_mid, w_router))
    gates = jax.nn.softmax(jnp.take_along_axis(logits, routes, axis=1), axis=-1)
    blocks = routes.reshape(QUERY_GROUPS, TOK_DEV, TOPK)
    slot_index = jax.vmap(functools.partial(slot_rank, experts=EXPERTS))(blocks)
    source = jnp.arange(QUERY_GROUPS, dtype=jnp.int32)[:, None, None]
    target = jnp.where(slot_index < CAP, (blocks * QUERY_GROUPS + source) * CAP + slot_index, EXPERTS * QUERY_GROUPS * CAP).reshape(-1)
    spread = jnp.broadcast_to(hidden_mid[:, None, :], (span_length, TOPK, MODEL_DIM)).reshape(-1, MODEL_DIM)
    arrived = jnp.zeros((EXPERTS * QUERY_GROUPS * CAP + 1, MODEL_DIM), jnp.float32).at[target].add(spread)[:-1]
    arrived = lower_bound_back(arrived).reshape(EXPERTS, QUERY_GROUPS * CAP, MODEL_DIM)
    gate_act = lower_bound_back(jnp.einsum('ecd,edf->ecf', arrived, w_gate, precision=HIGHEST))
    up_act = lower_bound_back(jnp.einsum('ecd,edf->ecf', arrived, w_up, precision=HIGHEST))
    inner_act = lower_bound(jax.nn.silu(gate_act) * up_act)
    expert_out = lower_bound_back(lower_bound(jnp.einsum('ecf,efd->ecd', inner_act, w_down, precision=HIGHEST)))
    padded = jnp.concatenate([expert_out.reshape(-1, MODEL_DIM), jnp.zeros((1, MODEL_DIM), jnp.float32)], axis=0)
    gathered = padded[target].reshape(span_length, TOPK, MODEL_DIM)
    return resid + lax.optimization_barrier(jnp.sum(gates[:, :, None] * gathered, axis=1))

def reference(activations, cotangent, segments, routing, attn_gain, mlp_gain, query_gain, key_gain, w_query, key_weight, value_weight, w_out, w_router, w_gate, w_up, w_down):
    params = tuple((weight.astype(jnp.float32) for weight in (attn_gain, mlp_gain, query_gain, key_gain, w_query, key_weight, value_weight, w_out, w_router, w_gate, w_up, w_down)))

    def one_sequence(running, sequence):
        tokens, upstream, segment, routes = sequence

        def forward(token_values, *weights):
            return layer(token_values, segment, routes, *weights)
        output, pullback = jax.vjp(forward, tokens.astype(jnp.float32), *params)
        grads = pullback(upstream.astype(jnp.float32))
        running = tuple((summed + fresh for summed, fresh in zip(running, grads[1:])))
        return (running, (output.astype(jnp.bfloat16), grads[0]))
    initial = tuple((jnp.zeros_like(weight) for weight in params))
    totals, (mixed_out, input_grad) = lax.scan(one_sequence, initial, (activations, cotangent, segments, routing))
    return (mixed_out, input_grad, totals[0], totals[1], totals[2], totals[3], totals[4], totals[5], totals[6], totals[7], totals[8], totals[9], totals[10], totals[11])
```

```python
import functools
import math

import jax
import jax.numpy as jnp
from jax import lax
from jax.experimental import pallas as pl
from jax.experimental.pallas import tpu as pltpu
from jax.sharding import PartitionSpec as P

EPSILON = 1e-06
THETA = 1000000.0
BF16 = jnp.bfloat16
F32 = jnp.float32
MESH = pl.DeviceIdType.MESH
MIB = 1 << 20
LOG2E = math.log2(math.e)


def ring_of(chip, chips):
    return (chip % 2) * (chips - 1 - chip // 2) + (1 - chip % 2) * (chip // 2)


def chip_of(position, chips):
    upper = position // (chips // 2)
    return (1 - upper) * (2 * position) + upper * (2 * (chips - 1 - position) + 1)


def places(count):
    me = lax.axis_index("seq")
    chips = count // 2
    lane = me % 2
    position = ring_of(me // 2, chips)
    step = 1 - 2 * lane
    following = chip_of((position + step + chips) % chips, chips) * 2 + lane
    previous = chip_of((position - step + chips) % chips, chips) * 2 + lane
    sibling = me + 1 - 2 * lane
    return me, chips, lane, position, step, following, previous, sibling


def greet(senders):
    barrier = pltpu.get_barrier_semaphore()
    for device in senders:
        pl.semaphore_signal(barrier, inc=1, device_id={"seq": device}, device_id_type=MESH)
    pl.semaphore_wait(barrier, len(senders))


def gather_kernel(count, cuts, x_ref, o_ref, own_sem, ring_out, ring_in, side_out, side_in):
    me, chips, lane, position, step, following, previous, sibling = places(count)
    rows = x_ref.shape[0] // cuts
    greet((previous, sibling))

    def hop(src, owner, s, c, device, out_sem, in_sem):
        return pltpu.make_async_remote_copy(
            src_ref=src,
            dst_ref=o_ref.at[owner, pl.ds(c * rows, rows)],
            send_sem=out_sem.at[s, c],
            recv_sem=in_sem.at[s, c],
            device_id={"seq": device},
            device_id_type=MESH,
        )

    def ring(src, owner, s, c):
        return hop(src, owner, s, c, following, ring_out, ring_in)

    def side(src, owner, s, c):
        return hop(src, owner, s, c, sibling, side_out, side_in)

    own = pltpu.make_async_copy(x_ref, o_ref.at[me], own_sem)
    own.start()
    for c in range(cuts):
        src = x_ref.at[pl.ds(c * rows, rows)]
        ring(src, me, 0, c).start()
        side(src, me, 0, c).start()
    for s in range(1, chips):
        owner = chip_of((position - s * step + chips) % chips, chips) * 2 + lane
        for c in range(cuts):
            src = o_ref.at[owner, pl.ds(c * rows, rows)]
            ring(src, owner, s - 1, c).wait_recv()
            if s < chips - 1:
                ring(src, owner, s, c).start()
            side(src, owner, s, c).start()
    for s in range(chips):
        for c in range(cuts):
            src = x_ref.at[pl.ds(c * rows, rows)]
            side(src, me, s, c).wait()
            if s < chips - 1:
                ring(src, me, s, c).wait_send()
    own.wait()


def gather_seq(x, count, call, cuts=4):
    chips = count // 2
    return pl.pallas_call(
        functools.partial(gather_kernel, count, cuts),
        out_shape=jax.ShapeDtypeStruct((count,) + x.shape, x.dtype),
        in_specs=[pl.BlockSpec(memory_space=pl.ANY)],
        out_specs=pl.BlockSpec(memory_space=pl.ANY),
        scratch_shapes=[pltpu.SemaphoreType.DMA]
        + [pltpu.SemaphoreType.DMA((chips, cuts))] * 4,
        compiler_params=pltpu.CompilerParams(collective_id=call, has_side_effects=True),
    )(x)


def scatter_kernel(
    count, cuts, p_ref, o_ref, own, sent, came, given, own_sem, ring_out, ring_in, side_out, side_in
):
    me, chips, lane, position, step, following, previous, sibling = places(count)
    rows = p_ref.shape[1] // cuts
    greet((previous, sibling))

    def my_block(k):
        return chip_of((position - (k + 1) * step + 2 * chips) % chips, chips) * 2 + lane

    def sibling_block(k):
        return chip_of((position + (k + 1) * step + 2 * chips) % chips, chips) * 2 + 1 - lane

    def ring(k, c):
        return pltpu.make_async_remote_copy(
            src_ref=sent.at[k, pl.ds(c * rows, rows)],
            dst_ref=came.at[k, pl.ds(c * rows, rows)],
            send_sem=ring_out.at[k, c],
            recv_sem=ring_in.at[k, c],
            device_id={"seq": following},
            device_id_type=MESH,
        )

    def side(k):
        return pltpu.make_async_remote_copy(
            src_ref=p_ref.at[sibling_block(k)],
            dst_ref=given.at[k],
            send_sem=side_out.at[k],
            recv_sem=side_in.at[k],
            device_id={"seq": sibling},
            device_id_type=MESH,
        )

    def load(k):
        return pltpu.make_async_copy(p_ref.at[my_block(k)], own.at[k], own_sem.at[k])

    for k in range(chips):
        side(k).start()
        load(k).start()
    for k in range(chips):
        load(k).wait()
        side(k).wait_recv()
        for c in range(cuts):
            part = pl.ds(c * rows, rows)
            total = own[k, part].astype(F32) + given[k, part].astype(F32)
            if k > 0:
                ring(k - 1, c).wait_recv()
                total = total + came[k - 1, part].astype(F32)
            if k < chips - 1:
                sent[k, part] = total.astype(BF16)
                ring(k, c).start()
            else:
                o_ref[part] = total
    for k in range(chips):
        side(k).wait_send()
        if k < chips - 1:
            for c in range(cuts):
                ring(k, c).wait_send()


def scatter_seq(p, count, call, cuts=2):
    chips = count // 2
    _, rows, columns = p.shape
    return pl.pallas_call(
        functools.partial(scatter_kernel, count, cuts),
        out_shape=jax.ShapeDtypeStruct((rows, columns), F32),
        in_specs=[pl.BlockSpec(memory_space=pl.ANY)],
        out_specs=pl.BlockSpec(memory_space=pltpu.VMEM),
        scratch_shapes=[
            pltpu.VMEM((chips, rows, columns), BF16),
            pltpu.VMEM((chips - 1, rows, columns), BF16),
            pltpu.VMEM((chips - 1, rows, columns), BF16),
            pltpu.VMEM((chips, rows, columns), BF16),
            pltpu.SemaphoreType.DMA((chips,)),
            pltpu.SemaphoreType.DMA((chips, cuts)),
            pltpu.SemaphoreType.DMA((chips, cuts)),
            pltpu.SemaphoreType.DMA((chips,)),
            pltpu.SemaphoreType.DMA((chips,)),
        ],
        compiler_params=pltpu.CompilerParams(
            collective_id=call, has_side_effects=True, vmem_limit_bytes=48 * MIB
        ),
    )(p)


NT = (((1,), (1,)), ((), ()))
TN = (((0,), (0,)), ((), ()))


def attend_kernel(heads, tile, q_ref, k_ref, v_ref, start_ref, o_ref, total_ref):
    span = q_ref.shape[0]
    width = k_ref.shape[1]
    for i in range(span // tile):
        rows = pl.ds(i * tile, tile)
        start = start_ref[rows, :]
        row = i * tile + lax.broadcasted_iota(jnp.int32, (tile, tile), 0)
        for h in range(heads):
            cols = pl.ds(h * width, width)
            q = q_ref[rows, cols]
            total = jnp.zeros((tile, 2 * width), F32)
            for j in range(i + 1):
                keys = pl.ds(j * tile, tile)
                s = lax.dot_general(q, k_ref[keys, :], NT, preferred_element_type=F32)
                col = j * tile + lax.broadcasted_iota(jnp.int32, (tile, tile), 1)
                keep = col >= start
                if i == j:
                    keep = keep & (col <= row)
                p = jnp.where(keep, jnp.exp2(s), 0.0).astype(BF16)
                total = total + jnp.dot(p, v_ref[keys, :], preferred_element_type=F32)
            weight = total[:, width:]
            o_ref[rows, cols] = (total[:, :width] / weight).astype(BF16)
            total_ref[rows, cols] = jnp.log2(weight)


def attend(q, k, v, start, tile=512):
    span, width = k.shape
    heads = q.shape[1] // width
    vx = jnp.concatenate([v, jnp.ones_like(v)], axis=1)
    return pl.pallas_call(
        functools.partial(attend_kernel, heads, min(tile, span)),
        out_shape=(
            jax.ShapeDtypeStruct((span, heads * width), BF16),
            jax.ShapeDtypeStruct((span, heads * width), F32),
        ),
        in_specs=[pl.BlockSpec(memory_space=pltpu.VMEM)] * 4,
        out_specs=[pl.BlockSpec(memory_space=pltpu.VMEM)] * 2,
        compiler_params=pltpu.CompilerParams(vmem_limit_bytes=48 * MIB),
    )(q, k, vx, start[:, None])


def attend_back_kernel(
    heads, tile, q_ref, k_ref, v_ref, g_ref, start_ref, dq_ref, dk_ref, dv_ref
):
    span = q_ref.shape[0]
    width = k_ref.shape[1] // 2
    dq_ref[...] = jnp.zeros_like(dq_ref)
    for j in range(span // tile):
        keys = pl.ds(j * tile, tile)
        kx = k_ref[keys, :]
        vx = v_ref[keys, :]
        dk = jnp.zeros((tile, width), F32)
        dv = jnp.zeros((tile, width), F32)
        key = j * tile + lax.broadcasted_iota(jnp.int32, (tile, tile), 0)
        for i in range(j, span // tile):
            rows = pl.ds(i * tile, tile)
            keep = key >= start_ref[:, rows]
            if i == j:
                row = i * tile + lax.broadcasted_iota(jnp.int32, (tile, tile), 1)
                keep = keep & (key <= row)
            for h in range(heads):
                qx = q_ref[rows, pl.ds(2 * h * width, 2 * width)]
                gx = g_ref[rows, pl.ds(2 * h * width, 2 * width)]
                s = lax.dot_general(kx, qx, NT, preferred_element_type=F32)
                p = jnp.where(keep, jnp.exp2(s), 0.0)
                dp = lax.dot_general(vx, gx, NT, preferred_element_type=F32)
                ds = (p * dp).astype(BF16)
                dv = dv + jnp.dot(p.astype(BF16), gx[:, :width], preferred_element_type=F32)
                dk = dk + jnp.dot(ds, qx[:, :width], preferred_element_type=F32)
                dq_ref[rows, pl.ds(h * width, width)] += lax.dot_general(
                    ds, kx[:, :width], TN, preferred_element_type=F32
                )
        dk_ref[keys, :] = dk
        dv_ref[keys, :] = dv


def attend_back(qx, kx, vx, gx, start, tile=512):
    span = qx.shape[0]
    width = kx.shape[1] // 2
    heads = qx.shape[1] // (2 * width)
    return pl.pallas_call(
        functools.partial(attend_back_kernel, heads, min(tile, span)),
        out_shape=(
            jax.ShapeDtypeStruct((span, heads * width), F32),
            jax.ShapeDtypeStruct((span, width), F32),
            jax.ShapeDtypeStruct((span, width), F32),
        ),
        in_specs=[pl.BlockSpec(memory_space=pltpu.VMEM)] * 5,
        out_specs=[pl.BlockSpec(memory_space=pltpu.VMEM)] * 3,
        compiler_params=pltpu.CompilerParams(vmem_limit_bytes=56 * MIB),
    )(qx, kx, vx, gx, start[None, :])


def split3(x):
    first = x.astype(BF16)
    rest = x - first.astype(F32)
    second = rest.astype(BF16)
    return first, second, (rest - second.astype(F32)).astype(BF16)


def norm_rows(values, scaling):
    return values * lax.rsqrt(jnp.mean(values * values, axis=-1, keepdims=True) + EPSILON) * scaling


def rotate(values, cosine, sine):
    half = values.shape[-1] // 2
    first = values[..., :half]
    second = values[..., half:]
    return jnp.concatenate([first * cosine - second * sine, second * cosine + first * sine], axis=-1)


def run_starts(segment):
    position = jnp.arange(segment.shape[0], dtype=jnp.int32)
    fresh = jnp.concatenate([jnp.ones((1,), dtype=bool), segment[1:] != segment[:-1]])
    return position, lax.cummax(jnp.where(fresh, position, jnp.zeros_like(position)), axis=0)


def angles(offset, head_size):
    frequency = jnp.exp(
        jnp.arange(head_size // 2, dtype=F32) * (-2.0 * math.log(THETA) / head_size)
    )
    phases = offset[:, None] * frequency[None, :]
    return jnp.cos(phases), jnp.sin(phases)


def dot(a, b, dims=(((1,), (0,)), ((), ()))):
    return lax.dot_general(a, b, dims, preferred_element_type=F32)


def per_device(
    activations,
    cotangent,
    segments,
    routing,
    attn_gain,
    mlp_gain,
    query_gain,
    key_gain,
    w_query,
    key_weight,
    value_weight,
    w_out,
    w_router,
    w_gate,
    w_up,
    w_down,
):
    count = lax.axis_size("seq")
    shards = lax.axis_size("fsdp")
    me = lax.axis_index("seq")
    chips = count // 2
    x = activations[0].astype(F32)
    dy = cotangent[0]
    segment = segments[0]
    routes = routing[0]
    tok, dim = x.shape
    span = segment.shape[0]
    top = routes.shape[1]
    hd = query_gain.shape[0] * shards
    heads = w_query.shape[1] // hd
    kv_heads = key_weight.shape[1] // hd
    share = heads // count
    experts = w_router.shape[1]
    local_rows = w_out.shape[0]
    capacity = tok * top * 9 // (8 * experts)
    group = (me % 2) * chips + me // 2
    gcols = share * hd
    kv_head = group * share // (heads // kv_heads)

    small = jnp.concatenate(
        [attn_gain, mlp_gain, query_gain, key_gain, w_router.reshape(-1)], axis=0
    )
    small = lax.all_gather(small, "fsdp", axis=0, tiled=False)
    local_dim = attn_gain.shape[0]
    local_hd = query_gain.shape[0]
    cut = [local_dim, 2 * local_dim, 2 * local_dim + local_hd, 2 * local_dim + 2 * local_hd]
    g_attn, g_mlp, g_query, g_key, router = jnp.split(small, cut, axis=1)
    g_attn = g_attn.reshape(-1).astype(F32)
    g_mlp = g_mlp.reshape(-1).astype(F32)
    g_query = g_query.reshape(-1).astype(F32)
    g_key = g_key.reshape(-1).astype(F32)
    router = router.reshape(dim, experts)
    qkv_local = jnp.concatenate(
        [
            lax.dynamic_slice_in_dim(w_query, group * gcols, gcols, 1),
            lax.dynamic_slice_in_dim(key_weight, kv_head * hd, hd, 1),
            lax.dynamic_slice_in_dim(value_weight, kv_head * hd, hd, 1),
        ],
        axis=1,
    )
    w_qkv = lax.all_gather(qkv_local, "fsdp", axis=0, tiled=True)
    first_row = group * gcols
    out_owner = first_row // local_rows
    out_local = lax.dynamic_slice_in_dim(w_out, first_row % local_rows, gcols, 0)
    w_o = lax.dynamic_index_in_dim(
        lax.all_gather(out_local, "fsdp", axis=0, tiled=False), out_owner, 0, keepdims=False
    )
    wg = lax.all_gather(w_gate[0], "fsdp", axis=0, tiled=True)
    wu = lax.all_gather(w_up[0], "fsdp", axis=0, tiled=True)
    wd = lax.all_gather(w_down[0], "fsdp", axis=1, tiled=True)
    routes_all = lax.all_gather(routes, "seq", axis=0, tiled=False)

    r1 = lax.rsqrt(jnp.mean(x * x, axis=-1, keepdims=True) + EPSILON)
    h1 = (x * r1 * g_attn).astype(BF16)
    h1_all = gather_seq(h1, count, 1).reshape(span, dim)
    qkv = dot(h1_all, w_qkv).astype(BF16)
    position, doc_start = run_starts(segment)
    cosine, sine = angles((position - doc_start).astype(F32), hd)
    start = jnp.where(segment > 0, doc_start, position)

    def prep_query(raw, scaling):
        return rotate(norm_rows(raw, scaling), cosine[:, None], sine[:, None])

    def prep_key(raw, scaling):
        return rotate(norm_rows(raw, scaling), cosine, sine)

    q_raw = qkv[:, :gcols].reshape(span, share, hd).astype(F32)
    k_raw = qkv[:, gcols : gcols + hd].astype(F32)
    v = qkv[:, gcols + hd :]
    q_rot, query_pullback = jax.vjp(prep_query, q_raw, g_query)
    k_rot, key_pullback = jax.vjp(prep_key, k_raw, g_key)
    scale = hd**-0.5
    qs = (q_rot * (scale * LOG2E)).astype(BF16)
    kn = k_rot.astype(BF16)
    o, weight = attend(qs.reshape(span, gcols), kn, v, start)
    x2_parts = dot(o, w_o).astype(BF16).reshape(count, tok, dim)
    x2 = x + scatter_seq(x2_parts, count, 2)

    r2 = lax.rsqrt(jnp.mean(x2 * x2, axis=-1, keepdims=True) + EPSILON)
    h2 = (x2 * r2 * g_mlp).astype(BF16)
    h2_all = gather_seq(h2, count, 3)
    dy_all = gather_seq(dy, count, 4)

    def gates_of(hidden, chosen):
        logits = dot(hidden, router)
        return jax.nn.softmax(jnp.where(chosen, logits, -1e30), axis=-1) * chosen

    def chosen_of(named):
        names = jnp.arange(experts, dtype=jnp.int32)
        return jnp.any(named[..., :, None] == names, axis=-2)

    hit = jnp.any(routes_all == me, axis=-1)
    rank = jnp.cumsum(hit.astype(jnp.int32), axis=1) - hit
    slots = jnp.arange(capacity, dtype=jnp.int32)
    pick = hit[:, None, :] & (rank[:, None, :] == slots[None, :, None])
    one_hot = pick.astype(BF16)
    gates_all = gates_of(h2_all.reshape(span, dim), chosen_of(routes_all.reshape(span, top)))
    gate_tok = lax.dynamic_index_in_dim(gates_all, me, 1, keepdims=False).reshape(count, tok)
    gate_slot = jnp.sum(jnp.where(pick, gate_tok[:, None, :], 0.0), axis=-1).reshape(-1, 1)

    def to_slots(rows):
        return (
            jnp.einsum("bri,bid->brd", one_hot, rows, preferred_element_type=F32)
            .astype(BF16)
            .reshape(count * capacity, dim)
        )

    def to_tokens(rows):
        return jnp.einsum(
            "bri,brd->bid",
            one_hot,
            rows.reshape(count, capacity, dim),
            preferred_element_type=F32,
        )

    xs = to_slots(h2_all)
    dys = to_slots(dy_all)
    gate_act = dot(xs, wg)
    up_act = dot(xs, wu)
    sig = jax.nn.sigmoid(gate_act)
    silu = gate_act * sig
    inner = (silu * up_act).astype(BF16)
    e_out = dot(inner, wd)
    mixed_parts = to_tokens((gate_slot * e_out).astype(BF16)).astype(BF16)
    mixed = x2 + scatter_seq(mixed_parts, count, 5)

    dgate_slot = jnp.sum(dys.astype(F32) * e_out, axis=-1).reshape(count, capacity)
    dgate_tok = jnp.sum(jnp.where(pick, dgate_slot[:, :, None], 0.0), axis=1)
    de = (gate_slot * dys.astype(F32)).astype(BF16)
    dinner = dot(de, wd, NT)
    dg = (dinner * up_act * (sig + silu * (1.0 - sig))).astype(BF16)
    du = (dinner * silu).astype(BF16)
    w_down_part = dot(inner, de, TN)
    w_gate_part = dot(xs, dg, TN)
    w_up_part = dot(xs, du, TN)
    dxs = (dot(dg, wg, NT) + dot(du, wu, NT)).astype(BF16)
    own_lane = (jnp.arange(128, dtype=jnp.int32) == me)[None, None, :]
    dgate_hi, dgate_lo, _ = split3(dgate_tok[:, :, None])
    zero = jnp.zeros((), BF16)
    lanes = jnp.where(own_lane, dgate_hi, zero) + jnp.where(
        jnp.roll(own_lane, 64, axis=-1), dgate_lo, zero
    )
    dh2_parts = jnp.concatenate([to_tokens(dxs).astype(BF16), lanes], axis=2)
    dh2_wide = scatter_seq(dh2_parts, count, 6)
    dgate = dh2_wide[:, dim : dim + experts] + dh2_wide[:, dim + 64 : dim + 64 + experts]
    gates = gates_of(h2, chosen_of(routes))
    dlogits = (gates * (dgate - jnp.sum(gates * dgate, axis=-1, keepdims=True))).astype(BF16)
    dh2 = dh2_wide[:, :dim] + dot(dlogits, router, NT)
    router_part = dot(h2, dlogits, TN)
    xh = x2 * r2
    mlp_gain_part = jnp.sum(dh2 * xh, axis=0)
    dn = dh2 * g_mlp
    dx2 = dy.astype(F32) + r2 * (dn - xh * jnp.mean(dn * xh, axis=-1, keepdims=True))

    da_all = gather_seq(dx2.astype(BF16), count, 7).reshape(span, dim)
    do = dot(da_all, w_o, NT).astype(BF16)
    w_out_part = dot(o, da_all, TN).astype(BF16)
    do_h = do.reshape(span, share, hd)
    inner_sum = jnp.sum(
        do_h.astype(F32) * o.reshape(span, share, hd).astype(F32), axis=-1, keepdims=True
    )

    def widen(values, extra):
        cols = list(split3(extra))
        pad = jnp.zeros(values.shape[:-1] + (hd - len(cols),), BF16)
        return jnp.concatenate([values] + cols + [pad], axis=-1)

    qx = widen(qs, -weight.reshape(span, share, hd)[:, :, :1]).reshape(span, 2 * gcols)
    gx = widen(do_h, -inner_sum).reshape(span, 2 * gcols)
    ones = jnp.ones_like(kn)
    dq_rot, dk_rot, dv = attend_back(
        qx, jnp.concatenate([kn, ones], axis=1), jnp.concatenate([v, ones], axis=1), gx, start
    )
    dq, query_gain_part = query_pullback(dq_rot.reshape(span, share, hd) * scale)
    dk, key_gain_part = key_pullback(dk_rot * (1.0 / LOG2E))
    dqkv = jnp.concatenate(
        [dq.reshape(span, gcols).astype(BF16), dk.astype(BF16), dv.astype(BF16)], axis=1
    )
    qkv_part = dot(h1_all, dqkv, TN).astype(BF16)
    dh1 = scatter_seq(dot(dqkv, w_qkv, NT).astype(BF16).reshape(count, tok, dim), count, 8)
    xh1 = x * r1
    dn1 = dh1 * g_attn
    input_grad = dx2 + r1 * (dn1 - xh1 * jnp.mean(dn1 * xh1, axis=-1, keepdims=True))

    def sum_fsdp(part, axis):
        return lax.psum_scatter(part.astype(BF16), "fsdp", scatter_dimension=axis, tiled=True)

    w_gate_grad = sum_fsdp(w_gate_part, 0).astype(F32)
    w_up_grad = sum_fsdp(w_up_part, 0).astype(F32)
    w_down_grad = sum_fsdp(w_down_part, 1).astype(F32)

    small_part = jnp.concatenate(
        [
            router_part.reshape(shards, -1),
            mlp_gain_part.reshape(shards, -1),
            query_gain_part.reshape(shards, -1),
            key_gain_part.reshape(shards, -1),
        ],
        axis=1,
    )
    small_sum = lax.psum(sum_fsdp(small_part, 0), "seq").astype(F32)[0]
    router_grad, mlp_gain_grad, query_gain_grad, key_gain_grad = jnp.split(
        small_sum,
        [local_dim * experts, local_dim * (experts + 1), local_dim * (experts + 1) + local_hd],
    )
    router_grad = router_grad.reshape(local_dim, experts)

    out_sum = jnp.sum(
        lax.all_gather(w_out_part, "fsdp", axis=0, tiled=False).astype(F32), axis=0
    ).astype(BF16)
    pair = lax.all_gather(
        out_sum,
        "seq",
        axis=0,
        tiled=False,
        axis_index_groups=[[2 * c, 2 * c + 1] for c in range(chips)],
    )
    w_out_grad = out_rows(pair, out_sum, count, shards, tok)

    qkv_sum = sum_fsdp(qkv_part, 0)
    qkv_all = gather_seq(qkv_sum, count, 10)
    order = [(g % chips) * 2 + g // chips for g in range(count)]
    qkv_groups = qkv_all[jnp.array(order)].astype(F32)
    w_query_grad = jnp.swapaxes(qkv_groups[:, :, :gcols], 0, 1).reshape(local_dim, heads * hd)
    kv_groups = qkv_groups[:, :, gcols:].reshape(kv_heads, count // kv_heads, local_dim, 2 * hd)
    kv_groups = jnp.swapaxes(jnp.sum(kv_groups, axis=1), 0, 1)
    w_key_grad = kv_groups[:, :, :hd].reshape(local_dim, kv_heads * hd)
    w_value_grad = kv_groups[:, :, hd:].reshape(local_dim, kv_heads * hd)
    attn_gain_grad = (
        jnp.sum(w_query.astype(F32) * w_query_grad, axis=1)
        + jnp.sum(key_weight.astype(F32) * w_key_grad, axis=1)
        + jnp.sum(value_weight.astype(F32) * w_value_grad, axis=1)
    ) / attn_gain.astype(F32)
    return (
        mixed.astype(BF16)[None],
        input_grad[None],
        attn_gain_grad,
        mlp_gain_grad,
        query_gain_grad,
        key_gain_grad,
        w_query_grad,
        w_key_grad,
        w_value_grad,
        w_out_grad,
        router_grad,
        w_gate_grad[None],
        w_up_grad[None],
        w_down_grad[None],
    )


def out_rows(pair, out_sum, count, shards, tok):
    chips = count // 2
    gcols, dim = out_sum.shape
    me = lax.axis_index("seq")
    mine = lax.axis_index("fsdp")
    if shards == 2:
        half = lax.dynamic_slice(
            pair, (mine, (me % 2) * (gcols // 2), 0), (1, gcols // 2, dim)
        )[0]
        return gather_seq(half, count, 9).reshape(chips * gcols, dim).astype(F32)
    groups = count // shards
    first = mine * groups
    group = (me % 2) * chips + me // 2
    place = jnp.clip(group - first, 0, groups - 1)
    keep = (group >= first) & (group < first + groups)
    rows = jnp.where(keep, out_sum, jnp.zeros_like(out_sum))
    blank = jnp.zeros((groups * gcols, dim), BF16)
    return lax.psum(lax.dynamic_update_slice(blank, rows, (place * gcols, 0)), "seq").astype(F32)


def solution(mesh):
    tokens = P("fsdp", "seq", None)
    rows = P("fsdp", None)
    vector = P("fsdp")
    expert_rows = P("seq", "fsdp", None)
    expert_columns = P("seq", None, "fsdp")
    return jax.shard_map(
        per_device,
        mesh=mesh,
        in_specs=(tokens, tokens, rows, tokens)
        + (vector,) * 4
        + (rows,) * 5
        + (expert_rows, expert_rows, expert_columns),
        out_specs=(tokens, tokens)
        + (vector,) * 4
        + (rows,) * 5
        + (expert_rows, expert_rows, expert_columns),
        check_vma=False,
    )
```

```python
import functools
import math

import jax
import jax.numpy as jnp
from jax import lax
from jax.experimental import pallas as pl
from jax.experimental.pallas import tpu as pltpu
from jax.sharding import PartitionSpec as P

EPSILON = 1e-06
THETA = 1000000.0
BF16 = jnp.bfloat16
F32 = jnp.float32
MESH = pl.DeviceIdType.MESH
MIB = 1 << 20
LOG2E = math.log2(math.e)


def ring_of(chip, chips):
    return (chip % 2) * (chips - 1 - chip // 2) + (1 - chip % 2) * (chip // 2)


def chip_of(position, chips):
    upper = position // (chips // 2)
    return (1 - upper) * (2 * position) + upper * (2 * (chips - 1 - position) + 1)


def places(count):
    me = lax.axis_index("seq")
    chips = count // 2
    lane = me % 2
    position = ring_of(me // 2, chips)
    step = 1 - 2 * lane
    following = chip_of((position + step + chips) % chips, chips) * 2 + lane
    previous = chip_of((position - step + chips) % chips, chips) * 2 + lane
    sibling = me + 1 - 2 * lane
    return me, chips, lane, position, step, following, previous, sibling


def greet(senders):
    barrier = pltpu.get_barrier_semaphore()
    for device in senders:
        pl.semaphore_signal(barrier, inc=1, device_id={"seq": device}, device_id_type=MESH)
    pl.semaphore_wait(barrier, len(senders))


def row_parts(rows, cuts):
    if cuts == 1:
        return [pl.ds(0, rows)]
    size = rows // cuts // 16 * 16
    return [pl.ds(c * size, size) for c in range(cuts - 1)] + [
        pl.ds((cuts - 1) * size, rows - (cuts - 1) * size)
    ]


def gather_kernel(count, cuts, *refs):
    arrays = len(cuts)
    x_refs, o_refs = refs[:arrays], refs[arrays : 2 * arrays]
    own_sem, ring_out, ring_in, side_out, side_in = refs[2 * arrays :]
    me, chips, lane, position, step, following, previous, sibling = places(count)
    greet((previous, sibling))
    pieces = []
    for a in range(arrays):
        pieces += [(x_refs[a], o_refs[a], part) for part in row_parts(x_refs[a].shape[0], cuts[a])]

    def hop(c, owner, s, device, out_sem, in_sem, first):
        x_ref, o_ref, part = pieces[c]
        return pltpu.make_async_remote_copy(
            src_ref=x_ref.at[part] if first else o_ref.at[owner, part],
            dst_ref=o_ref.at[owner, part],
            send_sem=out_sem.at[s, c],
            recv_sem=in_sem.at[s, c],
            device_id={"seq": device},
            device_id_type=MESH,
        )

    def ring(c, owner, s, first=False):
        return hop(c, owner, s, following, ring_out, ring_in, first)

    def side(c, owner, s, first=False):
        return hop(c, owner, s, sibling, side_out, side_in, first)

    own = [
        pltpu.make_async_copy(x_refs[a], o_refs[a].at[me], own_sem.at[a]) for a in range(arrays)
    ]
    for copy in own:
        copy.start()
    for c in range(len(pieces)):
        ring(c, me, 0, True).start()
        side(c, me, 0, True).start()
    for s in range(1, chips):
        owner = chip_of((position - s * step + chips) % chips, chips) * 2 + lane
        for c in range(len(pieces)):
            ring(c, owner, s - 1).wait_recv()
            if s < chips - 1:
                ring(c, owner, s).start()
            side(c, owner, s).start()
    for s in range(chips):
        for c in range(len(pieces)):
            side(c, me, s).wait()
            if s < chips - 1:
                ring(c, me, s).wait_send()
    for copy in own:
        copy.wait()


def gather_seq(arrays, count, call, cuts):
    chips = count // 2
    anywhere = pl.BlockSpec(memory_space=pl.ANY)
    return pl.pallas_call(
        functools.partial(gather_kernel, count, cuts),
        out_shape=[jax.ShapeDtypeStruct((count,) + x.shape, x.dtype) for x in arrays],
        in_specs=[anywhere] * len(arrays),
        out_specs=[anywhere] * len(arrays),
        scratch_shapes=[pltpu.SemaphoreType.DMA((len(arrays),))]
        + [pltpu.SemaphoreType.DMA((chips, sum(cuts)))] * 4,
        compiler_params=pltpu.CompilerParams(collective_id=call, has_side_effects=True),
    )(*arrays)


def scatter_kernel(
    count, cuts, p_ref, o_ref, own, sent, came, given, own_sem, ring_out, ring_in, side_out, side_in
):
    me, chips, lane, position, step, following, previous, sibling = places(count)
    rows = p_ref.shape[1] // cuts
    greet((previous, sibling))

    def my_block(k):
        return chip_of((position - (k + 1) * step + 2 * chips) % chips, chips) * 2 + lane

    def sibling_block(k):
        return chip_of((position + (k + 1) * step + 2 * chips) % chips, chips) * 2 + 1 - lane

    def ring(k, c):
        return pltpu.make_async_remote_copy(
            src_ref=sent.at[k, pl.ds(c * rows, rows)],
            dst_ref=came.at[k, pl.ds(c * rows, rows)],
            send_sem=ring_out.at[k, c],
            recv_sem=ring_in.at[k, c],
            device_id={"seq": following},
            device_id_type=MESH,
        )

    def side(k):
        return pltpu.make_async_remote_copy(
            src_ref=p_ref.at[sibling_block(k)],
            dst_ref=given.at[k],
            send_sem=side_out.at[k],
            recv_sem=side_in.at[k],
            device_id={"seq": sibling},
            device_id_type=MESH,
        )

    def load(k):
        return pltpu.make_async_copy(p_ref.at[my_block(k)], own.at[k], own_sem.at[k])

    for k in range(chips):
        side(k).start()
        load(k).start()
    for k in range(chips):
        load(k).wait()
        side(k).wait_recv()
        for c in range(cuts):
            part = pl.ds(c * rows, rows)
            total = own[k, part].astype(F32) + given[k, part].astype(F32)
            if k > 0:
                ring(k - 1, c).wait_recv()
                total = total + came[k - 1, part].astype(F32)
            if k < chips - 1:
                sent[k, part] = total.astype(BF16)
                ring(k, c).start()
            else:
                o_ref[part] = total
    for k in range(chips):
        side(k).wait_send()
        if k < chips - 1:
            for c in range(cuts):
                ring(k, c).wait_send()


def scatter_seq(p, count, call, cuts=2):
    chips = count // 2
    _, rows, columns = p.shape
    return pl.pallas_call(
        functools.partial(scatter_kernel, count, cuts),
        out_shape=jax.ShapeDtypeStruct((rows, columns), F32),
        in_specs=[pl.BlockSpec(memory_space=pl.ANY)],
        out_specs=pl.BlockSpec(memory_space=pltpu.VMEM),
        scratch_shapes=[
            pltpu.VMEM((chips, rows, columns), BF16),
            pltpu.VMEM((chips - 1, rows, columns), BF16),
            pltpu.VMEM((chips - 1, rows, columns), BF16),
            pltpu.VMEM((chips, rows, columns), BF16),
            pltpu.SemaphoreType.DMA((chips,)),
            pltpu.SemaphoreType.DMA((chips, cuts)),
            pltpu.SemaphoreType.DMA((chips, cuts)),
            pltpu.SemaphoreType.DMA((chips,)),
            pltpu.SemaphoreType.DMA((chips,)),
        ],
        compiler_params=pltpu.CompilerParams(
            collective_id=call, has_side_effects=True, vmem_limit_bytes=48 * MIB
        ),
    )(p)


NT = (((1,), (1,)), ((), ()))
TN = (((0,), (0,)), ((), ()))


def split3(x):
    first = x.astype(BF16)
    rest = x - first.astype(F32)
    second = rest.astype(BF16)
    return first, second, (rest - second.astype(F32)).astype(BF16)


def in_lanes(x):
    lane = lax.broadcasted_iota(jnp.int32, x.shape, 1)
    first = x.astype(BF16).astype(F32)
    second = (x - first).astype(BF16).astype(F32)
    third = x - first - second
    spread = jnp.where(lane == 0, first, jnp.where(lane == 1, second, third))
    return jnp.where(lane < 3, spread, 0.0).astype(BF16)


def swap_halves(x):
    half = x.shape[1] // 2
    return jnp.concatenate([x[:, half:], x[:, :half]], axis=1)


def unit_rows(u):
    r = lax.rsqrt(jnp.mean(u * u, axis=1, keepdims=True) + EPSILON)
    return r, u * r


def attend_kernel(
    heads, tile, qkv_ref, gq_ref, gk_ref, cos_ref, sin_ref, start_ref, o_ref, qx_ref, kn_ref, vx_ref
):
    span = qkv_ref.shape[0]
    width = kn_ref.shape[1]
    scale = width**-0.5 * LOG2E
    for i in range(span // tile):
        rows = pl.ds(i * tile, tile)
        cos, sin = cos_ref[rows, :], sin_ref[rows, :]
        for h in range(heads + 1):
            _, unit = unit_rows(qkv_ref[rows, pl.ds(h * width, width)].astype(F32))
            u = unit * (gk_ref[...] if h == heads else gq_ref[...])
            u = u * cos + swap_halves(u) * sin
            if h == heads:
                kn_ref[rows, :] = u.astype(BF16)
            else:
                qx_ref[rows, pl.ds(2 * h * width, width)] = (u * scale).astype(BF16)
        vx_ref[rows, :width] = qkv_ref[rows, pl.ds((heads + 1) * width, width)]
        vx_ref[rows, width:] = jnp.ones((tile, width), BF16)
    for i in range(span // tile):
        rows = pl.ds(i * tile, tile)
        start = start_ref[rows, :]
        row = i * tile + lax.broadcasted_iota(jnp.int32, (tile, tile), 0)
        for h in range(heads):
            q = qx_ref[rows, pl.ds(2 * h * width, width)]
            total = jnp.zeros((tile, 2 * width), F32)
            for j in range(i + 1):
                keys = pl.ds(j * tile, tile)
                s = lax.dot_general(q, kn_ref[keys, :], NT, preferred_element_type=F32)
                col = j * tile + lax.broadcasted_iota(jnp.int32, (tile, tile), 1)
                keep = col >= start
                if i == j:
                    keep = keep & (col <= row)
                p = jnp.where(keep, jnp.exp2(s), 0.0).astype(BF16)
                total = total + jnp.dot(p, vx_ref[keys, :], preferred_element_type=F32)
            weight = total[:, width:]
            o_ref[rows, pl.ds(h * width, width)] = (total[:, :width] / weight).astype(BF16)
            qx_ref[rows, pl.ds((2 * h + 1) * width, width)] = in_lanes(-jnp.log2(weight))


def attend(qkv, gq, gk, cos, sin, start, tile=512):
    span = qkv.shape[0]
    width = gq.shape[0]
    heads = qkv.shape[1] // width - 2
    vmem = pl.BlockSpec(memory_space=pltpu.VMEM)
    return pl.pallas_call(
        functools.partial(attend_kernel, heads, min(tile, span)),
        out_shape=(
            jax.ShapeDtypeStruct((span, heads * width), BF16),
            jax.ShapeDtypeStruct((span, 2 * heads * width), BF16),
            jax.ShapeDtypeStruct((span, width), BF16),
        ),
        in_specs=[vmem] * 6,
        out_specs=[vmem] * 3,
        scratch_shapes=[pltpu.VMEM((span, 2 * width), BF16)],
        compiler_params=pltpu.CompilerParams(vmem_limit_bytes=48 * MIB),
    )(qkv, gq[None, :], gk[None, :], cos, sin, start[:, None])


def attend_back_kernel(
    heads,
    tile,
    qx_ref,
    kn_ref,
    qkv_ref,
    o_ref,
    do_ref,
    gq_ref,
    gk_ref,
    cos_ref,
    sin_ref,
    start_ref,
    dqkv_ref,
    gains_ref,
    gx_ref,
    dq_ref,
):
    span = qx_ref.shape[0]
    width = kn_ref.shape[1]
    scale = width**-0.5
    ones = jnp.ones((tile, width), BF16)

    def to_raw(d, h, rows, gain):
        r, unit = unit_rows(qkv_ref[rows, pl.ds(h * width, width)].astype(F32))
        d = d * cos_ref[rows, :] + swap_halves(d * sin_ref[rows, :])
        dg = d * gain
        raw = r * (dg - unit * jnp.mean(dg * unit, axis=1, keepdims=True))
        dqkv_ref[rows, pl.ds(h * width, width)] = raw.astype(BF16)
        return jnp.sum(d * unit, axis=0, keepdims=True)

    for i in range(span // tile):
        rows = pl.ds(i * tile, tile)
        for h in range(heads):
            cols = pl.ds(h * width, width)
            do = do_ref[rows, cols]
            inner = jnp.sum(do.astype(F32) * o_ref[rows, cols].astype(F32), axis=1, keepdims=True)
            gx_ref[rows, pl.ds(2 * h * width, width)] = do
            gx_ref[rows, pl.ds((2 * h + 1) * width, width)] = in_lanes(
                jnp.broadcast_to(-inner, (tile, width))
            )
    dq_ref[...] = jnp.zeros_like(dq_ref)
    key_gain = jnp.zeros((1, width), F32)
    for j in range(span // tile):
        keys = pl.ds(j * tile, tile)
        kn = kn_ref[keys, :]
        kx = jnp.concatenate([kn, ones], axis=1)
        vx = jnp.concatenate([qkv_ref[keys, pl.ds((heads + 1) * width, width)], ones], axis=1)
        dk = jnp.zeros((tile, width), F32)
        dv = jnp.zeros((tile, width), F32)
        key = j * tile + lax.broadcasted_iota(jnp.int32, (tile, tile), 0)
        for i in range(j, span // tile):
            rows = pl.ds(i * tile, tile)
            keep = key >= start_ref[:, rows]
            if i == j:
                row = i * tile + lax.broadcasted_iota(jnp.int32, (tile, tile), 1)
                keep = keep & (key <= row)
            for h in range(heads):
                qx = qx_ref[rows, pl.ds(2 * h * width, 2 * width)]
                gx = gx_ref[rows, pl.ds(2 * h * width, 2 * width)]
                s = lax.dot_general(kx, qx, NT, preferred_element_type=F32)
                p = jnp.where(keep, jnp.exp2(s), 0.0)
                dp = lax.dot_general(vx, gx, NT, preferred_element_type=F32)
                ds = (p * dp).astype(BF16)
                dv = dv + jnp.dot(p.astype(BF16), gx[:, :width], preferred_element_type=F32)
                dk = dk + jnp.dot(ds, qx[:, :width], preferred_element_type=F32)
                dq_ref[rows, pl.ds(h * width, width)] += lax.dot_general(
                    ds, kn, TN, preferred_element_type=F32
                )
        dqkv_ref[keys, pl.ds((heads + 1) * width, width)] = dv.astype(BF16)
        key_gain = key_gain + to_raw(dk * (1.0 / LOG2E), heads, keys, gk_ref[...])
    query_gain = jnp.zeros((1, width), F32)
    for i in range(span // tile):
        rows = pl.ds(i * tile, tile)
        for h in range(heads):
            dq = dq_ref[rows, pl.ds(h * width, width)] * scale
            query_gain = query_gain + to_raw(dq, h, rows, gq_ref[...])
    gains_ref[0:1, :] = query_gain
    gains_ref[1:2, :] = key_gain


def attend_back(qx, kn, qkv, o, do, gq, gk, cos, sin, start, tile=512):
    span, width = kn.shape
    heads = o.shape[1] // width
    vmem = pl.BlockSpec(memory_space=pltpu.VMEM)
    return pl.pallas_call(
        functools.partial(attend_back_kernel, heads, min(tile, span)),
        out_shape=(
            jax.ShapeDtypeStruct(qkv.shape, BF16),
            jax.ShapeDtypeStruct((2, width), F32),
        ),
        in_specs=[vmem] * 10,
        out_specs=[vmem] * 2,
        scratch_shapes=[
            pltpu.VMEM((span, 2 * heads * width), BF16),
            pltpu.VMEM((span, heads * width), F32),
        ],
        compiler_params=pltpu.CompilerParams(vmem_limit_bytes=56 * MIB),
    )(qx, kn, qkv, o, do, gq[None, :], gk[None, :], cos, sin, start[None, :])


def last_gather_kernel(
    count, members, cuts, q_ref, kv_ref, q_all, kv_all, heap, kv_sum, sems, own_sem, mo, mi, ro, ri, so, si
):
    me, chips, lane, position, step, following, previous, sibling = places(count)
    chip = me // 2
    place = chip % members
    first = chip - place
    rows = kv_sum.shape[0]

    def member(i):
        return (first + (place + i) % members) * 2 + lane

    greet([previous, sibling] + [member(i) for i in range(1, members)])

    def give(i):
        target = (place + i) % members
        return pltpu.make_async_remote_copy(
            src_ref=kv_ref.at[pl.ds(target * rows, rows)],
            dst_ref=heap.at[i - 1],
            send_sem=mo.at[i - 1],
            recv_sem=mi.at[i - 1],
            device_id={"seq": member(i)},
            device_id_type=MESH,
        )

    pieces = [(q_ref, q_all, part) for part in row_parts(q_ref.shape[0], cuts)]
    pieces.append((kv_sum, kv_all, pl.ds(0, rows)))

    def hop(c, owner, s, device, out_sem, in_sem, first_hop):
        x_ref, o_ref, part = pieces[c]
        return pltpu.make_async_remote_copy(
            src_ref=x_ref.at[part] if first_hop else o_ref.at[owner, part],
            dst_ref=o_ref.at[owner, part],
            send_sem=out_sem.at[s, c],
            recv_sem=in_sem.at[s, c],
            device_id={"seq": device},
            device_id_type=MESH,
        )

    def ring(c, owner, s, first_hop=False):
        return hop(c, owner, s, following, ro, ri, first_hop)

    def side(c, owner, s, first_hop=False):
        return hop(c, owner, s, sibling, so, si, first_hop)

    for i in range(1, members):
        give(i).start()
    mine = pltpu.make_async_copy(kv_ref.at[pl.ds(place * rows, rows)], kv_sum, own_sem.at[0])
    mine.start()
    own_q = pltpu.make_async_copy(q_ref, q_all.at[me], own_sem.at[1])
    own_q.start()
    for c in range(cuts):
        ring(c, me, 0, True).start()
        side(c, me, 0, True).start()
    mine.wait()
    total = kv_sum[...].astype(F32)
    for i in range(1, members):
        give(i).wait_recv()
        total = total + heap[i - 1].astype(F32)
    kv_sum[...] = total.astype(BF16)
    own_kv = pltpu.make_async_copy(kv_sum, kv_all.at[me], own_sem.at[2])
    own_kv.start()
    ring(cuts, me, 0, True).start()
    side(cuts, me, 0, True).start()
    for s in range(1, chips):
        owner = chip_of((position - s * step + chips) % chips, chips) * 2 + lane
        for c in range(cuts + 1):
            ring(c, owner, s - 1).wait_recv()
            if s < chips - 1:
                ring(c, owner, s).start()
            side(c, owner, s).start()
    for i in range(1, members):
        give(i).wait_send()
    for s in range(chips):
        for c in range(cuts + 1):
            side(c, me, s).wait()
            if s < chips - 1:
                ring(c, me, s).wait_send()
    own_q.wait()
    own_kv.wait()


def last_gather(q, kv, count, members, call, cuts=4):
    chips = count // 2
    rows = kv.shape[0] // members
    anywhere = pl.BlockSpec(memory_space=pl.ANY)
    dma = pltpu.SemaphoreType.DMA
    return pl.pallas_call(
        functools.partial(last_gather_kernel, count, members, cuts),
        out_shape=(
            jax.ShapeDtypeStruct((count,) + q.shape, BF16),
            jax.ShapeDtypeStruct((count, rows, kv.shape[1]), BF16),
        ),
        in_specs=[anywhere] * 2,
        out_specs=[anywhere] * 2,
        scratch_shapes=[
            pltpu.VMEM((members - 1, rows, kv.shape[1]), BF16),
            pltpu.VMEM((rows, kv.shape[1]), BF16),
            dma,
            dma((3,)),
            dma((members - 1,)),
            dma((members - 1,)),
        ]
        + [dma((chips, cuts + 1))] * 4,
        compiler_params=pltpu.CompilerParams(collective_id=call, has_side_effects=True),
    )(q, kv)


def finish_kernel(
    count, kv_heads, tile, q_ref, kv_ref, wq_ref, wk_ref, wv_ref, gain_ref, dq_ref, dk_ref, dv_ref, dg_ref
):
    chips = count // 2
    members = count // kv_heads
    width = q_ref.shape[2]
    hd = kv_ref.shape[2] // 2
    member = pl.program_id(0) * members // pl.num_programs(0)

    def place(group):
        return (group % chips) * 2 + group // chips

    total = jnp.zeros((tile, 1), F32)
    for g in range(count):
        cols = pl.ds(g * width, width)
        grad = q_ref[place(g)].astype(F32)
        dq_ref[:, cols] = grad
        total += jnp.sum(grad * wq_ref[:, cols].astype(F32), axis=1, keepdims=True)
    for j in range(kv_heads):
        cols = pl.ds(j * hd, hd)
        pair = kv_ref[place(j * members + member)].astype(F32)
        dk_ref[:, cols] = pair[:, :hd]
        dv_ref[:, cols] = pair[:, hd:]
        total += jnp.sum(pair[:, :hd] * wk_ref[:, cols].astype(F32), axis=1, keepdims=True)
        total += jnp.sum(pair[:, hd:] * wv_ref[:, cols].astype(F32), axis=1, keepdims=True)
    dg_ref[...] = total / gain_ref[...].astype(F32)


def finish(q_all, kv_all, w_query, key_weight, value_weight, gain, kv_heads):
    count = q_all.shape[0]
    local, columns = w_query.shape
    rows = kv_all.shape[1]
    tile = min(128, rows)
    per = rows // tile
    kv_columns = key_weight.shape[1]

    def row_block(n):
        return pl.BlockSpec((tile, n), lambda r: (r, 0))

    return pl.pallas_call(
        functools.partial(finish_kernel, count, kv_heads, tile),
        grid=(local // tile,),
        out_shape=(
            jax.ShapeDtypeStruct((local, columns), F32),
            jax.ShapeDtypeStruct((local, kv_columns), F32),
            jax.ShapeDtypeStruct((local, kv_columns), F32),
            jax.ShapeDtypeStruct((local, 1), F32),
        ),
        in_specs=[
            pl.BlockSpec((count, tile, q_all.shape[2]), lambda r: (0, r, 0)),
            pl.BlockSpec((count, tile, kv_all.shape[2]), lambda r: (0, r % per, 0)),
            row_block(columns),
            row_block(kv_columns),
            row_block(kv_columns),
            row_block(1),
        ],
        out_specs=[row_block(columns), row_block(kv_columns), row_block(kv_columns), row_block(1)],
        compiler_params=pltpu.CompilerParams(vmem_limit_bytes=48 * MIB),
    )(q_all, kv_all, w_query, key_weight, value_weight, gain[:, None])


def run_starts(segment):
    position = jnp.arange(segment.shape[0], dtype=jnp.int32)
    fresh = jnp.concatenate([jnp.ones((1,), dtype=bool), segment[1:] != segment[:-1]])
    return position, lax.cummax(jnp.where(fresh, position, jnp.zeros_like(position)), axis=0)


def angles(offset, head_size):
    frequency = jnp.exp(
        jnp.arange(head_size // 2, dtype=F32) * (-2.0 * math.log(THETA) / head_size)
    )
    phases = offset[:, None] * frequency[None, :]
    return jnp.cos(phases), jnp.sin(phases)


def dot(a, b, dims=(((1,), (0,)), ((), ()))):
    return lax.dot_general(a, b, dims, preferred_element_type=F32)


def per_device(
    activations,
    cotangent,
    segments,
    routing,
    attn_gain,
    mlp_gain,
    query_gain,
    key_gain,
    w_query,
    key_weight,
    value_weight,
    w_out,
    w_router,
    w_gate,
    w_up,
    w_down,
):
    count = lax.axis_size("seq")
    shards = lax.axis_size("fsdp")
    me = lax.axis_index("seq")
    chips = count // 2
    x = activations[0].astype(F32)
    dy = cotangent[0]
    segment = segments[0]
    routes = routing[0]
    tok, dim = x.shape
    span = segment.shape[0]
    top = routes.shape[1]
    hd = query_gain.shape[0] * shards
    heads = w_query.shape[1] // hd
    kv_heads = key_weight.shape[1] // hd
    share = heads // count
    experts = w_router.shape[1]
    local_rows = w_out.shape[0]
    capacity = tok * top * 9 // (8 * experts)
    group = (me % 2) * chips + me // 2
    gcols = share * hd
    kv_head = group * share // (heads // kv_heads)

    small = jnp.concatenate(
        [attn_gain, mlp_gain, query_gain, key_gain, w_router.reshape(-1)], axis=0
    )
    small = lax.all_gather(small, "fsdp", axis=0, tiled=False)
    local_dim = attn_gain.shape[0]
    local_hd = query_gain.shape[0]
    cut = [local_dim, 2 * local_dim, 2 * local_dim + local_hd, 2 * local_dim + 2 * local_hd]
    g_attn, g_mlp, g_query, g_key, router = jnp.split(small, cut, axis=1)
    g_attn = g_attn.reshape(-1).astype(F32)
    g_mlp = g_mlp.reshape(-1).astype(F32)
    g_query = g_query.reshape(-1).astype(F32)
    g_key = g_key.reshape(-1).astype(F32)
    router = router.reshape(dim, experts)
    qkv_local = jnp.concatenate(
        [
            lax.dynamic_slice_in_dim(w_query, group * gcols, gcols, 1),
            lax.dynamic_slice_in_dim(key_weight, kv_head * hd, hd, 1),
            lax.dynamic_slice_in_dim(value_weight, kv_head * hd, hd, 1),
        ],
        axis=1,
    )
    w_qkv = lax.all_gather(qkv_local, "fsdp", axis=0, tiled=True)
    first_row = group * gcols
    out_owner = first_row // local_rows
    out_local = lax.dynamic_slice_in_dim(w_out, first_row % local_rows, gcols, 0)
    w_o = lax.dynamic_index_in_dim(
        lax.all_gather(out_local, "fsdp", axis=0, tiled=False), out_owner, 0, keepdims=False
    )
    wg = lax.all_gather(w_gate[0], "fsdp", axis=0, tiled=True)
    wu = lax.all_gather(w_up[0], "fsdp", axis=0, tiled=True)
    wd = lax.all_gather(w_down[0], "fsdp", axis=1, tiled=True)

    r1 = lax.rsqrt(jnp.mean(x * x, axis=-1, keepdims=True) + EPSILON)
    h1 = (x * r1 * g_attn).astype(BF16)
    h1_all = gather_seq([h1], count, 1, (4,))[0].reshape(span, dim)
    qkv = dot(h1_all, w_qkv).astype(BF16)
    position, doc_start = run_starts(segment)
    cosine, sine = angles((position - doc_start).astype(F32), hd)
    start = jnp.where(segment > 0, doc_start, position)

    cos_full = jnp.concatenate([cosine, cosine], axis=1)
    sin_full = jnp.concatenate([-sine, sine], axis=1)
    o, qx, kn = attend(qkv, g_query, g_key, cos_full, sin_full, start)
    x2_parts = dot(o, w_o).astype(BF16).reshape(count, tok, dim)
    x2 = x + scatter_seq(x2_parts, count, 2)

    r2 = lax.rsqrt(jnp.mean(x2 * x2, axis=-1, keepdims=True) + EPSILON)
    h2 = (x2 * r2 * g_mlp).astype(BF16)
    h2_all = gather_seq([h2], count, 3, (4,))[0]
    dy_all, routes_all = gather_seq([dy, routes], count, 4, (4, 1))

    def gates_of(hidden, chosen):
        logits = dot(hidden, router)
        return jax.nn.softmax(jnp.where(chosen, logits, -1e30), axis=-1) * chosen

    def chosen_of(named):
        names = jnp.arange(experts, dtype=jnp.int32)
        return jnp.any(named[..., :, None] == names, axis=-2)

    hit = jnp.any(routes_all == me, axis=-1)
    rank = jnp.cumsum(hit.astype(jnp.int32), axis=1) - hit
    slots = jnp.arange(capacity, dtype=jnp.int32)
    pick = hit[:, None, :] & (rank[:, None, :] == slots[None, :, None])
    one_hot = pick.astype(BF16)
    gates_all = gates_of(h2_all.reshape(span, dim), chosen_of(routes_all.reshape(span, top)))
    gate_tok = lax.dynamic_index_in_dim(gates_all, me, 1, keepdims=False).reshape(count, tok)
    gate_slot = jnp.sum(jnp.where(pick, gate_tok[:, None, :], 0.0), axis=-1).reshape(-1, 1)

    def to_slots(rows):
        return (
            jnp.einsum("bri,bid->brd", one_hot, rows, preferred_element_type=F32)
            .astype(BF16)
            .reshape(count * capacity, dim)
        )

    def to_tokens(rows):
        return jnp.einsum(
            "bri,brd->bid",
            one_hot,
            rows.reshape(count, capacity, dim),
            preferred_element_type=F32,
        )

    xs = to_slots(h2_all)
    dys = to_slots(dy_all)
    gate_act = dot(xs, wg)
    up_act = dot(xs, wu)
    sig = jax.nn.sigmoid(gate_act)
    silu = gate_act * sig
    inner = (silu * up_act).astype(BF16)
    e_out = dot(inner, wd)
    mixed_parts = to_tokens((gate_slot * e_out).astype(BF16)).astype(BF16)
    mixed = x2 + scatter_seq(mixed_parts, count, 5)

    dgate_slot = jnp.sum(dys.astype(F32) * e_out, axis=-1).reshape(count, capacity)
    dgate_tok = jnp.sum(jnp.where(pick, dgate_slot[:, :, None], 0.0), axis=1)
    de = (gate_slot * dys.astype(F32)).astype(BF16)
    dinner = dot(de, wd, NT)
    dg = (dinner * up_act * (sig + silu * (1.0 - sig))).astype(BF16)
    du = (dinner * silu).astype(BF16)
    w_down_part = dot(inner, de, TN)
    w_gate_part = dot(xs, dg, TN)
    w_up_part = dot(xs, du, TN)
    dxs = (dot(dg, wg, NT) + dot(du, wu, NT)).astype(BF16)
    own_lane = (jnp.arange(128, dtype=jnp.int32) == me)[None, None, :]
    dgate_hi, dgate_lo, _ = split3(dgate_tok[:, :, None])
    zero = jnp.zeros((), BF16)
    lanes = jnp.where(own_lane, dgate_hi, zero) + jnp.where(
        jnp.roll(own_lane, 64, axis=-1), dgate_lo, zero
    )
    dh2_parts = jnp.concatenate([to_tokens(dxs).astype(BF16), lanes], axis=2)
    dh2_wide = scatter_seq(dh2_parts, count, 6)
    dgate = dh2_wide[:, dim : dim + experts] + dh2_wide[:, dim + 64 : dim + 64 + experts]
    gates = gates_of(h2, chosen_of(routes))
    dlogits = (gates * (dgate - jnp.sum(gates * dgate, axis=-1, keepdims=True))).astype(BF16)
    dh2 = dh2_wide[:, :dim] + dot(dlogits, router, NT)
    router_part = dot(h2, dlogits, TN)
    xh = x2 * r2
    mlp_gain_part = jnp.sum(dh2 * xh, axis=0)
    dn = dh2 * g_mlp
    dx2 = dy.astype(F32) + r2 * (dn - xh * jnp.mean(dn * xh, axis=-1, keepdims=True))

    da_all = gather_seq([dx2.astype(BF16)], count, 7, (4,))[0].reshape(span, dim)
    do = dot(da_all, w_o, NT).astype(BF16)
    w_out_part = dot(o, da_all, TN).astype(BF16)
    dqkv, head_gains = attend_back(
        qx, kn, qkv, o, do, g_query, g_key, cos_full, sin_full, start
    )
    qkv_part = dot(h1_all, dqkv, TN).astype(BF16)
    dh1 = scatter_seq(dot(dqkv, w_qkv, NT).astype(BF16).reshape(count, tok, dim), count, 8)
    xh1 = x * r1
    dn1 = dh1 * g_attn
    input_grad = dx2 + r1 * (dn1 - xh1 * jnp.mean(dn1 * xh1, axis=-1, keepdims=True))

    def sum_fsdp(part, axis):
        return lax.psum_scatter(part.astype(BF16), "fsdp", scatter_dimension=axis, tiled=True)

    w_gate_grad = sum_fsdp(w_gate_part, 0).astype(F32)
    w_up_grad = sum_fsdp(w_up_part, 0).astype(F32)
    w_down_grad = sum_fsdp(w_down_part, 1).astype(F32)

    small_part = jnp.concatenate(
        [router_part.reshape(shards, -1), mlp_gain_part.reshape(shards, -1)], axis=1
    )
    small_rows = -(-small_part.shape[1] // dim // 16) * 16
    small_part = jnp.pad(small_part, ((0, 0), (0, small_rows * dim - small_part.shape[1])))
    small_sum = sum_fsdp(small_part, 0).reshape(small_rows, dim)

    out_sum = jnp.sum(
        lax.all_gather(w_out_part, "fsdp", axis=0, tiled=False).astype(F32), axis=0
    ).astype(BF16)
    pair = lax.all_gather(
        out_sum,
        "seq",
        axis=0,
        tiled=False,
        axis_index_groups=[[2 * c, 2 * c + 1] for c in range(chips)],
    )
    w_out_grad, small_all = out_rows(pair, out_sum, small_sum, count, shards)
    small_total = jnp.sum(small_all.astype(F32), axis=0).reshape(-1)
    router_grad = small_total[: local_dim * experts].reshape(local_dim, experts)
    mlp_gain_grad = small_total[local_dim * experts : local_dim * (experts + 1)]

    gains_part = jnp.concatenate(
        [head_gains[0].reshape(shards, 1, local_hd), head_gains[1].reshape(shards, 1, local_hd)],
        axis=2,
    ).astype(BF16)
    gains_part = jnp.pad(
        gains_part, ((0, 0), (0, 15), (0, qkv_part.shape[1] - 2 * local_hd))
    )
    qkv_part = jnp.concatenate(
        [qkv_part.reshape(shards, local_dim, -1), gains_part], axis=1
    ).reshape(shards * (local_dim + 16), -1)
    qkv_sum = sum_fsdp(qkv_part, 0)
    q_all, kv_all = last_gather(
        qkv_sum[:, :gcols], qkv_sum[:local_dim, gcols:], count, count // kv_heads, 10
    )
    w_query_grad, w_key_grad, w_value_grad, attn_gain_grad = finish(
        q_all, kv_all, w_query, key_weight, value_weight, attn_gain, kv_heads
    )
    attn_gain_grad = attn_gain_grad[:, 0]
    head_gain_grads = jnp.sum(q_all[:, local_dim, : 2 * local_hd].astype(F32), axis=0)
    query_gain_grad = head_gain_grads[:local_hd]
    key_gain_grad = head_gain_grads[local_hd:]
    return (
        mixed.astype(BF16)[None],
        input_grad[None],
        attn_gain_grad,
        mlp_gain_grad,
        query_gain_grad,
        key_gain_grad,
        w_query_grad,
        w_key_grad,
        w_value_grad,
        w_out_grad,
        router_grad,
        w_gate_grad[None],
        w_up_grad[None],
        w_down_grad[None],
    )


def out_rows(pair, out_sum, small_sum, count, shards):
    chips = count // 2
    gcols, dim = out_sum.shape
    me = lax.axis_index("seq")
    mine = lax.axis_index("fsdp")
    if shards == 2:
        half = lax.dynamic_slice(pair, (mine, (me % 2) * (gcols // 2), 0), (1, gcols // 2, dim))[0]
        halves, small_all = gather_seq([half, small_sum], count, 9, (4, 1))
        return halves.reshape(chips * gcols, dim).astype(F32), small_all
    small_all = gather_seq([small_sum], count, 9, (1,))[0]
    groups = count // shards
    first = mine * groups
    group = (me % 2) * chips + me // 2
    place = jnp.clip(group - first, 0, groups - 1)
    keep = (group >= first) & (group < first + groups)
    rows = jnp.where(keep, out_sum, jnp.zeros_like(out_sum))
    blank = jnp.zeros((groups * gcols, dim), BF16)
    total = lax.psum(lax.dynamic_update_slice(blank, rows, (place * gcols, 0)), "seq")
    return total.astype(F32), small_all


def solution(mesh):
    tokens = P("fsdp", "seq", None)
    rows = P("fsdp", None)
    vector = P("fsdp")
    expert_rows = P("seq", "fsdp", None)
    expert_columns = P("seq", None, "fsdp")
    return jax.shard_map(
        per_device,
        mesh=mesh,
        in_specs=(tokens, tokens, rows, tokens)
        + (vector,) * 4
        + (rows,) * 5
        + (expert_rows, expert_rows, expert_columns),
        out_specs=(tokens, tokens)
        + (vector,) * 4
        + (rows,) * 5
        + (expert_rows, expert_rows, expert_columns),
        check_vma=False,
    )
```

```python
import functools
import math

import jax
import jax.numpy as jnp
from jax import lax
from jax.experimental import pallas as pl
from jax.experimental.pallas import tpu as pltpu
from jax.sharding import PartitionSpec as P

EPSILON = 1e-06
THETA = 1000000.0
BF16 = jnp.bfloat16
F32 = jnp.float32
MESH = pl.DeviceIdType.MESH
MIB = 1 << 20
LOG2E = math.log2(math.e)


def ring_of(chip, chips):
    return (chip % 2) * (chips - 1 - chip // 2) + (1 - chip % 2) * (chip // 2)


def chip_of(position, chips):
    upper = position // (chips // 2)
    return (1 - upper) * (2 * position) + upper * (2 * (chips - 1 - position) + 1)


def places(count):
    me = lax.axis_index("seq")
    chips = count // 2
    lane = me % 2
    position = ring_of(me // 2, chips)
    step = 1 - 2 * lane
    following = chip_of((position + step + chips) % chips, chips) * 2 + lane
    previous = chip_of((position - step + chips) % chips, chips) * 2 + lane
    sibling = me + 1 - 2 * lane
    return me, chips, lane, position, step, following, previous, sibling


def greet(senders):
    barrier = pltpu.get_barrier_semaphore()
    for device in senders:
        pl.semaphore_signal(barrier, inc=1, device_id={"seq": device}, device_id_type=MESH)
    pl.semaphore_wait(barrier, len(senders))


def row_parts(rows, cuts):
    if cuts == 1:
        return [pl.ds(0, rows)]
    size = rows // cuts // 16 * 16
    return [pl.ds(c * size, size) for c in range(cuts - 1)] + [
        pl.ds((cuts - 1) * size, rows - (cuts - 1) * size)
    ]


def gather_kernel(count, cuts, *refs):
    arrays = len(cuts)
    x_refs, o_refs = refs[:arrays], refs[arrays : 2 * arrays]
    own_sem, ring_out, ring_in, side_out, side_in = refs[2 * arrays :]
    me, chips, lane, position, step, following, previous, sibling = places(count)
    greet((previous, sibling))
    pieces = []
    for a in range(arrays):
        pieces += [(x_refs[a], o_refs[a], part) for part in row_parts(x_refs[a].shape[0], cuts[a])]

    def hop(c, owner, s, device, out_sem, in_sem, first):
        x_ref, o_ref, part = pieces[c]
        return pltpu.make_async_remote_copy(
            src_ref=x_ref.at[part] if first else o_ref.at[owner, part],
            dst_ref=o_ref.at[owner, part],
            send_sem=out_sem.at[s, c],
            recv_sem=in_sem.at[s, c],
            device_id={"seq": device},
            device_id_type=MESH,
        )

    def ring(c, owner, s, first=False):
        return hop(c, owner, s, following, ring_out, ring_in, first)

    def side(c, owner, s, first=False):
        return hop(c, owner, s, sibling, side_out, side_in, first)

    own = [
        pltpu.make_async_copy(x_refs[a], o_refs[a].at[me], own_sem.at[a]) for a in range(arrays)
    ]
    for copy in own:
        copy.start()
    for c in range(len(pieces)):
        ring(c, me, 0, True).start()
        side(c, me, 0, True).start()
    for s in range(1, chips):
        owner = chip_of((position - s * step + chips) % chips, chips) * 2 + lane
        for c in range(len(pieces)):
            ring(c, owner, s - 1).wait_recv()
            if s < chips - 1:
                ring(c, owner, s).start()
            side(c, owner, s).start()
    for s in range(chips):
        for c in range(len(pieces)):
            side(c, me, s).wait()
            if s < chips - 1:
                ring(c, me, s).wait_send()
    for copy in own:
        copy.wait()


def gather_seq(arrays, count, call, cuts):
    chips = count // 2
    anywhere = pl.BlockSpec(memory_space=pl.ANY)
    return pl.pallas_call(
        functools.partial(gather_kernel, count, cuts),
        out_shape=[jax.ShapeDtypeStruct((count,) + x.shape, x.dtype) for x in arrays],
        in_specs=[anywhere] * len(arrays),
        out_specs=[anywhere] * len(arrays),
        scratch_shapes=[pltpu.SemaphoreType.DMA((len(arrays),))]
        + [pltpu.SemaphoreType.DMA((chips, sum(cuts)))] * 4,
        compiler_params=pltpu.CompilerParams(collective_id=call, has_side_effects=True),
    )(*arrays)


NT = (((1,), (1,)), ((), ()))
TN = (((0,), (0,)), ((), ()))
NN = (((1,), (0,)), ((), ()))


def mm(a, b, dims=NN):
    return lax.dot_general(a, b, dims, preferred_element_type=F32)


def gather_steps(count, cuts, x_ref, land, sems, use):
    me, chips, lane, position, step, following, previous, sibling = places(count)
    ring_out, ring_in, side_out, side_in = sems
    block = x_ref.shape[0]
    rows = block // cuts
    greet((previous, sibling))

    def ring(s, c):
        part = pl.ds(c * rows, rows)
        return pltpu.make_async_remote_copy(
            src_ref=land.at[s, part],
            dst_ref=land.at[s + 1, part],
            send_sem=ring_out.at[s, c],
            recv_sem=ring_in.at[s, c],
            device_id={"seq": following},
            device_id_type=MESH,
        )

    def side(s, c):
        return pltpu.make_async_remote_copy(
            src_ref=land.at[s, pl.ds(c * rows, rows)],
            dst_ref=land.at[s, pl.ds(block + c * rows, rows)],
            send_sem=side_out.at[s, c],
            recv_sem=side_in.at[s, c],
            device_id={"seq": sibling},
            device_id_type=MESH,
        )

    land[0, :block] = x_ref[...]

    def one(s, carry):
        for c in range(cuts):

            @pl.when(s > 0)
            def _():
                ring(s - 1, c).wait_recv()

            @pl.when(s < chips - 1)
            def _():
                ring(s, c).start()

            side(s, c).start()
        for c in range(cuts):
            side(s, c).wait_recv()
        first = chip_of((position - s * step + chips) % chips, chips) * 2 + lane
        second = chip_of((position + s * step + chips) % chips, chips) * 2 + 1 - lane
        use(s, first, second)
        return carry

    lax.fori_loop(0, chips, one, 0)

    def close(s, carry):
        for c in range(cuts):
            side(s, c).wait_send()

            @pl.when(s < chips - 1)
            def _():
                ring(s, c).wait_send()

        return carry

    lax.fori_loop(0, chips, close, 0)


def gather_scratch(count, cuts, block, columns):
    chips = count // 2
    return [pltpu.VMEM((chips, 2 * block, columns), BF16)] + [
        pltpu.SemaphoreType.DMA((chips, cuts))
    ] * 4


def scatter_steps(count, cuts, o_ref, bufs, sems, produce, extra=None):
    me, chips, lane, position, step, following, previous, sibling = places(count)
    own, sent, came, give, given = bufs
    ring_out, ring_in, side_out, side_in = sems
    rows = own.shape[0] // cuts
    greet((previous, sibling))

    def ring(k, c):
        part = pl.ds(c * rows, rows)
        return pltpu.make_async_remote_copy(
            src_ref=sent.at[k, part],
            dst_ref=came.at[k, part],
            send_sem=ring_out.at[k, c],
            recv_sem=ring_in.at[k, c],
            device_id={"seq": following},
            device_id_type=MESH,
        )

    def side(k):
        return pltpu.make_async_remote_copy(
            src_ref=give.at[k],
            dst_ref=given.at[k],
            send_sem=side_out.at[k],
            recv_sem=side_in.at[k],
            device_id={"seq": sibling},
            device_id_type=MESH,
        )

    def one(k, carry):
        first = chip_of((position - (k + 1) * step + chips) % chips, chips) * 2 + lane
        second = chip_of((position + (k + 1) * step + chips) % chips, chips) * 2 + 1 - lane
        mine, theirs = produce(k, first, second)
        give[k] = theirs.astype(BF16)
        side(k).start()
        own[...] = mine
        side(k).wait_recv()
        for c in range(cuts):
            part = pl.ds(c * rows, rows)

            @pl.when(k > 0)
            def _():
                ring(k - 1, c).wait_recv()
                own[part] += came[k - 1, part].astype(F32)

            total = own[part] + given[k, part].astype(F32)

            @pl.when(k < chips - 1)
            def _():
                sent[k, part] = total.astype(BF16)
                ring(k, c).start()

            @pl.when(k == chips - 1)
            def _():
                o_ref[part] = total

        if extra is not None:
            extra(k)
        return carry

    lax.fori_loop(0, chips, one, 0)

    def close(k, carry):
        side(k).wait_send()

        @pl.when(k < chips - 1)
        def _():
            for c in range(cuts):
                ring(k, c).wait_send()

        return carry

    lax.fori_loop(0, chips, close, 0)


def scatter_scratch(count, cuts, rows, columns):
    chips = count // 2
    dma = pltpu.SemaphoreType.DMA
    return [
        pltpu.VMEM((rows, columns), F32),
        pltpu.VMEM((chips - 1, rows, columns), BF16),
        pltpu.VMEM((chips - 1, rows, columns), BF16),
        pltpu.VMEM((chips, rows, columns), BF16),
        pltpu.VMEM((chips, rows, columns), BF16),
        dma((chips, cuts)),
        dma((chips, cuts)),
        dma((chips,)),
        dma((chips,)),
    ]


def remote_params(call, mib):
    return pltpu.CompilerParams(
        collective_id=call, has_side_effects=True, vmem_limit_bytes=mib * MIB
    )


VMEM = pl.BlockSpec(memory_space=pltpu.VMEM)
ANY = pl.BlockSpec(memory_space=pl.ANY)


def project_kernel(count, cuts, h_ref, w_ref, all_ref, y_ref, land, *rest):
    sems, out_sem = rest[:4], rest[4]
    block = h_ref.shape[0]

    def out(s, owner, half):
        return pltpu.make_async_copy(
            land.at[s, pl.ds(half * block, block)],
            all_ref.at[pl.ds(pl.multiple_of(owner * block, block), block)],
            out_sem.at[half],
        )

    def use(s, first, second):
        out(s, first, 0).start()
        out(s, second, 1).start()
        y = mm(land[s], w_ref[...]).astype(BF16)
        y_ref[pl.ds(pl.multiple_of(first * block, block), block), :] = y[:block]
        y_ref[pl.ds(pl.multiple_of(second * block, block), block), :] = y[block:]

    gather_steps(count, cuts, h_ref, land, sems, use)
    half_rows = all_ref.shape[0] // 2
    for half in range(2):
        pltpu.make_async_copy(
            all_ref.at[pl.ds(0, half_rows)], all_ref.at[pl.ds(0, half_rows)], out_sem.at[half]
        ).wait()


def project_gathered(h, w, count, call, cuts=4):
    block, dim = h.shape
    return pl.pallas_call(
        functools.partial(project_kernel, count, cuts),
        out_shape=(
            jax.ShapeDtypeStruct((count * block, dim), BF16),
            jax.ShapeDtypeStruct((count * block, w.shape[1]), BF16),
        ),
        in_specs=[VMEM, VMEM],
        out_specs=[ANY, VMEM],
        scratch_shapes=gather_scratch(count, cuts, block, dim) + [pltpu.SemaphoreType.DMA((2,))],
        compiler_params=remote_params(call, 48),
    )(h, w)


def out_back_kernel(count, cuts, da_ref, w_ref, o_ref, do_ref, part_ref, land, *rest):
    sems, total = rest[:4], rest[4]
    block = da_ref.shape[0]
    total[...] = jnp.zeros_like(total)

    def use(s, first, second):
        pair = land[s]
        a = pl.ds(pl.multiple_of(first * block, block), block)
        b = pl.ds(pl.multiple_of(second * block, block), block)
        do = mm(pair, w_ref[...], NT).astype(BF16)
        do_ref[a, :] = do[:block]
        do_ref[b, :] = do[block:]
        total[...] += mm(jnp.concatenate([o_ref[a, :], o_ref[b, :]], axis=0), pair, TN)

    gather_steps(count, cuts, da_ref, land, sems, use)
    part_ref[...] = total[...].astype(BF16)


def out_back(da, w, o, count, call, cuts=4):
    block, dim = da.shape
    return pl.pallas_call(
        functools.partial(out_back_kernel, count, cuts),
        out_shape=(jax.ShapeDtypeStruct(o.shape, BF16), jax.ShapeDtypeStruct(w.shape, BF16)),
        in_specs=[VMEM] * 3,
        out_specs=[VMEM] * 2,
        scratch_shapes=gather_scratch(count, cuts, block, dim) + [pltpu.VMEM(w.shape, F32)],
        compiler_params=remote_params(call, 48),
    )(da, w, o)


def product_kernel(count, cuts, dims, y_ref, w_ref, o_ref, *rest):
    block = o_ref.shape[0]

    def produce(k, first, second):
        a = y_ref[pl.ds(pl.multiple_of(first * block, block), block), :]
        b = y_ref[pl.ds(pl.multiple_of(second * block, block), block), :]
        both = mm(jnp.concatenate([a, b], axis=0), w_ref[...], dims)
        return both[:block], both[block:]

    scatter_steps(count, cuts, o_ref, rest[:5], rest[5:], produce)


def product_scattered(y, w, dims, count, call, cuts=2):
    block = y.shape[0] // count
    columns = w.shape[1 - dims[0][1][0]]
    return pl.pallas_call(
        functools.partial(product_kernel, count, cuts, dims),
        out_shape=jax.ShapeDtypeStruct((block, columns), F32),
        in_specs=[VMEM, VMEM],
        out_specs=VMEM,
        scratch_shapes=scatter_scratch(count, cuts, block, columns),
        compiler_params=remote_params(call, 48),
    )(y, w)


def one_hot_of(slot_ref, first, second, capacity):
    a = slot_ref[pl.ds(first, 1), :]
    b = slot_ref[pl.ds(second, 1), :]
    wanted = jnp.concatenate([a, jnp.where(b >= 0, b + capacity, -1)], axis=1)
    row = lax.broadcasted_iota(jnp.int32, (2 * capacity, wanted.shape[1]), 0)
    return jnp.where(row == wanted, 1.0, 0.0).astype(BF16)


def expert_kernel(
    count,
    cuts,
    capacity,
    h_ref,
    slot_ref,
    chosen_ref,
    router_ref,
    dy_ref,
    wg_ref,
    wu_ref,
    wd_ref,
    xs_out,
    de_out,
    dx_out,
    ce_out,
    hid_out,
    dgu_out,
    land,
    ring_out,
    ring_in,
    side_out,
    side_in,
    wg,
    wu,
    wd,
    dyb,
    xs,
    de,
    dx,
    ce,
    hid,
    dgu,
    w_sem,
    dy_sem,
    out_sem,
):
    block, dim = h_ref.shape
    ffe = wg.shape[1]
    me, chips, lane, position, step, _, _, _ = places(count)
    weights = [
        pltpu.make_async_copy(src, dst, w_sem.at[i])
        for i, (src, dst) in enumerate(((wg_ref, wg), (wu_ref, wu), (wd_ref, wd)))
    ]
    staged = ((xs, xs_out), (de, de_out), (dx, dx_out), (ce, ce_out), (hid, hid_out), (dgu, dgu_out))

    def dy_copies(s):
        first = chip_of((position - s * step + chips) % chips, chips) * 2 + lane
        second = chip_of((position + s * step + chips) % chips, chips) * 2 + 1 - lane
        return [
            pltpu.make_async_copy(
                dy_ref.at[owner], dyb.at[s % 2, pl.ds(half * block, block)], dy_sem.at[s % 2, half]
            )
            for half, owner in ((0, first), (1, second))
        ]

    for copy in weights + dy_copies(0):
        copy.start()

    def use(s, first, second):
        @pl.when(s == 0)
        def _():
            for copy in weights:
                copy.wait()

        @pl.when(s < chips - 1)
        def _():
            for copy in dy_copies(s + 1):
                copy.start()

        for copy in dy_copies(s):
            copy.wait()
        rows = pl.ds(pl.multiple_of(s * 2 * capacity, 16), 2 * capacity)
        pick = one_hot_of(slot_ref, first, second, capacity)
        x = mm(pick, land[s]).astype(BF16)
        xs[rows, :] = x
        chosen = mm(
            pick,
            jnp.concatenate(
                [
                    chosen_ref[pl.ds(pl.multiple_of(first * block, block), block), :],
                    chosen_ref[pl.ds(pl.multiple_of(second * block, block), block), :],
                ],
                axis=0,
            ),
        )
        logits = jnp.where(chosen > 0.5, mm(x, router_ref[...]), -1e30)
        weight = jnp.exp(logits - jnp.max(logits, axis=1, keepdims=True)) * chosen
        mass = jnp.sum(weight, axis=1, keepdims=True)
        expert_lane = lax.broadcasted_iota(jnp.int32, weight.shape, 1)
        gate = jnp.sum(jnp.where(expert_lane == me, weight, 0.0), axis=1, keepdims=True)
        gate = gate / jnp.where(mass > 0.0, mass, 1.0)
        g = mm(x, wg[...])
        u = mm(x, wu[...])
        sig = jax.nn.sigmoid(g)
        silu = g * sig
        h = (silu * u).astype(BF16)
        hid[rows, :] = h
        e = mm(h, wd[...])
        ce[rows, :] = (gate * e).astype(BF16)
        dys = mm(pick, dyb[s % 2])
        dgate = jnp.sum(dys * e, axis=1, keepdims=True)
        d = (gate * dys).astype(BF16)
        de[rows, :] = d
        dh = mm(d, wd[...], NT)
        dg = (dh * u * (sig + silu * (1.0 - sig))).astype(BF16)
        du = (dh * silu).astype(BF16)
        dgu[rows, :ffe] = dg
        dgu[rows, ffe:] = du
        dx[rows, :dim] = (mm(dg, wg[...], NT) + mm(du, wu[...], NT)).astype(BF16)
        high = dgate.astype(BF16).astype(F32)
        dx[rows, dim:] = jnp.where(
            expert_lane == me, high, jnp.where(expert_lane == me + 64, dgate - high, 0.0)
        ).astype(BF16)
        for i, (src, dst) in enumerate(staged):
            pltpu.make_async_copy(src.at[rows], dst.at[rows], out_sem.at[i]).start()

    gather_steps(count, cuts, h_ref, land, (ring_out, ring_in, side_out, side_in), use)
    for i, (src, dst) in enumerate(staged):
        pltpu.make_async_copy(src, dst, out_sem.at[i]).wait()


def expert_gathered(h2, slot, chosen, router, dy_all, wg, wu, wd, capacity, count, call, cuts=4):
    block, dim = h2.shape
    ffe = wg.shape[1]
    total = count * capacity
    widths = (dim, dim, dim + 128, dim, ffe, 2 * ffe)
    dma = pltpu.SemaphoreType.DMA
    return pl.pallas_call(
        functools.partial(expert_kernel, count, cuts, capacity),
        out_shape=[jax.ShapeDtypeStruct((total, n), BF16) for n in widths],
        in_specs=[VMEM] * 4 + [ANY] * 4,
        out_specs=[ANY] * 6,
        scratch_shapes=gather_scratch(count, cuts, block, dim)
        + [
            pltpu.VMEM(wg.shape, BF16),
            pltpu.VMEM(wu.shape, BF16),
            pltpu.VMEM(wd.shape, BF16),
            pltpu.VMEM((2, 2 * block, dim), BF16),
        ]
        + [pltpu.VMEM((total, n), BF16) for n in widths]
        + [dma((3,)), dma((2, 2)), dma((6,))],
        compiler_params=remote_params(call, 60),
    )(h2, slot, chosen, router, dy_all, wg, wu, wd)


def slots_kernel(count, cuts, capacity, slot_ref, rows_ref, o_ref, *rest):
    bufs, sems, held, held_sem = rest[:5], rest[5:9], rest[9], rest[10]
    chips = count // 2
    block = o_ref.shape[0]
    load = pltpu.make_async_copy(rows_ref, held, held_sem)
    load.start()

    def produce(k, first, second):
        @pl.when(k == 0)
        def _():
            load.wait()

        pair = pl.multiple_of((k + 1) % chips * 2 * capacity, 16)
        pick = one_hot_of(slot_ref, first, second, capacity)
        both = mm(pick, held[pl.ds(pair, 2 * capacity), :], TN)
        return both[:block], both[block:]

    scatter_steps(count, cuts, o_ref, bufs, sems, produce)


def slots_scattered(rows, slot, capacity, count, call, cuts=2):
    block = slot.shape[1]
    columns = rows.shape[1]
    return pl.pallas_call(
        functools.partial(slots_kernel, count, cuts, capacity),
        out_shape=jax.ShapeDtypeStruct((block, columns), F32),
        in_specs=[VMEM, ANY],
        out_specs=VMEM,
        scratch_shapes=scatter_scratch(count, cuts, block, columns)
        + [pltpu.VMEM(rows.shape, BF16), pltpu.SemaphoreType.DMA],
        compiler_params=remote_params(call, 48),
    )(slot, rows)


def slots_back_kernel(
    count, cuts, capacity, slot_ref, dx_ref, xs_ref, de_ref, hid_ref, dgu_ref, o_ref, gu_out, down_out, *rest
):
    bufs, sems = rest[:5], rest[5:9]
    dx, xs, de, hid, dgu, gu, down, sem, gu_sem, down_sem = rest[9:]
    chips = count // 2
    block = o_ref.shape[0]
    loads = [
        pltpu.make_async_copy(src, dst, sem.at[i])
        for i, (src, dst) in enumerate(
            ((dx_ref, dx), (xs_ref, xs), (dgu_ref, dgu), (hid_ref, hid), (de_ref, de))
        )
    ]
    for load in loads:
        load.start()
    part = xs.shape[1] // chips
    down_part = 256
    downs = hid.shape[1] // down_part

    def produce(k, first, second):
        @pl.when(k == 0)
        def _():
            loads[0].wait()

        pair = pl.multiple_of((k + 1) % chips * 2 * capacity, 16)
        pick = one_hot_of(slot_ref, first, second, capacity)
        both = mm(pick, dx[pl.ds(pair, 2 * capacity), :], TN)
        return both[:block], both[block:]

    def extra(k):
        @pl.when(k == 0)
        def _():
            for load in loads[1:]:
                load.wait()

        columns = pl.ds(pl.multiple_of(k * part, 128), part)
        rows = pl.ds(pl.multiple_of(k * part, 16), part)
        gu[rows, :] = mm(xs[:, columns], dgu[...], TN).astype(BF16)
        pltpu.make_async_copy(gu.at[rows], gu_out.at[rows], gu_sem).start()

        @pl.when((k % 2 == 0) & (k // 2 < downs))
        def _():
            start = pl.multiple_of(k // 2 * down_part, 128)
            down_rows = pl.ds(start, down_part)
            down[down_rows, :] = mm(hid[:, down_rows], de[...], TN).astype(BF16)
            pltpu.make_async_copy(down.at[down_rows], down_out.at[down_rows], down_sem).start()

    scatter_steps(count, cuts, o_ref, bufs, sems, produce, extra)
    pltpu.make_async_copy(gu, gu_out, gu_sem).wait()
    pltpu.make_async_copy(down, down_out, down_sem).wait()


def slots_back(slot, dx, xs, de, hid, dgu, capacity, count, call, cuts=2):
    block = slot.shape[1]
    columns = dx.shape[1]
    dim, ffe = xs.shape[1], hid.shape[1]
    dma = pltpu.SemaphoreType.DMA
    return pl.pallas_call(
        functools.partial(slots_back_kernel, count, cuts, capacity),
        out_shape=(
            jax.ShapeDtypeStruct((block, columns), F32),
            jax.ShapeDtypeStruct((dim, 2 * ffe), BF16),
            jax.ShapeDtypeStruct((ffe, dim), BF16),
        ),
        in_specs=[VMEM] + [ANY] * 5,
        out_specs=[VMEM, ANY, ANY],
        scratch_shapes=scatter_scratch(count, cuts, block, columns)
        + [pltpu.VMEM(a.shape, BF16) for a in (dx, xs, de, hid, dgu)]
        + [pltpu.VMEM((dim, 2 * ffe), BF16), pltpu.VMEM((ffe, dim), BF16)]
        + [dma((5,)), dma, dma],
        compiler_params=remote_params(call, 60),
    )(slot, dx, xs, de, hid, dgu)


def split3(x):
    first = x.astype(BF16)
    rest = x - first.astype(F32)
    second = rest.astype(BF16)
    return first, second, (rest - second.astype(F32)).astype(BF16)


def in_lanes(x):
    lane = lax.broadcasted_iota(jnp.int32, x.shape, 1)
    first = x.astype(BF16).astype(F32)
    second = (x - first).astype(BF16).astype(F32)
    third = x - first - second
    spread = jnp.where(lane == 0, first, jnp.where(lane == 1, second, third))
    return jnp.where(lane < 3, spread, 0.0).astype(BF16)


def swap_halves(x):
    half = x.shape[1] // 2
    return jnp.concatenate([x[:, half:], x[:, :half]], axis=1)


def unit_rows(u):
    r = lax.rsqrt(jnp.mean(u * u, axis=1, keepdims=True) + EPSILON)
    return r, u * r


def attend_kernel(
    heads, tile, qkv_ref, gq_ref, gk_ref, cos_ref, sin_ref, start_ref, o_ref, qx_ref, kn_ref, vx_ref
):
    span = qkv_ref.shape[0]
    width = kn_ref.shape[1]
    scale = width**-0.5 * LOG2E
    for i in range(span // tile):
        rows = pl.ds(i * tile, tile)
        cos, sin = cos_ref[rows, :], sin_ref[rows, :]
        for h in range(heads + 1):
            _, unit = unit_rows(qkv_ref[rows, pl.ds(h * width, width)].astype(F32))
            u = unit * (gk_ref[...] if h == heads else gq_ref[...])
            u = u * cos + swap_halves(u) * sin
            if h == heads:
                kn_ref[rows, :] = u.astype(BF16)
            else:
                qx_ref[rows, pl.ds(2 * h * width, width)] = (u * scale).astype(BF16)
        vx_ref[rows, :width] = qkv_ref[rows, pl.ds((heads + 1) * width, width)]
        vx_ref[rows, width:] = jnp.ones((tile, width), BF16)
    for i in range(span // tile):
        rows = pl.ds(i * tile, tile)
        start = start_ref[rows, :]
        row = i * tile + lax.broadcasted_iota(jnp.int32, (tile, tile), 0)
        for h in range(heads):
            q = qx_ref[rows, pl.ds(2 * h * width, width)]
            total = jnp.zeros((tile, 2 * width), F32)
            for j in range(i + 1):
                keys = pl.ds(j * tile, tile)
                s = lax.dot_general(q, kn_ref[keys, :], NT, preferred_element_type=F32)
                col = j * tile + lax.broadcasted_iota(jnp.int32, (tile, tile), 1)
                keep = col >= start
                if i == j:
                    keep = keep & (col <= row)
                p = jnp.where(keep, jnp.exp2(s), 0.0).astype(BF16)
                total = total + jnp.dot(p, vx_ref[keys, :], preferred_element_type=F32)
            weight = total[:, width:]
            o_ref[rows, pl.ds(h * width, width)] = (total[:, :width] / weight).astype(BF16)
            qx_ref[rows, pl.ds((2 * h + 1) * width, width)] = in_lanes(-jnp.log2(weight))


def attend(qkv, gq, gk, cos, sin, start, tile=512):
    span = qkv.shape[0]
    width = gq.shape[0]
    heads = qkv.shape[1] // width - 2
    vmem = pl.BlockSpec(memory_space=pltpu.VMEM)
    return pl.pallas_call(
        functools.partial(attend_kernel, heads, min(tile, span)),
        out_shape=(
            jax.ShapeDtypeStruct((span, heads * width), BF16),
            jax.ShapeDtypeStruct((span, 2 * heads * width), BF16),
            jax.ShapeDtypeStruct((span, width), BF16),
        ),
        in_specs=[vmem] * 6,
        out_specs=[vmem] * 3,
        scratch_shapes=[pltpu.VMEM((span, 2 * width), BF16)],
        compiler_params=pltpu.CompilerParams(vmem_limit_bytes=48 * MIB),
    )(qkv, gq[None, :], gk[None, :], cos, sin, start[:, None])


def attend_back_kernel(
    heads,
    tile,
    qx_ref,
    kn_ref,
    qkv_ref,
    o_ref,
    do_ref,
    gq_ref,
    gk_ref,
    cos_ref,
    sin_ref,
    start_ref,
    dqkv_ref,
    gains_ref,
    gx_ref,
    dq_ref,
):
    span = qx_ref.shape[0]
    width = kn_ref.shape[1]
    scale = width**-0.5
    ones = jnp.ones((tile, width), BF16)

    def to_raw(d, h, rows, gain):
        r, unit = unit_rows(qkv_ref[rows, pl.ds(h * width, width)].astype(F32))
        d = d * cos_ref[rows, :] + swap_halves(d * sin_ref[rows, :])
        dg = d * gain
        raw = r * (dg - unit * jnp.mean(dg * unit, axis=1, keepdims=True))
        dqkv_ref[rows, pl.ds(h * width, width)] = raw.astype(BF16)
        return jnp.sum(d * unit, axis=0, keepdims=True)

    for i in range(span // tile):
        rows = pl.ds(i * tile, tile)
        for h in range(heads):
            cols = pl.ds(h * width, width)
            do = do_ref[rows, cols]
            inner = jnp.sum(do.astype(F32) * o_ref[rows, cols].astype(F32), axis=1, keepdims=True)
            gx_ref[rows, pl.ds(2 * h * width, width)] = do
            gx_ref[rows, pl.ds((2 * h + 1) * width, width)] = in_lanes(
                jnp.broadcast_to(-inner, (tile, width))
            )
    dq_ref[...] = jnp.zeros_like(dq_ref)
    key_gain = jnp.zeros((1, width), F32)
    for j in range(span // tile):
        keys = pl.ds(j * tile, tile)
        kn = kn_ref[keys, :]
        kx = jnp.concatenate([kn, ones], axis=1)
        vx = jnp.concatenate([qkv_ref[keys, pl.ds((heads + 1) * width, width)], ones], axis=1)
        dk = jnp.zeros((tile, width), F32)
        dv = jnp.zeros((tile, width), F32)
        key = j * tile + lax.broadcasted_iota(jnp.int32, (tile, tile), 0)
        for i in range(j, span // tile):
            rows = pl.ds(i * tile, tile)
            keep = key >= start_ref[:, rows]
            if i == j:
                row = i * tile + lax.broadcasted_iota(jnp.int32, (tile, tile), 1)
                keep = keep & (key <= row)
            for h in range(heads):
                qx = qx_ref[rows, pl.ds(2 * h * width, 2 * width)]
                gx = gx_ref[rows, pl.ds(2 * h * width, 2 * width)]
                s = lax.dot_general(kx, qx, NT, preferred_element_type=F32)
                p = jnp.where(keep, jnp.exp2(s), 0.0)
                dp = lax.dot_general(vx, gx, NT, preferred_element_type=F32)
                ds = (p * dp).astype(BF16)
                dv = dv + jnp.dot(p.astype(BF16), gx[:, :width], preferred_element_type=F32)
                dk = dk + jnp.dot(ds, qx[:, :width], preferred_element_type=F32)
                dq_ref[rows, pl.ds(h * width, width)] += lax.dot_general(
                    ds, kn, TN, preferred_element_type=F32
                )
        dqkv_ref[keys, pl.ds((heads + 1) * width, width)] = dv.astype(BF16)
        key_gain = key_gain + to_raw(dk * (1.0 / LOG2E), heads, keys, gk_ref[...])
    query_gain = jnp.zeros((1, width), F32)
    for i in range(span // tile):
        rows = pl.ds(i * tile, tile)
        for h in range(heads):
            dq = dq_ref[rows, pl.ds(h * width, width)] * scale
            query_gain = query_gain + to_raw(dq, h, rows, gq_ref[...])
    gains_ref[0:1, :] = query_gain
    gains_ref[1:2, :] = key_gain


def attend_back(qx, kn, qkv, o, do, gq, gk, cos, sin, start, tile=512):
    span, width = kn.shape
    heads = o.shape[1] // width
    vmem = pl.BlockSpec(memory_space=pltpu.VMEM)
    return pl.pallas_call(
        functools.partial(attend_back_kernel, heads, min(tile, span)),
        out_shape=(
            jax.ShapeDtypeStruct(qkv.shape, BF16),
            jax.ShapeDtypeStruct((2, width), F32),
        ),
        in_specs=[vmem] * 10,
        out_specs=[vmem] * 2,
        scratch_shapes=[
            pltpu.VMEM((span, 2 * heads * width), BF16),
            pltpu.VMEM((span, heads * width), F32),
        ],
        compiler_params=pltpu.CompilerParams(vmem_limit_bytes=56 * MIB),
    )(qx, kn, qkv, o, do, gq[None, :], gk[None, :], cos, sin, start[None, :])


def last_gather_kernel(
    count, members, cuts, q_ref, kv_ref, q_all, kv_all, heap, kv_sum, sems, own_sem, mo, mi, ro, ri, so, si
):
    me, chips, lane, position, step, following, previous, sibling = places(count)
    chip = me // 2
    place = chip % members
    first = chip - place
    rows = kv_sum.shape[0]

    def member(i):
        return (first + (place + i) % members) * 2 + lane

    greet([previous, sibling] + [member(i) for i in range(1, members)])

    def give(i):
        target = (place + i) % members
        return pltpu.make_async_remote_copy(
            src_ref=kv_ref.at[pl.ds(target * rows, rows)],
            dst_ref=heap.at[i - 1],
            send_sem=mo.at[i - 1],
            recv_sem=mi.at[i - 1],
            device_id={"seq": member(i)},
            device_id_type=MESH,
        )

    pieces = [(q_ref, q_all, part) for part in row_parts(q_ref.shape[0], cuts)]
    pieces.append((kv_sum, kv_all, pl.ds(0, rows)))

    def hop(c, owner, s, device, out_sem, in_sem, first_hop):
        x_ref, o_ref, part = pieces[c]
        return pltpu.make_async_remote_copy(
            src_ref=x_ref.at[part] if first_hop else o_ref.at[owner, part],
            dst_ref=o_ref.at[owner, part],
            send_sem=out_sem.at[s, c],
            recv_sem=in_sem.at[s, c],
            device_id={"seq": device},
            device_id_type=MESH,
        )

    def ring(c, owner, s, first_hop=False):
        return hop(c, owner, s, following, ro, ri, first_hop)

    def side(c, owner, s, first_hop=False):
        return hop(c, owner, s, sibling, so, si, first_hop)

    for i in range(1, members):
        give(i).start()
    mine = pltpu.make_async_copy(kv_ref.at[pl.ds(place * rows, rows)], kv_sum, own_sem.at[0])
    mine.start()
    own_q = pltpu.make_async_copy(q_ref, q_all.at[me], own_sem.at[1])
    own_q.start()
    for c in range(cuts):
        ring(c, me, 0, True).start()
        side(c, me, 0, True).start()
    mine.wait()
    total = kv_sum[...].astype(F32)
    for i in range(1, members):
        give(i).wait_recv()
        total = total + heap[i - 1].astype(F32)
    kv_sum[...] = total.astype(BF16)
    own_kv = pltpu.make_async_copy(kv_sum, kv_all.at[me], own_sem.at[2])
    own_kv.start()
    ring(cuts, me, 0, True).start()
    side(cuts, me, 0, True).start()
    for s in range(1, chips):
        owner = chip_of((position - s * step + chips) % chips, chips) * 2 + lane
        for c in range(cuts + 1):
            ring(c, owner, s - 1).wait_recv()
            if s < chips - 1:
                ring(c, owner, s).start()
            side(c, owner, s).start()
    for i in range(1, members):
        give(i).wait_send()
    for s in range(chips):
        for c in range(cuts + 1):
            side(c, me, s).wait()
            if s < chips - 1:
                ring(c, me, s).wait_send()
    own_q.wait()
    own_kv.wait()


def last_gather(q, kv, count, members, call, cuts=4):
    chips = count // 2
    rows = kv.shape[0] // members
    anywhere = pl.BlockSpec(memory_space=pl.ANY)
    dma = pltpu.SemaphoreType.DMA
    return pl.pallas_call(
        functools.partial(last_gather_kernel, count, members, cuts),
        out_shape=(
            jax.ShapeDtypeStruct((count,) + q.shape, BF16),
            jax.ShapeDtypeStruct((count, rows, kv.shape[1]), BF16),
        ),
        in_specs=[anywhere] * 2,
        out_specs=[anywhere] * 2,
        scratch_shapes=[
            pltpu.VMEM((members - 1, rows, kv.shape[1]), BF16),
            pltpu.VMEM((rows, kv.shape[1]), BF16),
            dma,
            dma((3,)),
            dma((members - 1,)),
            dma((members - 1,)),
        ]
        + [dma((chips, cuts + 1))] * 4,
        compiler_params=pltpu.CompilerParams(collective_id=call, has_side_effects=True),
    )(q, kv)


def finish_kernel(
    count, kv_heads, tile, q_ref, kv_ref, wq_ref, wk_ref, wv_ref, gain_ref, dq_ref, dk_ref, dv_ref, dg_ref
):
    chips = count // 2
    members = count // kv_heads
    width = q_ref.shape[2]
    hd = kv_ref.shape[2] // 2
    member = pl.program_id(0) * members // pl.num_programs(0)

    def place(group):
        return (group % chips) * 2 + group // chips

    total = jnp.zeros((tile, 1), F32)
    for g in range(count):
        cols = pl.ds(g * width, width)
        grad = q_ref[place(g)].astype(F32)
        dq_ref[:, cols] = grad
        total += jnp.sum(grad * wq_ref[:, cols].astype(F32), axis=1, keepdims=True)
    for j in range(kv_heads):
        cols = pl.ds(j * hd, hd)
        pair = kv_ref[place(j * members + member)].astype(F32)
        dk_ref[:, cols] = pair[:, :hd]
        dv_ref[:, cols] = pair[:, hd:]
        total += jnp.sum(pair[:, :hd] * wk_ref[:, cols].astype(F32), axis=1, keepdims=True)
        total += jnp.sum(pair[:, hd:] * wv_ref[:, cols].astype(F32), axis=1, keepdims=True)
    dg_ref[...] = total / gain_ref[...].astype(F32)


def finish(q_all, kv_all, w_query, key_weight, value_weight, gain, kv_heads):
    count = q_all.shape[0]
    local, columns = w_query.shape
    rows = kv_all.shape[1]
    tile = min(128, rows)
    per = rows // tile
    kv_columns = key_weight.shape[1]

    def row_block(n):
        return pl.BlockSpec((tile, n), lambda r: (r, 0))

    return pl.pallas_call(
        functools.partial(finish_kernel, count, kv_heads, tile),
        grid=(local // tile,),
        out_shape=(
            jax.ShapeDtypeStruct((local, columns), F32),
            jax.ShapeDtypeStruct((local, kv_columns), F32),
            jax.ShapeDtypeStruct((local, kv_columns), F32),
            jax.ShapeDtypeStruct((local, 1), F32),
        ),
        in_specs=[
            pl.BlockSpec((count, tile, q_all.shape[2]), lambda r: (0, r, 0)),
            pl.BlockSpec((count, tile, kv_all.shape[2]), lambda r: (0, r % per, 0)),
            row_block(columns),
            row_block(kv_columns),
            row_block(kv_columns),
            row_block(1),
        ],
        out_specs=[row_block(columns), row_block(kv_columns), row_block(kv_columns), row_block(1)],
        compiler_params=pltpu.CompilerParams(vmem_limit_bytes=48 * MIB),
    )(q_all, kv_all, w_query, key_weight, value_weight, gain[:, None])


def run_starts(segment):
    position = jnp.arange(segment.shape[0], dtype=jnp.int32)
    fresh = jnp.concatenate([jnp.ones((1,), dtype=bool), segment[1:] != segment[:-1]])
    return position, lax.cummax(jnp.where(fresh, position, jnp.zeros_like(position)), axis=0)


def angles(offset, head_size):
    frequency = jnp.exp(
        jnp.arange(head_size // 2, dtype=F32) * (-2.0 * math.log(THETA) / head_size)
    )
    phases = offset[:, None] * frequency[None, :]
    return jnp.cos(phases), jnp.sin(phases)


def per_device(
    activations,
    cotangent,
    segments,
    routing,
    attn_gain,
    mlp_gain,
    query_gain,
    key_gain,
    w_query,
    key_weight,
    value_weight,
    w_out,
    w_router,
    w_gate,
    w_up,
    w_down,
):
    count = lax.axis_size("seq")
    shards = lax.axis_size("fsdp")
    me = lax.axis_index("seq")
    chips = count // 2
    x = activations[0].astype(F32)
    dy = cotangent[0]
    segment = segments[0]
    routes = routing[0]
    tok, dim = x.shape
    span = segment.shape[0]
    top = routes.shape[1]
    hd = query_gain.shape[0] * shards
    heads = w_query.shape[1] // hd
    kv_heads = key_weight.shape[1] // hd
    share = heads // count
    experts = w_router.shape[1]
    local_rows = w_out.shape[0]
    capacity = tok * top * 9 // (8 * experts)
    group = (me % 2) * chips + me // 2
    gcols = share * hd
    kv_head = group * share // (heads // kv_heads)

    small = jnp.concatenate(
        [attn_gain, mlp_gain, query_gain, key_gain, w_router.reshape(-1)], axis=0
    )
    small = lax.all_gather(small, "fsdp", axis=0, tiled=False)
    local_dim = attn_gain.shape[0]
    local_hd = query_gain.shape[0]
    cut = [local_dim, 2 * local_dim, 2 * local_dim + local_hd, 2 * local_dim + 2 * local_hd]
    g_attn, g_mlp, g_query, g_key, router = jnp.split(small, cut, axis=1)
    g_attn = g_attn.reshape(-1).astype(F32)
    g_mlp = g_mlp.reshape(-1).astype(F32)
    g_query = g_query.reshape(-1).astype(F32)
    g_key = g_key.reshape(-1).astype(F32)
    router = router.reshape(dim, experts)
    qkv_local = jnp.concatenate(
        [
            lax.dynamic_slice_in_dim(w_query, group * gcols, gcols, 1),
            lax.dynamic_slice_in_dim(key_weight, kv_head * hd, hd, 1),
            lax.dynamic_slice_in_dim(value_weight, kv_head * hd, hd, 1),
        ],
        axis=1,
    )
    w_qkv = lax.all_gather(qkv_local, "fsdp", axis=0, tiled=True)
    first_row = group * gcols
    out_owner = first_row // local_rows
    out_local = lax.dynamic_slice_in_dim(w_out, first_row % local_rows, gcols, 0)
    w_o = lax.dynamic_index_in_dim(
        lax.all_gather(out_local, "fsdp", axis=0, tiled=False), out_owner, 0, keepdims=False
    )
    wg = lax.all_gather(w_gate[0], "fsdp", axis=0, tiled=True)
    wu = lax.all_gather(w_up[0], "fsdp", axis=0, tiled=True)
    wd = lax.all_gather(w_down[0], "fsdp", axis=1, tiled=True)

    r1 = lax.rsqrt(jnp.mean(x * x, axis=-1, keepdims=True) + EPSILON)
    h1 = (x * r1 * g_attn).astype(BF16)
    dy_all, routes_all = gather_seq([dy, routes], count, 4, (4, 1))
    h1, dy_all = lax.optimization_barrier((h1, dy_all))
    h1_all, qkv = project_gathered(h1, w_qkv, count, 1)
    position, doc_start = run_starts(segment)
    cosine, sine = angles((position - doc_start).astype(F32), hd)
    start = jnp.where(segment > 0, doc_start, position)

    cos_full = jnp.concatenate([cosine, cosine], axis=1)
    sin_full = jnp.concatenate([-sine, sine], axis=1)
    o, qx, kn = attend(qkv, g_query, g_key, cos_full, sin_full, start)
    x2 = x + product_scattered(o, w_o, NN, count, 2)

    r2 = lax.rsqrt(jnp.mean(x2 * x2, axis=-1, keepdims=True) + EPSILON)
    h2 = (x2 * r2 * g_mlp).astype(BF16)
    def gates_of(hidden, chosen):
        logits = mm(hidden, router)
        return jax.nn.softmax(jnp.where(chosen, logits, -1e30), axis=-1) * chosen

    def chosen_of(named):
        names = jnp.arange(experts, dtype=jnp.int32)
        return jnp.any(named[..., :, None] == names, axis=-2)

    hit = jnp.any(routes_all == me, axis=-1)
    rank = jnp.cumsum(hit.astype(jnp.int32), axis=1) - hit
    slot = jnp.where(hit & (rank < capacity), rank, -1)
    chosen_all = chosen_of(routes_all.reshape(span, top)).astype(BF16)
    chosen_all = jnp.pad(chosen_all, ((0, 0), (0, 128 - experts)))
    router_wide = jnp.pad(router, ((0, 0), (0, 128 - experts)))
    xs, de, dxs, ce, hid, dgu = expert_gathered(
        h2, slot, chosen_all, router_wide, dy_all, wg, wu, wd, capacity, count, 3
    )
    dh2_wide, w_gate_up_part, w_down_part = slots_back(
        slot, dxs, xs, de, hid, dgu, capacity, count, 6
    )
    mixed = x2 + slots_scattered(ce, slot, capacity, count, 5)
    dgate = dh2_wide[:, dim : dim + experts] + dh2_wide[:, dim + 64 : dim + 64 + experts]
    gates = gates_of(h2, chosen_of(routes))
    dlogits = (gates * (dgate - jnp.sum(gates * dgate, axis=-1, keepdims=True))).astype(BF16)
    dh2 = dh2_wide[:, :dim] + mm(dlogits, router, NT)
    router_part = mm(h2, dlogits, TN)
    xh = x2 * r2
    mlp_gain_part = jnp.sum(dh2 * xh, axis=0)
    dn = dh2 * g_mlp
    dx2 = dy.astype(F32) + r2 * (dn - xh * jnp.mean(dn * xh, axis=-1, keepdims=True))

    do, w_out_part = out_back(dx2.astype(BF16), w_o, o, count, 7)
    dqkv, head_gains = attend_back(
        qx, kn, qkv, o, do, g_query, g_key, cos_full, sin_full, start
    )
    qkv_part = mm(h1_all, dqkv, TN).astype(BF16)
    dh1 = product_scattered(dqkv, w_qkv, NT, count, 8)
    xh1 = x * r1
    dn1 = dh1 * g_attn
    input_grad = dx2 + r1 * (dn1 - xh1 * jnp.mean(dn1 * xh1, axis=-1, keepdims=True))

    def sum_fsdp(part, axis):
        return lax.psum_scatter(part.astype(BF16), "fsdp", scatter_dimension=axis, tiled=True)

    w_gate_up_grad = sum_fsdp(w_gate_up_part, 0).astype(F32)
    w_gate_grad = w_gate_up_grad[:, : wg.shape[1]]
    w_up_grad = w_gate_up_grad[:, wg.shape[1] :]
    w_down_grad = sum_fsdp(w_down_part, 1).astype(F32)

    small_part = jnp.concatenate(
        [router_part.reshape(shards, -1), mlp_gain_part.reshape(shards, -1)], axis=1
    )
    small_rows = -(-small_part.shape[1] // dim // 16) * 16
    small_part = jnp.pad(small_part, ((0, 0), (0, small_rows * dim - small_part.shape[1])))
    small_sum = sum_fsdp(small_part, 0).reshape(small_rows, dim)

    out_sum = jnp.sum(
        lax.all_gather(w_out_part, "fsdp", axis=0, tiled=False).astype(F32), axis=0
    ).astype(BF16)
    pair = lax.all_gather(
        out_sum,
        "seq",
        axis=0,
        tiled=False,
        axis_index_groups=[[2 * c, 2 * c + 1] for c in range(chips)],
    )
    w_out_grad, small_all = out_rows(pair, out_sum, small_sum, count, shards)
    small_total = jnp.sum(small_all.astype(F32), axis=0).reshape(-1)
    router_grad = small_total[: local_dim * experts].reshape(local_dim, experts)
    mlp_gain_grad = small_total[local_dim * experts : local_dim * (experts + 1)]

    gains_part = jnp.concatenate(
        [head_gains[0].reshape(shards, 1, local_hd), head_gains[1].reshape(shards, 1, local_hd)],
        axis=2,
    ).astype(BF16)
    gains_part = jnp.pad(
        gains_part, ((0, 0), (0, 15), (0, qkv_part.shape[1] - 2 * local_hd))
    )
    qkv_part = jnp.concatenate(
        [qkv_part.reshape(shards, local_dim, -1), gains_part], axis=1
    ).reshape(shards * (local_dim + 16), -1)
    qkv_sum = sum_fsdp(qkv_part, 0)
    q_all, kv_all = last_gather(
        qkv_sum[:, :gcols], qkv_sum[:local_dim, gcols:], count, count // kv_heads, 10
    )
    w_query_grad, w_key_grad, w_value_grad, attn_gain_grad = finish(
        q_all, kv_all, w_query, key_weight, value_weight, attn_gain, kv_heads
    )
    attn_gain_grad = attn_gain_grad[:, 0]
    head_gain_grads = jnp.sum(q_all[:, local_dim, : 2 * local_hd].astype(F32), axis=0)
    query_gain_grad = head_gain_grads[:local_hd]
    key_gain_grad = head_gain_grads[local_hd:]
    return (
        mixed.astype(BF16)[None],
        input_grad[None],
        attn_gain_grad,
        mlp_gain_grad,
        query_gain_grad,
        key_gain_grad,
        w_query_grad,
        w_key_grad,
        w_value_grad,
        w_out_grad,
        router_grad,
        w_gate_grad[None],
        w_up_grad[None],
        w_down_grad[None],
    )


def out_rows(pair, out_sum, small_sum, count, shards):
    chips = count // 2
    gcols, dim = out_sum.shape
    me = lax.axis_index("seq")
    mine = lax.axis_index("fsdp")
    if shards == 2:
        half = lax.dynamic_slice(pair, (mine, (me % 2) * (gcols // 2), 0), (1, gcols // 2, dim))[0]
        halves, small_all = gather_seq([half, small_sum], count, 9, (4, 1))
        return halves.reshape(chips * gcols, dim).astype(F32), small_all
    small_all = gather_seq([small_sum], count, 9, (1,))[0]
    groups = count // shards
    first = mine * groups
    group = (me % 2) * chips + me // 2
    place = jnp.clip(group - first, 0, groups - 1)
    keep = (group >= first) & (group < first + groups)
    rows = jnp.where(keep, out_sum, jnp.zeros_like(out_sum))
    blank = jnp.zeros((groups * gcols, dim), BF16)
    total = lax.psum(lax.dynamic_update_slice(blank, rows, (place * gcols, 0)), "seq")
    return total.astype(F32), small_all


def solution(mesh):
    tokens = P("fsdp", "seq", None)
    rows = P("fsdp", None)
    vector = P("fsdp")
    expert_rows = P("seq", "fsdp", None)
    expert_columns = P("seq", None, "fsdp")
    return jax.shard_map(
        per_device,
        mesh=mesh,
        in_specs=(tokens, tokens, rows, tokens)
        + (vector,) * 4
        + (rows,) * 5
        + (expert_rows, expert_rows, expert_columns),
        out_specs=(tokens, tokens)
        + (vector,) * 4
        + (rows,) * 5
        + (expert_rows, expert_rows, expert_columns),
        check_vma=False,
    )
```

```python
import functools
import math

import jax
import jax.numpy as jnp
from jax import lax
from jax.experimental import pallas as pl
from jax.experimental.pallas import tpu as pltpu
from jax.sharding import PartitionSpec as P

EPSILON = 1e-06
THETA = 1000000.0
BF16 = jnp.bfloat16
F32 = jnp.float32
MESH = pl.DeviceIdType.MESH
MIB = 1 << 20
LOG2E = math.log2(math.e)


def ring_of(chip, chips):
    return (chip % 2) * (chips - 1 - chip // 2) + (1 - chip % 2) * (chip // 2)


def chip_of(position, chips):
    upper = position // (chips // 2)
    return (1 - upper) * (2 * position) + upper * (2 * (chips - 1 - position) + 1)


def places(count):
    me = lax.axis_index("seq")
    chips = count // 2
    lane = me % 2
    position = ring_of(me // 2, chips)
    step = 1 - 2 * lane
    following = chip_of((position + step + chips) % chips, chips) * 2 + lane
    previous = chip_of((position - step + chips) % chips, chips) * 2 + lane
    sibling = me + 1 - 2 * lane
    return me, chips, lane, position, step, following, previous, sibling


def greet(places_over_seq, shards=1):
    barrier = pltpu.get_barrier_semaphore()
    for device in places_over_seq:
        pl.semaphore_signal(barrier, inc=1, device_id={"seq": device}, device_id_type=MESH)
    for i in range(1, shards):
        peer = (lax.axis_index("fsdp") + i) % shards
        pl.semaphore_signal(barrier, inc=1, device_id={"fsdp": peer}, device_id_type=MESH)
    pl.semaphore_wait(barrier, len(places_over_seq) + shards - 1)


def crossing(shards, items, out_sems, in_sems, own_sems=None):
    mine = lax.axis_index("fsdp")

    def place(src, dst, axis):
        if axis is None:
            return dst.at[mine]
        size = src.shape[axis]
        part = pl.ds(pl.multiple_of(mine * size, 128 if axis else 16), size)
        return dst.at[:, part] if axis else dst.at[part]

    def own(n):
        src, dst, axis = items[n]
        return pltpu.make_async_copy(src, place(src, dst, axis), own_sems.at[n])

    def send(n, i):
        src, dst, axis = items[n]
        return pltpu.make_async_remote_copy(
            src_ref=src,
            dst_ref=place(src, dst, axis),
            send_sem=out_sems.at[n, i - 1],
            recv_sem=in_sems.at[n, i - 1],
            device_id={"fsdp": (mine + i) % shards},
            device_id_type=MESH,
        )

    def start(n):
        for i in range(1, shards):
            send(n, i).start()
        if own_sems is not None:
            own(n).start()

    def wait(n):
        for i in range(1, shards):
            send(n, i).wait()
        if own_sems is not None:
            own(n).wait()

    return start, wait


def crossing_scratch(shards, items):
    dma = pltpu.SemaphoreType.DMA
    return [dma((items, max(1, shards - 1))), dma((items, max(1, shards - 1)))]


def spread_units(units, steps):
    total = sum(weight for weight, _ in units)
    plan = [[] for _ in range(steps)]
    done = 0.0
    for weight, run in units:
        plan[min(steps - 1, int((done + weight / 2) * steps / total))].append(run)
        done += weight
    return plan


def run_units(plan, k):
    for step, units in enumerate(plan):
        if units:

            @pl.when(k == step)
            def _(units=units):
                for run in units:
                    run()


def row_parts(rows, cuts):
    if cuts == 1:
        return [pl.ds(0, rows)]
    size = rows // cuts // 16 * 16
    return [pl.ds(c * size, size) for c in range(cuts - 1)] + [
        pl.ds((cuts - 1) * size, rows - (cuts - 1) * size)
    ]


def gather_kernel(count, cuts, *refs):
    arrays = len(cuts)
    x_refs, o_refs = refs[:arrays], refs[arrays : 2 * arrays]
    own_sem, ring_out, ring_in, side_out, side_in = refs[2 * arrays :]
    me, chips, lane, position, step, following, previous, sibling = places(count)
    greet((previous, sibling))
    pieces = []
    for a in range(arrays):
        pieces += [(x_refs[a], o_refs[a], part) for part in row_parts(x_refs[a].shape[0], cuts[a])]

    def hop(c, owner, s, device, out_sem, in_sem, first):
        x_ref, o_ref, part = pieces[c]
        return pltpu.make_async_remote_copy(
            src_ref=x_ref.at[part] if first else o_ref.at[owner, part],
            dst_ref=o_ref.at[owner, part],
            send_sem=out_sem.at[s, c],
            recv_sem=in_sem.at[s, c],
            device_id={"seq": device},
            device_id_type=MESH,
        )

    def ring(c, owner, s, first=False):
        return hop(c, owner, s, following, ring_out, ring_in, first)

    def side(c, owner, s, first=False):
        return hop(c, owner, s, sibling, side_out, side_in, first)

    own = [
        pltpu.make_async_copy(x_refs[a], o_refs[a].at[me], own_sem.at[a]) for a in range(arrays)
    ]
    for copy in own:
        copy.start()
    for c in range(len(pieces)):
        ring(c, me, 0, True).start()
        side(c, me, 0, True).start()
    for s in range(1, chips):
        owner = chip_of((position - s * step + chips) % chips, chips) * 2 + lane
        for c in range(len(pieces)):
            ring(c, owner, s - 1).wait_recv()
            if s < chips - 1:
                ring(c, owner, s).start()
            side(c, owner, s).start()
    for s in range(chips):
        for c in range(len(pieces)):
            side(c, me, s).wait()
            if s < chips - 1:
                ring(c, me, s).wait_send()
    for copy in own:
        copy.wait()


def gather_seq(arrays, count, call, cuts):
    chips = count // 2
    anywhere = pl.BlockSpec(memory_space=pl.ANY)
    return pl.pallas_call(
        functools.partial(gather_kernel, count, cuts),
        out_shape=[jax.ShapeDtypeStruct((count,) + x.shape, x.dtype) for x in arrays],
        in_specs=[pl.BlockSpec(memory_space=pltpu.VMEM)] * len(arrays),
        out_specs=[anywhere] * len(arrays),
        scratch_shapes=[pltpu.SemaphoreType.DMA((len(arrays),))]
        + [pltpu.SemaphoreType.DMA((chips, sum(cuts)))] * 4,
        compiler_params=pltpu.CompilerParams(collective_id=call, has_side_effects=True),
    )(*arrays)


NT = (((1,), (1,)), ((), ()))
TN = (((0,), (0,)), ((), ()))
NN = (((1,), (0,)), ((), ()))


def mm(a, b, dims=NN):
    return lax.dot_general(a, b, dims, preferred_element_type=F32)


def gather_steps(count, cuts, x_ref, land, sems, use, shards=1, begin=None, tag=None):
    me, chips, lane, position, step, following, previous, sibling = places(count)
    ring_out, ring_in, side_out, side_in = sems
    block = x_ref.shape[0]
    rows = block // cuts
    pieces = cuts + (tag is not None)
    greet((previous, sibling), shards)

    def ring(s, c):
        part = pl.ds(c * rows, rows)
        return pltpu.make_async_remote_copy(
            src_ref=tag.at[s, 0] if c == cuts else land.at[s, part],
            dst_ref=tag.at[s + 1, 0] if c == cuts else land.at[s + 1, part],
            send_sem=ring_out.at[s, c],
            recv_sem=ring_in.at[s, c],
            device_id={"seq": following},
            device_id_type=MESH,
        )

    def side(s, c):
        return pltpu.make_async_remote_copy(
            src_ref=tag.at[s, 0] if c == cuts else land.at[s, pl.ds(c * rows, rows)],
            dst_ref=tag.at[s, 1] if c == cuts else land.at[s, pl.ds(block + c * rows, rows)],
            send_sem=side_out.at[s, c],
            recv_sem=side_in.at[s, c],
            device_id={"seq": sibling},
            device_id_type=MESH,
        )

    def forward(s, c):
        @pl.when(s < chips - 1)
        def _():
            ring(s, c).start()

        side(s, c).start()

    land[0, :block] = x_ref[...]
    for c in range(pieces):
        forward(0, c)
    if begin is not None:
        begin()

    def one(s, carry):
        def pump(c):
            @pl.when(s < chips - 1)
            def _():
                ring(s, c).wait_recv()
                forward(s + 1, c)

        for c in range(pieces):
            side(s, c).wait_recv()
        use(s, *pair_owners(count, s), pump)
        return carry

    lax.fori_loop(0, chips, one, 0)

    def close(s, carry):
        for c in range(pieces):
            side(s, c).wait_send()

            @pl.when(s < chips - 1)
            def _():
                ring(s, c).wait_send()

        return carry

    lax.fori_loop(0, chips, close, 0)


def pair_owners(count, s):
    _, chips, lane, position, step, _, _, _ = places(count)
    first = chip_of((position - s * step + chips) % chips, chips) * 2 + lane
    second = chip_of((position + s * step + chips) % chips, chips) * 2 + 1 - lane
    return first, second


def at_block(owner, block):
    return pl.ds(pl.multiple_of(owner * block, block), block)


def gather_scratch(count, pieces, block, columns):
    chips = count // 2
    return [pltpu.VMEM((chips, 2 * block, columns), BF16)] + [
        pltpu.SemaphoreType.DMA((chips, pieces))
    ] * 4


def scatter_steps(count, cuts, o_ref, bufs, sems, produce, extra=None, shards=1, begin=None):
    me, chips, lane, position, step, following, previous, sibling = places(count)
    own, sent, came, give, given = bufs
    ring_out, ring_in, side_out, side_in = sems
    rows = own.shape[0] // cuts
    greet((previous, sibling), shards)
    if begin is not None:
        begin()

    def ring(k, c):
        part = pl.ds(c * rows, rows)
        return pltpu.make_async_remote_copy(
            src_ref=sent.at[k, part],
            dst_ref=came.at[k, part],
            send_sem=ring_out.at[k, c],
            recv_sem=ring_in.at[k, c],
            device_id={"seq": following},
            device_id_type=MESH,
        )

    def side(k):
        return pltpu.make_async_remote_copy(
            src_ref=give.at[k],
            dst_ref=given.at[k],
            send_sem=side_out.at[k],
            recv_sem=side_in.at[k],
            device_id={"seq": sibling},
            device_id_type=MESH,
        )

    def make(k):
        mine, theirs = produce(k, *pair_owners(count, (k + 1) % chips))
        give[k] = theirs.astype(BF16)
        side(k).start()
        own[...] = mine

    make(0)

    def one(k, carry):
        side(k).wait_recv()
        for c in range(cuts):
            part = pl.ds(c * rows, rows)

            @pl.when(k > 0)
            def _():
                ring(k - 1, c).wait_recv()
                own[part] += came[k - 1, part].astype(F32)

            total = own[part] + given[k, part].astype(F32)

            @pl.when(k < chips - 1)
            def _():
                sent[k, part] = total.astype(BF16)
                ring(k, c).start()

            @pl.when(k == chips - 1)
            def _():
                o_ref[part] = total

        @pl.when(k < chips - 1)
        def _():
            make(k + 1)

        if extra is not None:
            extra(k)
        return carry

    lax.fori_loop(0, chips, one, 0)

    def close(k, carry):
        side(k).wait_send()

        @pl.when(k < chips - 1)
        def _():
            for c in range(cuts):
                ring(k, c).wait_send()

        return carry

    lax.fori_loop(0, chips, close, 0)


def scatter_scratch(count, cuts, rows, columns):
    chips = count // 2
    dma = pltpu.SemaphoreType.DMA
    return [
        pltpu.VMEM((rows, columns), F32),
        pltpu.VMEM((chips - 1, rows, columns), BF16),
        pltpu.VMEM((chips - 1, rows, columns), BF16),
        pltpu.VMEM((chips, rows, columns), BF16),
        pltpu.VMEM((chips, rows, columns), BF16),
        dma((chips, cuts)),
        dma((chips, cuts)),
        dma((chips,)),
        dma((chips,)),
    ]


def remote_params(call, mib):
    return pltpu.CompilerParams(
        collective_id=call, has_side_effects=True, vmem_limit_bytes=mib * MIB
    )


VMEM = pl.BlockSpec(memory_space=pltpu.VMEM)
ANY = pl.BlockSpec(memory_space=pl.ANY)


def front_kernel(
    count,
    shards,
    cuts,
    widths,
    x_ref,
    small_ref,
    wq_ref,
    wk_ref,
    wv_ref,
    wo_ref,
    wd_ref,
    h_all,
    qkv_ref,
    w_ref,
    wo_all,
    small_all,
    wd_all,
    land,
    ring_out,
    ring_in,
    side_out,
    side_in,
    x_out,
    x_in,
    x_own,
    d_out,
    d_in,
    h1,
    gain,
    h_sem,
    o_out,
    o_in,
    o_own,
):
    block, dim = x_ref.shape
    chips = count // 2
    gcols, hd, members = widths
    local = wq_ref.shape[0]
    me = lax.axis_index("seq")
    mine = lax.axis_index("fsdp")
    group = (me % 2) * chips + me // 2
    kv_cols = pl.ds(pl.multiple_of(group // members * hd, 128), hd)
    q_cols = pl.ds(pl.multiple_of(group * gcols, 128), gcols)
    items = [
        (small_ref, small_all, None),
        (wq_ref.at[:, q_cols], w_ref.at[:, pl.ds(0, gcols)], 0),
        (wk_ref.at[:, kv_cols], w_ref.at[:, pl.ds(gcols, hd)], 0),
        (wv_ref.at[:, kv_cols], w_ref.at[:, pl.ds(gcols + hd, hd)], 0),
    ]
    start, wait = crossing(shards, items, x_out, x_in, x_own)
    start_down, wait_down = crossing(shards, [(wd_ref, wd_all, 1)], d_out, d_in)
    owner = group * gcols // wo_ref.shape[0]
    wo_src = wo_ref.at[pl.ds(pl.multiple_of(group * gcols % wo_ref.shape[0], 16), gcols)]
    wo_own = pltpu.make_async_copy(wo_src, wo_all, o_own)

    def wo_send(i):
        return pltpu.make_async_remote_copy(
            src_ref=wo_src,
            dst_ref=wo_all,
            send_sem=o_out.at[i - 1],
            recv_sem=o_in,
            device_id={"fsdp": (mine + i) % shards},
            device_id_type=MESH,
        )

    def begin():
        for n in range(len(items)):
            start(n)

        @pl.when(mine == owner)
        def _():
            wo_own.start()
            for i in range(1, shards):
                wo_send(i).start()

        start_down(0)

    def h_copy(s, holder, half):
        return pltpu.make_async_copy(
            h1.at[s, pl.ds(half * block, block)], h_all.at[at_block(holder, block)], h_sem.at[half]
        )

    def multiply(p):
        first, second = pair_owners(count, p)
        y = mm(h1[p], w_ref[...]).astype(BF16)
        qkv_ref[at_block(first, block), :] = y[:block]
        qkv_ref[at_block(second, block), :] = y[block:]

    def use(s, first, second, pump):
        @pl.when(s == 0)
        def _():
            wait(0)
            for f in range(shards):
                for r in range(local // 128):
                    gain[:, pl.ds(f * local + r * 128, 128)] = small_all[f, r : r + 1, :].astype(F32)

        x = land[s].astype(F32)
        r1 = lax.rsqrt(jnp.mean(x * x, axis=1, keepdims=True) + EPSILON)
        h1[s] = (x * r1 * gain[...]).astype(BF16)
        h_copy(s, first, 0).start()
        h_copy(s, second, 1).start()
        pump(0)

        @pl.when(s == chips // 2)
        def _():
            for n in range(1, len(items)):
                wait(n)

        @pl.when(s >= chips // 2)
        def _():
            multiply(2 * s - chips)
            pump(1)
            multiply(2 * s - chips + 1)

        @pl.when(s < chips // 2)
        def _():
            pump(1)

        for c in range(2, cuts):
            pump(c)

    gather_steps(
        count, cuts, x_ref, land, (ring_out, ring_in, side_out, side_in), use, shards, begin
    )

    @pl.when(mine == owner)
    def _():
        wo_own.wait()
        for i in range(1, shards):
            wo_send(i).wait_send()

    @pl.when(mine != owner)
    def _():
        wo_send(1).wait_recv()

    wait_down(0)
    half_rows = count * block // 2
    for half in range(2):
        pltpu.make_async_copy(
            h_all.at[pl.ds(0, half_rows)], h_all.at[pl.ds(0, half_rows)], h_sem.at[half]
        ).wait()


def front(
    x, small, w_query, key_weight, value_weight, w_out, w_down, hd, count, shards, call, cuts=4
):
    block, dim = x.shape
    gcols = w_query.shape[1] // count
    members = count * hd // key_weight.shape[1]
    columns = gcols + 2 * hd
    chips = count // 2
    dma = pltpu.SemaphoreType.DMA
    return pl.pallas_call(
        functools.partial(front_kernel, count, shards, cuts, (gcols, hd, members)),
        out_shape=(
            jax.ShapeDtypeStruct((count * block, dim), BF16),
            jax.ShapeDtypeStruct((count * block, columns), BF16),
            jax.ShapeDtypeStruct((dim, columns), BF16),
            jax.ShapeDtypeStruct((gcols, w_out.shape[1]), BF16),
            jax.ShapeDtypeStruct((shards,) + small.shape, BF16),
            whole_of(w_down, 1, shards),
        ),
        in_specs=[VMEM, VMEM] + [ANY] * 5,
        out_specs=[ANY, VMEM, VMEM, VMEM, VMEM, ANY],
        scratch_shapes=gather_scratch(count, cuts, block, dim)
        + crossing_scratch(shards, 4)
        + [
            dma((4,)),
        ]
        + crossing_scratch(shards, 1)
        + [
            pltpu.VMEM((chips, 2 * block, dim), BF16),
            pltpu.VMEM((1, dim), F32),
            dma((2,)),
            dma((max(1, shards - 1),)),
            dma,
            dma,
        ],
        compiler_params=remote_params(call, 48),
    )(x, small, w_query, key_weight, value_weight, w_out, w_down)


def out_back_kernel(
    count, cuts, da_ref, w_ref, o_ref, hid_ref, de_ref, do_ref, part_ref, down_ref, land, *rest
):
    sems = rest[:4]
    total, hid, de, hid_sem, de_sem = rest[4:]
    block = da_ref.shape[0]
    columns = de.shape[2]
    total[...] = jnp.zeros_like(total)
    load_hid = pltpu.make_async_copy(hid_ref, hid, hid_sem)

    def load_de(s):
        part = pl.ds(pl.multiple_of(s * columns, 128), columns)
        return pltpu.make_async_copy(de_ref.at[:, part], de.at[s % 2], de_sem.at[s % 2])

    def begin():
        load_hid.start()
        load_de(0).start()

    def use(s, first, second, pump):
        @pl.when(s == 0)
        def _():
            load_hid.wait()

        @pl.when(s < count // 2 - 1)
        def _():
            load_de(s + 1).start()

        pair = land[s]
        a = at_block(first, block)
        b = at_block(second, block)
        do = mm(pair, w_ref[...], NT).astype(BF16)
        do_ref[a, :] = do[:block]
        do_ref[b, :] = do[block:]
        pump(0)
        total[...] += mm(jnp.concatenate([o_ref[a, :], o_ref[b, :]], axis=0), pair, TN)
        pump(1)
        load_de(s).wait()
        part = pl.ds(pl.multiple_of(s * columns, 128), columns)
        down_ref[:, part] = mm(hid[...], de[s % 2], TN).astype(BF16)
        for c in range(2, cuts):
            pump(c)

    gather_steps(count, cuts, da_ref, land, sems, use, 1, begin)
    part_ref[...] = total[...].astype(BF16)


def out_back(da, w, o, hid, de, count, call, cuts=4):
    block, dim = da.shape
    chips = count // 2
    dma = pltpu.SemaphoreType.DMA
    return pl.pallas_call(
        functools.partial(out_back_kernel, count, cuts),
        out_shape=(
            jax.ShapeDtypeStruct(o.shape, BF16),
            jax.ShapeDtypeStruct(w.shape, BF16),
            jax.ShapeDtypeStruct((hid.shape[1], dim), BF16),
        ),
        in_specs=[VMEM] * 3 + [ANY] * 2,
        out_specs=[VMEM] * 3,
        scratch_shapes=gather_scratch(count, cuts, block, dim)
        + [
            pltpu.VMEM(w.shape, F32),
            pltpu.VMEM(hid.shape, BF16),
            pltpu.VMEM((2, de.shape[0], dim // chips), BF16),
            dma,
            dma((2,)),
        ],
        compiler_params=remote_params(call, 48),
    )(da, w, o, hid, de)


def product_kernel(count, shards, cuts, dims, axes, y_ref, w_ref, *refs):
    cargo = len(axes)
    srcs, o_ref, dsts = refs[:cargo], refs[cargo], refs[cargo + 1 : 2 * cargo + 1]
    rest = refs[2 * cargo + 1 :]
    block = o_ref.shape[0]
    if cargo:
        start, wait = crossing(shards, list(zip(srcs, dsts, axes)), *rest[9:])

    def begin():
        for n in range(cargo):
            start(n)

    def produce(k, first, second):
        a = y_ref[at_block(first, block), :]
        b = y_ref[at_block(second, block), :]
        both = mm(jnp.concatenate([a, b], axis=0), w_ref[...], dims)
        return both[:block], both[block:]

    scatter_steps(
        count, cuts, o_ref, rest[:5], rest[5:9], produce, None, shards if cargo else 1, begin
    )
    for n in range(cargo):
        wait(n)


def whole_of(part, axis, shards):
    shape = list(part.shape)
    shape[axis] *= shards
    return jax.ShapeDtypeStruct(tuple(shape), part.dtype)


def product_scattered(y, w, dims, cargo, axes, count, shards, call, cuts=2):
    block = y.shape[0] // count
    columns = w.shape[1 - dims[0][1][0]]
    return pl.pallas_call(
        functools.partial(product_kernel, count, shards, cuts, dims, axes),
        out_shape=[jax.ShapeDtypeStruct((block, columns), F32)]
        + [whole_of(part, axis, shards) for part, axis in zip(cargo, axes)],
        in_specs=[VMEM, VMEM] + [ANY] * len(cargo),
        out_specs=[VMEM] + [ANY] * len(cargo),
        scratch_shapes=scatter_scratch(count, cuts, block, columns)
        + (crossing_scratch(shards, len(cargo)) if cargo else []),
        compiler_params=remote_params(call, 48),
    )(y, w, *cargo)


def one_hot_of(slot_ref, first, second, capacity):
    a = slot_ref[pl.ds(first, 1), :]
    b = slot_ref[pl.ds(second, 1), :]
    wanted = jnp.concatenate([a, jnp.where(b >= 0, b + capacity, -1)], axis=1)
    row = lax.broadcasted_iota(jnp.int32, (2 * capacity, wanted.shape[1]), 0)
    return jnp.where(row == wanted, 1.0, 0.0).astype(BF16)


def parts_of_own(i, shards, size, unit):
    place = (lax.axis_index("fsdp") + i) % shards
    return pl.ds(pl.multiple_of(place * (size // shards), unit), size // shards)


def gate_up_parts(i, shards, whole, own, wgu):
    rows = parts_of_own(i, shards, wgu.shape[0], 16)
    ffe = wgu.shape[1] // 2
    return [
        (whole[n].at[rows] if i else own[n], wgu.at[rows, pl.ds(n * ffe, ffe)]) for n in range(2)
    ]


def down_parts(i, shards, pieces, own, wd):
    columns = parts_of_own(i, shards, wd.shape[1], 128)
    parts = []
    first = 0
    for piece in pieces:
        rows = pl.ds(first, piece.shape[0])
        first += piece.shape[0]
        parts.append((piece.at[:, columns] if i else own.at[rows], wd.at[rows, columns]))
    return parts


def expert_kernel(
    count,
    shards,
    cuts,
    capacity,
    h_ref,
    slot_ref,
    chosen_ref,
    router_ref,
    dy_ref,
    wg_ref,
    wu_ref,
    wd1_ref,
    wd2_ref,
    wd3_ref,
    wg_own,
    wu_own,
    wd_own,
    xs_out,
    de_out,
    dl_out,
    ce_out,
    hid_out,
    dgu_out,
    land,
    ring_out,
    ring_in,
    side_out,
    side_in,
    wgu,
    wd,
    dyb,
    xs,
    de,
    dl,
    ce,
    hid,
    dgu,
    w_sem,
    dy_sem,
    out_sem,
):
    block, dim = h_ref.shape
    ffe = wd.shape[0]
    wd_refs = (wd1_ref, wd2_ref, wd3_ref)
    me = lax.axis_index("seq")
    chips = count // 2
    weights = [
        pltpu.make_async_copy(src, dst, w_sem.at[i, n])
        for i in range(shards)
        for n, (src, dst) in enumerate(
            gate_up_parts(i, shards, (wg_ref, wu_ref), (wg_own, wu_own), wgu)
            + down_parts(i, shards, wd_refs, wd_own, wd)
        )
    ]
    staged = ((xs, xs_out), (de, de_out), (dl, dl_out), (ce, ce_out), (hid, hid_out), (dgu, dgu_out))

    def dy_copies(s):
        first, second = pair_owners(count, s)
        return [
            pltpu.make_async_copy(
                dy_ref.at[at_block(owner, block)], dyb.at[s % 2, pl.ds(half * block, block)], dy_sem.at[s % 2, half]
            )
            for half, owner in ((0, first), (1, second))
        ]

    for copy in weights + dy_copies(0):
        copy.start()

    def use(s, first, second, pump):
        @pl.when(s < chips - 1)
        def _():
            for copy in dy_copies(s + 1):
                copy.start()

        rows = pl.ds(pl.multiple_of(s * 2 * capacity, 16), 2 * capacity)
        pick = one_hot_of(slot_ref, first, second, capacity)
        x = mm(pick, land[s]).astype(BF16)
        xs[rows, :] = x
        chosen = mm(
            pick,
            jnp.concatenate(
                [
                    chosen_ref[pl.ds(pl.multiple_of(first * block, block), block), :],
                    chosen_ref[pl.ds(pl.multiple_of(second * block, block), block), :],
                ],
                axis=0,
            ),
        )
        logits = jnp.where(chosen > 0.5, mm(x, router_ref[...]), -1e30)
        weight = jnp.exp(logits - jnp.max(logits, axis=1, keepdims=True)) * chosen
        mass = jnp.sum(weight, axis=1, keepdims=True)
        expert_lane = lax.broadcasted_iota(jnp.int32, weight.shape, 1)
        gate = jnp.sum(jnp.where(expert_lane == me, weight, 0.0), axis=1, keepdims=True)
        gate = gate / jnp.where(mass > 0.0, mass, 1.0)

        @pl.when(s == 0)
        def _():
            for copy in weights:
                copy.wait()

        gu = mm(x, wgu[...])
        pump(0)
        g, u = gu[:, :ffe], gu[:, ffe:]
        sig = jax.nn.sigmoid(g)
        silu = g * sig
        h = (silu * u).astype(BF16)
        hid[rows, :] = h
        e = mm(h, wd[...])
        ce[rows, :] = (gate * e).astype(BF16)
        pump(1)
        for copy in dy_copies(s):
            copy.wait()
        dys = mm(pick, dyb[s % 2])
        dgate = jnp.sum(dys * e, axis=1, keepdims=True)
        d = (gate * dys).astype(BF16)
        de[rows, :] = d
        pump(2)
        dh = mm(d, wd[...], NT)
        for c in range(3, cuts):
            pump(c)
        dg = (dh * u * (sig + silu * (1.0 - sig))).astype(BF16)
        du = (dh * silu).astype(BF16)
        dgu[rows, :ffe] = dg
        dgu[rows, ffe:] = du
        high = dgate.astype(BF16).astype(F32)
        dl[rows, :] = jnp.where(
            expert_lane == me, high, jnp.where(expert_lane == me + 64, dgate - high, 0.0)
        ).astype(BF16)
        for i, (src, dst) in enumerate(staged):
            pltpu.make_async_copy(src.at[rows], dst.at[rows], out_sem.at[i]).start()

    gather_steps(count, cuts, h_ref, land, (ring_out, ring_in, side_out, side_in), use)
    for i, (src, dst) in enumerate(staged):
        pltpu.make_async_copy(src, dst, out_sem.at[i]).wait()


def expert_gathered(h2, slot, chosen, router, dy_all, weights, capacity, count, shards, call, cuts=4):
    block, dim = h2.shape
    ffe = weights[0].shape[1]
    total = count * capacity
    widths = (dim, dim, 128, dim, ffe, 2 * ffe)
    dma = pltpu.SemaphoreType.DMA
    return pl.pallas_call(
        functools.partial(expert_kernel, count, shards, cuts, capacity),
        out_shape=[jax.ShapeDtypeStruct((total, n), BF16) for n in widths],
        in_specs=[VMEM] * 4 + [ANY] * 9,
        out_specs=[ANY] * 6,
        scratch_shapes=gather_scratch(count, cuts, block, dim)
        + [
            pltpu.VMEM((dim, 2 * ffe), BF16),
            pltpu.VMEM((ffe, dim), BF16),
            pltpu.VMEM((2, 2 * block, dim), BF16),
        ]
        + [pltpu.VMEM((total, n), BF16) for n in widths]
        + [dma((shards, 5)), dma((2, 2)), dma((6,))],
        compiler_params=remote_params(call, 60),
    )(h2, slot, chosen, router, dy_all, *weights)


def slots_back_kernel(
    count,
    shards,
    cuts,
    capacity,
    slot_ref,
    dl,
    xs_ref,
    dgu_ref,
    wg_ref,
    wu_ref,
    wg_own,
    wu_own,
    o_ref,
    gu_out,
    *rest,
):
    bufs, sems = rest[:5], rest[5:9]
    xs, dgu, wgu, gu, sem, w_sem, gu_sem = rest[9:]
    chips = count // 2
    block = o_ref.shape[0]
    dim = xs.shape[1]
    loads = [
        pltpu.make_async_copy(src, dst, sem.at[i])
        for i, (src, dst) in enumerate(((dgu_ref, dgu), (xs_ref, xs)))
    ]
    weights = [
        pltpu.make_async_copy(src, dst, w_sem.at[i, n])
        for i in range(shards)
        for n, (src, dst) in enumerate(
            gate_up_parts(i, shards, (wg_ref, wu_ref), (wg_own, wu_own), wgu)
        )
    ]
    for load in loads[:1] + weights + loads[1:]:
        load.start()
    part = xs.shape[1] // chips

    def produce(k, first, second):
        @pl.when(k == 0)
        def _():
            for load in loads[:1] + weights:
                load.wait()

        pair = pl.multiple_of((k + 1) % chips * 2 * capacity, 16)
        rows = pl.ds(pair, 2 * capacity)
        pick = one_hot_of(slot_ref, first, second, capacity)
        dx = mm(dgu[rows, :], wgu[...], NT).astype(BF16)
        both = jnp.concatenate([mm(pick, dx, TN), mm(pick, dl[rows, :], TN)], axis=1)
        return both[:block], both[block:]

    def extra(k):
        @pl.when(k == 0)
        def _():
            for load in loads[1:]:
                load.wait()

        columns = pl.ds(pl.multiple_of(k * part, 128), part)
        rows = pl.ds(pl.multiple_of(k * part, 16), part)
        gu[rows, :] = mm(xs[:, columns], dgu[...], TN).astype(BF16)
        pltpu.make_async_copy(gu.at[rows], gu_out.at[rows], gu_sem).start()

    scatter_steps(count, cuts, o_ref, bufs, sems, produce, extra)
    pltpu.make_async_copy(gu, gu_out, gu_sem).wait()


def slots_back(slot, dl, xs, dgu, weights, capacity, count, shards, call, cuts=2):
    block = slot.shape[1]
    dim, ffe = xs.shape[1], dgu.shape[1] // 2
    columns = dim + dl.shape[1]
    dma = pltpu.SemaphoreType.DMA
    return pl.pallas_call(
        functools.partial(slots_back_kernel, count, shards, cuts, capacity),
        out_shape=(
            jax.ShapeDtypeStruct((block, columns), F32),
            jax.ShapeDtypeStruct((dim, 2 * ffe), BF16),
        ),
        in_specs=[VMEM] * 2 + [ANY] * 6,
        out_specs=[VMEM, ANY],
        scratch_shapes=scatter_scratch(count, cuts, block, columns)
        + [pltpu.VMEM(a.shape, BF16) for a in (xs, dgu)]
        + [pltpu.VMEM((dim, 2 * ffe), BF16)] * 2
        + [dma((2,)), dma((shards, 2)), dma],
        compiler_params=remote_params(call, 60),
    )(slot, dl, xs, dgu, *weights)


def split3(x):
    first = x.astype(BF16)
    rest = x - first.astype(F32)
    second = rest.astype(BF16)
    return first, second, (rest - second.astype(F32)).astype(BF16)


def in_lanes(x):
    lane = lax.broadcasted_iota(jnp.int32, x.shape, 1)
    first = x.astype(BF16).astype(F32)
    second = (x - first).astype(BF16).astype(F32)
    third = x - first - second
    spread = jnp.where(lane == 0, first, jnp.where(lane == 1, second, third))
    return jnp.where(lane < 3, spread, 0.0).astype(BF16)


def swap_halves(x):
    half = x.shape[1] // 2
    return jnp.concatenate([x[:, half:], x[:, :half]], axis=1)


def unit_rows(u):
    r = lax.rsqrt(jnp.mean(u * u, axis=1, keepdims=True) + EPSILON)
    return r, u * r


def attend_kernel(
    count,
    shards,
    cuts,
    heads,
    tile,
    dy_ref,
    routes_ref,
    qkv_ref,
    gq_ref,
    gk_ref,
    cos_ref,
    sin_ref,
    start_ref,
    wg_ref,
    wd_ref,
    dy_all,
    routes_all,
    o_ref,
    qx_ref,
    kn_ref,
    wg_all,
    wd_all,
    land,
    ring_out,
    ring_in,
    side_out,
    side_in,
    x_out,
    x_in,
    tag,
    vx_ref,
    dy_sem,
):
    span = qkv_ref.shape[0]
    width = kn_ref.shape[1]
    block = dy_ref.shape[0]
    scale = width**-0.5 * LOG2E
    items = [(wg_ref, wg_all, 0), (wd_ref, wd_all, 1)]
    start_item, wait_item = crossing(shards, items, x_out, x_in)

    def prepare(i):
        rows = pl.ds(i * tile, tile)
        cos, sin = cos_ref[rows, :], sin_ref[rows, :]
        for h in range(heads + 1):
            _, unit = unit_rows(qkv_ref[rows, pl.ds(h * width, width)].astype(F32))
            u = unit * (gk_ref[...] if h == heads else gq_ref[...])
            u = u * cos + swap_halves(u) * sin
            if h == heads:
                kn_ref[rows, :] = u.astype(BF16)
            else:
                qx_ref[rows, pl.ds(2 * h * width, width)] = (u * scale).astype(BF16)
        vx_ref[rows, :width] = qkv_ref[rows, pl.ds((heads + 1) * width, width)]
        vx_ref[rows, width:] = jnp.ones((tile, width), BF16)

    def attend_rows(i, h):
        rows = pl.ds(i * tile, tile)
        start = start_ref[rows, :]
        row = i * tile + lax.broadcasted_iota(jnp.int32, (tile, tile), 0)
        q = qx_ref[rows, pl.ds(2 * h * width, width)]
        total = jnp.zeros((tile, 2 * width), F32)
        for j in range(i + 1):
            keys = pl.ds(j * tile, tile)
            s = mm(q, kn_ref[keys, :], NT)
            col = j * tile + lax.broadcasted_iota(jnp.int32, (tile, tile), 1)
            keep = col >= start
            if i == j:
                keep = keep & (col <= row)
            p = jnp.where(keep, jnp.exp2(s), 0.0).astype(BF16)
            total = total + mm(p, vx_ref[keys, :])
        weight = total[:, width:]
        o_ref[rows, pl.ds(h * width, width)] = (total[:, :width] / weight).astype(BF16)
        qx_ref[rows, pl.ds((2 * h + 1) * width, width)] = in_lanes(-jnp.log2(weight))

    units = []
    for i in range(span // tile):
        units.append((1.0, functools.partial(prepare, i)))
        units += [(0.7 * (i + 1), functools.partial(attend_rows, i, h)) for h in range(heads)]
    plan = spread_units(units, count // 2 - 1)

    def begin():
        for n in range(len(items)):
            start_item(n)

    tag[0, 0] = routes_ref[...]

    def use(s, first, second, pump):
        for half, owner in ((0, first), (1, second)):
            pltpu.make_async_copy(
                land.at[s, pl.ds(half * block, block)],
                dy_all.at[at_block(owner, block)],
                dy_sem.at[half],
            ).start()
            routes_all[owner] = tag[s, half]
        run_units(plan, s)
        for c in range(cuts + 1):
            pump(c)

    gather_steps(
        count, cuts, dy_ref, land, (ring_out, ring_in, side_out, side_in), use, shards, begin, tag
    )
    for n in range(len(items)):
        wait_item(n)
    half_rows = count * block // 2
    for half in range(2):
        pltpu.make_async_copy(
            dy_all.at[pl.ds(0, half_rows)], dy_all.at[pl.ds(0, half_rows)], dy_sem.at[half]
        ).wait()


def attend(dy, routes, qkv, gq, gk, cos, sin, start, w_gate, w_down, count, shards, call, tile=512, cuts=4):
    span = qkv.shape[0]
    width = gq.shape[0]
    heads = qkv.shape[1] // width - 2
    block, dim = dy.shape
    chips = count // 2
    return pl.pallas_call(
        functools.partial(attend_kernel, count, shards, cuts, heads, min(tile, span)),
        out_shape=(
            jax.ShapeDtypeStruct((count * block, dim), BF16),
            jax.ShapeDtypeStruct((count,) + routes.shape, BF16),
            jax.ShapeDtypeStruct((span, heads * width), BF16),
            jax.ShapeDtypeStruct((span, 2 * heads * width), BF16),
            jax.ShapeDtypeStruct((span, width), BF16),
            whole_of(w_gate, 0, shards),
            whole_of(w_down, 1, shards),
        ),
        in_specs=[VMEM] * 8 + [ANY] * 2,
        out_specs=[ANY] + [VMEM] * 4 + [ANY] * 2,
        scratch_shapes=gather_scratch(count, cuts + 1, block, dim)
        + crossing_scratch(shards, 2)
        + [
            pltpu.VMEM((chips, 2) + routes.shape, BF16),
            pltpu.VMEM((span, 2 * width), BF16),
            pltpu.SemaphoreType.DMA((2,)),
        ],
        compiler_params=remote_params(call, 56),
    )(dy, routes, qkv, gq[None, :], gk[None, :], cos, sin, start[:, None], w_gate, w_down)


def attend_back_kernel(
    count,
    cuts,
    capacity,
    heads,
    tile,
    qx_ref,
    kn_ref,
    qkv_ref,
    o_ref,
    do_ref,
    gq_ref,
    gk_ref,
    cos_ref,
    sin_ref,
    start_ref,
    slot_ref,
    ce_ref,
    dqkv_ref,
    gains_ref,
    mixed_ref,
    *rest,
):
    bufs, sems = rest[:5], rest[5:9]
    gx_ref, dq_ref, dk_ref, dv_ref, held, held_sem = rest[9:]
    span = qx_ref.shape[0]
    width = kn_ref.shape[1]
    scale = width**-0.5
    chips = count // 2
    block = mixed_ref.shape[0]
    load = pltpu.make_async_copy(ce_ref, held, held_sem)
    load.start()

    def produce(k, first, second):
        @pl.when(k == 0)
        def _():
            load.wait()

        pair = pl.multiple_of((k + 1) % chips * 2 * capacity, 16)
        pick = one_hot_of(slot_ref, first, second, capacity)
        both = mm(pick, held[pl.ds(pair, 2 * capacity), :], TN)
        return both[:block], both[block:]

    def to_raw(d, h, rows, gain, row):
        r, unit = unit_rows(qkv_ref[rows, pl.ds(h * width, width)].astype(F32))
        d = d * cos_ref[rows, :] + swap_halves(d * sin_ref[rows, :])
        dg = d * gain
        raw = r * (dg - unit * jnp.mean(dg * unit, axis=1, keepdims=True))
        dqkv_ref[rows, pl.ds(h * width, width)] = raw.astype(BF16)
        gains_ref[row : row + 1, :] += jnp.sum(d * unit, axis=0, keepdims=True)

    def prepare(i):
        rows = pl.ds(i * tile, tile)
        for h in range(heads):
            cols = pl.ds(h * width, width)
            do = do_ref[rows, cols]
            inner = jnp.sum(do.astype(F32) * o_ref[rows, cols].astype(F32), axis=1, keepdims=True)
            gx_ref[rows, pl.ds(2 * h * width, width)] = do
            gx_ref[rows, pl.ds((2 * h + 1) * width, width)] = in_lanes(
                jnp.broadcast_to(-inner, (tile, width))
            )

    def tile_back(j, i):
        keys = pl.ds(j * tile, tile)
        rows = pl.ds(i * tile, tile)
        ones = jnp.ones((tile, width), BF16)
        kn = kn_ref[keys, :]
        kx = jnp.concatenate([kn, ones], axis=1)
        vx = jnp.concatenate([qkv_ref[keys, pl.ds((heads + 1) * width, width)], ones], axis=1)
        key = j * tile + lax.broadcasted_iota(jnp.int32, (tile, tile), 0)
        keep = key >= start_ref[:, rows]
        if i == j:
            row = i * tile + lax.broadcasted_iota(jnp.int32, (tile, tile), 1)
            keep = keep & (key <= row)
        for h in range(heads):
            qx = qx_ref[rows, pl.ds(2 * h * width, 2 * width)]
            gx = gx_ref[rows, pl.ds(2 * h * width, 2 * width)]
            p = jnp.where(keep, jnp.exp2(mm(kx, qx, NT)), 0.0)
            ds = (p * mm(vx, gx, NT)).astype(BF16)
            dv_ref[keys, :] += mm(p.astype(BF16), gx[:, :width])
            dk_ref[keys, :] += mm(ds, qx[:, :width])
            dq_ref[rows, pl.ds(h * width, width)] += mm(ds, kn, TN)

    def finish_keys(j):
        keys = pl.ds(j * tile, tile)
        dqkv_ref[keys, pl.ds((heads + 1) * width, width)] = dv_ref[keys, :].astype(BF16)
        to_raw(dk_ref[keys, :] * (1.0 / LOG2E), heads, keys, gk_ref[...], 1)

    def finish_rows(i):
        rows = pl.ds(i * tile, tile)
        for h in range(heads):
            to_raw(dq_ref[rows, pl.ds(h * width, width)] * scale, h, rows, gq_ref[...], 0)

    tiles = span // tile
    units = [(0.3, functools.partial(prepare, i)) for i in range(tiles)]
    for j in range(tiles):
        units += [(2.0, functools.partial(tile_back, j, i)) for i in range(j, tiles)]
        units.append((0.3, functools.partial(finish_keys, j)))
        units.append((0.6, functools.partial(finish_rows, j)))
    plan = spread_units(units, chips - 1)
    for ref in (dq_ref, dk_ref, dv_ref, gains_ref):
        ref[...] = jnp.zeros_like(ref)

    def extra(k):
        run_units(plan, k)

    scatter_steps(count, cuts, mixed_ref, bufs, sems, produce, extra)


def attend_back(qx, kn, qkv, o, do, gq, gk, cos, sin, start, slot, ce, capacity, count, call, tile=512, cuts=2):
    span, width = kn.shape
    heads = o.shape[1] // width
    block = slot.shape[1]
    dim = ce.shape[1]
    return pl.pallas_call(
        functools.partial(attend_back_kernel, count, cuts, capacity, heads, min(tile, span)),
        out_shape=(
            jax.ShapeDtypeStruct(qkv.shape, BF16),
            jax.ShapeDtypeStruct((2, width), F32),
            jax.ShapeDtypeStruct((block, dim), F32),
        ),
        in_specs=[VMEM] * 11 + [ANY],
        out_specs=[VMEM] * 3,
        scratch_shapes=scatter_scratch(count, cuts, block, dim)
        + [
            pltpu.VMEM((span, 2 * heads * width), BF16),
            pltpu.VMEM((span, heads * width), F32),
            pltpu.VMEM((span, width), F32),
            pltpu.VMEM((span, width), F32),
            pltpu.VMEM(ce.shape, BF16),
            pltpu.SemaphoreType.DMA,
        ],
        compiler_params=remote_params(call, 60),
    )(qx, kn, qkv, o, do, gq[None, :], gk[None, :], cos, sin, start[None, :], slot, ce)


def last_gather_kernel(
    count, members, cuts, qkv_ref, q_all, kv_all, heap, kv_sum, sems, own_sem, mo, mi, ro, ri, so, si
):
    me, chips, lane, position, step, following, previous, sibling = places(count)
    chip = me // 2
    place = chip % members
    first = chip - place
    rows = kv_sum.shape[0]
    gcols = q_all.shape[2]
    q_ref = qkv_ref.at[:, pl.ds(0, gcols)]
    kv_ref = qkv_ref.at[pl.ds(0, rows * members), pl.ds(gcols, kv_sum.shape[1])]

    def member(i):
        return (first + (place + i) % members) * 2 + lane

    greet([previous, sibling] + [member(i) for i in range(1, members)])

    def give(i):
        target = (place + i) % members
        return pltpu.make_async_remote_copy(
            src_ref=kv_ref.at[pl.ds(target * rows, rows)],
            dst_ref=heap.at[i - 1],
            send_sem=mo.at[i - 1],
            recv_sem=mi.at[i - 1],
            device_id={"seq": member(i)},
            device_id_type=MESH,
        )

    pieces = [(q_ref, q_all, part) for part in row_parts(q_ref.shape[0], cuts)]
    pieces.append((kv_sum, kv_all, pl.ds(0, rows)))

    def hop(c, owner, s, device, out_sem, in_sem, first_hop):
        x_ref, o_ref, part = pieces[c]
        return pltpu.make_async_remote_copy(
            src_ref=x_ref.at[part] if first_hop else o_ref.at[owner, part],
            dst_ref=o_ref.at[owner, part],
            send_sem=out_sem.at[s, c],
            recv_sem=in_sem.at[s, c],
            device_id={"seq": device},
            device_id_type=MESH,
        )

    def ring(c, owner, s, first_hop=False):
        return hop(c, owner, s, following, ro, ri, first_hop)

    def side(c, owner, s, first_hop=False):
        return hop(c, owner, s, sibling, so, si, first_hop)

    for i in range(1, members):
        give(i).start()
    mine = pltpu.make_async_copy(kv_ref.at[pl.ds(place * rows, rows)], kv_sum, own_sem.at[0])
    mine.start()
    own_q = pltpu.make_async_copy(q_ref, q_all.at[me], own_sem.at[1])
    own_q.start()
    for c in range(cuts):
        ring(c, me, 0, True).start()
        side(c, me, 0, True).start()
    mine.wait()
    total = kv_sum[...].astype(F32)
    for i in range(1, members):
        give(i).wait_recv()
        total = total + heap[i - 1].astype(F32)
    kv_sum[...] = total.astype(BF16)
    own_kv = pltpu.make_async_copy(kv_sum, kv_all.at[me], own_sem.at[2])
    own_kv.start()
    ring(cuts, me, 0, True).start()
    side(cuts, me, 0, True).start()
    for s in range(1, chips):
        owner = chip_of((position - s * step + chips) % chips, chips) * 2 + lane
        for c in range(cuts + 1):
            ring(c, owner, s - 1).wait_recv()
            if s < chips - 1:
                ring(c, owner, s).start()
            side(c, owner, s).start()
    for i in range(1, members):
        give(i).wait_send()
    for s in range(chips):
        for c in range(cuts + 1):
            side(c, me, s).wait()
            if s < chips - 1:
                ring(c, me, s).wait_send()
    own_q.wait()
    own_kv.wait()


def last_gather(qkv, gcols, local, count, members, call, cuts=4):
    chips = count // 2
    rows = local // members
    columns = qkv.shape[1] - gcols
    anywhere = pl.BlockSpec(memory_space=pl.ANY)
    dma = pltpu.SemaphoreType.DMA
    return pl.pallas_call(
        functools.partial(last_gather_kernel, count, members, cuts),
        out_shape=(
            jax.ShapeDtypeStruct((count, qkv.shape[0], gcols), BF16),
            jax.ShapeDtypeStruct((count, rows, columns), BF16),
        ),
        in_specs=[VMEM],
        out_specs=[anywhere] * 2,
        scratch_shapes=[
            pltpu.VMEM((members - 1, rows, columns), BF16),
            pltpu.VMEM((rows, columns), BF16),
            dma,
            dma((3,)),
            dma((members - 1,)),
            dma((members - 1,)),
        ]
        + [dma((chips, cuts + 1))] * 4,
        compiler_params=pltpu.CompilerParams(collective_id=call, has_side_effects=True),
    )(qkv)


def finish_kernel(
    count, kv_heads, tile, q_ref, kv_ref, wq_ref, wk_ref, wv_ref, gain_ref, dq_ref, dk_ref, dv_ref, dg_ref
):
    chips = count // 2
    members = count // kv_heads
    width = q_ref.shape[2]
    hd = kv_ref.shape[2] // 2
    member = pl.program_id(0) * members // pl.num_programs(0)

    def place(group):
        return (group % chips) * 2 + group // chips

    total = jnp.zeros((tile, 1), F32)
    for g in range(count):
        cols = pl.ds(g * width, width)
        grad = q_ref[place(g)].astype(F32)
        dq_ref[:, cols] = grad
        total += jnp.sum(grad * wq_ref[:, cols].astype(F32), axis=1, keepdims=True)
    for j in range(kv_heads):
        cols = pl.ds(j * hd, hd)
        pair = kv_ref[place(j * members + member)].astype(F32)
        dk_ref[:, cols] = pair[:, :hd]
        dv_ref[:, cols] = pair[:, hd:]
        total += jnp.sum(pair[:, :hd] * wk_ref[:, cols].astype(F32), axis=1, keepdims=True)
        total += jnp.sum(pair[:, hd:] * wv_ref[:, cols].astype(F32), axis=1, keepdims=True)
    dg_ref[...] = total / gain_ref[...].astype(F32)


def finish(q_all, kv_all, w_query, key_weight, value_weight, gain, kv_heads):
    count = q_all.shape[0]
    local, columns = w_query.shape
    rows = kv_all.shape[1]
    tile = min(128, rows)
    per = rows // tile
    kv_columns = key_weight.shape[1]

    def row_block(n):
        return pl.BlockSpec((tile, n), lambda r: (r, 0))

    return pl.pallas_call(
        functools.partial(finish_kernel, count, kv_heads, tile),
        grid=(local // tile,),
        out_shape=(
            jax.ShapeDtypeStruct((local, columns), F32),
            jax.ShapeDtypeStruct((local, kv_columns), F32),
            jax.ShapeDtypeStruct((local, kv_columns), F32),
            jax.ShapeDtypeStruct((local, 1), F32),
        ),
        in_specs=[
            pl.BlockSpec((count, tile, q_all.shape[2]), lambda r: (0, r, 0)),
            pl.BlockSpec((count, tile, kv_all.shape[2]), lambda r: (0, r % per, 0)),
            row_block(columns),
            row_block(kv_columns),
            row_block(kv_columns),
            row_block(1),
        ],
        out_specs=[row_block(columns), row_block(kv_columns), row_block(kv_columns), row_block(1)],
        compiler_params=pltpu.CompilerParams(vmem_limit_bytes=48 * MIB),
    )(q_all, kv_all, w_query, key_weight, value_weight, gain[:, None])


def run_starts(segment):
    position = jnp.arange(segment.shape[0], dtype=jnp.int32)
    fresh = jnp.concatenate([jnp.ones((1,), dtype=bool), segment[1:] != segment[:-1]])
    return position, lax.cummax(jnp.where(fresh, position, jnp.zeros_like(position)), axis=0)


def angles(offset, head_size):
    frequency = jnp.exp(
        jnp.arange(head_size // 2, dtype=F32) * (-2.0 * math.log(THETA) / head_size)
    )
    phases = offset[:, None] * frequency[None, :]
    return jnp.cos(phases), jnp.sin(phases)


def per_device(
    activations,
    cotangent,
    segments,
    routing,
    attn_gain,
    mlp_gain,
    query_gain,
    key_gain,
    w_query,
    key_weight,
    value_weight,
    w_out,
    w_router,
    w_gate,
    w_up,
    w_down,
):
    count = lax.axis_size("seq")
    shards = lax.axis_size("fsdp")
    me = lax.axis_index("seq")
    chips = count // 2
    x = activations[0].astype(F32)
    dy = cotangent[0]
    segment = segments[0]
    routes = routing[0]
    tok, dim = x.shape
    span = segment.shape[0]
    top = routes.shape[1]
    hd = query_gain.shape[0] * shards
    heads = w_query.shape[1] // hd
    kv_heads = key_weight.shape[1] // hd
    share = heads // count
    experts = w_router.shape[1]
    local_rows = w_out.shape[0]
    capacity = tok * top * 9 // (8 * experts)
    gcols = share * hd

    small = jnp.concatenate(
        [attn_gain, mlp_gain, query_gain, key_gain, w_router.reshape(-1)], axis=0
    )
    local_dim = attn_gain.shape[0]
    local_hd = query_gain.shape[0]
    small = jnp.pad(small, (0, -small.shape[0] % (16 * 128))).reshape(-1, 128)
    down_rows = w_down.shape[1] // 3 // 16 * 16
    downs = (
        w_down[0, :down_rows],
        w_down[0, down_rows : 2 * down_rows],
        w_down[0, 2 * down_rows :],
    )
    h1_all, qkv, w_qkv, w_o, small, wd1 = front(
        activations[0],
        small,
        w_query,
        key_weight,
        value_weight,
        w_out,
        downs[0],
        hd,
        count,
        shards,
        1,
    )
    small = small.reshape(shards, -1)
    cut = [local_dim, 2 * local_dim, 2 * local_dim + local_hd, 2 * local_dim + 2 * local_hd]
    g_attn, g_mlp, g_query, g_key, router = jnp.split(small, cut, axis=1)
    g_attn = g_attn.reshape(-1).astype(F32)
    g_mlp = g_mlp.reshape(-1).astype(F32)
    g_query = g_query.reshape(-1).astype(F32)
    g_key = g_key.reshape(-1).astype(F32)
    router = router[:, : local_dim * experts].reshape(dim, experts)
    r1 = lax.rsqrt(jnp.mean(x * x, axis=-1, keepdims=True) + EPSILON)
    position, doc_start = run_starts(segment)
    cosine, sine = angles((position - doc_start).astype(F32), hd)
    start = jnp.where(segment > 0, doc_start, position)

    cos_full = jnp.concatenate([cosine, cosine], axis=1)
    sin_full = jnp.concatenate([-sine, sine], axis=1)
    routes_sent = jnp.pad(routes.T, ((0, -top % 16), (0, 0))).astype(BF16)
    dy_all, routes_all, o, qx, kn, wg, wd2 = attend(
        dy,
        routes_sent,
        qkv,
        g_query,
        g_key,
        cos_full,
        sin_full,
        start,
        w_gate[0],
        downs[1],
        count,
        shards,
        4,
    )
    x2, wu, wd3 = product_scattered(o, w_o, NN, [w_up[0], downs[2]], (0, 1), count, shards, 2)
    x2 = x + x2

    r2 = lax.rsqrt(jnp.mean(x2 * x2, axis=-1, keepdims=True) + EPSILON)
    h2 = (x2 * r2 * g_mlp).astype(BF16)
    def gates_of(hidden, chosen):
        logits = mm(hidden, router)
        return jax.nn.softmax(jnp.where(chosen, logits, -1e30), axis=-1) * chosen

    def chosen_of(named):
        names = jnp.arange(experts, dtype=jnp.int32)
        return jnp.any(named[..., :, None] == names, axis=-2)

    routes_all = jnp.swapaxes(routes_all[:, :top].astype(jnp.int32), 1, 2)
    hit = jnp.any(routes_all == me, axis=-1)
    rank = jnp.cumsum(hit.astype(jnp.int32), axis=1) - hit
    slot = jnp.where(hit & (rank < capacity), rank, -1)
    chosen_all = chosen_of(routes_all.reshape(span, top)).astype(BF16)
    chosen_all = jnp.pad(chosen_all, ((0, 0), (0, 128 - experts)))
    router_wide = jnp.pad(router, ((0, 0), (0, 128 - experts)))
    xs, de, dl, ce, hid, dgu = expert_gathered(
        h2,
        slot,
        chosen_all,
        router_wide,
        dy_all,
        (wg, wu, wd1, wd2, wd3, w_gate[0], w_up[0], w_down[0]),
        capacity,
        count,
        shards,
        3,
    )
    dh2_wide, w_gate_up_part = slots_back(
        slot, dl, xs, dgu, (wg, wu, w_gate[0], w_up[0]), capacity, count, shards, 6
    )
    dgate = dh2_wide[:, dim : dim + experts] + dh2_wide[:, dim + 64 : dim + 64 + experts]
    gates = gates_of(h2, chosen_of(routes))
    dlogits = (gates * (dgate - jnp.sum(gates * dgate, axis=-1, keepdims=True))).astype(BF16)
    dh2 = dh2_wide[:, :dim] + mm(dlogits, router, NT)
    router_part = mm(h2, dlogits, TN)
    xh = x2 * r2
    mlp_gain_part = jnp.sum(dh2 * xh, axis=0)
    dn = dh2 * g_mlp
    dx2 = dy.astype(F32) + r2 * (dn - xh * jnp.mean(dn * xh, axis=-1, keepdims=True))

    do, w_out_part, w_down_part = out_back(dx2.astype(BF16), w_o, o, hid, de, count, 7)
    dqkv, head_gains, mixed = attend_back(
        qx, kn, qkv, o, do, g_query, g_key, cos_full, sin_full, start, slot, ce, capacity, count, 5
    )
    mixed = x2 + mixed
    qkv_part = mm(h1_all, dqkv, TN).astype(BF16)
    dh1 = product_scattered(dqkv, w_qkv, NT, [], (), count, shards, 8)[0]
    xh1 = x * r1
    dn1 = dh1 * g_attn
    input_grad = dx2 + r1 * (dn1 - xh1 * jnp.mean(dn1 * xh1, axis=-1, keepdims=True))

    def sum_fsdp(part, axis):
        return lax.psum_scatter(part.astype(BF16), "fsdp", scatter_dimension=axis, tiled=True)

    w_gate_up_grad = sum_fsdp(w_gate_up_part, 0).astype(F32)
    w_gate_grad = w_gate_up_grad[:, : w_gate.shape[2]]
    w_up_grad = w_gate_up_grad[:, w_gate.shape[2] :]
    w_down_grad = sum_fsdp(w_down_part, 1).astype(F32)

    small_part = jnp.concatenate(
        [router_part.reshape(shards, -1), mlp_gain_part.reshape(shards, -1)], axis=1
    )
    small_rows = -(-small_part.shape[1] // dim // 16) * 16
    small_part = jnp.pad(small_part, ((0, 0), (0, small_rows * dim - small_part.shape[1])))
    small_sum = sum_fsdp(small_part, 0).reshape(small_rows, dim)

    out_sum = jnp.sum(
        lax.all_gather(w_out_part, "fsdp", axis=0, tiled=False).astype(F32), axis=0
    ).astype(BF16)
    pair = lax.all_gather(
        out_sum,
        "seq",
        axis=0,
        tiled=False,
        axis_index_groups=[[2 * c, 2 * c + 1] for c in range(chips)],
    )
    w_out_grad, small_all = out_rows(pair, out_sum, small_sum, count, shards)
    small_total = jnp.sum(small_all.astype(F32), axis=0).reshape(-1)
    router_grad = small_total[: local_dim * experts].reshape(local_dim, experts)
    mlp_gain_grad = small_total[local_dim * experts : local_dim * (experts + 1)]

    gains_part = jnp.concatenate(
        [head_gains[0].reshape(shards, 1, local_hd), head_gains[1].reshape(shards, 1, local_hd)],
        axis=2,
    ).astype(BF16)
    gains_part = jnp.pad(
        gains_part, ((0, 0), (0, 15), (0, qkv_part.shape[1] - 2 * local_hd))
    )
    qkv_part = jnp.concatenate(
        [qkv_part.reshape(shards, local_dim, -1), gains_part], axis=1
    ).reshape(shards * (local_dim + 16), -1)
    qkv_sum = sum_fsdp(qkv_part, 0)
    q_all, kv_all = last_gather(qkv_sum, gcols, local_dim, count, count // kv_heads, 10)
    w_query_grad, w_key_grad, w_value_grad, attn_gain_grad = finish(
        q_all, kv_all, w_query, key_weight, value_weight, attn_gain, kv_heads
    )
    attn_gain_grad = attn_gain_grad[:, 0]
    head_gain_grads = jnp.sum(q_all[:, local_dim, : 2 * local_hd].astype(F32), axis=0)
    query_gain_grad = head_gain_grads[:local_hd]
    key_gain_grad = head_gain_grads[local_hd:]
    return (
        mixed.astype(BF16)[None],
        input_grad[None],
        attn_gain_grad,
        mlp_gain_grad,
        query_gain_grad,
        key_gain_grad,
        w_query_grad,
        w_key_grad,
        w_value_grad,
        w_out_grad,
        router_grad,
        w_gate_grad[None],
        w_up_grad[None],
        w_down_grad[None],
    )


def out_rows(pair, out_sum, small_sum, count, shards):
    chips = count // 2
    gcols, dim = out_sum.shape
    me = lax.axis_index("seq")
    mine = lax.axis_index("fsdp")
    if shards == 2:
        half = lax.dynamic_slice(pair, (mine, (me % 2) * (gcols // 2), 0), (1, gcols // 2, dim))[0]
        halves, small_all = gather_seq([half, small_sum], count, 9, (4, 1))
        return halves.reshape(chips * gcols, dim).astype(F32), small_all
    small_all = gather_seq([small_sum], count, 9, (1,))[0]
    groups = count // shards
    first = mine * groups
    group = (me % 2) * chips + me // 2
    place = jnp.clip(group - first, 0, groups - 1)
    keep = (group >= first) & (group < first + groups)
    rows = jnp.where(keep, out_sum, jnp.zeros_like(out_sum))
    blank = jnp.zeros((groups * gcols, dim), BF16)
    total = lax.psum(lax.dynamic_update_slice(blank, rows, (place * gcols, 0)), "seq")
    return total.astype(F32), small_all


def solution(mesh):
    tokens = P("fsdp", "seq", None)
    rows = P("fsdp", None)
    vector = P("fsdp")
    expert_rows = P("seq", "fsdp", None)
    expert_columns = P("seq", None, "fsdp")
    return jax.shard_map(
        per_device,
        mesh=mesh,
        in_specs=(tokens, tokens, rows, tokens)
        + (vector,) * 4
        + (rows,) * 5
        + (expert_rows, expert_rows, expert_columns),
        out_specs=(tokens, tokens)
        + (vector,) * 4
        + (rows,) * 5
        + (expert_rows, expert_rows, expert_columns),
        check_vma=False,
    )
```

```python
import functools
import math

import jax
import jax.numpy as jnp
from jax import lax
from jax.experimental import pallas as pl
from jax.experimental.pallas import tpu as pltpu
from jax.sharding import PartitionSpec as P

EPSILON = 1e-06
THETA = 1000000.0
BF16 = jnp.bfloat16
F32 = jnp.float32
MESH = pl.DeviceIdType.MESH
MIB = 1 << 20
LOG2E = math.log2(math.e)


def ring_of(chip, chips):
    return (chip % 2) * (chips - 1 - chip // 2) + (1 - chip % 2) * (chip // 2)


def chip_of(position, chips):
    upper = position // (chips // 2)
    return (1 - upper) * (2 * position) + upper * (2 * (chips - 1 - position) + 1)


def places(count):
    me = lax.axis_index("seq")
    chips = count // 2
    lane = me % 2
    position = ring_of(me // 2, chips)
    step = 1 - 2 * lane
    following = chip_of((position + step + chips) % chips, chips) * 2 + lane
    previous = chip_of((position - step + chips) % chips, chips) * 2 + lane
    sibling = me + 1 - 2 * lane
    return me, chips, lane, position, step, following, previous, sibling


def greet(places_over_seq, shards=1, more=0):
    barrier = pltpu.get_barrier_semaphore()
    for device in places_over_seq:
        pl.semaphore_signal(barrier, inc=1, device_id={"seq": device}, device_id_type=MESH)
    for i in range(1, shards):
        peer = (lax.axis_index("fsdp") + i) % shards
        pl.semaphore_signal(barrier, inc=1, device_id={"fsdp": peer}, device_id_type=MESH)
    pl.semaphore_wait(barrier, len(places_over_seq) + shards - 1 + more)


def crossing(shards, items, out_sems, in_sems, own_sems=None):
    mine = lax.axis_index("fsdp")

    def place(src, dst, axis):
        if axis is None:
            return dst.at[mine]
        size = src.shape[axis]
        part = pl.ds(pl.multiple_of(mine * size, 128 if axis else 16), size)
        return dst.at[:, part] if axis else dst.at[part]

    def own(n):
        src, dst, axis = items[n]
        return pltpu.make_async_copy(src, place(src, dst, axis), own_sems.at[n])

    def send(n, i):
        src, dst, axis = items[n]
        return pltpu.make_async_remote_copy(
            src_ref=src,
            dst_ref=place(src, dst, axis),
            send_sem=out_sems.at[n, i - 1],
            recv_sem=in_sems.at[n, i - 1],
            device_id={"fsdp": (mine + i) % shards},
            device_id_type=MESH,
        )

    def start(n):
        for i in range(1, shards):
            send(n, i).start()
        if own_sems is not None:
            own(n).start()

    def wait(n):
        for i in range(1, shards):
            send(n, i).wait()
        if own_sems is not None:
            own(n).wait()

    return start, wait


def crossing_scratch(shards, items):
    dma = pltpu.SemaphoreType.DMA
    return [dma((items, max(1, shards - 1))), dma((items, max(1, shards - 1)))]


def spread_units(units, steps):
    total = sum(weight for weight, _ in units)
    plan = [[] for _ in range(steps)]
    done = 0.0
    for weight, run in units:
        plan[min(steps - 1, int((done + weight / 2) * steps / total))].append(run)
        done += weight
    return plan


def run_units(plan, k):
    for step, units in enumerate(plan):
        if units:

            @pl.when(k == step)
            def _(units=units):
                for run in units:
                    run()


def row_parts(rows, cuts):
    if cuts == 1:
        return [pl.ds(0, rows)]
    size = rows // cuts // 16 * 16
    return [pl.ds(c * size, size) for c in range(cuts - 1)] + [
        pl.ds((cuts - 1) * size, rows - (cuts - 1) * size)
    ]


NT = (((1,), (1,)), ((), ()))
TN = (((0,), (0,)), ((), ()))
NN = (((1,), (0,)), ((), ()))


def mm(a, b, dims=NN):
    return lax.dot_general(a, b, dims, preferred_element_type=F32)


def gather_steps(count, cuts, x_ref, land, sems, use, shards=1, begin=None, tag=None):
    me, chips, lane, position, step, following, previous, sibling = places(count)
    ring_out, ring_in, side_out, side_in = sems
    block = x_ref.shape[0]
    rows = block // cuts
    pieces = cuts + (tag is not None)
    greet((previous, sibling), shards)

    def ring(s, c):
        part = pl.ds(c * rows, rows)
        return pltpu.make_async_remote_copy(
            src_ref=tag.at[s, 0] if c == cuts else land.at[s, part],
            dst_ref=tag.at[s + 1, 0] if c == cuts else land.at[s + 1, part],
            send_sem=ring_out.at[s, c],
            recv_sem=ring_in.at[s, c],
            device_id={"seq": following},
            device_id_type=MESH,
        )

    def side(s, c):
        return pltpu.make_async_remote_copy(
            src_ref=tag.at[s, 0] if c == cuts else land.at[s, pl.ds(c * rows, rows)],
            dst_ref=tag.at[s, 1] if c == cuts else land.at[s, pl.ds(block + c * rows, rows)],
            send_sem=side_out.at[s, c],
            recv_sem=side_in.at[s, c],
            device_id={"seq": sibling},
            device_id_type=MESH,
        )

    def forward(s, c):
        @pl.when(s < chips - 1)
        def _():
            ring(s, c).start()

        side(s, c).start()

    land[0, :block] = x_ref[...]
    for c in range(pieces):
        forward(0, c)
    if begin is not None:
        begin()

    def one(s, carry):
        def pump(c):
            @pl.when(s < chips - 1)
            def _():
                ring(s, c).wait_recv()
                forward(s + 1, c)

        for c in range(pieces):
            side(s, c).wait_recv()
        use(s, *pair_owners(count, s), pump)
        return carry

    lax.fori_loop(0, chips, one, 0)

    def close(s, carry):
        for c in range(pieces):
            side(s, c).wait_send()

            @pl.when(s < chips - 1)
            def _():
                ring(s, c).wait_send()

        return carry

    lax.fori_loop(0, chips, close, 0)


def pair_owners(count, s):
    _, chips, lane, position, step, _, _, _ = places(count)
    first = chip_of((position - s * step + chips) % chips, chips) * 2 + lane
    second = chip_of((position + s * step + chips) % chips, chips) * 2 + 1 - lane
    return first, second


def at_block(owner, block):
    return pl.ds(pl.multiple_of(owner * block, block), block)


def gather_scratch(count, pieces, block, columns):
    chips = count // 2
    return [pltpu.VMEM((chips, 2 * block, columns), BF16)] + [
        pltpu.SemaphoreType.DMA((chips, pieces))
    ] * 4


def scatter_steps(count, cuts, o_ref, bufs, sems, produce, extra=None, shards=1, begin=None, meeting=None):
    me, chips, lane, position, step, following, previous, sibling = places(count)
    own, sent, came, give, given = bufs
    ring_out, ring_in, side_out, side_in = sems
    rows = own.shape[1] // cuts
    if meeting is None:
        greet((previous, sibling), shards)
    else:
        meeting[0]()
        greet((previous, sibling), shards, meeting[1])
    if begin is not None:
        begin()

    def ring(k, c):
        part = pl.ds(c * rows, rows)
        return pltpu.make_async_remote_copy(
            src_ref=sent.at[k, part],
            dst_ref=came.at[k, part],
            send_sem=ring_out.at[k, c],
            recv_sem=ring_in.at[k, c],
            device_id={"seq": following},
            device_id_type=MESH,
        )

    def side(k):
        return pltpu.make_async_remote_copy(
            src_ref=give.at[k],
            dst_ref=given.at[k],
            send_sem=side_out.at[k],
            recv_sem=side_in.at[k],
            device_id={"seq": sibling},
            device_id_type=MESH,
        )

    def make(k):
        mine, theirs = produce(k, *pair_owners(count, (k + 1) % chips))
        give[k] = theirs.astype(BF16)
        side(k).start()
        own[k % 2] = mine

    make(0)

    def one(k, carry):
        side(k).wait_recv()
        for c in range(cuts):
            part = pl.ds(c * rows, rows)

            @pl.when(k > 0)
            def _():
                ring(k - 1, c).wait_recv()
                own[k % 2, part] += came[k - 1, part].astype(F32)

            total = own[k % 2, part] + given[k, part].astype(F32)

            @pl.when(k < chips - 1)
            def _():
                sent[k, part] = total.astype(BF16)
                ring(k, c).start()

            @pl.when(k == chips - 1)
            def _():
                o_ref[part] = total

            if c == 0:

                @pl.when(k < chips - 1)
                def _():
                    make(k + 1)

        if extra is not None:
            extra(k)
        return carry

    lax.fori_loop(0, chips, one, 0)

    def close(k, carry):
        side(k).wait_send()

        @pl.when(k < chips - 1)
        def _():
            for c in range(cuts):
                ring(k, c).wait_send()

        return carry

    lax.fori_loop(0, chips, close, 0)


def scatter_scratch(count, cuts, rows, columns):
    chips = count // 2
    dma = pltpu.SemaphoreType.DMA
    return [
        pltpu.VMEM((2, rows, columns), F32),
        pltpu.VMEM((chips - 1, rows, columns), BF16),
        pltpu.VMEM((chips - 1, rows, columns), BF16),
        pltpu.VMEM((chips, rows, columns), BF16),
        pltpu.VMEM((chips, rows, columns), BF16),
        dma((chips, cuts)),
        dma((chips, cuts)),
        dma((chips,)),
        dma((chips,)),
    ]


def remote_params(call, mib):
    return pltpu.CompilerParams(
        collective_id=call, has_side_effects=True, vmem_limit_bytes=mib * MIB
    )


VMEM = pl.BlockSpec(memory_space=pltpu.VMEM)
ANY = pl.BlockSpec(memory_space=pl.ANY)


def front_kernel(
    count,
    shards,
    cuts,
    widths,
    x_ref,
    small_ref,
    wr_ref,
    wq_ref,
    wk_ref,
    wv_ref,
    wo_ref,
    wd_ref,
    h_all,
    qkv_ref,
    w_ref,
    wo_all,
    small_all,
    wr_all,
    wd_all,
    land,
    ring_out,
    ring_in,
    side_out,
    side_in,
    x_out,
    x_in,
    x_own,
    d_out,
    d_in,
    h1,
    gain,
    h_sem,
    o_out,
    o_in,
    o_own,
):
    block, dim = x_ref.shape
    chips = count // 2
    gcols, hd, members = widths
    local = wq_ref.shape[0]
    me = lax.axis_index("seq")
    mine = lax.axis_index("fsdp")
    group = (me % 2) * chips + me // 2
    kv_cols = pl.ds(pl.multiple_of(group // members * hd, 128), hd)
    q_cols = pl.ds(pl.multiple_of(group * gcols, 128), gcols)
    items = [
        (small_ref, small_all, None),
        (wq_ref.at[:, q_cols], w_ref.at[:, pl.ds(0, gcols)], 0),
        (wk_ref.at[:, kv_cols], w_ref.at[:, pl.ds(gcols, hd)], 0),
        (wv_ref.at[:, kv_cols], w_ref.at[:, pl.ds(gcols + hd, hd)], 0),
        (wr_ref, wr_all, 1),
    ]
    start, wait = crossing(shards, items, x_out, x_in, x_own)
    start_down, wait_down = crossing(
        shards, [(wd_ref.at[pl.ds(0, wd_all.shape[0])], wd_all, 1)], d_out, d_in
    )
    owner = group * gcols // wo_ref.shape[0]
    wo_src = wo_ref.at[pl.ds(pl.multiple_of(group * gcols % wo_ref.shape[0], 16), gcols)]
    wo_own = pltpu.make_async_copy(wo_src, wo_all, o_own)

    def wo_send(i):
        return pltpu.make_async_remote_copy(
            src_ref=wo_src,
            dst_ref=wo_all,
            send_sem=o_out.at[i - 1],
            recv_sem=o_in,
            device_id={"fsdp": (mine + i) % shards},
            device_id_type=MESH,
        )

    def begin():
        for n in range(len(items)):
            start(n)

        @pl.when(mine == owner)
        def _():
            wo_own.start()
            for i in range(1, shards):
                wo_send(i).start()

        start_down(0)

    def h_copy(s, holder, half):
        return pltpu.make_async_copy(
            h1.at[s, pl.ds(half * block, block)], h_all.at[at_block(holder, block)], h_sem.at[half]
        )

    def multiply(p):
        first, second = pair_owners(count, p)
        y = mm(h1[p], w_ref[...]).astype(BF16)
        qkv_ref[at_block(first, block), :] = y[:block]
        qkv_ref[at_block(second, block), :] = y[block:]

    def use(s, first, second, pump):
        @pl.when(s == 0)
        def _():
            wait(0)
            for f in range(shards):
                for r in range(local // 128):
                    gain[:, pl.ds(f * local + r * 128, 128)] = small_all[f, r : r + 1, :].astype(F32)

        x = land[s].astype(F32)
        r1 = lax.rsqrt(jnp.mean(x * x, axis=1, keepdims=True) + EPSILON)
        h1[s] = (x * r1 * gain[...]).astype(BF16)
        h_copy(s, first, 0).start()
        h_copy(s, second, 1).start()
        pump(0)

        @pl.when(s == chips // 2)
        def _():
            for n in range(1, len(items)):
                wait(n)

        @pl.when(s >= chips // 2)
        def _():
            multiply(2 * s - chips)
            pump(1)
            multiply(2 * s - chips + 1)

        @pl.when(s < chips // 2)
        def _():
            pump(1)

        for c in range(2, cuts):
            pump(c)

    gather_steps(
        count, cuts, x_ref, land, (ring_out, ring_in, side_out, side_in), use, shards, begin
    )

    @pl.when(mine == owner)
    def _():
        wo_own.wait()
        for i in range(1, shards):
            wo_send(i).wait_send()

    @pl.when(mine != owner)
    def _():
        wo_send(1).wait_recv()

    wait_down(0)
    half_rows = count * block // 2
    for half in range(2):
        pltpu.make_async_copy(
            h_all.at[pl.ds(0, half_rows)], h_all.at[pl.ds(0, half_rows)], h_sem.at[half]
        ).wait()


def front(
    x,
    small,
    w_router,
    w_query,
    key_weight,
    value_weight,
    w_out,
    w_down,
    down_rows,
    hd,
    count,
    shards,
    call,
    cuts=4,
):
    block, dim = x.shape
    gcols = w_query.shape[1] // count
    members = count * hd // key_weight.shape[1]
    columns = gcols + 2 * hd
    chips = count // 2
    dma = pltpu.SemaphoreType.DMA
    return pl.pallas_call(
        functools.partial(front_kernel, count, shards, cuts, (gcols, hd, members)),
        out_shape=(
            jax.ShapeDtypeStruct((count * block, dim), BF16),
            jax.ShapeDtypeStruct((count * block, columns), BF16),
            jax.ShapeDtypeStruct((dim, columns), BF16),
            jax.ShapeDtypeStruct((gcols, w_out.shape[1]), BF16),
            jax.ShapeDtypeStruct((shards,) + small.shape, BF16),
            whole_of(w_router, 1, shards),
            jax.ShapeDtypeStruct((down_rows, dim), BF16),
        ),
        in_specs=[VMEM, VMEM, VMEM] + [ANY] * 5,
        out_specs=[ANY, VMEM, VMEM, VMEM, VMEM, VMEM, ANY],
        scratch_shapes=gather_scratch(count, cuts, block, dim)
        + crossing_scratch(shards, 5)
        + [
            dma((5,)),
        ]
        + crossing_scratch(shards, 1)
        + [
            pltpu.VMEM((chips, 2 * block, dim), BF16),
            pltpu.VMEM((1, dim), F32),
            dma((2,)),
            dma((max(1, shards - 1),)),
            dma,
            dma,
        ],
        compiler_params=remote_params(call, 48),
    )(x, small, w_router, w_query, key_weight, value_weight, w_out, w_down)


def out_back_kernel(
    count,
    cuts,
    da_ref,
    w_ref,
    o_ref,
    hid_ref,
    de_ref,
    xs_ref,
    dgu_ref,
    do_ref,
    part_ref,
    down_ref,
    up_ref,
    land,
    *rest,
):
    sems = rest[:4]
    total, hid, du, de, xs, sem, tile_sem = rest[4:]
    block = da_ref.shape[0]
    columns = de.shape[2]
    ffe = hid.shape[1]
    total[...] = jnp.zeros_like(total)
    loads = [
        pltpu.make_async_copy(hid_ref, hid, sem.at[0]),
        pltpu.make_async_copy(dgu_ref.at[:, pl.ds(ffe, ffe)], du, sem.at[1]),
    ]

    def tiles(s):
        part = pl.ds(pl.multiple_of(s * columns, 128), columns)
        return [
            pltpu.make_async_copy(src.at[:, part], dst.at[s % 2], tile_sem.at[s % 2, n])
            for n, (src, dst) in enumerate(((de_ref, de), (xs_ref, xs)))
        ]

    def begin():
        for load in loads + tiles(0):
            load.start()

    def use(s, first, second, pump):
        @pl.when(s == 0)
        def _():
            for load in loads:
                load.wait()

        @pl.when(s < count // 2 - 1)
        def _():
            for load in tiles(s + 1):
                load.start()

        pair = land[s]
        a = at_block(first, block)
        b = at_block(second, block)
        do = mm(pair, w_ref[...], NT).astype(BF16)
        do_ref[a, :] = do[:block]
        do_ref[b, :] = do[block:]
        pump(0)
        total[...] += mm(jnp.concatenate([o_ref[a, :], o_ref[b, :]], axis=0), pair, TN)
        pump(1)
        for load in tiles(s):
            load.wait()
        part = pl.ds(pl.multiple_of(s * columns, 128), columns)
        down_ref[:, part] = mm(hid[...], de[s % 2], TN).astype(BF16)
        pump(2)
        rows = pl.ds(pl.multiple_of(s * columns, 16), columns)
        up_ref[rows, :] = mm(xs[s % 2], du[...], TN).astype(BF16)
        for c in range(3, cuts):
            pump(c)

    gather_steps(count, cuts, da_ref, land, sems, use, 1, begin)
    part_ref[...] = total[...].astype(BF16)


def out_back(da, w, o, hid, de, xs, dgu, count, call, cuts=4):
    block, dim = da.shape
    ffe = hid.shape[1]
    chips = count // 2
    dma = pltpu.SemaphoreType.DMA
    return pl.pallas_call(
        functools.partial(out_back_kernel, count, cuts),
        out_shape=(
            jax.ShapeDtypeStruct(o.shape, BF16),
            jax.ShapeDtypeStruct(w.shape, BF16),
            jax.ShapeDtypeStruct((ffe, dim), BF16),
            jax.ShapeDtypeStruct((dim, ffe), BF16),
        ),
        in_specs=[VMEM] * 3 + [ANY] * 4,
        out_specs=[VMEM] * 4,
        scratch_shapes=gather_scratch(count, cuts, block, dim)
        + [
            pltpu.VMEM(w.shape, F32),
            pltpu.VMEM(hid.shape, BF16),
            pltpu.VMEM(hid.shape, BF16),
            pltpu.VMEM((2, de.shape[0], dim // chips), BF16),
            pltpu.VMEM((2, xs.shape[0], dim // chips), BF16),
            dma((2,)),
            dma((2, 2)),
        ],
        compiler_params=remote_params(call, 56),
    )(da, w, o, hid, de, xs, dgu)


def product_kernel(count, shards, cuts, dims, axes, y_ref, w_ref, *refs):
    cargo = len(axes)
    srcs, o_ref, dsts = refs[:cargo], refs[cargo], refs[cargo + 1 : 2 * cargo + 1]
    rest = refs[2 * cargo + 1 :]
    block = o_ref.shape[0]
    if cargo:
        lasts = []
        for src, dst, axis in zip(srcs, dsts, axes):
            rows = dst.shape[0] if axis else src.shape[0]
            lasts.append((src.at[pl.ds(src.shape[0] - rows, rows)], dst, axis))
        start, wait = crossing(shards, lasts, *rest[9:])

    def begin():
        for n in range(cargo):
            start(n)

    def produce(k, first, second):
        a = y_ref[at_block(first, block), :]
        b = y_ref[at_block(second, block), :]
        both = mm(jnp.concatenate([a, b], axis=0), w_ref[...], dims)
        return both[:block], both[block:]

    scatter_steps(
        count, cuts, o_ref, rest[:5], rest[5:9], produce, None, shards if cargo else 1, begin
    )
    for n in range(cargo):
        wait(n)


def token_back_kernel(
    count,
    shards,
    cuts,
    y_ref,
    w_ref,
    gains_ref,
    h_ref,
    o_ref,
    sum_ref,
    *rest,
):
    chips = count // 2
    block = o_ref.shape[0]
    hbuf, grad, came, gains, h_sem, w_out, w_in, g_out, g_in = rest[9:]
    mine = lax.axis_index("fsdp")
    dim, columns = grad.shape
    local = dim // shards
    part = dim // chips
    per = local // part
    width = gains_ref.shape[1]

    def chunk(k):
        return (k + (mine + 1) % shards * per) % chips

    def load(k):
        cols = pl.ds(pl.multiple_of(chunk(k) * part, 128), part)
        return pltpu.make_async_copy(h_ref.at[:, cols], hbuf.at[k % 2], h_sem.at[k % 2])

    def send(k):
        n = chunk(k)
        owner = n // per
        slot = (owner - mine + shards) % shards - 1
        return pltpu.make_async_remote_copy(
            src_ref=grad.at[pl.ds(pl.multiple_of(n * part, 16), part)],
            dst_ref=came.at[slot, pl.ds(pl.multiple_of(n % per * part, 16), part)],
            send_sem=w_out.at[k],
            recv_sem=w_in.at[slot, n % per],
            device_id={"fsdp": owner},
            device_id_type=MESH,
        )

    def send_gains(i):
        return pltpu.make_async_remote_copy(
            src_ref=gains_ref,
            dst_ref=gains.at[i - 1],
            send_sem=g_out.at[i - 1],
            recv_sem=g_in.at[i - 1],
            device_id={"fsdp": (mine + i) % shards},
            device_id_type=MESH,
        )

    def begin():
        load(0).start()
        for i in range(1, shards):
            send_gains(i).start()

    def produce(k, first, second):
        a = y_ref[at_block(first, block), :]
        b = y_ref[at_block(second, block), :]
        both = mm(jnp.concatenate([a, b], axis=0), w_ref[...], NT)
        return both[:block], both[block:]

    def extra(k):
        load(k).wait()

        @pl.when(k < chips - 1)
        def _():
            load(k + 1).start()

        rows = pl.ds(pl.multiple_of(chunk(k) * part, 16), part)
        grad[rows, :] = mm(hbuf[k % 2], y_ref[...], TN).astype(BF16)

        @pl.when(k < chips - per)
        def _():
            send(k).start()

    scatter_steps(count, cuts, o_ref, rest[:5], rest[5:9], produce, extra, shards, begin)
    total = gains_ref[...]
    for i in range(1, shards):
        send_gains(i).wait()
        total = total + gains[i - 1]
    row = lax.broadcasted_iota(jnp.int32, (16, width), 0)
    sum_ref[pl.ds(local, 16), :] = jnp.zeros((16, columns), BF16)
    for n in range(2):
        sum_ref[pl.ds(local, 16), pl.ds(n * width, width)] = jnp.where(
            row == 0, jnp.broadcast_to(total[n : n + 1, :], (16, width)), 0.0
        ).astype(BF16)
    for k in range(chips - per):
        send(k).wait_send()
    for n in range(per):
        part_rows = pl.ds(n * part, part)
        own = grad[pl.ds(pl.multiple_of(mine * local + n * part, 16), part), :].astype(F32)
        for i in range(1, shards):
            pltpu.make_async_remote_copy(
                src_ref=grad.at[part_rows],
                dst_ref=came.at[i - 1, part_rows],
                send_sem=w_out.at[0],
                recv_sem=w_in.at[i - 1, n],
                device_id={"fsdp": (mine + i) % shards},
                device_id_type=MESH,
            ).wait_recv()
            own = own + came[i - 1, part_rows, :].astype(F32)
        sum_ref[part_rows, :] = own.astype(BF16)


def token_back(y, w, gains, h_all, count, shards, call, cuts=2):
    block = y.shape[0] // count
    dim, columns = w.shape
    chips = count // 2
    local = dim // shards
    others = max(1, shards - 1)
    dma = pltpu.SemaphoreType.DMA
    return pl.pallas_call(
        functools.partial(token_back_kernel, count, shards, cuts),
        out_shape=(
            jax.ShapeDtypeStruct((block, dim), F32),
            jax.ShapeDtypeStruct((local + 16, columns), BF16),
        ),
        in_specs=[VMEM] * 3 + [ANY],
        out_specs=[VMEM] * 2,
        scratch_shapes=scatter_scratch(count, cuts, block, dim)
        + [
            pltpu.VMEM((2, h_all.shape[0], dim // chips), BF16),
            pltpu.VMEM((dim, columns), BF16),
            pltpu.VMEM((others, local, columns), BF16),
            pltpu.VMEM((others,) + gains.shape, F32),
            dma((2,)),
            dma((chips,)),
            dma((others, chips // shards)),
            dma((others,)),
            dma((others,)),
        ],
        compiler_params=remote_params(call, 48),
    )(y, w, gains, h_all)


def whole_of(part, axis, shards):
    shape = list(part.shape)
    shape[axis] *= shards
    return jax.ShapeDtypeStruct(tuple(shape), part.dtype)


def product_scattered(y, w, dims, cargo, axes, wholes, count, shards, call, cuts=2):
    block = y.shape[0] // count
    columns = w.shape[1 - dims[0][1][0]]
    return pl.pallas_call(
        functools.partial(product_kernel, count, shards, cuts, dims, axes),
        out_shape=[jax.ShapeDtypeStruct((block, columns), F32)]
        + list(wholes),
        in_specs=[VMEM, VMEM] + [ANY] * len(cargo),
        out_specs=[VMEM] + [ANY] * len(cargo),
        scratch_shapes=scatter_scratch(count, cuts, block, columns)
        + (crossing_scratch(shards, len(cargo)) if cargo else []),
        compiler_params=remote_params(call, 48),
    )(y, w, *cargo)


def one_hot_of(slot_ref, first, second, capacity):
    a = slot_ref[pl.ds(first, 1), :]
    b = slot_ref[pl.ds(second, 1), :]
    wanted = jnp.concatenate([a, jnp.where(b >= 0, b + capacity, -1)], axis=1)
    row = lax.broadcasted_iota(jnp.int32, (2 * capacity, wanted.shape[1]), 0)
    return jnp.where(row == wanted, 1.0, 0.0).astype(BF16)


def parts_of_own(i, shards, size, unit):
    place = (lax.axis_index("fsdp") + i) % shards
    return pl.ds(pl.multiple_of(place * (size // shards), unit), size // shards)


def gate_up_parts(i, shards, whole, own, wgu):
    rows = parts_of_own(i, shards, wgu.shape[0], 16)
    ffe = wgu.shape[1] // 2
    return [
        (whole[n].at[rows] if i else own[n], wgu.at[rows, pl.ds(n * ffe, ffe)]) for n in range(2)
    ]


def down_parts(i, shards, pieces, own, wd):
    columns = parts_of_own(i, shards, wd.shape[1], 128)
    parts = []
    first = 0
    for piece in pieces:
        rows = pl.ds(first, piece.shape[0])
        first += piece.shape[0]
        parts.append((piece.at[:, columns] if i else own.at[rows], wd.at[rows, columns]))
    return parts


def expert_kernel(
    count,
    shards,
    cuts,
    capacity,
    h_ref,
    slot_ref,
    chosen_ref,
    router_ref,
    dy_ref,
    wg_ref,
    wu_ref,
    wd1_ref,
    wd2_ref,
    wd3_ref,
    wg_own,
    wu_own,
    wd_own,
    xs_out,
    de_out,
    dx_ref,
    dl_out,
    ce_out,
    hid_out,
    dgu_out,
    land,
    ring_out,
    ring_in,
    side_out,
    side_in,
    wgu,
    wd,
    dyb,
    xs,
    de,
    dl,
    ce,
    hid,
    dgu,
    w_sem,
    dy_sem,
    out_sem,
):
    block, dim = h_ref.shape
    ffe = wd.shape[0]
    wd_refs = (wd1_ref, wd2_ref, wd3_ref)
    me = lax.axis_index("seq")
    chips = count // 2
    weights = [
        pltpu.make_async_copy(src, dst, w_sem.at[i, n])
        for i in range(shards)
        for n, (src, dst) in enumerate(
            gate_up_parts(i, shards, (wg_ref, wu_ref), (wg_own, wu_own), wgu)
            + down_parts(i, shards, wd_refs, wd_own, wd)
        )
    ]
    staged = (
        (xs, xs_out),
        (de, de_out),
        (dl, dl_out),
        (ce, ce_out),
        (hid, hid_out),
        (dgu, dgu_out),
    )

    def dy_copies(s):
        first, second = pair_owners(count, s)
        return [
            pltpu.make_async_copy(
                dy_ref.at[at_block(owner, block)], dyb.at[s % 2, pl.ds(half * block, block)], dy_sem.at[s % 2, half]
            )
            for half, owner in ((0, first), (1, second))
        ]

    for copy in weights + dy_copies(0):
        copy.start()

    def use(s, first, second, pump):
        @pl.when(s < chips - 1)
        def _():
            for copy in dy_copies(s + 1):
                copy.start()

        rows = pl.ds(pl.multiple_of(s * 2 * capacity, 16), 2 * capacity)
        pick = one_hot_of(slot_ref, first, second, capacity)
        x = mm(pick, land[s]).astype(BF16)
        xs[rows, :] = x
        chosen = mm(
            pick,
            jnp.concatenate(
                [
                    chosen_ref[pl.ds(pl.multiple_of(first * block, block), block), :],
                    chosen_ref[pl.ds(pl.multiple_of(second * block, block), block), :],
                ],
                axis=0,
            ),
        )
        logits = jnp.where(chosen > 0.5, mm(x, router_ref[...], NT), -1e30)
        weight = jnp.exp(logits - jnp.max(logits, axis=1, keepdims=True)) * chosen
        mass = jnp.sum(weight, axis=1, keepdims=True)
        expert_lane = lax.broadcasted_iota(jnp.int32, weight.shape, 1)
        wide_lane = lax.broadcasted_iota(jnp.int32, (2 * capacity, dl.shape[1]), 1)
        gate = jnp.sum(jnp.where(expert_lane == me, weight, 0.0), axis=1, keepdims=True)
        gate = gate / jnp.where(mass > 0.0, mass, 1.0)

        @pl.when(s == 0)
        def _():
            for copy in weights:
                copy.wait()

        gu = mm(x, wgu[...])
        pump(0)
        g, u = gu[:, :ffe], gu[:, ffe:]
        sig = jax.nn.sigmoid(g)
        silu = g * sig
        h = (silu * u).astype(BF16)
        hid[rows, :] = h
        e = mm(h, wd[...])
        ce[rows, :] = (gate * e).astype(BF16)
        pump(1)
        for copy in dy_copies(s):
            copy.wait()
        dys = mm(pick, dyb[s % 2])
        dgate = jnp.sum(dys * e, axis=1, keepdims=True)
        d = (gate * dys).astype(BF16)
        de[rows, :] = d
        pump(2)
        dh = mm(d, wd[...], NT)
        for c in range(3, cuts):
            pump(c)
        dg = (dh * u * (sig + silu * (1.0 - sig))).astype(BF16)
        du = (dh * silu).astype(BF16)
        dgu[rows, :ffe] = dg
        dgu[rows, ffe:] = du

        @pl.when(s == 1)
        def _():
            dx_ref[...] = mm(dgu[rows, :], wgu[...], NT).astype(BF16)

        high = dgate.astype(BF16).astype(F32)
        dl[rows, :] = jnp.where(
            wide_lane == me, high, jnp.where(wide_lane == me + 64, dgate - high, 0.0)
        ).astype(BF16)
        for i, (src, dst) in enumerate(staged):
            pltpu.make_async_copy(src.at[rows], dst.at[rows], out_sem.at[i]).start()

    gather_steps(count, cuts, h_ref, land, (ring_out, ring_in, side_out, side_in), use)
    for i, (src, dst) in enumerate(staged):
        pltpu.make_async_copy(src, dst, out_sem.at[i]).wait()


def expert_gathered(h2, slot, chosen, router, dy_all, weights, capacity, count, shards, call, cuts=4):
    block, dim = h2.shape
    ffe = weights[0].shape[1]
    total = count * capacity
    widths = (dim, dim, 128, dim, ffe, 2 * ffe)
    dma = pltpu.SemaphoreType.DMA
    return pl.pallas_call(
        functools.partial(expert_kernel, count, shards, cuts, capacity),
        out_shape=[
            jax.ShapeDtypeStruct((2 * capacity if i == 2 else total, n), BF16)
            for i, n in enumerate(widths[:2] + (dim,) + widths[2:])
        ],
        in_specs=[VMEM] * 4 + [ANY] * 9,
        out_specs=[ANY] * 2 + [VMEM] + [ANY] * 4,
        scratch_shapes=gather_scratch(count, cuts, block, dim)
        + [
            pltpu.VMEM((dim, 2 * ffe), BF16),
            pltpu.VMEM((ffe, dim), BF16),
            pltpu.VMEM((2, 2 * block, dim), BF16),
        ]
        + [pltpu.VMEM((total, n), BF16) for n in widths]
        + [dma((shards, 5)), dma((2, 2)), dma((6,))],
        compiler_params=remote_params(call, 60),
    )(h2, slot, chosen, router, dy_all, *weights)


def slots_back_kernel(
    count,
    shards,
    cuts,
    capacity,
    slot_ref,
    dl,
    dx0_ref,
    xs_ref,
    dgu_ref,
    wg_ref,
    wu_ref,
    wg_own,
    wu_own,
    o_ref,
    gate_out,
    *rest,
):
    bufs, sems = rest[:5], rest[5:9]
    dx, xs, dgu, wgu, gate, sem, w_sem, gate_sem = rest[9:]
    chips = count // 2
    block = o_ref.shape[0]
    ffe = gate.shape[1]
    load_dgu = pltpu.make_async_copy(dgu_ref, dgu, sem.at[0])
    load_xs = pltpu.make_async_copy(xs_ref, xs, sem.at[1])
    weights = [
        pltpu.make_async_copy(src, dst, w_sem.at[i, n])
        for i in range(shards)
        for n, (src, dst) in enumerate(
            gate_up_parts(i, shards, (wg_ref, wu_ref), (wg_own, wu_own), wgu)
        )
    ]
    part = xs.shape[1] // chips

    def begin():
        for load in [load_dgu] + weights + [load_xs]:
            load.start()

    def produce(k, first, second):
        rows = pl.ds(pl.multiple_of((k + 1) % chips * 2 * capacity, 16), 2 * capacity)

        @pl.when(k == 0)
        def _():
            dx[...] = dx0_ref[...]

        @pl.when(k == 1)
        def _():
            for load in [load_dgu] + weights:
                load.wait()

        @pl.when(k > 0)
        def _():
            dx[...] = mm(dgu[rows, :], wgu[...], NT).astype(BF16)

        pick = one_hot_of(slot_ref, first, second, capacity)
        both = jnp.concatenate([mm(pick, dx[...], TN), mm(pick, dl[rows, :], TN)], axis=1)
        return both[:block], both[block:]

    def extra(k):
        @pl.when(k == 0)
        def _():
            load_xs.wait()

        columns = pl.ds(pl.multiple_of(k * part, 128), part)
        rows = pl.ds(pl.multiple_of(k * part, 16), part)
        gate[rows, :] = mm(xs[:, columns], dgu[:, :ffe], TN).astype(BF16)
        pltpu.make_async_copy(gate.at[rows], gate_out.at[rows], gate_sem).start()

    scatter_steps(count, cuts, o_ref, bufs, sems, produce, extra, 1, begin)
    pltpu.make_async_copy(gate, gate_out, gate_sem).wait()


def slots_back(slot, dl, dx0, xs, dgu, weights, capacity, count, shards, call, cuts=2):
    block = slot.shape[1]
    dim, ffe = xs.shape[1], dgu.shape[1] // 2
    columns = dim + dl.shape[1]
    dma = pltpu.SemaphoreType.DMA
    return pl.pallas_call(
        functools.partial(slots_back_kernel, count, shards, cuts, capacity),
        out_shape=(
            jax.ShapeDtypeStruct((block, columns), F32),
            jax.ShapeDtypeStruct((dim, ffe), BF16),
        ),
        in_specs=[VMEM] * 3 + [ANY] * 6,
        out_specs=[VMEM, ANY],
        scratch_shapes=scatter_scratch(count, cuts, block, columns)
        + [pltpu.VMEM(a.shape, BF16) for a in (dx0, xs, dgu)]
        + [pltpu.VMEM((dim, 2 * ffe), BF16), pltpu.VMEM((dim, ffe), BF16)]
        + [dma((2,)), dma((shards, 2)), dma],
        compiler_params=remote_params(call, 60),
    )(slot, dl, dx0, xs, dgu, *weights)


def split3(x):
    first = x.astype(BF16)
    rest = x - first.astype(F32)
    second = rest.astype(BF16)
    return first, second, (rest - second.astype(F32)).astype(BF16)


def in_lanes(x):
    lane = lax.broadcasted_iota(jnp.int32, x.shape, 1)
    first = x.astype(BF16).astype(F32)
    second = (x - first).astype(BF16).astype(F32)
    third = x - first - second
    spread = jnp.where(lane == 0, first, jnp.where(lane == 1, second, third))
    return jnp.where(lane < 3, spread, 0.0).astype(BF16)


def swap_halves(x):
    half = x.shape[1] // 2
    return jnp.concatenate([x[:, half:], x[:, :half]], axis=1)


def unit_rows(u):
    r = lax.rsqrt(jnp.mean(u * u, axis=1, keepdims=True) + EPSILON)
    return r, u * r


def attend_kernel(
    count,
    shards,
    cuts,
    heads,
    tile,
    dy_ref,
    routes_ref,
    qkv_ref,
    gq_ref,
    gk_ref,
    cos_ref,
    sin_ref,
    start_ref,
    wg_ref,
    wd_ref,
    dy_all,
    routes_all,
    o_ref,
    qx_ref,
    kn_ref,
    wg_all,
    wd_all,
    land,
    ring_out,
    ring_in,
    side_out,
    side_in,
    x_out,
    x_in,
    tag,
    vx_ref,
    dy_sem,
):
    span = qkv_ref.shape[0]
    width = kn_ref.shape[1]
    block = dy_ref.shape[0]
    scale = width**-0.5 * LOG2E
    down = wd_all.shape[0]
    items = [(wg_ref, wg_all, 0), (wd_ref.at[pl.ds(down, down)], wd_all, 1)]
    start_item, wait_item = crossing(shards, items, x_out, x_in)

    def prepare(i):
        rows = pl.ds(i * tile, tile)
        cos, sin = cos_ref[rows, :], sin_ref[rows, :]
        for h in range(heads + 1):
            _, unit = unit_rows(qkv_ref[rows, pl.ds(h * width, width)].astype(F32))
            u = unit * (gk_ref[...] if h == heads else gq_ref[...])
            u = u * cos + swap_halves(u) * sin
            if h == heads:
                kn_ref[rows, :] = u.astype(BF16)
            else:
                qx_ref[rows, pl.ds(2 * h * width, width)] = (u * scale).astype(BF16)
        vx_ref[rows, :width] = qkv_ref[rows, pl.ds((heads + 1) * width, width)]
        vx_ref[rows, width:] = jnp.ones((tile, width), BF16)

    def attend_rows(i, h):
        rows = pl.ds(i * tile, tile)
        start = start_ref[rows, :]
        row = i * tile + lax.broadcasted_iota(jnp.int32, (tile, tile), 0)
        q = qx_ref[rows, pl.ds(2 * h * width, width)]
        total = jnp.zeros((tile, 2 * width), F32)
        for j in range(i + 1):
            keys = pl.ds(j * tile, tile)
            s = mm(q, kn_ref[keys, :], NT)
            col = j * tile + lax.broadcasted_iota(jnp.int32, (tile, tile), 1)
            keep = col >= start
            if i == j:
                keep = keep & (col <= row)
            p = jnp.where(keep, jnp.exp2(s), 0.0).astype(BF16)
            total = total + mm(p, vx_ref[keys, :])
        weight = total[:, width:]
        o_ref[rows, pl.ds(h * width, width)] = (total[:, :width] / weight).astype(BF16)
        qx_ref[rows, pl.ds((2 * h + 1) * width, width)] = in_lanes(-jnp.log2(weight))

    units = []
    for i in range(span // tile):
        units.append((1.0, functools.partial(prepare, i)))
        units += [(0.7 * (i + 1), functools.partial(attend_rows, i, h)) for h in range(heads)]
    plan = spread_units(units, count // 2 - 1)

    def begin():
        for n in range(len(items)):
            start_item(n)

    tag[0, 0] = routes_ref[...]

    def use(s, first, second, pump):
        for half, owner in ((0, first), (1, second)):
            pltpu.make_async_copy(
                land.at[s, pl.ds(half * block, block)],
                dy_all.at[at_block(owner, block)],
                dy_sem.at[half],
            ).start()
            routes_all[owner] = tag[s, half]
        run_units(plan, s)
        for c in range(cuts + 1):
            pump(c)

    gather_steps(
        count, cuts, dy_ref, land, (ring_out, ring_in, side_out, side_in), use, shards, begin, tag
    )
    for n in range(len(items)):
        wait_item(n)
    half_rows = count * block // 2
    for half in range(2):
        pltpu.make_async_copy(
            dy_all.at[pl.ds(0, half_rows)], dy_all.at[pl.ds(0, half_rows)], dy_sem.at[half]
        ).wait()


def attend(dy, routes, qkv, gq, gk, cos, sin, start, w_gate, w_down, down_rows, count, shards, call, tile=512, cuts=4):
    span = qkv.shape[0]
    width = gq.shape[0]
    heads = qkv.shape[1] // width - 2
    block, dim = dy.shape
    chips = count // 2
    return pl.pallas_call(
        functools.partial(attend_kernel, count, shards, cuts, heads, min(tile, span)),
        out_shape=(
            jax.ShapeDtypeStruct((count * block, dim), BF16),
            jax.ShapeDtypeStruct((count,) + routes.shape, BF16),
            jax.ShapeDtypeStruct((span, heads * width), BF16),
            jax.ShapeDtypeStruct((span, 2 * heads * width), BF16),
            jax.ShapeDtypeStruct((span, width), BF16),
            whole_of(w_gate, 0, shards),
            jax.ShapeDtypeStruct((down_rows, dim), BF16),
        ),
        in_specs=[VMEM] * 8 + [ANY] * 2,
        out_specs=[ANY] + [VMEM] * 4 + [ANY] * 2,
        scratch_shapes=gather_scratch(count, cuts + 1, block, dim)
        + crossing_scratch(shards, 2)
        + [
            pltpu.VMEM((chips, 2) + routes.shape, BF16),
            pltpu.VMEM((span, 2 * width), BF16),
            pltpu.SemaphoreType.DMA((2,)),
        ],
        compiler_params=remote_params(call, 56),
    )(dy, routes, qkv, gq[None, :], gk[None, :], cos, sin, start[:, None], w_gate, w_down)


def attend_back_kernel(
    count,
    shards,
    cuts,
    capacity,
    heads,
    tile,
    qx_ref,
    kn_ref,
    qkv_ref,
    o_ref,
    do_ref,
    gq_ref,
    gk_ref,
    cos_ref,
    sin_ref,
    start_ref,
    slot_ref,
    part_ref,
    ce_ref,
    dqkv_ref,
    gains_ref,
    mixed_ref,
    half_ref,
    *rest,
):
    bufs, sems = rest[:5], rest[5:9]
    gx_ref, dq_ref, dk_ref, dv_ref, held, held_sem, pair, pair_own, pair_out, pair_in = rest[9:]
    span = qx_ref.shape[0]
    width = kn_ref.shape[1]
    scale = width**-0.5
    chips = count // 2
    block = mixed_ref.shape[0]
    load = pltpu.make_async_copy(ce_ref, held, held_sem)
    load.start()

    mine = lax.axis_index("fsdp")
    me = lax.axis_index("seq")
    lane = me % 2
    chip_first = me - lane
    half_rows = half_ref.shape[0]

    def give_half(c):
        return pltpu.make_async_remote_copy(
            src_ref=part_ref.at[pl.ds(c * half_rows, half_rows)],
            dst_ref=pair.at[(mine + lane) % 2],
            send_sem=pair_out.at[c],
            recv_sem=pair_in.at[(mine + lane) % 2],
            device_id={"fsdp": lane, "seq": chip_first + c},
            device_id_type=MESH,
        )

    def take_half(n):
        return pltpu.make_async_remote_copy(
            src_ref=part_ref.at[pl.ds(0, half_rows)],
            dst_ref=pair.at[n],
            send_sem=pair_out.at[0],
            recv_sem=pair_in.at[n],
            device_id={"fsdp": 1 - mine, "seq": chip_first + mine},
            device_id_type=MESH,
        )

    keep_half = pltpu.make_async_copy(
        part_ref.at[pl.ds(pl.multiple_of(lane * half_rows, 16), half_rows)], pair.at[0], pair_own
    )

    def meet():
        barrier = pltpu.get_barrier_semaphore()
        pl.semaphore_signal(
            barrier,
            inc=1,
            device_id={"fsdp": 1 - mine, "seq": chip_first + mine},
            device_id_type=MESH,
        )

        @pl.when(lane != mine)
        def _():
            pl.semaphore_signal(
                barrier, inc=1, device_id={"seq": chip_first + mine}, device_id_type=MESH
            )

    def begin():
        for c in range(2):

            @pl.when((mine != lane) | (lane != c))
            def _(c=c):
                give_half(c).start()

        @pl.when(mine == lane)
        def _():
            keep_half.start()

    def end():
        for c in range(2):

            @pl.when((mine != lane) | (lane != c))
            def _(c=c):
                give_half(c).wait_send()

        @pl.when(mine == lane)
        def _():
            keep_half.wait()

        @pl.when(mine != lane)
        def _():
            take_half(0).wait_recv()

        take_half(1).wait_recv()
        half_ref[...] = (pair[0].astype(F32) + pair[1].astype(F32)).astype(BF16)

    summing = shards == 2
    partners = 1 + (mine != lane).astype(jnp.int32)

    def produce(k, first, second):
        @pl.when(k == 0)
        def _():
            load.wait()

        pair = pl.multiple_of((k + 1) % chips * 2 * capacity, 16)
        pick = one_hot_of(slot_ref, first, second, capacity)
        both = mm(pick, held[pl.ds(pair, 2 * capacity), :], TN)
        return both[:block], both[block:]

    def to_raw(d, h, rows, gain, row):
        r, unit = unit_rows(qkv_ref[rows, pl.ds(h * width, width)].astype(F32))
        d = d * cos_ref[rows, :] + swap_halves(d * sin_ref[rows, :])
        dg = d * gain
        raw = r * (dg - unit * jnp.mean(dg * unit, axis=1, keepdims=True))
        dqkv_ref[rows, pl.ds(h * width, width)] = raw.astype(BF16)
        gains_ref[row : row + 1, :] += jnp.sum(d * unit, axis=0, keepdims=True)

    def prepare(i):
        rows = pl.ds(i * tile, tile)
        for h in range(heads):
            cols = pl.ds(h * width, width)
            do = do_ref[rows, cols]
            inner = jnp.sum(do.astype(F32) * o_ref[rows, cols].astype(F32), axis=1, keepdims=True)
            gx_ref[rows, pl.ds(2 * h * width, width)] = do
            gx_ref[rows, pl.ds((2 * h + 1) * width, width)] = in_lanes(
                jnp.broadcast_to(-inner, (tile, width))
            )

    def tile_back(j, i):
        keys = pl.ds(j * tile, tile)
        rows = pl.ds(i * tile, tile)
        ones = jnp.ones((tile, width), BF16)
        kn = kn_ref[keys, :]
        kx = jnp.concatenate([kn, ones], axis=1)
        vx = jnp.concatenate([qkv_ref[keys, pl.ds((heads + 1) * width, width)], ones], axis=1)
        key = j * tile + lax.broadcasted_iota(jnp.int32, (tile, tile), 0)
        keep = key >= start_ref[:, rows]
        if i == j:
            row = i * tile + lax.broadcasted_iota(jnp.int32, (tile, tile), 1)
            keep = keep & (key <= row)
        for h in range(heads):
            qx = qx_ref[rows, pl.ds(2 * h * width, 2 * width)]
            gx = gx_ref[rows, pl.ds(2 * h * width, 2 * width)]
            p = jnp.where(keep, jnp.exp2(mm(kx, qx, NT)), 0.0)
            ds = (p * mm(vx, gx, NT)).astype(BF16)
            dv_ref[keys, :] += mm(p.astype(BF16), gx[:, :width])
            dk_ref[keys, :] += mm(ds, qx[:, :width])
            dq_ref[rows, pl.ds(h * width, width)] += mm(ds, kn, TN)

    def finish_keys(j):
        keys = pl.ds(j * tile, tile)
        dqkv_ref[keys, pl.ds((heads + 1) * width, width)] = dv_ref[keys, :].astype(BF16)
        to_raw(dk_ref[keys, :] * (1.0 / LOG2E), heads, keys, gk_ref[...], 1)

    def finish_rows(i):
        rows = pl.ds(i * tile, tile)
        for h in range(heads):
            to_raw(dq_ref[rows, pl.ds(h * width, width)] * scale, h, rows, gq_ref[...], 0)

    tiles = span // tile
    units = [(0.3, functools.partial(prepare, i)) for i in range(tiles)]
    for j in range(tiles):
        units += [(2.0, functools.partial(tile_back, j, i)) for i in range(j, tiles)]
        units.append((0.3, functools.partial(finish_keys, j)))
        units.append((0.6, functools.partial(finish_rows, j)))
    plan = spread_units(units, chips - 1)
    for ref in (dq_ref, dk_ref, dv_ref, gains_ref):
        ref[...] = jnp.zeros_like(ref)

    def extra(k):
        run_units(plan, k)

    if summing:
        scatter_steps(
            count, cuts, mixed_ref, bufs, sems, produce, extra, 1, begin, (meet, partners)
        )
        end()
    else:
        scatter_steps(count, cuts, mixed_ref, bufs, sems, produce, extra)
        half_ref[...] = jnp.zeros_like(half_ref)


def attend_back(qx, kn, qkv, o, do, gq, gk, cos, sin, start, slot, part, ce, capacity, count, shards, call, tile=512, cuts=2):
    span, width = kn.shape
    heads = o.shape[1] // width
    block = slot.shape[1]
    dim = ce.shape[1]
    return pl.pallas_call(
        functools.partial(
            attend_back_kernel, count, shards, cuts, capacity, heads, min(tile, span)
        ),
        out_shape=(
            jax.ShapeDtypeStruct(qkv.shape, BF16),
            jax.ShapeDtypeStruct((8, width), F32),
            jax.ShapeDtypeStruct((block, dim), F32),
            jax.ShapeDtypeStruct((part.shape[0] // 2, dim), BF16),
        ),
        in_specs=[VMEM] * 12 + [ANY],
        out_specs=[VMEM] * 4,
        scratch_shapes=scatter_scratch(count, cuts, block, dim)
        + [
            pltpu.VMEM((span, 2 * heads * width), BF16),
            pltpu.VMEM((span, heads * width), F32),
            pltpu.VMEM((span, width), F32),
            pltpu.VMEM((span, width), F32),
            pltpu.VMEM(ce.shape, BF16),
            pltpu.SemaphoreType.DMA,
            pltpu.VMEM((2, part.shape[0] // 2, dim), BF16),
            pltpu.SemaphoreType.DMA,
            pltpu.SemaphoreType.DMA((2,)),
            pltpu.SemaphoreType.DMA((2,)),
        ],
        compiler_params=remote_params(call, 60),
    )(qx, kn, qkv, o, do, gq[None, :], gk[None, :], cos, sin, start[None, :], slot, part, ce)


def rows_kernel(count, cuts, x_ref, small_ref, all_ref, small_all, land, ro, ri, so, si, tag, sem):
    block = x_ref.shape[0]
    tag[0, 0] = small_ref[...]

    def use(s, first, second, pump):
        for c in range(cuts + 1):
            pump(c)
        for half, owner in ((0, first), (1, second)):
            pltpu.make_async_copy(
                land.at[s, pl.ds(half * block, block)],
                all_ref.at[at_block(owner, block)],
                sem.at[half],
            ).start()
            small_all[owner] = tag[s, half]

    gather_steps(count, cuts, x_ref, land, (ro, ri, so, si), use, 1, None, tag)
    half_rows = count * block // 2
    for half in range(2):
        pltpu.make_async_copy(
            all_ref.at[pl.ds(0, half_rows)], all_ref.at[pl.ds(0, half_rows)], sem.at[half]
        ).wait()


def gather_rows(x, small, count, call, cuts=4):
    block, dim = x.shape
    return pl.pallas_call(
        functools.partial(rows_kernel, count, cuts),
        out_shape=(
            jax.ShapeDtypeStruct((count * block, dim), BF16),
            jax.ShapeDtypeStruct((count,) + small.shape, BF16),
        ),
        in_specs=[VMEM] * 2,
        out_specs=[ANY, VMEM],
        scratch_shapes=gather_scratch(count, cuts + 1, block, dim)
        + [pltpu.VMEM((count // 2, 2) + small.shape, BF16), pltpu.SemaphoreType.DMA((2,))],
        compiler_params=remote_params(call, 48),
    )(x, small)


def row_parts(rows, cuts):
    if cuts == 1:
        return [pl.ds(0, rows)]
    size = rows // cuts // 16 * 16
    return [pl.ds(c * size, size) for c in range(cuts - 1)] + [
        pl.ds((cuts - 1) * size, rows - (cuts - 1) * size)
    ]


def last_gather_kernel(
    count, members, cuts, qkv_ref, q_all, kv_all, heap, kv_sum, sems, own_sem, mo, mi, ro, ri, so, si
):
    me, chips, lane, position, step, following, previous, sibling = places(count)
    chip = me // 2
    place = chip % members
    first = chip - place
    rows = kv_sum.shape[0]
    gcols = q_all.shape[2]
    q_ref = qkv_ref.at[:, pl.ds(0, gcols)]
    kv_ref = qkv_ref.at[pl.ds(0, rows * members), pl.ds(gcols, kv_sum.shape[1])]

    def member(i):
        return (first + (place + i) % members) * 2 + lane

    greet([previous, sibling] + [member(i) for i in range(1, members)])

    def give(i):
        target = (place + i) % members
        return pltpu.make_async_remote_copy(
            src_ref=kv_ref.at[pl.ds(target * rows, rows)],
            dst_ref=heap.at[i - 1],
            send_sem=mo.at[i - 1],
            recv_sem=mi.at[i - 1],
            device_id={"seq": member(i)},
            device_id_type=MESH,
        )

    pieces = [(q_ref, q_all, part) for part in row_parts(q_ref.shape[0], cuts)]
    pieces.append((kv_sum, kv_all, pl.ds(0, rows)))

    def hop(c, owner, s, device, out_sem, in_sem, first_hop):
        x_ref, o_ref, part = pieces[c]
        return pltpu.make_async_remote_copy(
            src_ref=x_ref.at[part] if first_hop else o_ref.at[owner, part],
            dst_ref=o_ref.at[owner, part],
            send_sem=out_sem.at[s, c],
            recv_sem=in_sem.at[s, c],
            device_id={"seq": device},
            device_id_type=MESH,
        )

    def ring(c, owner, s, first_hop=False):
        return hop(c, owner, s, following, ro, ri, first_hop)

    def side(c, owner, s, first_hop=False):
        return hop(c, owner, s, sibling, so, si, first_hop)

    for i in range(1, members):
        give(i).start()
    mine = pltpu.make_async_copy(kv_ref.at[pl.ds(place * rows, rows)], kv_sum, own_sem.at[0])
    mine.start()
    own_q = pltpu.make_async_copy(q_ref, q_all.at[me], own_sem.at[1])
    own_q.start()
    for c in range(cuts):
        ring(c, me, 0, True).start()
        side(c, me, 0, True).start()
    mine.wait()
    total = kv_sum[...].astype(F32)
    for i in range(1, members):
        give(i).wait_recv()
        total = total + heap[i - 1].astype(F32)
    kv_sum[...] = total.astype(BF16)
    own_kv = pltpu.make_async_copy(kv_sum, kv_all.at[me], own_sem.at[2])
    own_kv.start()
    ring(cuts, me, 0, True).start()
    side(cuts, me, 0, True).start()
    for s in range(1, chips):
        owner = chip_of((position - s * step + chips) % chips, chips) * 2 + lane
        for c in range(cuts + 1):
            ring(c, owner, s - 1).wait_recv()
            if s < chips - 1:
                ring(c, owner, s).start()
            side(c, owner, s).start()
    for i in range(1, members):
        give(i).wait_send()
    for s in range(chips):
        for c in range(cuts + 1):
            side(c, me, s).wait()
            if s < chips - 1:
                ring(c, me, s).wait_send()
    own_q.wait()
    own_kv.wait()


def last_gather(qkv, gcols, local, count, members, call, cuts=4):
    chips = count // 2
    rows = local // members
    columns = qkv.shape[1] - gcols
    anywhere = pl.BlockSpec(memory_space=pl.ANY)
    dma = pltpu.SemaphoreType.DMA
    return pl.pallas_call(
        functools.partial(last_gather_kernel, count, members, cuts),
        out_shape=(
            jax.ShapeDtypeStruct((count, qkv.shape[0], gcols), BF16),
            jax.ShapeDtypeStruct((count, rows, columns), BF16),
        ),
        in_specs=[VMEM],
        out_specs=[anywhere] * 2,
        scratch_shapes=[
            pltpu.VMEM((members - 1, rows, columns), BF16),
            pltpu.VMEM((rows, columns), BF16),
            dma,
            dma((3,)),
            dma((members - 1,)),
            dma((members - 1,)),
        ]
        + [dma((chips, cuts + 1))] * 4,
        compiler_params=pltpu.CompilerParams(collective_id=call, has_side_effects=True),
    )(qkv)


def finish_kernel(
    count,
    kv_heads,
    tile,
    q_ref,
    kv_ref,
    wq_ref,
    wk_ref,
    wv_ref,
    gain_ref,
    out_ref,
    gate_ref,
    up_ref,
    down_ref,
    dq_ref,
    dk_ref,
    dv_ref,
    dg_ref,
    dout_ref,
    dgate_ref,
    dup_ref,
    ddown_ref,
):
    dout_ref[...] = out_ref[...].astype(F32)
    dgate_ref[...] = gate_ref[...].astype(F32)
    dup_ref[...] = up_ref[...].astype(F32)
    ddown_ref[...] = down_ref[...].astype(F32)
    chips = count // 2
    members = count // kv_heads
    width = q_ref.shape[2]
    hd = kv_ref.shape[2] // 2
    member = pl.program_id(0) * members // pl.num_programs(0)

    def place(group):
        return (group % chips) * 2 + group // chips

    total = jnp.zeros((tile, 1), F32)
    for g in range(count):
        cols = pl.ds(g * width, width)
        grad = q_ref[place(g)].astype(F32)
        dq_ref[:, cols] = grad
        total += jnp.sum(grad * wq_ref[:, cols].astype(F32), axis=1, keepdims=True)
    for j in range(kv_heads):
        cols = pl.ds(j * hd, hd)
        pair = kv_ref[place(j * members + member)].astype(F32)
        dk_ref[:, cols] = pair[:, :hd]
        dv_ref[:, cols] = pair[:, hd:]
        total += jnp.sum(pair[:, :hd] * wk_ref[:, cols].astype(F32), axis=1, keepdims=True)
        total += jnp.sum(pair[:, hd:] * wv_ref[:, cols].astype(F32), axis=1, keepdims=True)
    dg_ref[...] = total / gain_ref[...].astype(F32)


def finish(q_all, kv_all, w_query, key_weight, value_weight, gain, others, kv_heads):
    count = q_all.shape[0]
    local, columns = w_query.shape
    rows = kv_all.shape[1]
    tile = min(128, rows)
    per = rows // tile
    kv_columns = key_weight.shape[1]

    steps = local // tile

    def row_block(n, rows=tile):
        return pl.BlockSpec((rows, n), lambda r: (r, 0))

    other_blocks = [row_block(a.shape[1], a.shape[0] // steps) for a in others]

    return pl.pallas_call(
        functools.partial(finish_kernel, count, kv_heads, tile),
        grid=(local // tile,),
        out_shape=(
            jax.ShapeDtypeStruct((local, columns), F32),
            jax.ShapeDtypeStruct((local, kv_columns), F32),
            jax.ShapeDtypeStruct((local, kv_columns), F32),
            jax.ShapeDtypeStruct((local, 1), F32),
        )
        + tuple(jax.ShapeDtypeStruct(a.shape, F32) for a in others),
        in_specs=[
            pl.BlockSpec((count, tile, q_all.shape[2]), lambda r: (0, r, 0)),
            pl.BlockSpec((count, tile, kv_all.shape[2]), lambda r: (0, r % per, 0)),
            row_block(columns),
            row_block(kv_columns),
            row_block(kv_columns),
            row_block(1),
        ]
        + other_blocks,
        out_specs=[row_block(columns), row_block(kv_columns), row_block(kv_columns), row_block(1)]
        + other_blocks,
        compiler_params=pltpu.CompilerParams(vmem_limit_bytes=48 * MIB),
    )(q_all, kv_all, w_query, key_weight, value_weight, gain[:, None], *others)


def run_starts(segment):
    position = jnp.arange(segment.shape[0], dtype=jnp.int32)
    fresh = jnp.concatenate([jnp.ones((1,), dtype=bool), segment[1:] != segment[:-1]])
    return position, lax.cummax(jnp.where(fresh, position, jnp.zeros_like(position)), axis=0)


def angles(offset, head_size):
    half = head_size // 2
    lane = jnp.arange(head_size, dtype=jnp.int32)
    frequency = jnp.exp((lane % half).astype(F32) * (-2.0 * math.log(THETA) / head_size))
    phases = offset[:, None] * frequency[None, :]
    sign = jnp.where(lane < half, -1.0, 1.0).astype(F32)
    return jnp.cos(phases), jnp.sin(phases) * sign[None, :]


def per_device(
    activations,
    cotangent,
    segments,
    routing,
    attn_gain,
    mlp_gain,
    query_gain,
    key_gain,
    w_query,
    key_weight,
    value_weight,
    w_out,
    w_router,
    w_gate,
    w_up,
    w_down,
):
    count = lax.axis_size("seq")
    shards = lax.axis_size("fsdp")
    me = lax.axis_index("seq")
    chips = count // 2
    x = activations[0].astype(F32)
    dy = cotangent[0]
    segment = segments[0]
    routes = routing[0]
    tok, dim = x.shape
    span = segment.shape[0]
    top = routes.shape[1]
    hd = query_gain.shape[0] * shards
    heads = w_query.shape[1] // hd
    kv_heads = key_weight.shape[1] // hd
    share = heads // count
    experts = w_router.shape[1]
    local_rows = w_out.shape[0]
    capacity = tok * top * 9 // (8 * experts)
    gcols = share * hd

    small = jnp.concatenate([attn_gain, mlp_gain, query_gain, key_gain], axis=0)
    local_dim = attn_gain.shape[0]
    local_hd = query_gain.shape[0]
    small = jnp.pad(small, (0, -small.shape[0] % (16 * 128))).reshape(-1, 128)
    ffe = w_down.shape[1]
    down_rows = ffe // 3 // 16 * 16
    h1_all, qkv, w_qkv, w_o, small, router, wd1 = front(
        activations[0],
        small,
        w_router.T,
        w_query,
        key_weight,
        value_weight,
        w_out,
        w_down[0],
        down_rows,
        hd,
        count,
        shards,
        1,
    )
    small = small.reshape(shards, -1)
    cut = [local_dim, 2 * local_dim, 2 * local_dim + local_hd, 2 * local_dim + 2 * local_hd]
    g_attn, g_mlp, g_query, g_key, _ = jnp.split(small, cut, axis=1)
    g_attn = g_attn.reshape(-1).astype(F32)
    g_mlp = g_mlp.reshape(-1).astype(F32)
    g_query = g_query.reshape(-1).astype(F32)
    g_key = g_key.reshape(-1).astype(F32)
    r1 = lax.rsqrt(jnp.mean(x * x, axis=-1, keepdims=True) + EPSILON)
    position, doc_start = run_starts(segment)
    cos_full, sin_full = angles((position - doc_start).astype(F32), hd)
    start = jnp.where(segment > 0, doc_start, position)

    routes_sent = jnp.pad(routes.T, ((0, -top % 16), (0, 0))).astype(BF16)
    dy_all, routes_all, o, qx, kn, wg, wd2 = attend(
        dy,
        routes_sent,
        qkv,
        g_query,
        g_key,
        cos_full,
        sin_full,
        start,
        w_gate[0],
        w_down[0],
        down_rows,
        count,
        shards,
        4,
    )
    wholes = (
        whole_of(w_up[0], 0, shards),
        jax.ShapeDtypeStruct((ffe - 2 * down_rows, dim), BF16),
    )
    x2, wu, wd3 = product_scattered(
        o, w_o, NN, [w_up[0], w_down[0]], (0, 1), wholes, count, shards, 2
    )
    x2 = x + x2

    r2 = lax.rsqrt(jnp.mean(x2 * x2, axis=-1, keepdims=True) + EPSILON)
    h2 = (x2 * r2 * g_mlp).astype(BF16)
    def gates_of(hidden, chosen):
        logits = mm(hidden, router, NT)
        return jax.nn.softmax(jnp.where(chosen, logits, -1e30), axis=-1) * chosen

    def chosen_of(named):
        names = jnp.arange(experts, dtype=jnp.int32)
        return jnp.any(named[..., :, None] == names, axis=-2)

    routes_all = jnp.swapaxes(routes_all[:, :top].astype(jnp.int32), 1, 2)
    hit = jnp.any(routes_all == me, axis=-1)
    rank = jnp.cumsum(hit.astype(jnp.int32), axis=1) - hit
    slot = jnp.where(hit & (rank < capacity), rank, -1)
    chosen_all = chosen_of(routes_all.reshape(span, top)).astype(BF16)
    xs, de, dx0, dl, ce, hid, dgu = expert_gathered(
        h2,
        slot,
        chosen_all,
        router,
        dy_all,
        (wg, wu, wd1, wd2, wd3, w_gate[0], w_up[0], w_down[0]),
        capacity,
        count,
        shards,
        3,
    )
    dh2_wide, w_gate_part = slots_back(
        slot, dl, dx0, xs, dgu, (wg, wu, w_gate[0], w_up[0]), capacity, count, shards, 6
    )
    dgate = dh2_wide[:, dim : dim + experts] + dh2_wide[:, dim + 64 : dim + 64 + experts]
    gates = gates_of(h2, chosen_of(routes))
    dlogits = (gates * (dgate - jnp.sum(gates * dgate, axis=-1, keepdims=True))).astype(BF16)
    dh2 = dh2_wide[:, :dim] + mm(dlogits, router)
    router_part = mm(dlogits, h2, TN)
    xh = x2 * r2
    mlp_gain_part = jnp.sum(dh2 * xh, axis=0)
    dn = dh2 * g_mlp
    dx2 = dy.astype(F32) + r2 * (dn - xh * jnp.mean(dn * xh, axis=-1, keepdims=True))

    do, w_out_part, w_down_part, w_up_part = out_back(
        dx2.astype(BF16), w_o, o, hid, de, xs, dgu, count, 7
    )
    dqkv, head_gains, mixed, out_half = attend_back(
        qx,
        kn,
        qkv,
        o,
        do,
        g_query,
        g_key,
        cos_full,
        sin_full,
        start,
        slot,
        w_out_part,
        ce,
        capacity,
        count,
        shards,
        5,
    )
    mixed = x2 + mixed
    dh1, qkv_sum = token_back(dqkv, w_qkv, head_gains, h1_all, count, shards, 8)
    xh1 = x * r1
    dn1 = dh1 * g_attn
    input_grad = dx2 + r1 * (dn1 - xh1 * jnp.mean(dn1 * xh1, axis=-1, keepdims=True))

    def sum_fsdp(part, axis):
        return lax.psum_scatter(part.astype(BF16), "fsdp", scatter_dimension=axis, tiled=True)

    w_gate_sum = sum_fsdp(w_gate_part, 0)
    w_up_sum = sum_fsdp(w_up_part, 0)
    w_down_sum = sum_fsdp(w_down_part, 1)

    small_part = jnp.concatenate([router_part, mlp_gain_part[None]], axis=0)
    small_part = jnp.pad(small_part, ((0, -small_part.shape[0] % 16), (0, 0)))
    small_sum = sum_fsdp(small_part, 1)
    if shards == 2:
        out_all, small_all = gather_rows(out_half, small_sum, count, 9)
    else:
        out_all, small_all = out_rows(w_out_part, small_sum, count, shards, local_rows)
    small_total = jnp.sum(small_all.astype(F32), axis=0)
    router_grad = small_total[:experts].T
    mlp_gain_grad = small_total[experts]
    q_all, kv_all = last_gather(qkv_sum, gcols, local_dim, count, count // kv_heads, 10)
    (
        w_query_grad,
        w_key_grad,
        w_value_grad,
        attn_gain_grad,
        w_out_grad,
        w_gate_grad,
        w_up_grad,
        w_down_grad,
    ) = finish(
        q_all,
        kv_all,
        w_query,
        key_weight,
        value_weight,
        attn_gain,
        (out_all, w_gate_sum, w_up_sum, w_down_sum),
        kv_heads,
    )
    attn_gain_grad = attn_gain_grad[:, 0]
    head_gain_grads = jnp.sum(q_all[:, local_dim, : 2 * hd].astype(F32), axis=0)
    own_half = lax.axis_index("fsdp") * local_hd
    query_gain_grad = lax.dynamic_slice_in_dim(head_gain_grads[:hd], own_half, local_hd)
    key_gain_grad = lax.dynamic_slice_in_dim(head_gain_grads[hd:], own_half, local_hd)
    return (
        mixed.astype(BF16)[None],
        input_grad[None],
        attn_gain_grad,
        mlp_gain_grad,
        query_gain_grad,
        key_gain_grad,
        w_query_grad,
        w_key_grad,
        w_value_grad,
        w_out_grad,
        router_grad,
        w_gate_grad[None],
        w_up_grad[None],
        w_down_grad[None],
    )


def out_rows(part, small_sum, count, shards, local_rows):
    chips = count // 2
    gcols, dim = part.shape
    me = lax.axis_index("seq")
    group = (me % 2) * chips + me // 2
    blank = jnp.zeros((count * gcols, dim), BF16)
    placed = lax.dynamic_update_slice(blank, part, (group * gcols, 0))
    mine = lax.psum_scatter(placed, "fsdp", scatter_dimension=0, tiled=True)
    return lax.psum(mine, "seq"), lax.all_gather(small_sum, "seq", axis=0, tiled=False)


def solution(mesh):
    tokens = P("fsdp", "seq", None)
    rows = P("fsdp", None)
    vector = P("fsdp")
    expert_rows = P("seq", "fsdp", None)
    expert_columns = P("seq", None, "fsdp")
    return jax.shard_map(
        per_device,
        mesh=mesh,
        in_specs=(tokens, tokens, rows, tokens)
        + (vector,) * 4
        + (rows,) * 5
        + (expert_rows, expert_rows, expert_columns),
        out_specs=(tokens, tokens)
        + (vector,) * 4
        + (rows,) * 5
        + (expert_rows, expert_rows, expert_columns),
        check_vma=False,
    )
```

```python
import functools
import math

import jax
import jax.numpy as jnp
from jax import lax
from jax.experimental import pallas as pl
from jax.experimental.pallas import tpu as pltpu
from jax.sharding import PartitionSpec as P

EPSILON = 1e-06
THETA = 1000000.0
BF16 = jnp.bfloat16
F32 = jnp.float32
MESH = pl.DeviceIdType.MESH
MIB = 1 << 20
LOG2E = math.log2(math.e)


def ring_of(chip, chips):
    return (chip % 2) * (chips - 1 - chip // 2) + (1 - chip % 2) * (chip // 2)


def chip_of(position, chips):
    upper = position // (chips // 2)
    return (1 - upper) * (2 * position) + upper * (2 * (chips - 1 - position) + 1)


def places(count):
    me = lax.axis_index("seq")
    chips = count // 2
    lane = me % 2
    position = ring_of(me // 2, chips)
    step = 1 - 2 * lane
    following = chip_of((position + step + chips) % chips, chips) * 2 + lane
    previous = chip_of((position - step + chips) % chips, chips) * 2 + lane
    sibling = me + 1 - 2 * lane
    return me, chips, lane, position, step, following, previous, sibling


def greet(places_over_seq, shards=1, more=0):
    barrier = pltpu.get_barrier_semaphore()
    for device in places_over_seq:
        pl.semaphore_signal(barrier, inc=1, device_id={"seq": device}, device_id_type=MESH)
    for i in range(1, shards):
        peer = (lax.axis_index("fsdp") + i) % shards
        pl.semaphore_signal(barrier, inc=1, device_id={"fsdp": peer}, device_id_type=MESH)
    pl.semaphore_wait(barrier, len(places_over_seq) + shards - 1 + more)


def crossing(shards, items, out_sems, in_sems, own_sems=None):
    mine = lax.axis_index("fsdp")

    def place(src, dst, axis):
        if axis is None:
            return dst.at[mine]
        size = src.shape[axis]
        part = pl.ds(pl.multiple_of(mine * size, 128 if axis else 16), size)
        return dst.at[:, part] if axis else dst.at[part]

    def own(n):
        src, dst, axis = items[n]
        return pltpu.make_async_copy(src, place(src, dst, axis), own_sems.at[n])

    def send(n, i):
        src, dst, axis = items[n]
        return pltpu.make_async_remote_copy(
            src_ref=src,
            dst_ref=place(src, dst, axis),
            send_sem=out_sems.at[n, i - 1],
            recv_sem=in_sems.at[n, i - 1],
            device_id={"fsdp": (mine + i) % shards},
            device_id_type=MESH,
        )

    def start(n):
        for i in range(1, shards):
            send(n, i).start()
        if own_sems is not None:
            own(n).start()

    def wait(n):
        for i in range(1, shards):
            send(n, i).wait()
        if own_sems is not None:
            own(n).wait()

    return start, wait


def crossing_scratch(shards, items):
    dma = pltpu.SemaphoreType.DMA
    return [dma((items, max(1, shards - 1))), dma((items, max(1, shards - 1)))]


def spread_units(units, steps):
    total = sum(weight for weight, _ in units)
    plan = [[] for _ in range(steps)]
    done = 0.0
    for weight, run in units:
        plan[min(steps - 1, int((done + weight / 2) * steps / total))].append(run)
        done += weight
    return plan


def run_units(plan, k):
    for step, units in enumerate(plan):
        if units:

            @pl.when(k == step)
            def _(units=units):
                for run in units:
                    run()


def row_parts(rows, cuts):
    if cuts == 1:
        return [pl.ds(0, rows)]
    size = rows // cuts // 16 * 16
    return [pl.ds(c * size, size) for c in range(cuts - 1)] + [
        pl.ds((cuts - 1) * size, rows - (cuts - 1) * size)
    ]


NT = (((1,), (1,)), ((), ()))
TN = (((0,), (0,)), ((), ()))
NN = (((1,), (0,)), ((), ()))


def mm(a, b, dims=NN):
    return lax.dot_general(a, b, dims, preferred_element_type=F32)


def gather_steps(count, cuts, x_ref, land, sems, use, shards=1, begin=None, tag=None):
    me, chips, lane, position, step, following, previous, sibling = places(count)
    ring_out, ring_in, side_out, side_in = sems
    block = x_ref.shape[0]
    rows = block // cuts
    pieces = cuts + (tag is not None)
    greet((previous, sibling), shards)

    def ring(s, c):
        part = pl.ds(c * rows, rows)
        return pltpu.make_async_remote_copy(
            src_ref=tag.at[s, 0] if c == cuts else land.at[s, part],
            dst_ref=tag.at[s + 1, 0] if c == cuts else land.at[s + 1, part],
            send_sem=ring_out.at[s, c],
            recv_sem=ring_in.at[s, c],
            device_id={"seq": following},
            device_id_type=MESH,
        )

    def side(s, c):
        return pltpu.make_async_remote_copy(
            src_ref=tag.at[s, 0] if c == cuts else land.at[s, pl.ds(c * rows, rows)],
            dst_ref=tag.at[s, 1] if c == cuts else land.at[s, pl.ds(block + c * rows, rows)],
            send_sem=side_out.at[s, c],
            recv_sem=side_in.at[s, c],
            device_id={"seq": sibling},
            device_id_type=MESH,
        )

    def forward(s, c):
        @pl.when(s < chips - 1)
        def _():
            ring(s, c).start()

        side(s, c).start()

    land[0, :block] = x_ref[...]
    for c in range(pieces):
        forward(0, c)
    if begin is not None:
        begin()

    def one(s, carry):
        def pump(c):
            @pl.when(s < chips - 1)
            def _():
                ring(s, c).wait_recv()
                forward(s + 1, c)

        for c in range(pieces):
            side(s, c).wait_recv()
        use(s, *pair_owners(count, s), pump)
        return carry

    lax.fori_loop(0, chips, one, 0)

    def close(s, carry):
        for c in range(pieces):
            side(s, c).wait_send()

            @pl.when(s < chips - 1)
            def _():
                ring(s, c).wait_send()

        return carry

    lax.fori_loop(0, chips, close, 0)


def pair_owners(count, s):
    _, chips, lane, position, step, _, _, _ = places(count)
    first = chip_of((position - s * step + chips) % chips, chips) * 2 + lane
    second = chip_of((position + s * step + chips) % chips, chips) * 2 + 1 - lane
    return first, second


def at_block(owner, block):
    return pl.ds(pl.multiple_of(owner * block, block), block)


def gather_scratch(count, pieces, block, columns):
    chips = count // 2
    return [pltpu.VMEM((chips, 2 * block, columns), BF16)] + [
        pltpu.SemaphoreType.DMA((chips, pieces))
    ] * 4


def scatter_steps(count, cuts, o_ref, bufs, sems, produce, extra=None, shards=1, begin=None, meeting=None):
    me, chips, lane, position, step, following, previous, sibling = places(count)
    own, sent, came, give, given = bufs
    ring_out, ring_in, side_out, side_in = sems
    rows = own.shape[1] // cuts
    if meeting is None:
        greet((previous, sibling), shards)
    else:
        meeting[0]()
        greet((previous, sibling), shards, meeting[1])
    if begin is not None:
        begin()

    def ring(k, c):
        part = pl.ds(c * rows, rows)
        return pltpu.make_async_remote_copy(
            src_ref=sent.at[k, part],
            dst_ref=came.at[k, part],
            send_sem=ring_out.at[k, c],
            recv_sem=ring_in.at[k, c],
            device_id={"seq": following},
            device_id_type=MESH,
        )

    def side(k):
        return pltpu.make_async_remote_copy(
            src_ref=give.at[k],
            dst_ref=given.at[k],
            send_sem=side_out.at[k],
            recv_sem=side_in.at[k],
            device_id={"seq": sibling},
            device_id_type=MESH,
        )

    def make(k):
        mine, theirs = produce(k, *pair_owners(count, (k + 1) % chips))
        give[k] = theirs.astype(BF16)
        side(k).start()
        own[k % 2] = mine

    make(0)

    def one(k, carry):
        side(k).wait_recv()
        for c in range(cuts):
            part = pl.ds(c * rows, rows)

            @pl.when(k > 0)
            def _():
                ring(k - 1, c).wait_recv()
                own[k % 2, part] += came[k - 1, part].astype(F32)

            total = own[k % 2, part] + given[k, part].astype(F32)

            @pl.when(k < chips - 1)
            def _():
                sent[k, part] = total.astype(BF16)
                ring(k, c).start()

            @pl.when(k == chips - 1)
            def _():
                o_ref[part] = total

            if c == 0:

                @pl.when(k < chips - 1)
                def _():
                    make(k + 1)

        if extra is not None:
            extra(k)
        return carry

    lax.fori_loop(0, chips, one, 0)

    def close(k, carry):
        side(k).wait_send()

        @pl.when(k < chips - 1)
        def _():
            for c in range(cuts):
                ring(k, c).wait_send()

        return carry

    lax.fori_loop(0, chips, close, 0)


def scatter_scratch(count, cuts, rows, columns):
    chips = count // 2
    dma = pltpu.SemaphoreType.DMA
    return [
        pltpu.VMEM((2, rows, columns), F32),
        pltpu.VMEM((chips - 1, rows, columns), BF16),
        pltpu.VMEM((chips - 1, rows, columns), BF16),
        pltpu.VMEM((chips, rows, columns), BF16),
        pltpu.VMEM((chips, rows, columns), BF16),
        dma((chips, cuts)),
        dma((chips, cuts)),
        dma((chips,)),
        dma((chips,)),
    ]


def remote_params(call, mib):
    return pltpu.CompilerParams(
        collective_id=call, has_side_effects=True, vmem_limit_bytes=mib * MIB
    )


VMEM = pl.BlockSpec(memory_space=pltpu.VMEM)
ANY = pl.BlockSpec(memory_space=pl.ANY)


def front_kernel(
    count,
    shards,
    cuts,
    widths,
    x_ref,
    small_ref,
    wr_ref,
    wq_ref,
    wk_ref,
    wv_ref,
    wo_ref,
    wd_ref,
    h_all,
    qkv_ref,
    w_ref,
    wo_all,
    small_all,
    wr_all,
    wd_all,
    land,
    ring_out,
    ring_in,
    side_out,
    side_in,
    x_out,
    x_in,
    x_own,
    d_out,
    d_in,
    h1,
    gain,
    h_sem,
    o_out,
    o_in,
    o_own,
):
    block, dim = x_ref.shape
    chips = count // 2
    gcols, hd, members = widths
    local = wq_ref.shape[0]
    me = lax.axis_index("seq")
    mine = lax.axis_index("fsdp")
    group = (me % 2) * chips + me // 2
    kv_cols = pl.ds(pl.multiple_of(group // members * hd, 128), hd)
    q_cols = pl.ds(pl.multiple_of(group * gcols, 128), gcols)
    items = [
        (small_ref, small_all, None),
        (wq_ref.at[:, q_cols], w_ref.at[:, pl.ds(0, gcols)], 0),
        (wk_ref.at[:, kv_cols], w_ref.at[:, pl.ds(gcols, hd)], 0),
        (wv_ref.at[:, kv_cols], w_ref.at[:, pl.ds(gcols + hd, hd)], 0),
        (wr_ref, wr_all, 1),
    ]
    start, wait = crossing(shards, items, x_out, x_in, x_own)
    start_down, wait_down = crossing(
        shards, [(wd_ref.at[pl.ds(0, wd_all.shape[0])], wd_all, 1)], d_out, d_in
    )
    owner = group * gcols // wo_ref.shape[0]
    wo_src = wo_ref.at[pl.ds(pl.multiple_of(group * gcols % wo_ref.shape[0], 16), gcols)]
    wo_own = pltpu.make_async_copy(wo_src, wo_all, o_own)

    def wo_send(i):
        return pltpu.make_async_remote_copy(
            src_ref=wo_src,
            dst_ref=wo_all,
            send_sem=o_out.at[i - 1],
            recv_sem=o_in,
            device_id={"fsdp": (mine + i) % shards},
            device_id_type=MESH,
        )

    def begin():
        for n in range(len(items)):
            start(n)

        @pl.when(mine == owner)
        def _():
            wo_own.start()
            for i in range(1, shards):
                wo_send(i).start()

        start_down(0)

    def h_copy(s, holder, half):
        return pltpu.make_async_copy(
            h1.at[s, pl.ds(half * block, block)], h_all.at[at_block(holder, block)], h_sem.at[half]
        )

    def multiply(p):
        first, second = pair_owners(count, p)
        y = mm(h1[p], w_ref[...]).astype(BF16)
        qkv_ref[at_block(first, block), :] = y[:block]
        qkv_ref[at_block(second, block), :] = y[block:]

    def use(s, first, second, pump):
        @pl.when(s == 0)
        def _():
            wait(0)
            for f in range(shards):
                for r in range(local // 128):
                    gain[:, pl.ds(f * local + r * 128, 128)] = small_all[f, r : r + 1, :]

        x = land[s].astype(F32)
        r1 = lax.rsqrt(jnp.mean(x * x, axis=1, keepdims=True) + EPSILON)
        h1[s] = (x * r1 * gain[...]).astype(BF16)
        h_copy(s, first, 0).start()
        h_copy(s, second, 1).start()
        pump(0)

        @pl.when(s == chips // 2)
        def _():
            for n in range(1, len(items)):
                wait(n)

        @pl.when(s >= chips // 2)
        def _():
            multiply(2 * s - chips)
            pump(1)
            multiply(2 * s - chips + 1)

        @pl.when(s < chips // 2)
        def _():
            pump(1)

        for c in range(2, cuts):
            pump(c)

    gather_steps(
        count, cuts, x_ref, land, (ring_out, ring_in, side_out, side_in), use, shards, begin
    )

    @pl.when(mine == owner)
    def _():
        wo_own.wait()
        for i in range(1, shards):
            wo_send(i).wait_send()

    @pl.when(mine != owner)
    def _():
        wo_send(1).wait_recv()

    wait_down(0)
    half_rows = count * block // 2
    for half in range(2):
        pltpu.make_async_copy(
            h_all.at[pl.ds(0, half_rows)], h_all.at[pl.ds(0, half_rows)], h_sem.at[half]
        ).wait()


def front(
    x,
    small,
    w_router,
    w_query,
    key_weight,
    value_weight,
    w_out,
    w_down,
    down_rows,
    hd,
    count,
    shards,
    call,
    cuts=4,
):
    block, dim = x.shape
    gcols = w_query.shape[1] // count
    members = count * hd // key_weight.shape[1]
    columns = gcols + 2 * hd
    chips = count // 2
    dma = pltpu.SemaphoreType.DMA
    return pl.pallas_call(
        functools.partial(front_kernel, count, shards, cuts, (gcols, hd, members)),
        out_shape=(
            jax.ShapeDtypeStruct((count * block, dim), BF16),
            jax.ShapeDtypeStruct((count * block, columns), BF16),
            jax.ShapeDtypeStruct((dim, columns), BF16),
            jax.ShapeDtypeStruct((gcols, w_out.shape[1]), BF16),
            jax.ShapeDtypeStruct((shards,) + small.shape, F32),
            whole_of(w_router, 1, shards),
            jax.ShapeDtypeStruct((down_rows, dim), BF16),
        ),
        in_specs=[VMEM, VMEM, VMEM] + [ANY] * 5,
        out_specs=[ANY, VMEM, VMEM, VMEM, VMEM, VMEM, ANY],
        scratch_shapes=gather_scratch(count, cuts, block, dim)
        + crossing_scratch(shards, 5)
        + [
            dma((5,)),
        ]
        + crossing_scratch(shards, 1)
        + [
            pltpu.VMEM((chips, 2 * block, dim), BF16),
            pltpu.VMEM((1, dim), F32),
            dma((2,)),
            dma((max(1, shards - 1),)),
            dma,
            dma,
        ],
        compiler_params=remote_params(call, 48),
    )(x, small, w_router, w_query, key_weight, value_weight, w_out, w_down)


def out_back_kernel(
    count,
    cuts,
    da_ref,
    w_ref,
    o_ref,
    hid_ref,
    de_ref,
    xs_ref,
    dgu_ref,
    do_ref,
    part_ref,
    down_out,
    up_out,
    land,
    *rest,
):
    sems = rest[:4]
    total, hid, du, de, xs, down_ref, up_ref, sem, tile_sem, store_sem = rest[4:]
    block = da_ref.shape[0]
    columns = de.shape[2]
    ffe = hid.shape[1]
    total[...] = jnp.zeros_like(total)
    loads = [
        pltpu.make_async_copy(hid_ref, hid, sem.at[0]),
        pltpu.make_async_copy(dgu_ref.at[:, pl.ds(ffe, ffe)], du, sem.at[1]),
    ]

    def tiles(s):
        part = pl.ds(pl.multiple_of(s * columns, 128), columns)
        return [
            pltpu.make_async_copy(src.at[:, part], dst.at[s % 2], tile_sem.at[s % 2, n])
            for n, (src, dst) in enumerate(((de_ref, de), (xs_ref, xs)))
        ]

    def begin():
        for load in loads + tiles(0):
            load.start()

    def use(s, first, second, pump):
        @pl.when(s == 0)
        def _():
            for load in loads:
                load.wait()

        @pl.when(s < count // 2 - 1)
        def _():
            for load in tiles(s + 1):
                load.start()

        pair = land[s]
        a = at_block(first, block)
        b = at_block(second, block)
        do = mm(pair, w_ref[...], NT).astype(BF16)
        do_ref[a, :] = do[:block]
        do_ref[b, :] = do[block:]
        pump(0)
        total[...] += mm(jnp.concatenate([o_ref[a, :], o_ref[b, :]], axis=0), pair, TN)
        pump(1)
        for load in tiles(s):
            load.wait()
        part = pl.ds(pl.multiple_of(s * columns, 128), columns)
        down_ref[:, part] = mm(hid[...], de[s % 2], TN).astype(BF16)
        pump(2)
        rows = pl.ds(pl.multiple_of(s * columns, 16), columns)
        up_ref[rows, :] = mm(xs[s % 2], du[...], TN).astype(BF16)
        pltpu.make_async_copy(down_ref.at[:, part], down_out.at[:, part], store_sem.at[0]).start()
        pltpu.make_async_copy(up_ref.at[rows], up_out.at[rows], store_sem.at[1]).start()
        for c in range(3, cuts):
            pump(c)

    gather_steps(count, cuts, da_ref, land, sems, use, 1, begin)
    part_ref[...] = total[...].astype(BF16)
    pltpu.make_async_copy(down_ref, down_out, store_sem.at[0]).wait()
    pltpu.make_async_copy(up_ref, up_out, store_sem.at[1]).wait()


def out_back(da, w, o, hid, de, xs, dgu, count, call, cuts=4):
    block, dim = da.shape
    ffe = hid.shape[1]
    chips = count // 2
    dma = pltpu.SemaphoreType.DMA
    return pl.pallas_call(
        functools.partial(out_back_kernel, count, cuts),
        out_shape=(
            jax.ShapeDtypeStruct(o.shape, BF16),
            jax.ShapeDtypeStruct(w.shape, BF16),
            jax.ShapeDtypeStruct((ffe, dim), BF16),
            jax.ShapeDtypeStruct((dim, ffe), BF16),
        ),
        in_specs=[VMEM] * 3 + [ANY] * 4,
        out_specs=[VMEM] * 2 + [ANY] * 2,
        scratch_shapes=gather_scratch(count, cuts, block, dim)
        + [
            pltpu.VMEM(w.shape, F32),
            pltpu.VMEM(hid.shape, BF16),
            pltpu.VMEM(hid.shape, BF16),
            pltpu.VMEM((2, de.shape[0], dim // chips), BF16),
            pltpu.VMEM((2, xs.shape[0], dim // chips), BF16),
            pltpu.VMEM((ffe, dim), BF16),
            pltpu.VMEM((dim, ffe), BF16),
            dma((2,)),
            dma((2, 2)),
            dma((2,)),
        ],
        compiler_params=remote_params(call, 56),
    )(da, w, o, hid, de, xs, dgu)


def product_kernel(count, shards, cuts, dims, axes, y_ref, w_ref, *refs):
    cargo = len(axes)
    srcs, o_ref, dsts = refs[:cargo], refs[cargo], refs[cargo + 1 : 2 * cargo + 1]
    rest = refs[2 * cargo + 1 :]
    block = o_ref.shape[0]
    if cargo:
        lasts = []
        for src, dst, axis in zip(srcs, dsts, axes):
            rows = dst.shape[0] if axis else src.shape[0]
            lasts.append((src.at[pl.ds(src.shape[0] - rows, rows)], dst, axis))
        start, wait = crossing(shards, lasts, *rest[9:])

    def begin():
        for n in range(cargo):
            start(n)

    def produce(k, first, second):
        a = y_ref[at_block(first, block), :]
        b = y_ref[at_block(second, block), :]
        both = mm(jnp.concatenate([a, b], axis=0), w_ref[...], dims)
        return both[:block], both[block:]

    scatter_steps(
        count, cuts, o_ref, rest[:5], rest[5:9], produce, None, shards if cargo else 1, begin
    )
    for n in range(cargo):
        wait(n)


def token_back_kernel(
    count,
    shards,
    cuts,
    y_ref,
    w_ref,
    gains_ref,
    h_ref,
    o_ref,
    sum_ref,
    *rest,
):
    chips = count // 2
    block = o_ref.shape[0]
    hbuf, grad, came, gains, h_sem, w_out, w_in, g_out, g_in = rest[9:]
    mine = lax.axis_index("fsdp")
    dim, columns = grad.shape
    local = dim // shards
    part = dim // chips
    per = local // part
    width = gains_ref.shape[1]

    def chunk(k):
        return (k + (mine + 1) % shards * per) % chips

    def load(k):
        cols = pl.ds(pl.multiple_of(chunk(k) * part, 128), part)
        return pltpu.make_async_copy(h_ref.at[:, cols], hbuf.at[k % 2], h_sem.at[k % 2])

    def send(k):
        n = chunk(k)
        owner = n // per
        slot = (owner - mine + shards) % shards - 1
        return pltpu.make_async_remote_copy(
            src_ref=grad.at[pl.ds(pl.multiple_of(n * part, 16), part)],
            dst_ref=came.at[slot, pl.ds(pl.multiple_of(n % per * part, 16), part)],
            send_sem=w_out.at[k],
            recv_sem=w_in.at[slot, n % per],
            device_id={"fsdp": owner},
            device_id_type=MESH,
        )

    def send_gains(i):
        return pltpu.make_async_remote_copy(
            src_ref=gains_ref,
            dst_ref=gains.at[i - 1],
            send_sem=g_out.at[i - 1],
            recv_sem=g_in.at[i - 1],
            device_id={"fsdp": (mine + i) % shards},
            device_id_type=MESH,
        )

    def begin():
        load(0).start()
        for i in range(1, shards):
            send_gains(i).start()

    def produce(k, first, second):
        a = y_ref[at_block(first, block), :]
        b = y_ref[at_block(second, block), :]
        both = mm(jnp.concatenate([a, b], axis=0), w_ref[...], NT)
        return both[:block], both[block:]

    def extra(k):
        load(k).wait()

        @pl.when(k < chips - 1)
        def _():
            load(k + 1).start()

        rows = pl.ds(pl.multiple_of(chunk(k) * part, 16), part)
        grad[rows, :] = mm(hbuf[k % 2], y_ref[...], TN).astype(BF16)

        @pl.when(k < chips - per)
        def _():
            send(k).start()

    scatter_steps(count, cuts, o_ref, rest[:5], rest[5:9], produce, extra, shards, begin)
    total = gains_ref[...]
    for i in range(1, shards):
        send_gains(i).wait()
        total = total + gains[i - 1]
    row = lax.broadcasted_iota(jnp.int32, (16, width), 0)
    sum_ref[pl.ds(local, 16), :] = jnp.zeros((16, columns), BF16)
    for n in range(2):
        sum_ref[pl.ds(local, 16), pl.ds(n * width, width)] = jnp.where(
            row == 0, jnp.broadcast_to(total[n : n + 1, :], (16, width)), 0.0
        ).astype(BF16)
    for k in range(chips - per):
        send(k).wait_send()
    for n in range(per):
        part_rows = pl.ds(n * part, part)
        own = grad[pl.ds(pl.multiple_of(mine * local + n * part, 16), part), :].astype(F32)
        for i in range(1, shards):
            pltpu.make_async_remote_copy(
                src_ref=grad.at[part_rows],
                dst_ref=came.at[i - 1, part_rows],
                send_sem=w_out.at[0],
                recv_sem=w_in.at[i - 1, n],
                device_id={"fsdp": (mine + i) % shards},
                device_id_type=MESH,
            ).wait_recv()
            own = own + came[i - 1, part_rows, :].astype(F32)
        sum_ref[part_rows, :] = own.astype(BF16)


def token_back(y, w, gains, h_all, count, shards, call, cuts=2):
    block = y.shape[0] // count
    dim, columns = w.shape
    chips = count // 2
    local = dim // shards
    others = max(1, shards - 1)
    dma = pltpu.SemaphoreType.DMA
    return pl.pallas_call(
        functools.partial(token_back_kernel, count, shards, cuts),
        out_shape=(
            jax.ShapeDtypeStruct((block, dim), F32),
            jax.ShapeDtypeStruct((local + 16, columns), BF16),
        ),
        in_specs=[VMEM] * 3 + [ANY],
        out_specs=[VMEM] * 2,
        scratch_shapes=scatter_scratch(count, cuts, block, dim)
        + [
            pltpu.VMEM((2, h_all.shape[0], dim // chips), BF16),
            pltpu.VMEM((dim, columns), BF16),
            pltpu.VMEM((others, local, columns), BF16),
            pltpu.VMEM((others,) + gains.shape, F32),
            dma((2,)),
            dma((chips,)),
            dma((others, chips // shards)),
            dma((others,)),
            dma((others,)),
        ],
        compiler_params=remote_params(call, 48),
    )(y, w, gains, h_all)


def whole_of(part, axis, shards):
    shape = list(part.shape)
    shape[axis] *= shards
    return jax.ShapeDtypeStruct(tuple(shape), part.dtype)


def product_scattered(y, w, dims, cargo, axes, wholes, count, shards, call, cuts=2):
    block = y.shape[0] // count
    columns = w.shape[1 - dims[0][1][0]]
    return pl.pallas_call(
        functools.partial(product_kernel, count, shards, cuts, dims, axes),
        out_shape=[jax.ShapeDtypeStruct((block, columns), F32)]
        + list(wholes),
        in_specs=[VMEM, VMEM] + [ANY] * len(cargo),
        out_specs=[VMEM] + [ANY] * len(cargo),
        scratch_shapes=scatter_scratch(count, cuts, block, columns)
        + (crossing_scratch(shards, len(cargo)) if cargo else []),
        compiler_params=remote_params(call, 48),
    )(y, w, *cargo)


def one_hot_of(slot_ref, first, second, capacity):
    a = slot_ref[pl.ds(first, 1), :]
    b = slot_ref[pl.ds(second, 1), :]
    wanted = jnp.concatenate([a, jnp.where(b >= 0, b + capacity, -1)], axis=1)
    row = lax.broadcasted_iota(jnp.int32, (2 * capacity, wanted.shape[1]), 0)
    return jnp.where(row == wanted, 1.0, 0.0).astype(BF16)


def parts_of_own(i, shards, size, unit):
    place = (lax.axis_index("fsdp") + i) % shards
    return pl.ds(pl.multiple_of(place * (size // shards), unit), size // shards)


def gate_up_parts(i, shards, whole, own, wgu):
    rows = parts_of_own(i, shards, wgu.shape[0], 16)
    ffe = wgu.shape[1] // 2
    return [
        (whole[n].at[rows] if i else own[n], wgu.at[rows, pl.ds(n * ffe, ffe)]) for n in range(2)
    ]


def down_parts(i, shards, pieces, own, wd):
    columns = parts_of_own(i, shards, wd.shape[1], 128)
    parts = []
    first = 0
    for piece in pieces:
        rows = pl.ds(first, piece.shape[0])
        first += piece.shape[0]
        parts.append((piece.at[:, columns] if i else own.at[rows], wd.at[rows, columns]))
    return parts


def expert_kernel(
    count,
    shards,
    cuts,
    capacity,
    h_ref,
    slot_ref,
    chosen_ref,
    router_ref,
    dy_ref,
    wg_ref,
    wu_ref,
    wd1_ref,
    wd2_ref,
    wd3_ref,
    wg_own,
    wu_own,
    wd_own,
    xs_out,
    de_out,
    dx_ref,
    dl_out,
    ce_out,
    hid_out,
    dgu_out,
    land,
    ring_out,
    ring_in,
    side_out,
    side_in,
    wgu,
    wd,
    dyb,
    xs,
    de,
    dl,
    ce,
    hid,
    dgu,
    w_sem,
    dy_sem,
    out_sem,
):
    block, dim = h_ref.shape
    ffe = wd.shape[0]
    wd_refs = (wd1_ref, wd2_ref, wd3_ref)
    me = lax.axis_index("seq")
    chips = count // 2
    weights = [
        pltpu.make_async_copy(src, dst, w_sem.at[i, n])
        for i in range(shards)
        for n, (src, dst) in enumerate(
            gate_up_parts(i, shards, (wg_ref, wu_ref), (wg_own, wu_own), wgu)
            + down_parts(i, shards, wd_refs, wd_own, wd)
        )
    ]
    staged = (
        (xs, xs_out),
        (de, de_out),
        (dl, dl_out),
        (ce, ce_out),
        (hid, hid_out),
        (dgu, dgu_out),
    )

    def dy_copies(s):
        first, second = pair_owners(count, s)
        return [
            pltpu.make_async_copy(
                dy_ref.at[at_block(owner, block)], dyb.at[s % 2, pl.ds(half * block, block)], dy_sem.at[s % 2, half]
            )
            for half, owner in ((0, first), (1, second))
        ]

    for copy in weights + dy_copies(0):
        copy.start()

    def use(s, first, second, pump):
        @pl.when(s < chips - 1)
        def _():
            for copy in dy_copies(s + 1):
                copy.start()

        rows = pl.ds(pl.multiple_of(s * 2 * capacity, 16), 2 * capacity)
        pick = one_hot_of(slot_ref, first, second, capacity)
        x = mm(pick, land[s]).astype(BF16)
        xs[rows, :] = x
        chosen = mm(
            pick,
            jnp.concatenate(
                [
                    chosen_ref[pl.ds(pl.multiple_of(first * block, block), block), :],
                    chosen_ref[pl.ds(pl.multiple_of(second * block, block), block), :],
                ],
                axis=0,
            ),
        )
        logits = jnp.where(chosen > 0.5, mm(x, router_ref[...], NT), -1e30)
        weight = jnp.exp(logits - jnp.max(logits, axis=1, keepdims=True)) * chosen
        mass = jnp.sum(weight, axis=1, keepdims=True)
        expert_lane = lax.broadcasted_iota(jnp.int32, weight.shape, 1)
        wide_lane = lax.broadcasted_iota(jnp.int32, (2 * capacity, dl.shape[1]), 1)
        gate = jnp.sum(jnp.where(expert_lane == me, weight, 0.0), axis=1, keepdims=True)
        gate = gate / jnp.where(mass > 0.0, mass, 1.0)

        @pl.when(s == 0)
        def _():
            for copy in weights:
                copy.wait()

        gu = mm(x, wgu[...])
        pump(0)
        g, u = gu[:, :ffe], gu[:, ffe:]
        sig = jax.nn.sigmoid(g)
        silu = g * sig
        h = (silu * u).astype(BF16)
        hid[rows, :] = h
        e = mm(h, wd[...])
        ce[rows, :] = (gate * e).astype(BF16)
        pump(1)
        for copy in dy_copies(s):
            copy.wait()
        dys = mm(pick, dyb[s % 2])
        dgate = jnp.sum(dys * e, axis=1, keepdims=True)
        d = (gate * dys).astype(BF16)
        de[rows, :] = d
        pump(2)
        dh = mm(d, wd[...], NT)
        for c in range(3, cuts):
            pump(c)
        dg = (dh * u * (sig + silu * (1.0 - sig))).astype(BF16)
        du = (dh * silu).astype(BF16)
        dgu[rows, :ffe] = dg
        dgu[rows, ffe:] = du

        @pl.when(s == 1)
        def _():
            dx_ref[...] = mm(dgu[rows, :], wgu[...], NT).astype(BF16)

        high = dgate.astype(BF16).astype(F32)
        dl[rows, :] = jnp.where(
            wide_lane == me, high, jnp.where(wide_lane == me + 64, dgate - high, 0.0)
        ).astype(BF16)
        for i, (src, dst) in enumerate(staged):
            pltpu.make_async_copy(src.at[rows], dst.at[rows], out_sem.at[i]).start()

    gather_steps(count, cuts, h_ref, land, (ring_out, ring_in, side_out, side_in), use)
    for i, (src, dst) in enumerate(staged):
        pltpu.make_async_copy(src, dst, out_sem.at[i]).wait()


def expert_gathered(h2, slot, chosen, router, dy_all, weights, capacity, count, shards, call, cuts=4):
    block, dim = h2.shape
    ffe = weights[0].shape[1]
    total = count * capacity
    widths = (dim, dim, 128, dim, ffe, 2 * ffe)
    dma = pltpu.SemaphoreType.DMA
    return pl.pallas_call(
        functools.partial(expert_kernel, count, shards, cuts, capacity),
        out_shape=[
            jax.ShapeDtypeStruct((2 * capacity if i == 2 else total, n), BF16)
            for i, n in enumerate(widths[:2] + (dim,) + widths[2:])
        ],
        in_specs=[VMEM] * 4 + [ANY] * 9,
        out_specs=[ANY] * 2 + [VMEM] + [ANY] * 4,
        scratch_shapes=gather_scratch(count, cuts, block, dim)
        + [
            pltpu.VMEM((dim, 2 * ffe), BF16),
            pltpu.VMEM((ffe, dim), BF16),
            pltpu.VMEM((2, 2 * block, dim), BF16),
        ]
        + [pltpu.VMEM((total, n), BF16) for n in widths]
        + [dma((shards, 5)), dma((2, 2)), dma((6,))],
        compiler_params=remote_params(call, 60),
    )(h2, slot, chosen, router, dy_all, *weights)


def slots_back_kernel(
    count,
    shards,
    cuts,
    capacity,
    slot_ref,
    dl,
    dx0_ref,
    xs_ref,
    dgu_ref,
    wg_ref,
    wu_ref,
    wg_own,
    wu_own,
    o_ref,
    gate_out,
    *rest,
):
    bufs, sems = rest[:5], rest[5:9]
    dx, xs, dgu, wgu, gate, sem, w_sem, gate_sem = rest[9:]
    chips = count // 2
    block = o_ref.shape[0]
    ffe = gate.shape[1]
    load_dgu = pltpu.make_async_copy(dgu_ref, dgu, sem.at[0])
    load_xs = pltpu.make_async_copy(xs_ref, xs, sem.at[1])
    weights = [
        pltpu.make_async_copy(src, dst, w_sem.at[i, n])
        for i in range(shards)
        for n, (src, dst) in enumerate(
            gate_up_parts(i, shards, (wg_ref, wu_ref), (wg_own, wu_own), wgu)
        )
    ]
    part = xs.shape[1] // chips

    def begin():
        for load in [load_dgu] + weights + [load_xs]:
            load.start()

    def produce(k, first, second):
        rows = pl.ds(pl.multiple_of((k + 1) % chips * 2 * capacity, 16), 2 * capacity)

        @pl.when(k == 0)
        def _():
            dx[...] = dx0_ref[...]

        @pl.when(k == 1)
        def _():
            for load in [load_dgu] + weights:
                load.wait()

        @pl.when(k > 0)
        def _():
            dx[...] = mm(dgu[rows, :], wgu[...], NT).astype(BF16)

        pick = one_hot_of(slot_ref, first, second, capacity)
        both = jnp.concatenate([mm(pick, dx[...], TN), mm(pick, dl[rows, :], TN)], axis=1)
        return both[:block], both[block:]

    def extra(k):
        @pl.when(k == 0)
        def _():
            load_xs.wait()

        columns = pl.ds(pl.multiple_of(k * part, 128), part)
        rows = pl.ds(pl.multiple_of(k * part, 16), part)
        gate[rows, :] = mm(xs[:, columns], dgu[:, :ffe], TN).astype(BF16)
        pltpu.make_async_copy(gate.at[rows], gate_out.at[rows], gate_sem).start()

    scatter_steps(count, cuts, o_ref, bufs, sems, produce, extra, 1, begin)
    pltpu.make_async_copy(gate, gate_out, gate_sem).wait()


def slots_back(slot, dl, dx0, xs, dgu, weights, capacity, count, shards, call, cuts=2):
    block = slot.shape[1]
    dim, ffe = xs.shape[1], dgu.shape[1] // 2
    columns = dim + dl.shape[1]
    dma = pltpu.SemaphoreType.DMA
    return pl.pallas_call(
        functools.partial(slots_back_kernel, count, shards, cuts, capacity),
        out_shape=(
            jax.ShapeDtypeStruct((block, columns), F32),
            jax.ShapeDtypeStruct((dim, ffe), BF16),
        ),
        in_specs=[VMEM] * 3 + [ANY] * 6,
        out_specs=[VMEM, ANY],
        scratch_shapes=scatter_scratch(count, cuts, block, columns)
        + [pltpu.VMEM(a.shape, BF16) for a in (dx0, xs, dgu)]
        + [pltpu.VMEM((dim, 2 * ffe), BF16), pltpu.VMEM((dim, ffe), BF16)]
        + [dma((2,)), dma((shards, 2)), dma],
        compiler_params=remote_params(call, 60),
    )(slot, dl, dx0, xs, dgu, *weights)


def split3(x):
    first = x.astype(BF16)
    rest = x - first.astype(F32)
    second = rest.astype(BF16)
    return first, second, (rest - second.astype(F32)).astype(BF16)


def in_lanes(x):
    lane = lax.broadcasted_iota(jnp.int32, x.shape, 1)
    first = x.astype(BF16).astype(F32)
    second = (x - first).astype(BF16).astype(F32)
    third = x - first - second
    spread = jnp.where(lane == 0, first, jnp.where(lane == 1, second, third))
    return jnp.where(lane < 3, spread, 0.0).astype(BF16)


def swap_halves(x):
    half = x.shape[1] // 2
    return jnp.concatenate([x[:, half:], x[:, :half]], axis=1)


def rope_tables(cos_ref, sin_ref, i, tile):
    rows, width = cos_ref.shape
    late = i * tile // rows
    part = pl.ds(i * tile - late * rows, tile)
    lanes = slice(late * (width // 2), (late + 1) * (width // 2))
    cos = cos_ref[part, :][:, lanes]
    sin = sin_ref[part, :][:, lanes]
    return jnp.concatenate([cos, cos], axis=1), jnp.concatenate([-sin, sin], axis=1)


def unit_rows(u):
    r = lax.rsqrt(jnp.mean(u * u, axis=1, keepdims=True) + EPSILON)
    return r, u * r


def attend_kernel(
    count,
    shards,
    cuts,
    heads,
    tile,
    dy_ref,
    routes_ref,
    qkv_ref,
    gq_ref,
    gk_ref,
    cos_ref,
    sin_ref,
    start_ref,
    wg_ref,
    wd_ref,
    dy_all,
    routes_all,
    o_ref,
    qx_ref,
    kn_ref,
    wg_all,
    wd_all,
    land,
    ring_out,
    ring_in,
    side_out,
    side_in,
    x_out,
    x_in,
    tag,
    vx_ref,
    dy_sem,
):
    span = qkv_ref.shape[0]
    width = kn_ref.shape[1]
    block = dy_ref.shape[0]
    scale = width**-0.5 * LOG2E
    down = wd_all.shape[0]
    items = [(wg_ref, wg_all, 0), (wd_ref.at[pl.ds(down, down)], wd_all, 1)]
    start_item, wait_item = crossing(shards, items, x_out, x_in)

    def prepare(i):
        rows = pl.ds(i * tile, tile)
        cos, sin = rope_tables(cos_ref, sin_ref, i, tile)
        for h in range(heads + 1):
            _, unit = unit_rows(qkv_ref[rows, pl.ds(h * width, width)].astype(F32))
            u = unit * (gk_ref[...] if h == heads else gq_ref[...])
            u = u * cos + swap_halves(u) * sin
            if h == heads:
                kn_ref[rows, :] = u.astype(BF16)
            else:
                qx_ref[rows, pl.ds(2 * h * width, width)] = (u * scale).astype(BF16)
        vx_ref[rows, :width] = qkv_ref[rows, pl.ds((heads + 1) * width, width)]
        vx_ref[rows, width:] = jnp.ones((tile, width), BF16)

    def attend_rows(i, h):
        rows = pl.ds(i * tile, tile)
        start = start_ref[rows, :]
        row = i * tile + lax.broadcasted_iota(jnp.int32, (tile, tile), 0)
        q = qx_ref[rows, pl.ds(2 * h * width, width)]
        total = jnp.zeros((tile, 2 * width), F32)
        for j in range(i + 1):
            keys = pl.ds(j * tile, tile)
            s = mm(q, kn_ref[keys, :], NT)
            col = j * tile + lax.broadcasted_iota(jnp.int32, (tile, tile), 1)
            keep = col >= start
            if i == j:
                keep = keep & (col <= row)
            p = jnp.where(keep, jnp.exp2(s), 0.0).astype(BF16)
            total = total + mm(p, vx_ref[keys, :])
        weight = total[:, width:]
        o_ref[rows, pl.ds(h * width, width)] = (total[:, :width] / weight).astype(BF16)
        qx_ref[rows, pl.ds((2 * h + 1) * width, width)] = in_lanes(-jnp.log2(weight))

    units = []
    for i in range(span // tile):
        units.append((1.0, functools.partial(prepare, i)))
        units += [(0.7 * (i + 1), functools.partial(attend_rows, i, h)) for h in range(heads)]
    plan = spread_units(units, count // 2 - 1)

    def begin():
        for n in range(len(items)):
            start_item(n)

    tag[0, 0] = routes_ref[...]

    def use(s, first, second, pump):
        for half, owner in ((0, first), (1, second)):
            pltpu.make_async_copy(
                land.at[s, pl.ds(half * block, block)],
                dy_all.at[at_block(owner, block)],
                dy_sem.at[half],
            ).start()
            routes_all[owner] = tag[s, half]
        run_units(plan, s)
        for c in range(cuts + 1):
            pump(c)

    gather_steps(
        count, cuts, dy_ref, land, (ring_out, ring_in, side_out, side_in), use, shards, begin, tag
    )
    for n in range(len(items)):
        wait_item(n)
    half_rows = count * block // 2
    for half in range(2):
        pltpu.make_async_copy(
            dy_all.at[pl.ds(0, half_rows)], dy_all.at[pl.ds(0, half_rows)], dy_sem.at[half]
        ).wait()


def attend(dy, routes, qkv, gq, gk, cos, sin, start, w_gate, w_down, down_rows, count, shards, call, tile=512, cuts=4):
    span = qkv.shape[0]
    width = gq.shape[0]
    heads = qkv.shape[1] // width - 2
    block, dim = dy.shape
    chips = count // 2
    return pl.pallas_call(
        functools.partial(attend_kernel, count, shards, cuts, heads, min(tile, span // 2)),
        out_shape=(
            jax.ShapeDtypeStruct((count * block, dim), BF16),
            jax.ShapeDtypeStruct((count,) + routes.shape, BF16),
            jax.ShapeDtypeStruct((span, heads * width), BF16),
            jax.ShapeDtypeStruct((span, 2 * heads * width), BF16),
            jax.ShapeDtypeStruct((span, width), BF16),
            whole_of(w_gate, 0, shards),
            jax.ShapeDtypeStruct((down_rows, dim), BF16),
        ),
        in_specs=[VMEM] * 8 + [ANY] * 2,
        out_specs=[ANY] + [VMEM] * 4 + [ANY] * 2,
        scratch_shapes=gather_scratch(count, cuts + 1, block, dim)
        + crossing_scratch(shards, 2)
        + [
            pltpu.VMEM((chips, 2) + routes.shape, BF16),
            pltpu.VMEM((span, 2 * width), BF16),
            pltpu.SemaphoreType.DMA((2,)),
        ],
        compiler_params=remote_params(call, 56),
    )(dy, routes, qkv, gq[None, :], gk[None, :], cos, sin, start[:, None], w_gate, w_down)


def attend_back_kernel(
    count,
    shards,
    cuts,
    capacity,
    heads,
    tile,
    qx_ref,
    kn_ref,
    qkv_ref,
    o_ref,
    do_ref,
    gq_ref,
    gk_ref,
    cos_ref,
    sin_ref,
    start_ref,
    slot_ref,
    part_ref,
    ce_ref,
    dqkv_ref,
    gains_ref,
    mixed_ref,
    half_ref,
    *rest,
):
    bufs, sems = rest[:5], rest[5:9]
    gx_ref, dq_ref, dk_ref, dv_ref, held, held_sem, pair, pair_own, pair_out, pair_in = rest[9:]
    span = qx_ref.shape[0]
    width = kn_ref.shape[1]
    scale = width**-0.5
    chips = count // 2
    block = mixed_ref.shape[0]
    load = pltpu.make_async_copy(ce_ref, held, held_sem)
    load.start()

    mine = lax.axis_index("fsdp")
    me = lax.axis_index("seq")
    lane = me % 2
    chip_first = me - lane
    half_rows = half_ref.shape[0]

    def give_half(c):
        return pltpu.make_async_remote_copy(
            src_ref=part_ref.at[pl.ds(c * half_rows, half_rows)],
            dst_ref=pair.at[(mine + lane) % 2],
            send_sem=pair_out.at[c],
            recv_sem=pair_in.at[(mine + lane) % 2],
            device_id={"fsdp": lane, "seq": chip_first + c},
            device_id_type=MESH,
        )

    def take_half(n):
        return pltpu.make_async_remote_copy(
            src_ref=part_ref.at[pl.ds(0, half_rows)],
            dst_ref=pair.at[n],
            send_sem=pair_out.at[0],
            recv_sem=pair_in.at[n],
            device_id={"fsdp": 1 - mine, "seq": chip_first + mine},
            device_id_type=MESH,
        )

    keep_half = pltpu.make_async_copy(
        part_ref.at[pl.ds(pl.multiple_of(lane * half_rows, 16), half_rows)], pair.at[0], pair_own
    )

    def meet():
        barrier = pltpu.get_barrier_semaphore()
        pl.semaphore_signal(
            barrier,
            inc=1,
            device_id={"fsdp": 1 - mine, "seq": chip_first + mine},
            device_id_type=MESH,
        )

        @pl.when(lane != mine)
        def _():
            pl.semaphore_signal(
                barrier, inc=1, device_id={"seq": chip_first + mine}, device_id_type=MESH
            )

    def begin():
        for c in range(2):

            @pl.when((mine != lane) | (lane != c))
            def _(c=c):
                give_half(c).start()

        @pl.when(mine == lane)
        def _():
            keep_half.start()

    def end():
        for c in range(2):

            @pl.when((mine != lane) | (lane != c))
            def _(c=c):
                give_half(c).wait_send()

        @pl.when(mine == lane)
        def _():
            keep_half.wait()

        @pl.when(mine != lane)
        def _():
            take_half(0).wait_recv()

        take_half(1).wait_recv()
        half_ref[...] = (pair[0].astype(F32) + pair[1].astype(F32)).astype(BF16)

    summing = shards == 2
    partners = 1 + (mine != lane).astype(jnp.int32)

    def produce(k, first, second):
        @pl.when(k == 0)
        def _():
            load.wait()

        pair = pl.multiple_of((k + 1) % chips * 2 * capacity, 16)
        pick = one_hot_of(slot_ref, first, second, capacity)
        both = mm(pick, held[pl.ds(pair, 2 * capacity), :], TN)
        return both[:block], both[block:]

    def to_raw(d, h, i, gain, row):
        rows = pl.ds(i * tile, tile)
        cos, sin = rope_tables(cos_ref, sin_ref, i, tile)
        r, unit = unit_rows(qkv_ref[rows, pl.ds(h * width, width)].astype(F32))
        d = d * cos + swap_halves(d * sin)
        dg = d * gain
        raw = r * (dg - unit * jnp.mean(dg * unit, axis=1, keepdims=True))
        dqkv_ref[rows, pl.ds(h * width, width)] = raw.astype(BF16)
        gains_ref[row : row + 1, :] += jnp.sum(d * unit, axis=0, keepdims=True)

    def prepare(i):
        rows = pl.ds(i * tile, tile)
        for h in range(heads):
            cols = pl.ds(h * width, width)
            do = do_ref[rows, cols]
            inner = jnp.sum(do.astype(F32) * o_ref[rows, cols].astype(F32), axis=1, keepdims=True)
            gx_ref[rows, pl.ds(2 * h * width, width)] = do
            gx_ref[rows, pl.ds((2 * h + 1) * width, width)] = in_lanes(
                jnp.broadcast_to(-inner, (tile, width))
            )

    def tile_back(j, i):
        keys = pl.ds(j * tile, tile)
        rows = pl.ds(i * tile, tile)
        ones = jnp.ones((tile, width), BF16)
        kn = kn_ref[keys, :]
        kx = jnp.concatenate([kn, ones], axis=1)
        vx = jnp.concatenate([qkv_ref[keys, pl.ds((heads + 1) * width, width)], ones], axis=1)
        key = j * tile + lax.broadcasted_iota(jnp.int32, (tile, tile), 0)
        keep = key >= start_ref[:, rows]
        if i == j:
            row = i * tile + lax.broadcasted_iota(jnp.int32, (tile, tile), 1)
            keep = keep & (key <= row)
        for h in range(heads):
            qx = qx_ref[rows, pl.ds(2 * h * width, 2 * width)]
            gx = gx_ref[rows, pl.ds(2 * h * width, 2 * width)]
            p = jnp.where(keep, jnp.exp2(mm(kx, qx, NT)), 0.0)
            ds = (p * mm(vx, gx, NT)).astype(BF16)
            dv_ref[keys, :] += mm(p.astype(BF16), gx[:, :width])
            dk_ref[keys, :] += mm(ds, qx[:, :width])
            dq_ref[rows, pl.ds(h * width, width)] += mm(ds, kn, TN)

    def finish_keys(j):
        keys = pl.ds(j * tile, tile)
        dqkv_ref[keys, pl.ds((heads + 1) * width, width)] = dv_ref[keys, :].astype(BF16)
        to_raw(dk_ref[keys, :] * (1.0 / LOG2E), heads, j, gk_ref[...], 1)

    def finish_rows(i):
        rows = pl.ds(i * tile, tile)
        for h in range(heads):
            to_raw(dq_ref[rows, pl.ds(h * width, width)] * scale, h, i, gq_ref[...], 0)

    tiles = span // tile
    units = [(0.3, functools.partial(prepare, i)) for i in range(tiles)]
    for j in range(tiles):
        units += [(2.0, functools.partial(tile_back, j, i)) for i in range(j, tiles)]
        units.append((0.3, functools.partial(finish_keys, j)))
        units.append((0.6, functools.partial(finish_rows, j)))
    plan = spread_units(units, chips - 1)
    for ref in (dq_ref, dk_ref, dv_ref, gains_ref):
        ref[...] = jnp.zeros_like(ref)

    def extra(k):
        run_units(plan, k)

    if summing:
        scatter_steps(
            count, cuts, mixed_ref, bufs, sems, produce, extra, 1, begin, (meet, partners)
        )
        end()
    else:
        scatter_steps(count, cuts, mixed_ref, bufs, sems, produce, extra)
        half_ref[...] = jnp.zeros_like(half_ref)


def attend_back(qx, kn, qkv, o, do, gq, gk, cos, sin, start, slot, part, ce, capacity, count, shards, call, tile=512, cuts=2):
    span, width = kn.shape
    heads = o.shape[1] // width
    block = slot.shape[1]
    dim = ce.shape[1]
    return pl.pallas_call(
        functools.partial(
            attend_back_kernel, count, shards, cuts, capacity, heads, min(tile, span // 2)
        ),
        out_shape=(
            jax.ShapeDtypeStruct(qkv.shape, BF16),
            jax.ShapeDtypeStruct((8, width), F32),
            jax.ShapeDtypeStruct((block, dim), F32),
            jax.ShapeDtypeStruct((part.shape[0] // 2, dim), BF16),
        ),
        in_specs=[VMEM] * 12 + [ANY],
        out_specs=[VMEM] * 4,
        scratch_shapes=scatter_scratch(count, cuts, block, dim)
        + [
            pltpu.VMEM((span, 2 * heads * width), BF16),
            pltpu.VMEM((span, heads * width), F32),
            pltpu.VMEM((span, width), F32),
            pltpu.VMEM((span, width), F32),
            pltpu.VMEM(ce.shape, BF16),
            pltpu.SemaphoreType.DMA,
            pltpu.VMEM((2, part.shape[0] // 2, dim), BF16),
            pltpu.SemaphoreType.DMA,
            pltpu.SemaphoreType.DMA((2,)),
            pltpu.SemaphoreType.DMA((2,)),
        ],
        compiler_params=remote_params(call, 60),
    )(qx, kn, qkv, o, do, gq[None, :], gk[None, :], cos, sin, start[None, :], slot, part, ce)


def last_gather_kernel(count, members, cuts, extras, qkv_ref, *refs):
    x_refs, (q_all, kv_all) = refs[:extras], refs[extras : extras + 2]
    x_alls = refs[extras + 2 : 2 * extras + 2]
    heap, kv_sum, own_sem, mo, mi, ro, ri, so, si = refs[2 * extras + 2 :]
    me, chips, lane, position, step, following, previous, sibling = places(count)
    chip = me // 2
    place = chip % members
    first = chip - place
    rows = kv_sum.shape[0]
    gcols = q_all.shape[2]
    q_ref = qkv_ref.at[:, pl.ds(0, gcols)]
    kv_ref = qkv_ref.at[pl.ds(0, rows * members), pl.ds(gcols, kv_sum.shape[1])]

    def member(i):
        return (first + (place + i) % members) * 2 + lane

    greet([previous, sibling] + [member(i) for i in range(1, members)])

    def give(i):
        target = (place + i) % members
        return pltpu.make_async_remote_copy(
            src_ref=kv_ref.at[pl.ds(target * rows, rows)],
            dst_ref=heap.at[i - 1],
            send_sem=mo.at[i - 1],
            recv_sem=mi.at[i - 1],
            device_id={"seq": member(i)},
            device_id_type=MESH,
        )

    pieces = []
    for x_ref, x_all in zip(x_refs, x_alls):
        parts = row_parts(x_ref.shape[0], cuts if x_ref.shape[0] >= 64 else 1)
        pieces += [(x_ref, x_all, part) for part in parts]
    pieces += [(q_ref, q_all, part) for part in row_parts(q_ref.shape[0], cuts)]
    last = len(pieces)
    pieces.append((kv_sum, kv_all, pl.ds(0, rows)))

    def hop(c, owner, s, device, out_sem, in_sem, first_hop):
        x_ref, o_ref, part = pieces[c]
        return pltpu.make_async_remote_copy(
            src_ref=x_ref.at[part] if first_hop else o_ref.at[owner, part],
            dst_ref=o_ref.at[owner, part],
            send_sem=out_sem.at[s, c],
            recv_sem=in_sem.at[s, c],
            device_id={"seq": device},
            device_id_type=MESH,
        )

    def ring(c, owner, s, first_hop=False):
        return hop(c, owner, s, following, ro, ri, first_hop)

    def side(c, owner, s, first_hop=False):
        return hop(c, owner, s, sibling, so, si, first_hop)

    for i in range(1, members):
        give(i).start()
    mine = pltpu.make_async_copy(kv_ref.at[pl.ds(place * rows, rows)], kv_sum, own_sem.at[0])
    mine.start()
    own = [
        pltpu.make_async_copy(src, dst.at[me], own_sem.at[n + 2])
        for n, (src, dst) in enumerate(zip((q_ref,) + x_refs, (q_all,) + x_alls))
    ]
    for c in range(last):
        ring(c, me, 0, True).start()
        side(c, me, 0, True).start()
    for copy in own:
        copy.start()
    mine.wait()
    total = kv_sum[...].astype(F32)
    for i in range(1, members):
        give(i).wait_recv()
        total = total + heap[i - 1].astype(F32)
    kv_sum[...] = total.astype(BF16)
    own_kv = pltpu.make_async_copy(kv_sum, kv_all.at[me], own_sem.at[1])
    own_kv.start()
    ring(last, me, 0, True).start()
    side(last, me, 0, True).start()
    for s in range(1, chips):
        owner = chip_of((position - s * step + chips) % chips, chips) * 2 + lane
        for c in range(last + 1):
            ring(c, owner, s - 1).wait_recv()
            if s < chips - 1:
                ring(c, owner, s).start()
            side(c, owner, s).start()
    for i in range(1, members):
        give(i).wait_send()
    for s in range(chips):
        for c in range(last + 1):
            side(c, me, s).wait()
            if s < chips - 1:
                ring(c, me, s).wait_send()
    for copy in own + [own_kv]:
        copy.wait()


def last_gather(qkv, extras, gcols, local, count, members, call, cuts=4):
    chips = count // 2
    rows = local // members
    columns = qkv.shape[1] - gcols
    pieces = cuts + 1 + sum(cuts if x.shape[0] >= 64 else 1 for x in extras)
    dma = pltpu.SemaphoreType.DMA
    return pl.pallas_call(
        functools.partial(last_gather_kernel, count, members, cuts, len(extras)),
        out_shape=[
            jax.ShapeDtypeStruct((count, qkv.shape[0], gcols), BF16),
            jax.ShapeDtypeStruct((count, rows, columns), BF16),
        ]
        + [jax.ShapeDtypeStruct((count,) + x.shape, BF16) for x in extras],
        in_specs=[VMEM] * (1 + len(extras)),
        out_specs=[ANY] * (2 + len(extras)),
        scratch_shapes=[
            pltpu.VMEM((members - 1, rows, columns), BF16),
            pltpu.VMEM((rows, columns), BF16),
            dma((3 + len(extras),)),
            dma((members - 1,)),
            dma((members - 1,)),
        ]
        + [dma((chips, pieces))] * 4,
        compiler_params=pltpu.CompilerParams(collective_id=call, has_side_effects=True),
    )(qkv, *extras)


def finish_kernel(
    count,
    kv_heads,
    tile,
    q_ref,
    kv_ref,
    wq_ref,
    wk_ref,
    wv_ref,
    gain_ref,
    out_ref,
    gate_ref,
    up_ref,
    down_ref,
    dq_ref,
    dk_ref,
    dv_ref,
    dg_ref,
    dout_ref,
    dgate_ref,
    dup_ref,
    ddown_ref,
):
    dout_ref[...] = out_ref[...].astype(F32)
    dgate_ref[...] = gate_ref[...].astype(F32)
    dup_ref[...] = up_ref[...].astype(F32)
    ddown_ref[...] = down_ref[...].astype(F32)
    chips = count // 2
    members = count // kv_heads
    width = q_ref.shape[2]
    hd = kv_ref.shape[2] // 2
    member = pl.program_id(0) * members // pl.num_programs(0)

    def place(group):
        return (group % chips) * 2 + group // chips

    total = jnp.zeros((tile, 1), F32)
    for g in range(count):
        cols = pl.ds(g * width, width)
        grad = q_ref[place(g)].astype(F32)
        dq_ref[:, cols] = grad
        total += jnp.sum(grad * wq_ref[:, cols].astype(F32), axis=1, keepdims=True)
    for j in range(kv_heads):
        cols = pl.ds(j * hd, hd)
        pair = kv_ref[place(j * members + member)].astype(F32)
        dk_ref[:, cols] = pair[:, :hd]
        dv_ref[:, cols] = pair[:, hd:]
        total += jnp.sum(pair[:, :hd] * wk_ref[:, cols].astype(F32), axis=1, keepdims=True)
        total += jnp.sum(pair[:, hd:] * wv_ref[:, cols].astype(F32), axis=1, keepdims=True)
    dg_ref[...] = total / gain_ref[...].astype(F32)


def finish(q_all, kv_all, w_query, key_weight, value_weight, gain, others, kv_heads):
    count = q_all.shape[0]
    local, columns = w_query.shape
    rows = kv_all.shape[1]
    tile = min(128, rows)
    per = rows // tile
    kv_columns = key_weight.shape[1]

    steps = local // tile

    def row_block(n, rows=tile):
        return pl.BlockSpec((rows, n), lambda r: (r, 0))

    other_blocks = [row_block(a.shape[1], a.shape[0] // steps) for a in others]

    return pl.pallas_call(
        functools.partial(finish_kernel, count, kv_heads, tile),
        grid=(local // tile,),
        out_shape=(
            jax.ShapeDtypeStruct((local, columns), F32),
            jax.ShapeDtypeStruct((local, kv_columns), F32),
            jax.ShapeDtypeStruct((local, kv_columns), F32),
            jax.ShapeDtypeStruct((local, 1), F32),
        )
        + tuple(jax.ShapeDtypeStruct(a.shape, F32) for a in others),
        in_specs=[
            pl.BlockSpec((count, tile, q_all.shape[2]), lambda r: (0, r, 0)),
            pl.BlockSpec((count, tile, kv_all.shape[2]), lambda r: (0, r % per, 0)),
            row_block(columns),
            row_block(kv_columns),
            row_block(kv_columns),
            row_block(1),
        ]
        + other_blocks,
        out_specs=[row_block(columns), row_block(kv_columns), row_block(kv_columns), row_block(1)]
        + other_blocks,
        compiler_params=pltpu.CompilerParams(vmem_limit_bytes=48 * MIB),
    )(q_all, kv_all, w_query, key_weight, value_weight, gain[:, None], *others)


def run_starts(segment):
    position = jnp.arange(segment.shape[0], dtype=jnp.int32)
    fresh = jnp.concatenate([jnp.ones((1,), dtype=bool), segment[1:] != segment[:-1]])
    return position, lax.cummax(jnp.where(fresh, position, jnp.zeros_like(position)), axis=0)


def angles(offset, head_size):
    half = head_size // 2
    lane = jnp.arange(head_size, dtype=jnp.int32)
    frequency = jnp.exp((lane % half).astype(F32) * (-2.0 * math.log(THETA) / head_size))
    early, late = offset.reshape(2, -1)
    phases = jnp.where(lane[None, :] < half, early[:, None], late[:, None]) * frequency[None, :]
    return jnp.cos(phases), jnp.sin(phases)


def per_device(
    activations,
    cotangent,
    segments,
    routing,
    attn_gain,
    mlp_gain,
    query_gain,
    key_gain,
    w_query,
    key_weight,
    value_weight,
    w_out,
    w_router,
    w_gate,
    w_up,
    w_down,
):
    count = lax.axis_size("seq")
    shards = lax.axis_size("fsdp")
    me = lax.axis_index("seq")
    chips = count // 2
    x = activations[0].astype(F32)
    dy = cotangent[0]
    segment = segments[0]
    routes = routing[0]
    tok, dim = x.shape
    span = segment.shape[0]
    top = routes.shape[1]
    hd = query_gain.shape[0] * shards
    heads = w_query.shape[1] // hd
    kv_heads = key_weight.shape[1] // hd
    share = heads // count
    experts = w_router.shape[1]
    local_rows = w_out.shape[0]
    capacity = tok * top * 9 // (8 * experts)
    gcols = share * hd

    local_dim = attn_gain.shape[0]
    local_hd = query_gain.shape[0]
    head_gains = jnp.concatenate([query_gain, key_gain], axis=0)
    head_gains = jnp.pad(head_gains, (0, -head_gains.shape[0] % 128))
    small = jnp.concatenate(
        [v.astype(F32).reshape(-1, 128) for v in (attn_gain, mlp_gain, head_gains)], axis=0
    )
    small = jnp.pad(small, ((0, -small.shape[0] % 8), (0, 0)))
    ffe = w_down.shape[1]
    down_rows = ffe // 3 // 16 * 16
    h1_all, qkv, w_qkv, w_o, small, router, wd1 = front(
        activations[0],
        small,
        w_router.T,
        w_query,
        key_weight,
        value_weight,
        w_out,
        w_down[0],
        down_rows,
        hd,
        count,
        shards,
        1,
    )
    gain_rows = local_dim // 128
    g_attn = small[:, :gain_rows].reshape(-1)
    g_mlp = small[:, gain_rows : 2 * gain_rows].reshape(-1)
    g_query = small[:, 2 * gain_rows, :local_hd].reshape(-1)
    g_key = small[:, 2 * gain_rows, local_hd : 2 * local_hd].reshape(-1)
    r1 = lax.rsqrt(jnp.mean(x * x, axis=-1, keepdims=True) + EPSILON)
    position, doc_start = run_starts(segment)
    cos_full, sin_full = angles((position - doc_start).astype(F32), hd)
    start = jnp.where(segment > 0, doc_start, position)

    routes_sent = jnp.pad(routes.T, ((0, -top % 16), (0, 0))).astype(BF16)
    dy_all, routes_all, o, qx, kn, wg, wd2 = attend(
        dy,
        routes_sent,
        qkv,
        g_query,
        g_key,
        cos_full,
        sin_full,
        start,
        w_gate[0],
        w_down[0],
        down_rows,
        count,
        shards,
        4,
    )
    wholes = (
        whole_of(w_up[0], 0, shards),
        jax.ShapeDtypeStruct((ffe - 2 * down_rows, dim), BF16),
    )
    x2, wu, wd3 = product_scattered(
        o, w_o, NN, [w_up[0], w_down[0]], (0, 1), wholes, count, shards, 2
    )
    x2 = x + x2

    r2 = lax.rsqrt(jnp.mean(x2 * x2, axis=-1, keepdims=True) + EPSILON)
    h2 = (x2 * r2 * g_mlp).astype(BF16)
    def gates_of(hidden, chosen):
        logits = mm(hidden, router, NT)
        return jax.nn.softmax(jnp.where(chosen, logits, -1e30), axis=-1) * chosen

    def chosen_of(named):
        names = jnp.arange(experts, dtype=jnp.int32)
        return jnp.any(named[..., :, None] == names, axis=-2)

    routes_all = jnp.swapaxes(routes_all[:, :top].astype(jnp.int32), 1, 2)
    hit = jnp.any(routes_all == me, axis=-1)
    rank = jnp.cumsum(hit.astype(jnp.int32), axis=1) - hit
    slot = jnp.where(hit & (rank < capacity), rank, -1)
    chosen_all = chosen_of(routes_all.reshape(span, top)).astype(BF16)
    xs, de, dx0, dl, ce, hid, dgu = expert_gathered(
        h2,
        slot,
        chosen_all,
        router,
        dy_all,
        (wg, wu, wd1, wd2, wd3, w_gate[0], w_up[0], w_down[0]),
        capacity,
        count,
        shards,
        3,
    )
    dh2_wide, w_gate_part = slots_back(
        slot, dl, dx0, xs, dgu, (wg, wu, w_gate[0], w_up[0]), capacity, count, shards, 6
    )
    dgate = dh2_wide[:, dim : dim + experts] + dh2_wide[:, dim + 64 : dim + 64 + experts]
    gates = gates_of(h2, chosen_of(routes))
    dlogits = (gates * (dgate - jnp.sum(gates * dgate, axis=-1, keepdims=True))).astype(BF16)
    dh2 = dh2_wide[:, :dim] + mm(dlogits, router)
    router_part = mm(dlogits, h2, TN)
    xh = x2 * r2
    mlp_gain_part = jnp.sum(dh2 * xh, axis=0)
    dn = dh2 * g_mlp
    dx2 = dy.astype(F32) + r2 * (dn - xh * jnp.mean(dn * xh, axis=-1, keepdims=True))

    do, w_out_part, w_down_part, w_up_part = out_back(
        dx2.astype(BF16), w_o, o, hid, de, xs, dgu, count, 7
    )
    dqkv, head_gains, mixed, out_half = attend_back(
        qx,
        kn,
        qkv,
        o,
        do,
        g_query,
        g_key,
        cos_full,
        sin_full,
        start,
        slot,
        w_out_part,
        ce,
        capacity,
        count,
        shards,
        5,
    )
    mixed = x2 + mixed
    dh1, qkv_sum = token_back(dqkv, w_qkv, head_gains, h1_all, count, shards, 8)
    xh1 = x * r1
    dn1 = dh1 * g_attn
    input_grad = dx2 + r1 * (dn1 - xh1 * jnp.mean(dn1 * xh1, axis=-1, keepdims=True))

    def sum_fsdp(part, axis):
        return lax.psum_scatter(part.astype(BF16), "fsdp", scatter_dimension=axis, tiled=True)

    w_gate_sum = sum_fsdp(w_gate_part, 0)
    w_up_sum = sum_fsdp(w_up_part, 0)
    w_down_sum = sum_fsdp(w_down_part, 1)

    small_part = jnp.concatenate([router_part, mlp_gain_part[None]], axis=0)
    small_part = jnp.pad(small_part, ((0, -small_part.shape[0] % 16), (0, 0)))
    small_sum = sum_fsdp(small_part, 1)
    extras = [out_half, small_sum] if shards == 2 else []
    q_all, kv_all, *rows_all = last_gather(
        qkv_sum, extras, gcols, local_dim, count, count // kv_heads, 10
    )
    if shards == 2:
        out_all, small_all = rows_all
        out_all = out_all.reshape(local_rows, dim)
    else:
        out_all, small_all = out_rows(w_out_part, small_sum, count)
    small_total = jnp.sum(small_all.astype(F32), axis=0)
    router_grad = small_total[:experts].T
    mlp_gain_grad = small_total[experts]
    (
        w_query_grad,
        w_key_grad,
        w_value_grad,
        attn_gain_grad,
        w_out_grad,
        w_gate_grad,
        w_up_grad,
        w_down_grad,
    ) = finish(
        q_all,
        kv_all,
        w_query,
        key_weight,
        value_weight,
        attn_gain,
        (out_all, w_gate_sum, w_up_sum, w_down_sum),
        kv_heads,
    )
    attn_gain_grad = attn_gain_grad[:, 0]
    head_gain_grads = jnp.sum(q_all[:, local_dim, : 2 * hd].astype(F32), axis=0)
    own_half = lax.axis_index("fsdp") * local_hd
    query_gain_grad = lax.dynamic_slice_in_dim(head_gain_grads[:hd], own_half, local_hd)
    key_gain_grad = lax.dynamic_slice_in_dim(head_gain_grads[hd:], own_half, local_hd)
    return (
        mixed.astype(BF16)[None],
        input_grad[None],
        attn_gain_grad,
        mlp_gain_grad,
        query_gain_grad,
        key_gain_grad,
        w_query_grad,
        w_key_grad,
        w_value_grad,
        w_out_grad,
        router_grad,
        w_gate_grad[None],
        w_up_grad[None],
        w_down_grad[None],
    )


def out_rows(part, small_sum, count):
    chips = count // 2
    gcols, dim = part.shape
    me = lax.axis_index("seq")
    group = (me % 2) * chips + me // 2
    blank = jnp.zeros((count * gcols, dim), BF16)
    placed = lax.dynamic_update_slice(blank, part, (group * gcols, 0))
    mine = lax.psum_scatter(placed, "fsdp", scatter_dimension=0, tiled=True)
    return lax.psum(mine, "seq"), lax.all_gather(small_sum, "seq", axis=0, tiled=False)


def solution(mesh):
    tokens = P("fsdp", "seq", None)
    rows = P("fsdp", None)
    vector = P("fsdp")
    expert_rows = P("seq", "fsdp", None)
    expert_columns = P("seq", None, "fsdp")
    return jax.shard_map(
        per_device,
        mesh=mesh,
        in_specs=(tokens, tokens, rows, tokens)
        + (vector,) * 4
        + (rows,) * 5
        + (expert_rows, expert_rows, expert_columns),
        out_specs=(tokens, tokens)
        + (vector,) * 4
        + (rows,) * 5
        + (expert_rows, expert_rows, expert_columns),
        check_vma=False,
    )
```

```python
import functools
import math

import jax
import jax.numpy as jnp
from jax import lax
from jax.experimental import pallas as pl
from jax.experimental.pallas import tpu as pltpu
from jax.sharding import PartitionSpec as P

EPSILON = 1e-06
THETA = 1000000.0
BF16 = jnp.bfloat16
F32 = jnp.float32
MESH = pl.DeviceIdType.MESH
MIB = 1 << 20
LOG2E = math.log2(math.e)


def ring_of(chip, chips):
    return (chip % 2) * (chips - 1 - chip // 2) + (1 - chip % 2) * (chip // 2)


def chip_of(position, chips):
    upper = position // (chips // 2)
    return (1 - upper) * (2 * position) + upper * (2 * (chips - 1 - position) + 1)


def places(count):
    me = lax.axis_index("seq")
    chips = count // 2
    lane = me % 2
    position = ring_of(me // 2, chips)
    step = 1 - 2 * lane
    following = chip_of((position + step + chips) % chips, chips) * 2 + lane
    previous = chip_of((position - step + chips) % chips, chips) * 2 + lane
    sibling = me + 1 - 2 * lane
    return me, chips, lane, position, step, following, previous, sibling


def greet(places_over_seq, shards=1, more=0):
    barrier = pltpu.get_barrier_semaphore()
    for device in places_over_seq:
        pl.semaphore_signal(barrier, inc=1, device_id={"seq": device}, device_id_type=MESH)
    for i in range(1, shards):
        peer = (lax.axis_index("fsdp") + i) % shards
        pl.semaphore_signal(barrier, inc=1, device_id={"fsdp": peer}, device_id_type=MESH)
    pl.semaphore_wait(barrier, len(places_over_seq) + shards - 1 + more)


def crossing(shards, items, out_sems, in_sems, own_sems=None):
    mine = lax.axis_index("fsdp")

    def place(src, dst, axis):
        if axis is None:
            return dst.at[mine]
        size = src.shape[axis]
        part = pl.ds(pl.multiple_of(mine * size, 128 if axis else 16), size)
        return dst.at[:, part] if axis else dst.at[part]

    def own(n):
        src, dst, axis = items[n]
        return pltpu.make_async_copy(src, place(src, dst, axis), own_sems.at[n])

    def send(n, i):
        src, dst, axis = items[n]
        return pltpu.make_async_remote_copy(
            src_ref=src,
            dst_ref=place(src, dst, axis),
            send_sem=out_sems.at[n, i - 1],
            recv_sem=in_sems.at[n, i - 1],
            device_id={"fsdp": (mine + i) % shards},
            device_id_type=MESH,
        )

    def start(n):
        for i in range(1, shards):
            send(n, i).start()
        if own_sems is not None:
            own(n).start()

    def wait(n):
        for i in range(1, shards):
            send(n, i).wait()
        if own_sems is not None:
            own(n).wait()

    return start, wait


def crossing_scratch(shards, items):
    dma = pltpu.SemaphoreType.DMA
    return [dma((items, max(1, shards - 1))), dma((items, max(1, shards - 1)))]


def spread_units(units, steps):
    total = sum(weight for weight, _ in units)
    plan = [[] for _ in range(steps)]
    done = 0.0
    for weight, run in units:
        plan[min(steps - 1, int((done + weight / 2) * steps / total))].append(run)
        done += weight
    return plan


def run_units(plan, k):
    for step, units in enumerate(plan):
        if units:

            @pl.when(k == step)
            def _(units=units):
                for run in units:
                    run()


def row_parts(rows, cuts):
    if cuts == 1:
        return [pl.ds(0, rows)]
    size = rows // cuts // 16 * 16
    return [pl.ds(c * size, size) for c in range(cuts - 1)] + [
        pl.ds((cuts - 1) * size, rows - (cuts - 1) * size)
    ]


NT = (((1,), (1,)), ((), ()))
TN = (((0,), (0,)), ((), ()))
NN = (((1,), (0,)), ((), ()))


def mm(a, b, dims=NN):
    return lax.dot_general(a, b, dims, preferred_element_type=F32)


def gather_steps(count, cuts, x_ref, land, sems, use, shards=1, begin=None, tag=None):
    me, chips, lane, position, step, following, previous, sibling = places(count)
    ring_out, ring_in, side_out, side_in = sems
    block = x_ref.shape[0]
    rows = block // cuts
    pieces = cuts + (tag is not None)
    greet((previous, sibling), shards)

    def ring(s, c):
        part = pl.ds(c * rows, rows)
        return pltpu.make_async_remote_copy(
            src_ref=tag.at[s, 0] if c == cuts else land.at[s, part],
            dst_ref=tag.at[s + 1, 0] if c == cuts else land.at[s + 1, part],
            send_sem=ring_out.at[s, c],
            recv_sem=ring_in.at[s, c],
            device_id={"seq": following},
            device_id_type=MESH,
        )

    def side(s, c):
        return pltpu.make_async_remote_copy(
            src_ref=tag.at[s, 0] if c == cuts else land.at[s, pl.ds(c * rows, rows)],
            dst_ref=tag.at[s, 1] if c == cuts else land.at[s, pl.ds(block + c * rows, rows)],
            send_sem=side_out.at[s, c],
            recv_sem=side_in.at[s, c],
            device_id={"seq": sibling},
            device_id_type=MESH,
        )

    def forward(s, c):
        @pl.when(s < chips - 1)
        def _():
            ring(s, c).start()

        side(s, c).start()

    land[0, :block] = x_ref[...]
    for c in range(pieces):
        forward(0, c)
    if begin is not None:
        begin()

    def one(s, carry):
        def pump(c):
            @pl.when(s < chips - 1)
            def _():
                ring(s, c).wait_recv()
                forward(s + 1, c)

        for c in range(pieces):
            side(s, c).wait_recv()
        use(s, *pair_owners(count, s), pump)
        return carry

    lax.fori_loop(0, chips, one, 0)

    def close(s, carry):
        for c in range(pieces):
            side(s, c).wait_send()

            @pl.when(s < chips - 1)
            def _():
                ring(s, c).wait_send()

        return carry

    lax.fori_loop(0, chips, close, 0)


def pair_owners(count, s):
    _, chips, lane, position, step, _, _, _ = places(count)
    first = chip_of((position - s * step + chips) % chips, chips) * 2 + lane
    second = chip_of((position + s * step + chips) % chips, chips) * 2 + 1 - lane
    return first, second


def at_block(owner, block):
    return pl.ds(pl.multiple_of(owner * block, block), block)


def gather_scratch(count, pieces, block, columns):
    chips = count // 2
    return [pltpu.VMEM((chips, 2 * block, columns), BF16)] + [
        pltpu.SemaphoreType.DMA((chips, pieces))
    ] * 4


def scatter_steps(count, cuts, o_ref, bufs, sems, produce, extra=None, shards=1, begin=None, meeting=None):
    me, chips, lane, position, step, following, previous, sibling = places(count)
    own, sent, came, give, given = bufs
    ring_out, ring_in, side_out, side_in = sems
    rows = own.shape[1] // cuts
    if meeting is None:
        greet((previous, sibling), shards)
    else:
        meeting[0]()
        greet((previous, sibling), shards, meeting[1])
    if begin is not None:
        begin()

    def ring(k, c):
        part = pl.ds(c * rows, rows)
        return pltpu.make_async_remote_copy(
            src_ref=sent.at[k, part],
            dst_ref=came.at[k, part],
            send_sem=ring_out.at[k, c],
            recv_sem=ring_in.at[k, c],
            device_id={"seq": following},
            device_id_type=MESH,
        )

    def side(k):
        return pltpu.make_async_remote_copy(
            src_ref=give.at[k],
            dst_ref=given.at[k],
            send_sem=side_out.at[k],
            recv_sem=side_in.at[k],
            device_id={"seq": sibling},
            device_id_type=MESH,
        )

    def make(k):
        mine, theirs = produce(k, *pair_owners(count, (k + 1) % chips))
        give[k] = theirs.astype(BF16)
        side(k).start()
        own[k % 2] = mine

    make(0)

    def one(k, carry):
        side(k).wait_recv()
        for c in range(cuts):
            part = pl.ds(c * rows, rows)

            @pl.when(k > 0)
            def _():
                ring(k - 1, c).wait_recv()
                own[k % 2, part] += came[k - 1, part].astype(F32)

            total = own[k % 2, part] + given[k, part].astype(F32)

            @pl.when(k < chips - 1)
            def _():
                sent[k, part] = total.astype(BF16)
                ring(k, c).start()

            @pl.when(k == chips - 1)
            def _():
                o_ref[part] = total

            if c == 0:

                @pl.when(k < chips - 1)
                def _():
                    make(k + 1)

        if extra is not None:
            extra(k)
        return carry

    lax.fori_loop(0, chips, one, 0)

    def close(k, carry):
        side(k).wait_send()

        @pl.when(k < chips - 1)
        def _():
            for c in range(cuts):
                ring(k, c).wait_send()

        return carry

    lax.fori_loop(0, chips, close, 0)


def scatter_scratch(count, cuts, rows, columns):
    chips = count // 2
    dma = pltpu.SemaphoreType.DMA
    return [
        pltpu.VMEM((2, rows, columns), F32),
        pltpu.VMEM((chips - 1, rows, columns), BF16),
        pltpu.VMEM((chips - 1, rows, columns), BF16),
        pltpu.VMEM((chips, rows, columns), BF16),
        pltpu.VMEM((chips, rows, columns), BF16),
        dma((chips, cuts)),
        dma((chips, cuts)),
        dma((chips,)),
        dma((chips,)),
    ]


def remote_params(call, mib):
    return pltpu.CompilerParams(
        collective_id=call, has_side_effects=True, vmem_limit_bytes=mib * MIB
    )


VMEM = pl.BlockSpec(memory_space=pltpu.VMEM)
ANY = pl.BlockSpec(memory_space=pl.ANY)


def front_kernel(
    count,
    shards,
    cuts,
    widths,
    x_ref,
    small_ref,
    wr_ref,
    wq_ref,
    wk_ref,
    wv_ref,
    wo_ref,
    wd_ref,
    h_all,
    qkv_ref,
    w_ref,
    wo_all,
    small_all,
    wr_all,
    wd_all,
    land,
    ring_out,
    ring_in,
    side_out,
    side_in,
    x_out,
    x_in,
    x_own,
    d_out,
    d_in,
    h1,
    gain,
    h_sem,
    o_out,
    o_in,
    o_own,
):
    block, dim = x_ref.shape
    chips = count // 2
    gcols, hd, members = widths
    local = wq_ref.shape[0]
    me = lax.axis_index("seq")
    mine = lax.axis_index("fsdp")
    group = (me % 2) * chips + me // 2
    kv_cols = pl.ds(pl.multiple_of(group // members * hd, 128), hd)
    q_cols = pl.ds(pl.multiple_of(group * gcols, 128), gcols)
    items = [
        (small_ref, small_all, None),
        (wq_ref.at[:, q_cols], w_ref.at[:, pl.ds(0, gcols)], 0),
        (wk_ref.at[:, kv_cols], w_ref.at[:, pl.ds(gcols, hd)], 0),
        (wv_ref.at[:, kv_cols], w_ref.at[:, pl.ds(gcols + hd, hd)], 0),
        (wr_ref, wr_all, 1),
    ]
    start, wait = crossing(shards, items, x_out, x_in, x_own)
    start_down, wait_down = crossing(
        shards, [(wd_ref.at[pl.ds(0, wd_all.shape[0])], wd_all, 1)], d_out, d_in
    )
    owner = group * gcols // wo_ref.shape[0]
    wo_src = wo_ref.at[pl.ds(pl.multiple_of(group * gcols % wo_ref.shape[0], 16), gcols)]
    wo_own = pltpu.make_async_copy(wo_src, wo_all, o_own)

    def wo_send(i):
        return pltpu.make_async_remote_copy(
            src_ref=wo_src,
            dst_ref=wo_all,
            send_sem=o_out.at[i - 1],
            recv_sem=o_in,
            device_id={"fsdp": (mine + i) % shards},
            device_id_type=MESH,
        )

    def begin():
        for n in range(len(items)):
            start(n)

        @pl.when(mine == owner)
        def _():
            wo_own.start()
            for i in range(1, shards):
                wo_send(i).start()

        start_down(0)

    def h_copy(s, holder, half):
        return pltpu.make_async_copy(
            h1.at[s, pl.ds(half * block, block)], h_all.at[at_block(holder, block)], h_sem.at[half]
        )

    def multiply(p):
        first, second = pair_owners(count, p)
        y = mm(h1[p], w_ref[...]).astype(BF16)
        qkv_ref[at_block(first, block), :] = y[:block]
        qkv_ref[at_block(second, block), :] = y[block:]

    def use(s, first, second, pump):
        @pl.when(s == 0)
        def _():
            wait(0)
            for f in range(shards):
                for r in range(local // 128):
                    gain[:, pl.ds(f * local + r * 128, 128)] = small_all[f, r : r + 1, :]

        x = land[s].astype(F32)
        r1 = lax.rsqrt(jnp.mean(x * x, axis=1, keepdims=True) + EPSILON)
        h1[s] = (x * r1 * gain[...]).astype(BF16)
        h_copy(s, first, 0).start()
        h_copy(s, second, 1).start()
        pump(0)

        @pl.when(s == chips // 2)
        def _():
            for n in range(1, len(items)):
                wait(n)

        @pl.when(s >= chips // 2)
        def _():
            multiply(2 * s - chips)
            pump(1)
            multiply(2 * s - chips + 1)

        @pl.when(s < chips // 2)
        def _():
            pump(1)

        for c in range(2, cuts):
            pump(c)

    gather_steps(
        count, cuts, x_ref, land, (ring_out, ring_in, side_out, side_in), use, shards, begin
    )

    @pl.when(mine == owner)
    def _():
        wo_own.wait()
        for i in range(1, shards):
            wo_send(i).wait_send()

    @pl.when(mine != owner)
    def _():
        wo_send(1).wait_recv()

    wait_down(0)
    half_rows = count * block // 2
    for half in range(2):
        pltpu.make_async_copy(
            h_all.at[pl.ds(0, half_rows)], h_all.at[pl.ds(0, half_rows)], h_sem.at[half]
        ).wait()


def front(
    x,
    small,
    w_router,
    w_query,
    key_weight,
    value_weight,
    w_out,
    w_down,
    down_rows,
    hd,
    count,
    shards,
    call,
    cuts=4,
):
    block, dim = x.shape
    gcols = w_query.shape[1] // count
    members = count * hd // key_weight.shape[1]
    columns = gcols + 2 * hd
    chips = count // 2
    dma = pltpu.SemaphoreType.DMA
    return pl.pallas_call(
        functools.partial(front_kernel, count, shards, cuts, (gcols, hd, members)),
        out_shape=(
            jax.ShapeDtypeStruct((count * block, dim), BF16),
            jax.ShapeDtypeStruct((count * block, columns), BF16),
            jax.ShapeDtypeStruct((dim, columns), BF16),
            jax.ShapeDtypeStruct((gcols, w_out.shape[1]), BF16),
            jax.ShapeDtypeStruct((shards,) + small.shape, F32),
            whole_of(w_router, 1, shards),
            jax.ShapeDtypeStruct((down_rows, dim), BF16),
        ),
        in_specs=[VMEM, VMEM, VMEM] + [ANY] * 5,
        out_specs=[ANY, VMEM, VMEM, VMEM, VMEM, VMEM, ANY],
        scratch_shapes=gather_scratch(count, cuts, block, dim)
        + crossing_scratch(shards, 5)
        + [
            dma((5,)),
        ]
        + crossing_scratch(shards, 1)
        + [
            pltpu.VMEM((chips, 2 * block, dim), BF16),
            pltpu.VMEM((1, dim), F32),
            dma((2,)),
            dma((max(1, shards - 1),)),
            dma,
            dma,
        ],
        compiler_params=remote_params(call, 48),
    )(x, small, w_router, w_query, key_weight, value_weight, w_out, w_down)


def out_back_kernel(
    count,
    cuts,
    da_ref,
    w_ref,
    o_ref,
    hid_ref,
    de_ref,
    xs_ref,
    dgu_ref,
    do_ref,
    part_ref,
    down_out,
    up_out,
    land,
    *rest,
):
    sems = rest[:4]
    total, hid, du, de, xs, down_ref, up_ref, sem, tile_sem, store_sem = rest[4:]
    block = da_ref.shape[0]
    columns = de.shape[2]
    ffe = hid.shape[1]
    total[...] = jnp.zeros_like(total)
    loads = [
        pltpu.make_async_copy(hid_ref, hid, sem.at[0]),
        pltpu.make_async_copy(dgu_ref.at[:, pl.ds(ffe, ffe)], du, sem.at[1]),
    ]

    def tiles(s):
        part = pl.ds(pl.multiple_of(s * columns, 128), columns)
        return [
            pltpu.make_async_copy(src.at[:, part], dst.at[s % 2], tile_sem.at[s % 2, n])
            for n, (src, dst) in enumerate(((de_ref, de), (xs_ref, xs)))
        ]

    def begin():
        for load in loads + tiles(0):
            load.start()

    def use(s, first, second, pump):
        @pl.when(s == 0)
        def _():
            for load in loads:
                load.wait()

        @pl.when(s < count // 2 - 1)
        def _():
            for load in tiles(s + 1):
                load.start()

        pair = land[s]
        a = at_block(first, block)
        b = at_block(second, block)
        do = mm(pair, w_ref[...], NT).astype(BF16)
        do_ref[a, :] = do[:block]
        do_ref[b, :] = do[block:]
        pump(0)
        total[...] += mm(jnp.concatenate([o_ref[a, :], o_ref[b, :]], axis=0), pair, TN)
        pump(1)
        for load in tiles(s):
            load.wait()
        part = pl.ds(pl.multiple_of(s * columns, 128), columns)
        down_ref[:, part] = mm(hid[...], de[s % 2], TN).astype(BF16)
        pump(2)
        rows = pl.ds(pl.multiple_of(s * columns, 16), columns)
        up_ref[rows, :] = mm(xs[s % 2], du[...], TN).astype(BF16)
        pltpu.make_async_copy(down_ref.at[:, part], down_out.at[:, part], store_sem.at[0]).start()
        pltpu.make_async_copy(up_ref.at[rows], up_out.at[rows], store_sem.at[1]).start()
        for c in range(3, cuts):
            pump(c)

    gather_steps(count, cuts, da_ref, land, sems, use, 1, begin)
    part_ref[...] = total[...].astype(BF16)
    pltpu.make_async_copy(down_ref, down_out, store_sem.at[0]).wait()
    pltpu.make_async_copy(up_ref, up_out, store_sem.at[1]).wait()


def out_back(da, w, o, hid, de, xs, dgu, count, call, cuts=4):
    block, dim = da.shape
    ffe = hid.shape[1]
    chips = count // 2
    dma = pltpu.SemaphoreType.DMA
    return pl.pallas_call(
        functools.partial(out_back_kernel, count, cuts),
        out_shape=(
            jax.ShapeDtypeStruct(o.shape, BF16),
            jax.ShapeDtypeStruct(w.shape, BF16),
            jax.ShapeDtypeStruct((ffe, dim), BF16),
            jax.ShapeDtypeStruct((dim, ffe), BF16),
        ),
        in_specs=[VMEM] * 3 + [ANY] * 4,
        out_specs=[VMEM] * 2 + [ANY] * 2,
        scratch_shapes=gather_scratch(count, cuts, block, dim)
        + [
            pltpu.VMEM(w.shape, F32),
            pltpu.VMEM(hid.shape, BF16),
            pltpu.VMEM(hid.shape, BF16),
            pltpu.VMEM((2, de.shape[0], dim // chips), BF16),
            pltpu.VMEM((2, xs.shape[0], dim // chips), BF16),
            pltpu.VMEM((ffe, dim), BF16),
            pltpu.VMEM((dim, ffe), BF16),
            dma((2,)),
            dma((2, 2)),
            dma((2,)),
        ],
        compiler_params=remote_params(call, 56),
    )(da, w, o, hid, de, xs, dgu)


def product_kernel(count, shards, cuts, dims, axes, y_ref, w_ref, *refs):
    cargo = len(axes)
    srcs, o_ref, dsts = refs[:cargo], refs[cargo], refs[cargo + 1 : 2 * cargo + 1]
    rest = refs[2 * cargo + 1 :]
    block = o_ref.shape[0]
    if cargo:
        lasts = []
        for src, dst, axis in zip(srcs, dsts, axes):
            rows = dst.shape[0] if axis else src.shape[0]
            lasts.append((src.at[pl.ds(src.shape[0] - rows, rows)], dst, axis))
        start, wait = crossing(shards, lasts, *rest[9:])

    def begin():
        for n in range(cargo):
            start(n)

    def produce(k, first, second):
        a = y_ref[at_block(first, block), :]
        b = y_ref[at_block(second, block), :]
        both = mm(jnp.concatenate([a, b], axis=0), w_ref[...], dims)
        return both[:block], both[block:]

    scatter_steps(
        count, cuts, o_ref, rest[:5], rest[5:9], produce, None, shards if cargo else 1, begin
    )
    for n in range(cargo):
        wait(n)


def token_back_kernel(
    count,
    shards,
    cuts,
    y_ref,
    w_ref,
    gains_ref,
    h_ref,
    o_ref,
    sum_ref,
    *rest,
):
    chips = count // 2
    block = o_ref.shape[0]
    hbuf, grad, came, gains, h_sem, w_out, w_in, g_out, g_in = rest[9:]
    mine = lax.axis_index("fsdp")
    dim, columns = grad.shape
    local = dim // shards
    part = dim // chips
    per = local // part
    width = gains_ref.shape[1]

    def chunk(k):
        return (k + (mine + 1) % shards * per) % chips

    def load(k):
        cols = pl.ds(pl.multiple_of(chunk(k) * part, 128), part)
        return pltpu.make_async_copy(h_ref.at[:, cols], hbuf.at[k % 2], h_sem.at[k % 2])

    def send(k):
        n = chunk(k)
        owner = n // per
        slot = (owner - mine + shards) % shards - 1
        return pltpu.make_async_remote_copy(
            src_ref=grad.at[pl.ds(pl.multiple_of(n * part, 16), part)],
            dst_ref=came.at[slot, pl.ds(pl.multiple_of(n % per * part, 16), part)],
            send_sem=w_out.at[k],
            recv_sem=w_in.at[slot, n % per],
            device_id={"fsdp": owner},
            device_id_type=MESH,
        )

    def send_gains(i):
        return pltpu.make_async_remote_copy(
            src_ref=gains_ref,
            dst_ref=gains.at[i - 1],
            send_sem=g_out.at[i - 1],
            recv_sem=g_in.at[i - 1],
            device_id={"fsdp": (mine + i) % shards},
            device_id_type=MESH,
        )

    def begin():
        load(0).start()
        for i in range(1, shards):
            send_gains(i).start()

    def produce(k, first, second):
        a = y_ref[at_block(first, block), :]
        b = y_ref[at_block(second, block), :]
        both = mm(jnp.concatenate([a, b], axis=0), w_ref[...], NT)
        return both[:block], both[block:]

    def extra(k):
        load(k).wait()

        @pl.when(k < chips - 1)
        def _():
            load(k + 1).start()

        rows = pl.ds(pl.multiple_of(chunk(k) * part, 16), part)
        grad[rows, :] = mm(hbuf[k % 2], y_ref[...], TN).astype(BF16)

        @pl.when(k < chips - per)
        def _():
            send(k).start()

    scatter_steps(count, cuts, o_ref, rest[:5], rest[5:9], produce, extra, shards, begin)
    total = gains_ref[...]
    for i in range(1, shards):
        send_gains(i).wait()
        total = total + gains[i - 1]
    row = lax.broadcasted_iota(jnp.int32, (16, width), 0)
    sum_ref[pl.ds(local, 16), :] = jnp.zeros((16, columns), BF16)
    for n in range(2):
        sum_ref[pl.ds(local, 16), pl.ds(n * width, width)] = jnp.where(
            row == 0, jnp.broadcast_to(total[n : n + 1, :], (16, width)), 0.0
        ).astype(BF16)
    for k in range(chips - per):
        send(k).wait_send()
    for n in range(per):
        part_rows = pl.ds(n * part, part)
        own = grad[pl.ds(pl.multiple_of(mine * local + n * part, 16), part), :].astype(F32)
        for i in range(1, shards):
            pltpu.make_async_remote_copy(
                src_ref=grad.at[part_rows],
                dst_ref=came.at[i - 1, part_rows],
                send_sem=w_out.at[0],
                recv_sem=w_in.at[i - 1, n],
                device_id={"fsdp": (mine + i) % shards},
                device_id_type=MESH,
            ).wait_recv()
            own = own + came[i - 1, part_rows, :].astype(F32)
        sum_ref[part_rows, :] = own.astype(BF16)


def token_back(y, w, gains, h_all, count, shards, call, cuts=2):
    block = y.shape[0] // count
    dim, columns = w.shape
    chips = count // 2
    local = dim // shards
    others = max(1, shards - 1)
    dma = pltpu.SemaphoreType.DMA
    return pl.pallas_call(
        functools.partial(token_back_kernel, count, shards, cuts),
        out_shape=(
            jax.ShapeDtypeStruct((block, dim), F32),
            jax.ShapeDtypeStruct((local + 16, columns), BF16),
        ),
        in_specs=[VMEM] * 3 + [ANY],
        out_specs=[VMEM] * 2,
        scratch_shapes=scatter_scratch(count, cuts, block, dim)
        + [
            pltpu.VMEM((2, h_all.shape[0], dim // chips), BF16),
            pltpu.VMEM((dim, columns), BF16),
            pltpu.VMEM((others, local, columns), BF16),
            pltpu.VMEM((others,) + gains.shape, F32),
            dma((2,)),
            dma((chips,)),
            dma((others, chips // shards)),
            dma((others,)),
            dma((others,)),
        ],
        compiler_params=remote_params(call, 48),
    )(y, w, gains, h_all)


def whole_of(part, axis, shards):
    shape = list(part.shape)
    shape[axis] *= shards
    return jax.ShapeDtypeStruct(tuple(shape), part.dtype)


def product_scattered(y, w, dims, cargo, axes, wholes, count, shards, call, cuts=2):
    block = y.shape[0] // count
    columns = w.shape[1 - dims[0][1][0]]
    return pl.pallas_call(
        functools.partial(product_kernel, count, shards, cuts, dims, axes),
        out_shape=[jax.ShapeDtypeStruct((block, columns), F32)]
        + list(wholes),
        in_specs=[VMEM, VMEM] + [ANY] * len(cargo),
        out_specs=[VMEM] + [ANY] * len(cargo),
        scratch_shapes=scatter_scratch(count, cuts, block, columns)
        + (crossing_scratch(shards, len(cargo)) if cargo else []),
        compiler_params=remote_params(call, 48),
    )(y, w, *cargo)


def one_hot_of(slot_ref, first, second, capacity):
    a = slot_ref[pl.ds(first, 1), :]
    b = slot_ref[pl.ds(second, 1), :]
    wanted = jnp.concatenate([a, jnp.where(b >= 0, b + capacity, -1)], axis=1)
    row = lax.broadcasted_iota(jnp.int32, (2 * capacity, wanted.shape[1]), 0)
    return jnp.where(row == wanted, 1.0, 0.0).astype(BF16)


def parts_of_own(i, shards, size, unit):
    place = (lax.axis_index("fsdp") + i) % shards
    return pl.ds(pl.multiple_of(place * (size // shards), unit), size // shards)


def gate_up_parts(i, shards, whole, own, wgu):
    rows = parts_of_own(i, shards, wgu.shape[0], 16)
    ffe = wgu.shape[1] // 2
    return [
        (whole[n].at[rows] if i else own[n], wgu.at[rows, pl.ds(n * ffe, ffe)]) for n in range(2)
    ]


def down_parts(i, shards, pieces, own, wd):
    columns = parts_of_own(i, shards, wd.shape[1], 128)
    parts = []
    first = 0
    for piece in pieces:
        rows = pl.ds(first, piece.shape[0])
        first += piece.shape[0]
        parts.append((piece.at[:, columns] if i else own.at[rows], wd.at[rows, columns]))
    return parts


def expert_kernel(
    count,
    shards,
    cuts,
    capacity,
    h_ref,
    slot_ref,
    chosen_ref,
    router_ref,
    dy_ref,
    wg_ref,
    wu_ref,
    wd1_ref,
    wd2_ref,
    wd3_ref,
    wg_own,
    wu_own,
    wd_own,
    xs_out,
    de_out,
    dx_ref,
    dl_out,
    ce_out,
    hid_out,
    dgu_out,
    land,
    ring_out,
    ring_in,
    side_out,
    side_in,
    wgu,
    wd,
    dyb,
    xs,
    de,
    dl,
    ce,
    hid,
    dgu,
    w_sem,
    dy_sem,
    out_sem,
):
    block, dim = h_ref.shape
    ffe = wd.shape[0]
    wd_refs = (wd1_ref, wd2_ref, wd3_ref)
    me = lax.axis_index("seq")
    chips = count // 2
    weights = [
        pltpu.make_async_copy(src, dst, w_sem.at[i, n])
        for i in range(shards)
        for n, (src, dst) in enumerate(
            gate_up_parts(i, shards, (wg_ref, wu_ref), (wg_own, wu_own), wgu)
            + down_parts(i, shards, wd_refs, wd_own, wd)
        )
    ]
    staged = (
        (xs, xs_out),
        (de, de_out),
        (dl, dl_out),
        (ce, ce_out),
        (hid, hid_out),
        (dgu, dgu_out),
    )

    def dy_copies(s):
        first, second = pair_owners(count, s)
        return [
            pltpu.make_async_copy(
                dy_ref.at[at_block(owner, block)], dyb.at[s % 2, pl.ds(half * block, block)], dy_sem.at[s % 2, half]
            )
            for half, owner in ((0, first), (1, second))
        ]

    for copy in weights + dy_copies(0):
        copy.start()

    def use(s, first, second, pump):
        @pl.when(s < chips - 1)
        def _():
            for copy in dy_copies(s + 1):
                copy.start()

        rows = pl.ds(pl.multiple_of(s * 2 * capacity, 16), 2 * capacity)
        pick = one_hot_of(slot_ref, first, second, capacity)
        x = mm(pick, land[s]).astype(BF16)
        xs[rows, :] = x
        chosen = mm(
            pick,
            jnp.concatenate(
                [
                    chosen_ref[pl.ds(pl.multiple_of(first * block, block), block), :],
                    chosen_ref[pl.ds(pl.multiple_of(second * block, block), block), :],
                ],
                axis=0,
            ),
        )
        logits = jnp.where(chosen > 0.5, mm(x, router_ref[...], NT), -1e30)
        weight = jnp.exp(logits - jnp.max(logits, axis=1, keepdims=True)) * chosen
        mass = jnp.sum(weight, axis=1, keepdims=True)
        expert_lane = lax.broadcasted_iota(jnp.int32, weight.shape, 1)
        wide_lane = lax.broadcasted_iota(jnp.int32, (2 * capacity, dl.shape[1]), 1)
        gate = jnp.sum(jnp.where(expert_lane == me, weight, 0.0), axis=1, keepdims=True)
        gate = gate / jnp.where(mass > 0.0, mass, 1.0)

        @pl.when(s == 0)
        def _():
            for copy in weights:
                copy.wait()

        gu = mm(x, wgu[...])
        pump(0)
        g, u = gu[:, :ffe], gu[:, ffe:]
        sig = jax.nn.sigmoid(g)
        silu = g * sig
        h = (silu * u).astype(BF16)
        hid[rows, :] = h
        e = mm(h, wd[...])
        ce[rows, :] = (gate * e).astype(BF16)
        pump(1)
        for copy in dy_copies(s):
            copy.wait()
        dys = mm(pick, dyb[s % 2])
        dgate = jnp.sum(dys * e, axis=1, keepdims=True)
        d = (gate * dys).astype(BF16)
        de[rows, :] = d
        pump(2)
        dh = mm(d, wd[...], NT)
        for c in range(3, cuts):
            pump(c)
        dg = (dh * u * (sig + silu * (1.0 - sig))).astype(BF16)
        du = (dh * silu).astype(BF16)
        dgu[rows, :ffe] = dg
        dgu[rows, ffe:] = du

        @pl.when(s == 1)
        def _():
            dx_ref[...] = mm(dgu[rows, :], wgu[...], NT).astype(BF16)

        high = dgate.astype(BF16).astype(F32)
        dl[rows, :] = jnp.where(
            wide_lane == me, high, jnp.where(wide_lane == me + 64, dgate - high, 0.0)
        ).astype(BF16)
        for i, (src, dst) in enumerate(staged):
            pltpu.make_async_copy(src.at[rows], dst.at[rows], out_sem.at[i]).start()

    gather_steps(count, cuts, h_ref, land, (ring_out, ring_in, side_out, side_in), use)
    for i, (src, dst) in enumerate(staged):
        pltpu.make_async_copy(src, dst, out_sem.at[i]).wait()


def expert_gathered(h2, slot, chosen, router, dy_all, weights, capacity, count, shards, call, cuts=4):
    block, dim = h2.shape
    ffe = weights[0].shape[1]
    total = count * capacity
    widths = (dim, dim, 128, dim, ffe, 2 * ffe)
    dma = pltpu.SemaphoreType.DMA
    return pl.pallas_call(
        functools.partial(expert_kernel, count, shards, cuts, capacity),
        out_shape=[
            jax.ShapeDtypeStruct((2 * capacity if i == 2 else total, n), BF16)
            for i, n in enumerate(widths[:2] + (dim,) + widths[2:])
        ],
        in_specs=[VMEM] * 4 + [ANY] * 9,
        out_specs=[ANY] * 2 + [VMEM] + [ANY] * 4,
        scratch_shapes=gather_scratch(count, cuts, block, dim)
        + [
            pltpu.VMEM((dim, 2 * ffe), BF16),
            pltpu.VMEM((ffe, dim), BF16),
            pltpu.VMEM((2, 2 * block, dim), BF16),
        ]
        + [pltpu.VMEM((total, n), BF16) for n in widths]
        + [dma((shards, 5)), dma((2, 2)), dma((6,))],
        compiler_params=remote_params(call, 60),
    )(h2, slot, chosen, router, dy_all, *weights)


def slots_back_kernel(
    count,
    shards,
    cuts,
    capacity,
    slot_ref,
    dl,
    dx0_ref,
    xs_ref,
    dgu_ref,
    wg_ref,
    wu_ref,
    wg_own,
    wu_own,
    o_ref,
    gate_out,
    *rest,
):
    bufs, sems = rest[:5], rest[5:9]
    dx, xs, dgu, wgu, gate, sem, w_sem, gate_sem = rest[9:]
    chips = count // 2
    block = o_ref.shape[0]
    ffe = gate.shape[1]
    load_dgu = pltpu.make_async_copy(dgu_ref, dgu, sem.at[0])
    load_xs = pltpu.make_async_copy(xs_ref, xs, sem.at[1])
    weights = [
        pltpu.make_async_copy(src, dst, w_sem.at[i, n])
        for i in range(shards)
        for n, (src, dst) in enumerate(
            gate_up_parts(i, shards, (wg_ref, wu_ref), (wg_own, wu_own), wgu)
        )
    ]
    part = xs.shape[1] // chips

    def begin():
        for load in [load_dgu] + weights + [load_xs]:
            load.start()

    def produce(k, first, second):
        rows = pl.ds(pl.multiple_of((k + 1) % chips * 2 * capacity, 16), 2 * capacity)

        @pl.when(k == 0)
        def _():
            dx[...] = dx0_ref[...]

        @pl.when(k == 1)
        def _():
            for load in [load_dgu] + weights:
                load.wait()

        @pl.when(k > 0)
        def _():
            dx[...] = mm(dgu[rows, :], wgu[...], NT).astype(BF16)

        pick = one_hot_of(slot_ref, first, second, capacity)
        both = jnp.concatenate([mm(pick, dx[...], TN), mm(pick, dl[rows, :], TN)], axis=1)
        return both[:block], both[block:]

    def extra(k):
        @pl.when(k == 0)
        def _():
            load_xs.wait()

        columns = pl.ds(pl.multiple_of(k * part, 128), part)
        rows = pl.ds(pl.multiple_of(k * part, 16), part)
        gate[rows, :] = mm(xs[:, columns], dgu[:, :ffe], TN).astype(BF16)
        pltpu.make_async_copy(gate.at[rows], gate_out.at[rows], gate_sem).start()

    scatter_steps(count, cuts, o_ref, bufs, sems, produce, extra, 1, begin)
    pltpu.make_async_copy(gate, gate_out, gate_sem).wait()


def slots_back(slot, dl, dx0, xs, dgu, weights, capacity, count, shards, call, cuts=2):
    block = slot.shape[1]
    dim, ffe = xs.shape[1], dgu.shape[1] // 2
    columns = dim + dl.shape[1]
    dma = pltpu.SemaphoreType.DMA
    return pl.pallas_call(
        functools.partial(slots_back_kernel, count, shards, cuts, capacity),
        out_shape=(
            jax.ShapeDtypeStruct((block, columns), F32),
            jax.ShapeDtypeStruct((dim, ffe), BF16),
        ),
        in_specs=[VMEM] * 3 + [ANY] * 6,
        out_specs=[VMEM, ANY],
        scratch_shapes=scatter_scratch(count, cuts, block, columns)
        + [pltpu.VMEM(a.shape, BF16) for a in (dx0, xs, dgu)]
        + [pltpu.VMEM((dim, 2 * ffe), BF16), pltpu.VMEM((dim, ffe), BF16)]
        + [dma((2,)), dma((shards, 2)), dma],
        compiler_params=remote_params(call, 60),
    )(slot, dl, dx0, xs, dgu, *weights)


def split3(x):
    first = x.astype(BF16)
    rest = x - first.astype(F32)
    second = rest.astype(BF16)
    return first, second, (rest - second.astype(F32)).astype(BF16)


def in_lanes(x):
    lane = lax.broadcasted_iota(jnp.int32, x.shape, 1)
    first = x.astype(BF16).astype(F32)
    second = (x - first).astype(BF16).astype(F32)
    third = x - first - second
    spread = jnp.where(lane == 0, first, jnp.where(lane == 1, second, third))
    return jnp.where(lane < 3, spread, 0.0).astype(BF16)


def swap_halves(x):
    half = x.shape[1] // 2
    return jnp.concatenate([x[:, half:], x[:, :half]], axis=1)


def rope_tables(cos_ref, sin_ref, i, tile):
    rows, width = cos_ref.shape
    late = i * tile // rows
    part = pl.ds(i * tile - late * rows, tile)
    lanes = slice(late * (width // 2), (late + 1) * (width // 2))
    cos = cos_ref[part, :][:, lanes]
    sin = sin_ref[part, :][:, lanes]
    return jnp.concatenate([cos, cos], axis=1), jnp.concatenate([-sin, sin], axis=1)


def unit_rows(u):
    r = lax.rsqrt(jnp.mean(u * u, axis=1, keepdims=True) + EPSILON)
    return r, u * r


def attend_kernel(
    count,
    shards,
    cuts,
    heads,
    tile,
    dy_ref,
    routes_ref,
    qkv_ref,
    gq_ref,
    gk_ref,
    cos_ref,
    sin_ref,
    start_ref,
    wg_ref,
    wd_ref,
    dy_all,
    routes_all,
    o_ref,
    qx_ref,
    kn_ref,
    wg_all,
    wd_all,
    land,
    ring_out,
    ring_in,
    side_out,
    side_in,
    x_out,
    x_in,
    tag,
    vx_ref,
    dy_sem,
):
    span = qkv_ref.shape[0]
    width = kn_ref.shape[1]
    block = dy_ref.shape[0]
    scale = width**-0.5 * LOG2E
    down = wd_all.shape[0]
    items = [(wg_ref, wg_all, 0), (wd_ref.at[pl.ds(down, down)], wd_all, 1)]
    start_item, wait_item = crossing(shards, items, x_out, x_in)

    def prepare(i):
        rows = pl.ds(i * tile, tile)
        cos, sin = rope_tables(cos_ref, sin_ref, i, tile)
        for h in range(heads + 1):
            _, unit = unit_rows(qkv_ref[rows, pl.ds(h * width, width)].astype(F32))
            u = unit * (gk_ref[...] if h == heads else gq_ref[...])
            u = u * cos + swap_halves(u) * sin
            if h == heads:
                kn_ref[rows, :] = u.astype(BF16)
            else:
                qx_ref[rows, pl.ds(2 * h * width, width)] = (u * scale).astype(BF16)
        vx_ref[rows, :width] = qkv_ref[rows, pl.ds((heads + 1) * width, width)]
        vx_ref[rows, width:] = jnp.ones((tile, width), BF16)

    def attend_rows(i, h):
        rows = pl.ds(i * tile, tile)
        start = start_ref[rows, :]
        row = i * tile + lax.broadcasted_iota(jnp.int32, (tile, tile), 0)
        q = qx_ref[rows, pl.ds(2 * h * width, width)]
        total = jnp.zeros((tile, 2 * width), F32)
        for j in range(i + 1):
            keys = pl.ds(j * tile, tile)
            s = mm(q, kn_ref[keys, :], NT)
            col = j * tile + lax.broadcasted_iota(jnp.int32, (tile, tile), 1)
            keep = col >= start
            if i == j:
                keep = keep & (col <= row)
            p = jnp.where(keep, jnp.exp2(s), 0.0).astype(BF16)
            total = total + mm(p, vx_ref[keys, :])
        weight = total[:, width:]
        o_ref[rows, pl.ds(h * width, width)] = (total[:, :width] / weight).astype(BF16)
        qx_ref[rows, pl.ds((2 * h + 1) * width, width)] = in_lanes(-jnp.log2(weight))

    units = []
    for i in range(span // tile):
        units.append((1.0, functools.partial(prepare, i)))
        units += [(0.7 * (i + 1), functools.partial(attend_rows, i, h)) for h in range(heads)]
    plan = spread_units(units, count // 2 - 1)

    def begin():
        for n in range(len(items)):
            start_item(n)

    tag[0, 0] = routes_ref[...]

    def use(s, first, second, pump):
        for half, owner in ((0, first), (1, second)):
            pltpu.make_async_copy(
                land.at[s, pl.ds(half * block, block)],
                dy_all.at[at_block(owner, block)],
                dy_sem.at[half],
            ).start()
            routes_all[owner] = tag[s, half]
        run_units(plan, s)
        for c in range(cuts + 1):
            pump(c)

    gather_steps(
        count, cuts, dy_ref, land, (ring_out, ring_in, side_out, side_in), use, shards, begin, tag
    )
    for n in range(len(items)):
        wait_item(n)
    half_rows = count * block // 2
    for half in range(2):
        pltpu.make_async_copy(
            dy_all.at[pl.ds(0, half_rows)], dy_all.at[pl.ds(0, half_rows)], dy_sem.at[half]
        ).wait()


def attend(dy, routes, qkv, gq, gk, cos, sin, start, w_gate, w_down, down_rows, count, shards, call, tile=512, cuts=4):
    span = qkv.shape[0]
    width = gq.shape[0]
    heads = qkv.shape[1] // width - 2
    block, dim = dy.shape
    chips = count // 2
    return pl.pallas_call(
        functools.partial(attend_kernel, count, shards, cuts, heads, min(tile, span // 2)),
        out_shape=(
            jax.ShapeDtypeStruct((count * block, dim), BF16),
            jax.ShapeDtypeStruct((count,) + routes.shape, BF16),
            jax.ShapeDtypeStruct((span, heads * width), BF16),
            jax.ShapeDtypeStruct((span, 2 * heads * width), BF16),
            jax.ShapeDtypeStruct((span, width), BF16),
            whole_of(w_gate, 0, shards),
            jax.ShapeDtypeStruct((down_rows, dim), BF16),
        ),
        in_specs=[VMEM] * 8 + [ANY] * 2,
        out_specs=[ANY] + [VMEM] * 4 + [ANY] * 2,
        scratch_shapes=gather_scratch(count, cuts + 1, block, dim)
        + crossing_scratch(shards, 2)
        + [
            pltpu.VMEM((chips, 2) + routes.shape, BF16),
            pltpu.VMEM((span, 2 * width), BF16),
            pltpu.SemaphoreType.DMA((2,)),
        ],
        compiler_params=remote_params(call, 56),
    )(dy, routes, qkv, gq[None, :], gk[None, :], cos, sin, start[:, None], w_gate, w_down)


def attend_back_kernel(
    count,
    shards,
    cuts,
    capacity,
    heads,
    tile,
    qx_ref,
    kn_ref,
    qkv_ref,
    o_ref,
    do_ref,
    gq_ref,
    gk_ref,
    cos_ref,
    sin_ref,
    start_ref,
    slot_ref,
    part_ref,
    ce_ref,
    dqkv_ref,
    gains_ref,
    mixed_ref,
    half_ref,
    *rest,
):
    bufs, sems = rest[:5], rest[5:9]
    gx_ref, dq_ref, dk_ref, dv_ref, held, held_sem, pair, pair_own, pair_out, pair_in = rest[9:]
    span = qx_ref.shape[0]
    width = kn_ref.shape[1]
    scale = width**-0.5
    chips = count // 2
    block = mixed_ref.shape[0]
    load = pltpu.make_async_copy(ce_ref, held, held_sem)
    load.start()

    mine = lax.axis_index("fsdp")
    me = lax.axis_index("seq")
    lane = me % 2
    chip_first = me - lane
    half_rows = half_ref.shape[0]

    def give_half(c):
        return pltpu.make_async_remote_copy(
            src_ref=part_ref.at[pl.ds(c * half_rows, half_rows)],
            dst_ref=pair.at[(mine + lane) % 2],
            send_sem=pair_out.at[c],
            recv_sem=pair_in.at[(mine + lane) % 2],
            device_id={"fsdp": lane, "seq": chip_first + c},
            device_id_type=MESH,
        )

    def take_half(n):
        return pltpu.make_async_remote_copy(
            src_ref=part_ref.at[pl.ds(0, half_rows)],
            dst_ref=pair.at[n],
            send_sem=pair_out.at[0],
            recv_sem=pair_in.at[n],
            device_id={"fsdp": 1 - mine, "seq": chip_first + mine},
            device_id_type=MESH,
        )

    keep_half = pltpu.make_async_copy(
        part_ref.at[pl.ds(pl.multiple_of(lane * half_rows, 16), half_rows)], pair.at[0], pair_own
    )

    def meet():
        barrier = pltpu.get_barrier_semaphore()
        pl.semaphore_signal(
            barrier,
            inc=1,
            device_id={"fsdp": 1 - mine, "seq": chip_first + mine},
            device_id_type=MESH,
        )

        @pl.when(lane != mine)
        def _():
            pl.semaphore_signal(
                barrier, inc=1, device_id={"seq": chip_first + mine}, device_id_type=MESH
            )

    def begin():
        for c in range(2):

            @pl.when((mine != lane) | (lane != c))
            def _(c=c):
                give_half(c).start()

        @pl.when(mine == lane)
        def _():
            keep_half.start()

    def end():
        for c in range(2):

            @pl.when((mine != lane) | (lane != c))
            def _(c=c):
                give_half(c).wait_send()

        @pl.when(mine == lane)
        def _():
            keep_half.wait()

        @pl.when(mine != lane)
        def _():
            take_half(0).wait_recv()

        take_half(1).wait_recv()
        half_ref[...] = (pair[0].astype(F32) + pair[1].astype(F32)).astype(BF16)

    summing = shards == 2
    partners = 1 + (mine != lane).astype(jnp.int32)

    def produce(k, first, second):
        @pl.when(k == 0)
        def _():
            load.wait()

        pair = pl.multiple_of((k + 1) % chips * 2 * capacity, 16)
        pick = one_hot_of(slot_ref, first, second, capacity)
        both = mm(pick, held[pl.ds(pair, 2 * capacity), :], TN)
        return both[:block], both[block:]

    def to_raw(d, h, i, gain, row):
        rows = pl.ds(i * tile, tile)
        cos, sin = rope_tables(cos_ref, sin_ref, i, tile)
        r, unit = unit_rows(qkv_ref[rows, pl.ds(h * width, width)].astype(F32))
        d = d * cos + swap_halves(d * sin)
        dg = d * gain
        raw = r * (dg - unit * jnp.mean(dg * unit, axis=1, keepdims=True))
        dqkv_ref[rows, pl.ds(h * width, width)] = raw.astype(BF16)
        gains_ref[row : row + 1, :] += jnp.sum(d * unit, axis=0, keepdims=True)

    def prepare(i):
        rows = pl.ds(i * tile, tile)
        for h in range(heads):
            cols = pl.ds(h * width, width)
            do = do_ref[rows, cols]
            inner = jnp.sum(do.astype(F32) * o_ref[rows, cols].astype(F32), axis=1, keepdims=True)
            gx_ref[rows, pl.ds(2 * h * width, width)] = do
            gx_ref[rows, pl.ds((2 * h + 1) * width, width)] = in_lanes(
                jnp.broadcast_to(-inner, (tile, width))
            )

    def tile_back(j, i):
        keys = pl.ds(j * tile, tile)
        rows = pl.ds(i * tile, tile)
        ones = jnp.ones((tile, width), BF16)
        kn = kn_ref[keys, :]
        kx = jnp.concatenate([kn, ones], axis=1)
        vx = jnp.concatenate([qkv_ref[keys, pl.ds((heads + 1) * width, width)], ones], axis=1)
        key = j * tile + lax.broadcasted_iota(jnp.int32, (tile, tile), 0)
        keep = key >= start_ref[:, rows]
        if i == j:
            row = i * tile + lax.broadcasted_iota(jnp.int32, (tile, tile), 1)
            keep = keep & (key <= row)
        for h in range(heads):
            qx = qx_ref[rows, pl.ds(2 * h * width, 2 * width)]
            gx = gx_ref[rows, pl.ds(2 * h * width, 2 * width)]
            p = jnp.where(keep, jnp.exp2(mm(kx, qx, NT)), 0.0)
            ds = (p * mm(vx, gx, NT)).astype(BF16)
            dv_ref[keys, :] += mm(p.astype(BF16), gx[:, :width])
            dk_ref[keys, :] += mm(ds, qx[:, :width])
            dq_ref[rows, pl.ds(h * width, width)] += mm(ds, kn, TN)

    def finish_keys(j):
        keys = pl.ds(j * tile, tile)
        dqkv_ref[keys, pl.ds((heads + 1) * width, width)] = dv_ref[keys, :].astype(BF16)
        to_raw(dk_ref[keys, :] * (1.0 / LOG2E), heads, j, gk_ref[...], 1)

    def finish_rows(i):
        rows = pl.ds(i * tile, tile)
        for h in range(heads):
            to_raw(dq_ref[rows, pl.ds(h * width, width)] * scale, h, i, gq_ref[...], 0)

    tiles = span // tile
    units = [(0.3, functools.partial(prepare, i)) for i in range(tiles)]
    for j in range(tiles):
        units += [(2.0, functools.partial(tile_back, j, i)) for i in range(j, tiles)]
        units.append((0.3, functools.partial(finish_keys, j)))
        units.append((0.6, functools.partial(finish_rows, j)))
    plan = spread_units(units, chips - 1)
    for ref in (dq_ref, dk_ref, dv_ref, gains_ref):
        ref[...] = jnp.zeros_like(ref)

    def extra(k):
        run_units(plan, k)

    if summing:
        scatter_steps(
            count, cuts, mixed_ref, bufs, sems, produce, extra, 1, begin, (meet, partners)
        )
        end()
    else:
        scatter_steps(count, cuts, mixed_ref, bufs, sems, produce, extra)
        half_ref[...] = jnp.zeros_like(half_ref)


def attend_back(qx, kn, qkv, o, do, gq, gk, cos, sin, start, slot, part, ce, capacity, count, shards, call, tile=512, cuts=2):
    span, width = kn.shape
    heads = o.shape[1] // width
    block = slot.shape[1]
    dim = ce.shape[1]
    return pl.pallas_call(
        functools.partial(
            attend_back_kernel, count, shards, cuts, capacity, heads, min(tile, span // 2)
        ),
        out_shape=(
            jax.ShapeDtypeStruct(qkv.shape, BF16),
            jax.ShapeDtypeStruct((8, width), F32),
            jax.ShapeDtypeStruct((block, dim), F32),
            jax.ShapeDtypeStruct((part.shape[0] // 2, dim), BF16),
        ),
        in_specs=[VMEM] * 12 + [ANY],
        out_specs=[VMEM] * 4,
        scratch_shapes=scatter_scratch(count, cuts, block, dim)
        + [
            pltpu.VMEM((span, 2 * heads * width), BF16),
            pltpu.VMEM((span, heads * width), F32),
            pltpu.VMEM((span, width), F32),
            pltpu.VMEM((span, width), F32),
            pltpu.VMEM(ce.shape, BF16),
            pltpu.SemaphoreType.DMA,
            pltpu.VMEM((2, part.shape[0] // 2, dim), BF16),
            pltpu.SemaphoreType.DMA,
            pltpu.SemaphoreType.DMA((2,)),
            pltpu.SemaphoreType.DMA((2,)),
        ],
        compiler_params=remote_params(call, 60),
    )(qx, kn, qkv, o, do, gq[None, :], gk[None, :], cos, sin, start[None, :], slot, part, ce)


def last_gather_kernel(count, members, cuts, extras, qkv_ref, *refs):
    x_refs, (q_all, kv_all) = refs[:extras], refs[extras : extras + 2]
    x_alls = refs[extras + 2 : 2 * extras + 2]
    heap, kv_sum, own_sem, mo, mi, ro, ri, so, si = refs[2 * extras + 2 :]
    me, chips, lane, position, step, following, previous, sibling = places(count)
    chip = me // 2
    place = chip % members
    first = chip - place
    rows = kv_sum.shape[0]
    gcols = q_all.shape[2]
    q_ref = qkv_ref.at[:, pl.ds(0, gcols)]
    kv_ref = qkv_ref.at[pl.ds(0, rows * members), pl.ds(gcols, kv_sum.shape[1])]

    def member(i):
        return (first + (place + i) % members) * 2 + lane

    greet([previous, sibling] + [member(i) for i in range(1, members)])

    def give(i):
        target = (place + i) % members
        return pltpu.make_async_remote_copy(
            src_ref=kv_ref.at[pl.ds(target * rows, rows)],
            dst_ref=heap.at[i - 1],
            send_sem=mo.at[i - 1],
            recv_sem=mi.at[i - 1],
            device_id={"seq": member(i)},
            device_id_type=MESH,
        )

    pieces = []
    for x_ref, x_all in zip(x_refs, x_alls):
        parts = row_parts(x_ref.shape[0], cuts if x_ref.shape[0] >= 64 else 1)
        pieces += [(x_ref, x_all, part) for part in parts]
    pieces += [(q_ref, q_all, part) for part in row_parts(q_ref.shape[0], cuts)]
    last = len(pieces)
    pieces.append((kv_sum, kv_all, pl.ds(0, rows)))

    def hop(c, owner, s, device, out_sem, in_sem, first_hop):
        x_ref, o_ref, part = pieces[c]
        return pltpu.make_async_remote_copy(
            src_ref=x_ref.at[part] if first_hop else o_ref.at[owner, part],
            dst_ref=o_ref.at[owner, part],
            send_sem=out_sem.at[s, c],
            recv_sem=in_sem.at[s, c],
            device_id={"seq": device},
            device_id_type=MESH,
        )

    def ring(c, owner, s, first_hop=False):
        return hop(c, owner, s, following, ro, ri, first_hop)

    def side(c, owner, s, first_hop=False):
        return hop(c, owner, s, sibling, so, si, first_hop)

    for i in range(1, members):
        give(i).start()
    mine = pltpu.make_async_copy(kv_ref.at[pl.ds(place * rows, rows)], kv_sum, own_sem.at[0])
    mine.start()
    own = [
        pltpu.make_async_copy(src, dst.at[me], own_sem.at[n + 2])
        for n, (src, dst) in enumerate(zip((q_ref,) + x_refs, (q_all,) + x_alls))
    ]
    for c in range(last):
        ring(c, me, 0, True).start()
        side(c, me, 0, True).start()
    for copy in own:
        copy.start()
    mine.wait()
    total = kv_sum[...].astype(F32)
    for i in range(1, members):
        give(i).wait_recv()
        total = total + heap[i - 1].astype(F32)
    kv_sum[...] = total.astype(BF16)
    own_kv = pltpu.make_async_copy(kv_sum, kv_all.at[me], own_sem.at[1])
    own_kv.start()
    ring(last, me, 0, True).start()
    side(last, me, 0, True).start()
    for s in range(1, chips):
        owner = chip_of((position - s * step + chips) % chips, chips) * 2 + lane
        for c in range(last + 1):
            ring(c, owner, s - 1).wait_recv()
            if s < chips - 1:
                ring(c, owner, s).start()
            side(c, owner, s).start()
    for i in range(1, members):
        give(i).wait_send()
    for s in range(chips):
        for c in range(last + 1):
            side(c, me, s).wait()
            if s < chips - 1:
                ring(c, me, s).wait_send()
    for copy in own + [own_kv]:
        copy.wait()


def last_gather(qkv, extras, gcols, local, count, members, call, cuts=4):
    chips = count // 2
    rows = local // members
    columns = qkv.shape[1] - gcols
    pieces = cuts + 1 + sum(cuts if x.shape[0] >= 64 else 1 for x in extras)
    dma = pltpu.SemaphoreType.DMA
    return pl.pallas_call(
        functools.partial(last_gather_kernel, count, members, cuts, len(extras)),
        out_shape=[
            jax.ShapeDtypeStruct((count, qkv.shape[0], gcols), BF16),
            jax.ShapeDtypeStruct((count, rows, columns), BF16),
        ]
        + [jax.ShapeDtypeStruct((count,) + x.shape, BF16) for x in extras],
        in_specs=[VMEM] * (1 + len(extras)),
        out_specs=[ANY] * (2 + len(extras)),
        scratch_shapes=[
            pltpu.VMEM((members - 1, rows, columns), BF16),
            pltpu.VMEM((rows, columns), BF16),
            dma((3 + len(extras),)),
            dma((members - 1,)),
            dma((members - 1,)),
        ]
        + [dma((chips, pieces))] * 4,
        compiler_params=pltpu.CompilerParams(collective_id=call, has_side_effects=True),
    )(qkv, *extras)


def finish_kernel(
    count,
    kv_heads,
    tile,
    q_ref,
    kv_ref,
    wq_ref,
    wk_ref,
    wv_ref,
    gain_ref,
    out_ref,
    gate_ref,
    up_ref,
    down_ref,
    dq_ref,
    dk_ref,
    dv_ref,
    dg_ref,
    dout_ref,
    dgate_ref,
    dup_ref,
    ddown_ref,
):
    dout_ref[...] = out_ref[...].astype(F32)
    dgate_ref[...] = gate_ref[...].astype(F32)
    dup_ref[...] = up_ref[...].astype(F32)
    ddown_ref[...] = down_ref[...].astype(F32)
    chips = count // 2
    members = count // kv_heads
    width = q_ref.shape[2]
    hd = kv_ref.shape[2] // 2
    member = pl.program_id(0) * members // pl.num_programs(0)

    def place(group):
        return (group % chips) * 2 + group // chips

    total = jnp.zeros((tile, 1), F32)
    for g in range(count):
        cols = pl.ds(g * width, width)
        grad = q_ref[place(g)].astype(F32)
        dq_ref[:, cols] = grad
        total += jnp.sum(grad * wq_ref[:, cols].astype(F32), axis=1, keepdims=True)
    for j in range(kv_heads):
        cols = pl.ds(j * hd, hd)
        pair = kv_ref[place(j * members + member)].astype(F32)
        dk_ref[:, cols] = pair[:, :hd]
        dv_ref[:, cols] = pair[:, hd:]
        total += jnp.sum(pair[:, :hd] * wk_ref[:, cols].astype(F32), axis=1, keepdims=True)
        total += jnp.sum(pair[:, hd:] * wv_ref[:, cols].astype(F32), axis=1, keepdims=True)
    dg_ref[...] = total / gain_ref[...].astype(F32)


def finish(q_all, kv_all, w_query, key_weight, value_weight, gain, others, kv_heads):
    count = q_all.shape[0]
    local, columns = w_query.shape
    rows = kv_all.shape[1]
    tile = min(128, rows)
    per = rows // tile
    kv_columns = key_weight.shape[1]

    steps = local // tile

    def row_block(n, rows=tile):
        return pl.BlockSpec((rows, n), lambda r: (r, 0))

    other_blocks = [row_block(a.shape[1], a.shape[0] // steps) for a in others]

    return pl.pallas_call(
        functools.partial(finish_kernel, count, kv_heads, tile),
        grid=(local // tile,),
        out_shape=(
            jax.ShapeDtypeStruct((local, columns), F32),
            jax.ShapeDtypeStruct((local, kv_columns), F32),
            jax.ShapeDtypeStruct((local, kv_columns), F32),
            jax.ShapeDtypeStruct((local, 1), F32),
        )
        + tuple(jax.ShapeDtypeStruct(a.shape, F32) for a in others),
        in_specs=[
            pl.BlockSpec((count, tile, q_all.shape[2]), lambda r: (0, r, 0)),
            pl.BlockSpec((count, tile, kv_all.shape[2]), lambda r: (0, r % per, 0)),
            row_block(columns),
            row_block(kv_columns),
            row_block(kv_columns),
            row_block(1),
        ]
        + other_blocks,
        out_specs=[row_block(columns), row_block(kv_columns), row_block(kv_columns), row_block(1)]
        + other_blocks,
        compiler_params=pltpu.CompilerParams(vmem_limit_bytes=48 * MIB),
    )(q_all, kv_all, w_query, key_weight, value_weight, gain[:, None], *others)


def run_starts(segment):
    position = jnp.arange(segment.shape[0], dtype=jnp.int32)
    fresh = jnp.concatenate([jnp.ones((1,), dtype=bool), segment[1:] != segment[:-1]])
    return position, lax.cummax(jnp.where(fresh, position, jnp.zeros_like(position)), axis=0)


def angles(offset, head_size):
    half = head_size // 2
    lane = jnp.arange(head_size, dtype=jnp.int32)
    frequency = jnp.exp((lane % half).astype(F32) * (-2.0 * math.log(THETA) / head_size))
    early, late = offset.reshape(2, -1)
    phases = jnp.where(lane[None, :] < half, early[:, None], late[:, None]) * frequency[None, :]
    return jnp.cos(phases), jnp.sin(phases)


def per_device(
    activations,
    cotangent,
    segments,
    routing,
    attn_gain,
    mlp_gain,
    query_gain,
    key_gain,
    w_query,
    key_weight,
    value_weight,
    w_out,
    w_router,
    w_gate,
    w_up,
    w_down,
):
    count = lax.axis_size("seq")
    shards = lax.axis_size("fsdp")
    me = lax.axis_index("seq")
    chips = count // 2
    x = activations[0].astype(F32)
    dy = cotangent[0]
    segment = segments[0]
    routes = routing[0]
    tok, dim = x.shape
    span = segment.shape[0]
    top = routes.shape[1]
    hd = query_gain.shape[0] * shards
    heads = w_query.shape[1] // hd
    kv_heads = key_weight.shape[1] // hd
    share = heads // count
    experts = w_router.shape[1]
    local_rows = w_out.shape[0]
    capacity = tok * top * 9 // (8 * experts)
    gcols = share * hd

    local_dim = attn_gain.shape[0]
    local_hd = query_gain.shape[0]
    head_gains = jnp.concatenate([query_gain, key_gain], axis=0)
    head_gains = jnp.pad(head_gains, (0, -head_gains.shape[0] % 128))
    small = jnp.concatenate(
        [v.astype(F32).reshape(-1, 128) for v in (attn_gain, mlp_gain, head_gains)], axis=0
    )
    small = jnp.pad(small, ((0, -small.shape[0] % 8), (0, 0)))
    ffe = w_down.shape[1]
    down_rows = ffe // 3 // 16 * 16
    h1_all, qkv, w_qkv, w_o, small, router, wd1 = front(
        activations[0],
        small,
        w_router.T,
        w_query,
        key_weight,
        value_weight,
        w_out,
        w_down[0],
        down_rows,
        hd,
        count,
        shards,
        1,
    )
    gain_rows = local_dim // 128
    g_attn = small[:, :gain_rows].reshape(-1)
    g_mlp = small[:, gain_rows : 2 * gain_rows].reshape(-1)
    g_query = small[:, 2 * gain_rows, :local_hd].reshape(-1)
    g_key = small[:, 2 * gain_rows, local_hd : 2 * local_hd].reshape(-1)
    r1 = lax.rsqrt(jnp.mean(x * x, axis=-1, keepdims=True) + EPSILON)
    position, doc_start = run_starts(segment)
    cos_full, sin_full = angles((position - doc_start).astype(F32), hd)
    start = jnp.where(segment > 0, doc_start, position)

    routes_sent = jnp.pad(routes.T, ((0, -top % 16), (0, 0))).astype(BF16)
    dy_all, routes_all, o, qx, kn, wg, wd2 = attend(
        dy,
        routes_sent,
        qkv,
        g_query,
        g_key,
        cos_full,
        sin_full,
        start,
        w_gate[0],
        w_down[0],
        down_rows,
        count,
        shards,
        4,
    )
    wholes = (
        whole_of(w_up[0], 0, shards),
        jax.ShapeDtypeStruct((ffe - 2 * down_rows, dim), BF16),
    )
    x2, wu, wd3 = product_scattered(
        o, w_o, NN, [w_up[0], w_down[0]], (0, 1), wholes, count, shards, 2
    )
    x2 = x + x2

    r2 = lax.rsqrt(jnp.mean(x2 * x2, axis=-1, keepdims=True) + EPSILON)
    h2 = (x2 * r2 * g_mlp).astype(BF16)
    def gates_of(hidden, chosen):
        logits = mm(hidden, router, NT)
        return jax.nn.softmax(jnp.where(chosen, logits, -1e30), axis=-1) * chosen

    def chosen_of(named):
        names = jnp.arange(experts, dtype=jnp.int32)
        return jnp.any(named[..., :, None] == names, axis=-2)

    routes_all = jnp.swapaxes(routes_all[:, :top].astype(jnp.int32), 1, 2)
    hit = jnp.any(routes_all == me, axis=-1)
    rank = jnp.cumsum(hit.astype(jnp.int32), axis=1) - hit
    slot = jnp.where(hit & (rank < capacity), rank, -1)
    chosen_all = chosen_of(routes_all.reshape(span, top)).astype(BF16)
    xs, de, dx0, dl, ce, hid, dgu = expert_gathered(
        h2,
        slot,
        chosen_all,
        router,
        dy_all,
        (wg, wu, wd1, wd2, wd3, w_gate[0], w_up[0], w_down[0]),
        capacity,
        count,
        shards,
        3,
    )
    dh2_wide, w_gate_part = slots_back(
        slot, dl, dx0, xs, dgu, (wg, wu, w_gate[0], w_up[0]), capacity, count, shards, 6
    )
    dgate = dh2_wide[:, dim : dim + experts] + dh2_wide[:, dim + 64 : dim + 64 + experts]
    gates = gates_of(h2, chosen_of(routes))
    dlogits = (gates * (dgate - jnp.sum(gates * dgate, axis=-1, keepdims=True))).astype(BF16)
    dh2 = dh2_wide[:, :dim] + mm(dlogits, router)
    router_part = mm(dlogits, h2, TN)
    xh = x2 * r2
    mlp_gain_part = jnp.sum(dh2 * xh, axis=0)
    dn = dh2 * g_mlp
    dx2 = dy.astype(F32) + r2 * (dn - xh * jnp.mean(dn * xh, axis=-1, keepdims=True))

    do, w_out_part, w_down_part, w_up_part = out_back(
        dx2.astype(BF16), w_o, o, hid, de, xs, dgu, count, 7
    )
    dqkv, head_gains, mixed, out_half = attend_back(
        qx,
        kn,
        qkv,
        o,
        do,
        g_query,
        g_key,
        cos_full,
        sin_full,
        start,
        slot,
        w_out_part,
        ce,
        capacity,
        count,
        shards,
        5,
    )
    mixed = x2 + mixed
    dh1, qkv_sum = token_back(dqkv, w_qkv, head_gains, h1_all, count, shards, 8)
    xh1 = x * r1
    dn1 = dh1 * g_attn
    input_grad = dx2 + r1 * (dn1 - xh1 * jnp.mean(dn1 * xh1, axis=-1, keepdims=True))

    def sum_fsdp(part, axis):
        return lax.psum_scatter(part.astype(BF16), "fsdp", scatter_dimension=axis, tiled=True)

    w_gate_sum = sum_fsdp(w_gate_part, 0)
    w_up_sum = sum_fsdp(w_up_part, 0)
    w_down_later, _ = lax.optimization_barrier((w_down_part, qkv_sum))
    w_down_sum = sum_fsdp(w_down_later, 1)

    small_part = jnp.concatenate([router_part, mlp_gain_part[None]], axis=0)
    small_part = jnp.pad(small_part, ((0, -small_part.shape[0] % 16), (0, 0)))
    small_sum = sum_fsdp(small_part, 1)
    extras = [out_half, small_sum] if shards == 2 else []
    q_all, kv_all, *rows_all = last_gather(
        qkv_sum, extras, gcols, local_dim, count, count // kv_heads, 10
    )
    if shards == 2:
        out_all, small_all = rows_all
        out_all = out_all.reshape(local_rows, dim)
    else:
        out_all, small_all = out_rows(w_out_part, small_sum, count)
    small_total = jnp.sum(small_all.astype(F32), axis=0)
    router_grad = small_total[:experts].T
    mlp_gain_grad = small_total[experts]
    (
        w_query_grad,
        w_key_grad,
        w_value_grad,
        attn_gain_grad,
        w_out_grad,
        w_gate_grad,
        w_up_grad,
        w_down_grad,
    ) = finish(
        q_all,
        kv_all,
        w_query,
        key_weight,
        value_weight,
        attn_gain,
        (out_all, w_gate_sum, w_up_sum, w_down_sum),
        kv_heads,
    )
    attn_gain_grad = attn_gain_grad[:, 0]
    head_gain_grads = jnp.sum(q_all[:, local_dim, : 2 * hd].astype(F32), axis=0)
    own_half = lax.axis_index("fsdp") * local_hd
    query_gain_grad = lax.dynamic_slice_in_dim(head_gain_grads[:hd], own_half, local_hd)
    key_gain_grad = lax.dynamic_slice_in_dim(head_gain_grads[hd:], own_half, local_hd)
    return (
        mixed.astype(BF16)[None],
        input_grad[None],
        attn_gain_grad,
        mlp_gain_grad,
        query_gain_grad,
        key_gain_grad,
        w_query_grad,
        w_key_grad,
        w_value_grad,
        w_out_grad,
        router_grad,
        w_gate_grad[None],
        w_up_grad[None],
        w_down_grad[None],
    )


def out_rows(part, small_sum, count):
    chips = count // 2
    gcols, dim = part.shape
    me = lax.axis_index("seq")
    group = (me % 2) * chips + me // 2
    blank = jnp.zeros((count * gcols, dim), BF16)
    placed = lax.dynamic_update_slice(blank, part, (group * gcols, 0))
    mine = lax.psum_scatter(placed, "fsdp", scatter_dimension=0, tiled=True)
    return lax.psum(mine, "seq"), lax.all_gather(small_sum, "seq", axis=0, tiled=False)


def solution(mesh):
    tokens = P("fsdp", "seq", None)
    rows = P("fsdp", None)
    vector = P("fsdp")
    expert_rows = P("seq", "fsdp", None)
    expert_columns = P("seq", None, "fsdp")
    return jax.shard_map(
        per_device,
        mesh=mesh,
        in_specs=(tokens, tokens, rows, tokens)
        + (vector,) * 4
        + (rows,) * 5
        + (expert_rows, expert_rows, expert_columns),
        out_specs=(tokens, tokens)
        + (vector,) * 4
        + (rows,) * 5
        + (expert_rows, expert_rows, expert_columns),
        check_vma=False,
    )
```

```python
import functools
import math

import jax
import jax.numpy as jnp
from jax import lax
from jax.experimental import pallas as pl
from jax.experimental.pallas import tpu as pltpu
from jax.sharding import PartitionSpec as P

EPSILON = 1e-06
THETA = 1000000.0
BF16 = jnp.bfloat16
F32 = jnp.float32
MESH = pl.DeviceIdType.MESH
MIB = 1 << 20
LOG2E = math.log2(math.e)


def ring_of(chip, chips):
    return (chip % 2) * (chips - 1 - chip // 2) + (1 - chip % 2) * (chip // 2)


def chip_of(position, chips):
    upper = position // (chips // 2)
    return (1 - upper) * (2 * position) + upper * (2 * (chips - 1 - position) + 1)


def places(count):
    me = lax.axis_index("seq")
    chips = count // 2
    lane = me % 2
    position = ring_of(me // 2, chips)
    step = 1 - 2 * lane
    following = chip_of((position + step + chips) % chips, chips) * 2 + lane
    previous = chip_of((position - step + chips) % chips, chips) * 2 + lane
    sibling = me + 1 - 2 * lane
    return me, chips, lane, position, step, following, previous, sibling


def greet(places_over_seq, shards=1, more=0):
    barrier = pltpu.get_barrier_semaphore()
    for device in places_over_seq:
        pl.semaphore_signal(barrier, inc=1, device_id={"seq": device}, device_id_type=MESH)
    for i in range(1, shards):
        peer = (lax.axis_index("fsdp") + i) % shards
        pl.semaphore_signal(barrier, inc=1, device_id={"fsdp": peer}, device_id_type=MESH)
    pl.semaphore_wait(barrier, len(places_over_seq) + shards - 1 + more)


def crossing(shards, items, out_sems, in_sems, own_sems=None):
    mine = lax.axis_index("fsdp")

    def place(src, dst, axis):
        if axis is None:
            return dst.at[mine]
        size = src.shape[axis]
        part = pl.ds(pl.multiple_of(mine * size, 128 if axis else 16), size)
        return dst.at[:, part] if axis else dst.at[part]

    def own(n):
        src, dst, axis = items[n]
        return pltpu.make_async_copy(src, place(src, dst, axis), own_sems.at[n])

    def send(n, i):
        src, dst, axis = items[n]
        return pltpu.make_async_remote_copy(
            src_ref=src,
            dst_ref=place(src, dst, axis),
            send_sem=out_sems.at[n, i - 1],
            recv_sem=in_sems.at[n, i - 1],
            device_id={"fsdp": (mine + i) % shards},
            device_id_type=MESH,
        )

    def start(n):
        for i in range(1, shards):
            send(n, i).start()
        if own_sems is not None:
            own(n).start()

    def wait(n):
        for i in range(1, shards):
            send(n, i).wait()
        if own_sems is not None:
            own(n).wait()

    return start, wait


def crossing_scratch(shards, items):
    dma = pltpu.SemaphoreType.DMA
    return [dma((items, max(1, shards - 1))), dma((items, max(1, shards - 1)))]


def spread_units(units, steps):
    total = sum(weight for weight, _ in units)
    plan = [[] for _ in range(steps)]
    done = 0.0
    for weight, run in units:
        plan[min(steps - 1, int((done + weight / 2) * steps / total))].append(run)
        done += weight
    return plan


def run_units(plan, k):
    for step, units in enumerate(plan):
        if units:

            @pl.when(k == step)
            def _(units=units):
                for run in units:
                    run()


def row_parts(rows, cuts):
    if cuts == 1:
        return [pl.ds(0, rows)]
    size = rows // cuts // 16 * 16
    return [pl.ds(c * size, size) for c in range(cuts - 1)] + [
        pl.ds((cuts - 1) * size, rows - (cuts - 1) * size)
    ]


NT = (((1,), (1,)), ((), ()))
TN = (((0,), (0,)), ((), ()))
NN = (((1,), (0,)), ((), ()))


def mm(a, b, dims=NN):
    return lax.dot_general(a, b, dims, preferred_element_type=F32)


def gather_steps(count, cuts, x_ref, land, sems, use, shards=1, begin=None, tag=None):
    me, chips, lane, position, step, following, previous, sibling = places(count)
    ring_out, ring_in, side_out, side_in = sems
    block = x_ref.shape[0]
    rows = block // cuts
    pieces = cuts + (tag is not None)
    greet((previous, sibling), shards)

    def ring(s, c):
        part = pl.ds(c * rows, rows)
        return pltpu.make_async_remote_copy(
            src_ref=tag.at[s, 0] if c == cuts else land.at[s, part],
            dst_ref=tag.at[s + 1, 0] if c == cuts else land.at[s + 1, part],
            send_sem=ring_out.at[s, c],
            recv_sem=ring_in.at[s, c],
            device_id={"seq": following},
            device_id_type=MESH,
        )

    def side(s, c):
        return pltpu.make_async_remote_copy(
            src_ref=tag.at[s, 0] if c == cuts else land.at[s, pl.ds(c * rows, rows)],
            dst_ref=tag.at[s, 1] if c == cuts else land.at[s, pl.ds(block + c * rows, rows)],
            send_sem=side_out.at[s, c],
            recv_sem=side_in.at[s, c],
            device_id={"seq": sibling},
            device_id_type=MESH,
        )

    def forward(s, c):
        @pl.when(s < chips - 1)
        def _():
            ring(s, c).start()

        side(s, c).start()

    land[0, :block] = x_ref[...]
    for c in range(pieces):
        forward(0, c)
    if begin is not None:
        begin()

    def one(s, carry):
        def pump(c):
            @pl.when(s < chips - 1)
            def _():
                ring(s, c).wait_recv()
                forward(s + 1, c)

        for c in range(pieces):
            side(s, c).wait_recv()
        use(s, *pair_owners(count, s), pump)
        return carry

    lax.fori_loop(0, chips, one, 0)

    def close(s, carry):
        for c in range(pieces):
            side(s, c).wait_send()

            @pl.when(s < chips - 1)
            def _():
                ring(s, c).wait_send()

        return carry

    lax.fori_loop(0, chips, close, 0)


def pair_owners(count, s):
    _, chips, lane, position, step, _, _, _ = places(count)
    first = chip_of((position - s * step + chips) % chips, chips) * 2 + lane
    second = chip_of((position + s * step + chips) % chips, chips) * 2 + 1 - lane
    return first, second


def at_block(owner, block):
    return pl.ds(pl.multiple_of(owner * block, block), block)


def gather_scratch(count, pieces, block, columns):
    chips = count // 2
    return [pltpu.VMEM((chips, 2 * block, columns), BF16)] + [
        pltpu.SemaphoreType.DMA((chips, pieces))
    ] * 4


def scatter_steps(count, cuts, o_ref, bufs, sems, produce, extra=None, shards=1, begin=None, meeting=None):
    me, chips, lane, position, step, following, previous, sibling = places(count)
    own, sent, came, give, given = bufs
    ring_out, ring_in, side_out, side_in = sems
    rows = own.shape[1] // cuts
    if meeting is None:
        greet((previous, sibling), shards)
    else:
        meeting[0]()
        greet((previous, sibling), shards, meeting[1])
    if begin is not None:
        begin()

    def ring(k, c):
        part = pl.ds(c * rows, rows)
        return pltpu.make_async_remote_copy(
            src_ref=sent.at[k, part],
            dst_ref=came.at[k, part],
            send_sem=ring_out.at[k, c],
            recv_sem=ring_in.at[k, c],
            device_id={"seq": following},
            device_id_type=MESH,
        )

    def side(k):
        return pltpu.make_async_remote_copy(
            src_ref=give.at[k],
            dst_ref=given.at[k],
            send_sem=side_out.at[k],
            recv_sem=side_in.at[k],
            device_id={"seq": sibling},
            device_id_type=MESH,
        )

    def make(k):
        mine, theirs = produce(k, *pair_owners(count, (k + 1) % chips))
        give[k] = theirs.astype(BF16)
        side(k).start()
        own[k % 2] = mine

    make(0)

    def one(k, carry):
        side(k).wait_recv()
        for c in range(cuts):
            part = pl.ds(c * rows, rows)

            @pl.when(k > 0)
            def _():
                ring(k - 1, c).wait_recv()
                own[k % 2, part] += came[k - 1, part].astype(F32)

            total = own[k % 2, part] + given[k, part].astype(F32)

            @pl.when(k < chips - 1)
            def _():
                sent[k, part] = total.astype(BF16)
                ring(k, c).start()

            @pl.when(k == chips - 1)
            def _():
                o_ref[part] = total

            if c == 0:

                @pl.when(k < chips - 1)
                def _():
                    make(k + 1)

        if extra is not None:
            extra(k)
        return carry

    lax.fori_loop(0, chips, one, 0)

    def close(k, carry):
        side(k).wait_send()

        @pl.when(k < chips - 1)
        def _():
            for c in range(cuts):
                ring(k, c).wait_send()

        return carry

    lax.fori_loop(0, chips, close, 0)


def scatter_scratch(count, cuts, rows, columns):
    chips = count // 2
    dma = pltpu.SemaphoreType.DMA
    return [
        pltpu.VMEM((2, rows, columns), F32),
        pltpu.VMEM((chips - 1, rows, columns), BF16),
        pltpu.VMEM((chips - 1, rows, columns), BF16),
        pltpu.VMEM((chips, rows, columns), BF16),
        pltpu.VMEM((chips, rows, columns), BF16),
        dma((chips, cuts)),
        dma((chips, cuts)),
        dma((chips,)),
        dma((chips,)),
    ]


def remote_params(call, mib):
    return pltpu.CompilerParams(
        collective_id=call, has_side_effects=True, vmem_limit_bytes=mib * MIB
    )


VMEM = pl.BlockSpec(memory_space=pltpu.VMEM)
ANY = pl.BlockSpec(memory_space=pl.ANY)


def front_kernel(
    count,
    shards,
    cuts,
    widths,
    x_ref,
    small_ref,
    wr_ref,
    wq_ref,
    wk_ref,
    wv_ref,
    wo_ref,
    wd_ref,
    h_all,
    qkv_ref,
    w_ref,
    wo_all,
    small_all,
    wr_all,
    wd_all,
    land,
    ring_out,
    ring_in,
    side_out,
    side_in,
    x_out,
    x_in,
    x_own,
    d_out,
    d_in,
    h1,
    gain,
    h_sem,
    o_out,
    o_in,
    o_own,
):
    block, dim = x_ref.shape
    chips = count // 2
    gcols, hd, members = widths
    local = wq_ref.shape[0]
    me = lax.axis_index("seq")
    mine = lax.axis_index("fsdp")
    group = (me % 2) * chips + me // 2
    kv_cols = pl.ds(pl.multiple_of(group // members * hd, 128), hd)
    q_cols = pl.ds(pl.multiple_of(group * gcols, 128), gcols)
    items = [
        (small_ref, small_all, None),
        (wq_ref.at[:, q_cols], w_ref.at[:, pl.ds(0, gcols)], 0),
        (wk_ref.at[:, kv_cols], w_ref.at[:, pl.ds(gcols, hd)], 0),
        (wv_ref.at[:, kv_cols], w_ref.at[:, pl.ds(gcols + hd, hd)], 0),
        (wr_ref, wr_all, 1),
    ]
    start, wait = crossing(shards, items, x_out, x_in, x_own)
    start_down, wait_down = crossing(
        shards, [(wd_ref.at[pl.ds(0, wd_all.shape[0])], wd_all, 1)], d_out, d_in
    )
    owner = group * gcols // wo_ref.shape[0]
    wo_src = wo_ref.at[pl.ds(pl.multiple_of(group * gcols % wo_ref.shape[0], 16), gcols)]
    wo_own = pltpu.make_async_copy(wo_src, wo_all, o_own)

    def wo_send(i):
        return pltpu.make_async_remote_copy(
            src_ref=wo_src,
            dst_ref=wo_all,
            send_sem=o_out.at[i - 1],
            recv_sem=o_in,
            device_id={"fsdp": (mine + i) % shards},
            device_id_type=MESH,
        )

    def begin():
        for n in range(len(items)):
            start(n)

        @pl.when(mine == owner)
        def _():
            wo_own.start()
            for i in range(1, shards):
                wo_send(i).start()

        start_down(0)

    def h_copy(s, holder, half):
        return pltpu.make_async_copy(
            h1.at[s, pl.ds(half * block, block)], h_all.at[at_block(holder, block)], h_sem.at[half]
        )

    def multiply(p):
        first, second = pair_owners(count, p)
        y = mm(h1[p], w_ref[...]).astype(BF16)
        qkv_ref[at_block(first, block), :] = y[:block]
        qkv_ref[at_block(second, block), :] = y[block:]

    def use(s, first, second, pump):
        @pl.when(s == 0)
        def _():
            wait(0)
            for f in range(shards):
                for r in range(local // 128):
                    gain[:, pl.ds(f * local + r * 128, 128)] = small_all[f, r : r + 1, :]

        x = land[s].astype(F32)
        r1 = lax.rsqrt(jnp.mean(x * x, axis=1, keepdims=True) + EPSILON)
        h1[s] = (x * r1 * gain[...]).astype(BF16)
        h_copy(s, first, 0).start()
        h_copy(s, second, 1).start()
        pump(0)

        @pl.when(s == chips // 2)
        def _():
            for n in range(1, len(items)):
                wait(n)

        @pl.when(s >= chips // 2)
        def _():
            multiply(2 * s - chips)
            pump(1)
            multiply(2 * s - chips + 1)

        @pl.when(s < chips // 2)
        def _():
            pump(1)

        for c in range(2, cuts):
            pump(c)

    gather_steps(
        count, cuts, x_ref, land, (ring_out, ring_in, side_out, side_in), use, shards, begin
    )

    @pl.when(mine == owner)
    def _():
        wo_own.wait()
        for i in range(1, shards):
            wo_send(i).wait_send()

    @pl.when(mine != owner)
    def _():
        wo_send(1).wait_recv()

    wait_down(0)
    half_rows = count * block // 2
    for half in range(2):
        pltpu.make_async_copy(
            h_all.at[pl.ds(0, half_rows)], h_all.at[pl.ds(0, half_rows)], h_sem.at[half]
        ).wait()


def front(
    x,
    small,
    w_router,
    w_query,
    key_weight,
    value_weight,
    w_out,
    w_down,
    down_rows,
    hd,
    count,
    shards,
    call,
    cuts=4,
):
    block, dim = x.shape
    gcols = w_query.shape[1] // count
    members = count * hd // key_weight.shape[1]
    columns = gcols + 2 * hd
    chips = count // 2
    dma = pltpu.SemaphoreType.DMA
    return pl.pallas_call(
        functools.partial(front_kernel, count, shards, cuts, (gcols, hd, members)),
        out_shape=(
            jax.ShapeDtypeStruct((count * block, dim), BF16),
            jax.ShapeDtypeStruct((count * block, columns), BF16),
            jax.ShapeDtypeStruct((dim, columns), BF16),
            jax.ShapeDtypeStruct((gcols, w_out.shape[1]), BF16),
            jax.ShapeDtypeStruct((shards,) + small.shape, F32),
            whole_of(w_router, 1, shards),
            jax.ShapeDtypeStruct((down_rows, dim), BF16),
        ),
        in_specs=[VMEM, VMEM, VMEM] + [ANY] * 5,
        out_specs=[ANY, VMEM, VMEM, VMEM, VMEM, VMEM, ANY],
        scratch_shapes=gather_scratch(count, cuts, block, dim)
        + crossing_scratch(shards, 5)
        + [
            dma((5,)),
        ]
        + crossing_scratch(shards, 1)
        + [
            pltpu.VMEM((chips, 2 * block, dim), BF16),
            pltpu.VMEM((1, dim), F32),
            dma((2,)),
            dma((max(1, shards - 1),)),
            dma,
            dma,
        ],
        compiler_params=remote_params(call, 48),
    )(x, small, w_router, w_query, key_weight, value_weight, w_out, w_down)


def out_back_kernel(
    count,
    cuts,
    da_ref,
    w_ref,
    o_ref,
    hid_ref,
    de_ref,
    xs_ref,
    dgu_ref,
    do_ref,
    part_ref,
    down_out,
    up_out,
    land,
    *rest,
):
    sems = rest[:4]
    total, hid, du, de, xs, down_ref, up_ref, sem, tile_sem, store_sem = rest[4:]
    block = da_ref.shape[0]
    columns = de.shape[2]
    ffe = hid.shape[1]
    total[...] = jnp.zeros_like(total)
    loads = [
        pltpu.make_async_copy(hid_ref, hid, sem.at[0]),
        pltpu.make_async_copy(dgu_ref.at[:, pl.ds(ffe, ffe)], du, sem.at[1]),
    ]

    def tiles(s):
        part = pl.ds(pl.multiple_of(s * columns, 128), columns)
        return [
            pltpu.make_async_copy(src.at[:, part], dst.at[s % 2], tile_sem.at[s % 2, n])
            for n, (src, dst) in enumerate(((de_ref, de), (xs_ref, xs)))
        ]

    def begin():
        for load in loads + tiles(0):
            load.start()

    def use(s, first, second, pump):
        @pl.when(s == 0)
        def _():
            for load in loads:
                load.wait()

        @pl.when(s < count // 2 - 1)
        def _():
            for load in tiles(s + 1):
                load.start()

        pair = land[s]
        a = at_block(first, block)
        b = at_block(second, block)
        do = mm(pair, w_ref[...], NT).astype(BF16)
        do_ref[a, :] = do[:block]
        do_ref[b, :] = do[block:]
        pump(0)
        total[...] += mm(jnp.concatenate([o_ref[a, :], o_ref[b, :]], axis=0), pair, TN)
        pump(1)
        for load in tiles(s):
            load.wait()
        part = pl.ds(pl.multiple_of(s * columns, 128), columns)
        down_ref[:, part] = mm(hid[...], de[s % 2], TN).astype(BF16)
        pump(2)
        rows = pl.ds(pl.multiple_of(s * columns, 16), columns)
        up_ref[rows, :] = mm(xs[s % 2], du[...], TN).astype(BF16)
        pltpu.make_async_copy(down_ref.at[:, part], down_out.at[:, part], store_sem.at[0]).start()
        pltpu.make_async_copy(up_ref.at[rows], up_out.at[rows], store_sem.at[1]).start()
        for c in range(3, cuts):
            pump(c)

    gather_steps(count, cuts, da_ref, land, sems, use, 1, begin)
    part_ref[...] = total[...].astype(BF16)
    pltpu.make_async_copy(down_ref, down_out, store_sem.at[0]).wait()
    pltpu.make_async_copy(up_ref, up_out, store_sem.at[1]).wait()


def out_back(da, w, o, hid, de, xs, dgu, count, call, cuts=4):
    block, dim = da.shape
    ffe = hid.shape[1]
    chips = count // 2
    dma = pltpu.SemaphoreType.DMA
    return pl.pallas_call(
        functools.partial(out_back_kernel, count, cuts),
        out_shape=(
            jax.ShapeDtypeStruct(o.shape, BF16),
            jax.ShapeDtypeStruct(w.shape, BF16),
            jax.ShapeDtypeStruct((ffe, dim), BF16),
            jax.ShapeDtypeStruct((dim, ffe), BF16),
        ),
        in_specs=[VMEM] * 3 + [ANY] * 4,
        out_specs=[VMEM] * 2 + [ANY] * 2,
        scratch_shapes=gather_scratch(count, cuts, block, dim)
        + [
            pltpu.VMEM(w.shape, F32),
            pltpu.VMEM(hid.shape, BF16),
            pltpu.VMEM(hid.shape, BF16),
            pltpu.VMEM((2, de.shape[0], dim // chips), BF16),
            pltpu.VMEM((2, xs.shape[0], dim // chips), BF16),
            pltpu.VMEM((ffe, dim), BF16),
            pltpu.VMEM((dim, ffe), BF16),
            dma((2,)),
            dma((2, 2)),
            dma((2,)),
        ],
        compiler_params=remote_params(call, 56),
    )(da, w, o, hid, de, xs, dgu)


def product_kernel(count, shards, cuts, dims, axes, y_ref, w_ref, *refs):
    cargo = len(axes)
    srcs, o_ref, dsts = refs[:cargo], refs[cargo], refs[cargo + 1 : 2 * cargo + 1]
    rest = refs[2 * cargo + 1 :]
    block = o_ref.shape[0]
    if cargo:
        lasts = []
        for src, dst, axis in zip(srcs, dsts, axes):
            rows = dst.shape[0] if axis else src.shape[0]
            lasts.append((src.at[pl.ds(src.shape[0] - rows, rows)], dst, axis))
        start, wait = crossing(shards, lasts, *rest[9:])

    def begin():
        for n in range(cargo):
            start(n)

    def produce(k, first, second):
        a = y_ref[at_block(first, block), :]
        b = y_ref[at_block(second, block), :]
        both = mm(jnp.concatenate([a, b], axis=0), w_ref[...], dims)
        return both[:block], both[block:]

    scatter_steps(
        count, cuts, o_ref, rest[:5], rest[5:9], produce, None, shards if cargo else 1, begin
    )
    for n in range(cargo):
        wait(n)


def token_back_kernel(
    count,
    shards,
    cuts,
    y_ref,
    w_ref,
    gains_ref,
    h_ref,
    o_ref,
    sum_ref,
    *rest,
):
    chips = count // 2
    block = o_ref.shape[0]
    hbuf, grad, came, gains, h_sem, w_out, w_in, g_out, g_in = rest[9:]
    mine = lax.axis_index("fsdp")
    dim, columns = grad.shape
    local = dim // shards
    part = dim // chips
    per = local // part
    width = gains_ref.shape[1]

    def chunk(k):
        return (k + (mine + 1) % shards * per) % chips

    def load(k):
        cols = pl.ds(pl.multiple_of(chunk(k) * part, 128), part)
        return pltpu.make_async_copy(h_ref.at[:, cols], hbuf.at[k % 2], h_sem.at[k % 2])

    def send(k):
        n = chunk(k)
        owner = n // per
        slot = (owner - mine + shards) % shards - 1
        return pltpu.make_async_remote_copy(
            src_ref=grad.at[pl.ds(pl.multiple_of(n * part, 16), part)],
            dst_ref=came.at[slot, pl.ds(pl.multiple_of(n % per * part, 16), part)],
            send_sem=w_out.at[k],
            recv_sem=w_in.at[slot, n % per],
            device_id={"fsdp": owner},
            device_id_type=MESH,
        )

    def send_gains(i):
        return pltpu.make_async_remote_copy(
            src_ref=gains_ref,
            dst_ref=gains.at[i - 1],
            send_sem=g_out.at[i - 1],
            recv_sem=g_in.at[i - 1],
            device_id={"fsdp": (mine + i) % shards},
            device_id_type=MESH,
        )

    def begin():
        load(0).start()
        for i in range(1, shards):
            send_gains(i).start()

    def produce(k, first, second):
        a = y_ref[at_block(first, block), :]
        b = y_ref[at_block(second, block), :]
        both = mm(jnp.concatenate([a, b], axis=0), w_ref[...], NT)
        return both[:block], both[block:]

    def extra(k):
        load(k).wait()

        @pl.when(k < chips - 1)
        def _():
            load(k + 1).start()

        rows = pl.ds(pl.multiple_of(chunk(k) * part, 16), part)
        grad[rows, :] = mm(hbuf[k % 2], y_ref[...], TN).astype(BF16)

        @pl.when(k < chips - per)
        def _():
            send(k).start()

    scatter_steps(count, cuts, o_ref, rest[:5], rest[5:9], produce, extra, shards, begin)
    total = gains_ref[...]
    for i in range(1, shards):
        send_gains(i).wait()
        total = total + gains[i - 1]
    row = lax.broadcasted_iota(jnp.int32, (16, width), 0)
    sum_ref[pl.ds(local, 16), :] = jnp.zeros((16, columns), BF16)
    for n in range(2):
        sum_ref[pl.ds(local, 16), pl.ds(n * width, width)] = jnp.where(
            row == 0, jnp.broadcast_to(total[n : n + 1, :], (16, width)), 0.0
        ).astype(BF16)
    for k in range(chips - per):
        send(k).wait_send()
    for n in range(per):
        part_rows = pl.ds(n * part, part)
        own = grad[pl.ds(pl.multiple_of(mine * local + n * part, 16), part), :].astype(F32)
        for i in range(1, shards):
            pltpu.make_async_remote_copy(
                src_ref=grad.at[part_rows],
                dst_ref=came.at[i - 1, part_rows],
                send_sem=w_out.at[0],
                recv_sem=w_in.at[i - 1, n],
                device_id={"fsdp": (mine + i) % shards},
                device_id_type=MESH,
            ).wait_recv()
            own = own + came[i - 1, part_rows, :].astype(F32)
        sum_ref[part_rows, :] = own.astype(BF16)


def token_back(y, w, gains, h_all, count, shards, call, cuts=2):
    block = y.shape[0] // count
    dim, columns = w.shape
    chips = count // 2
    local = dim // shards
    others = max(1, shards - 1)
    dma = pltpu.SemaphoreType.DMA
    return pl.pallas_call(
        functools.partial(token_back_kernel, count, shards, cuts),
        out_shape=(
            jax.ShapeDtypeStruct((block, dim), F32),
            jax.ShapeDtypeStruct((local + 16, columns), BF16),
        ),
        in_specs=[VMEM] * 3 + [ANY],
        out_specs=[VMEM] * 2,
        scratch_shapes=scatter_scratch(count, cuts, block, dim)
        + [
            pltpu.VMEM((2, h_all.shape[0], dim // chips), BF16),
            pltpu.VMEM((dim, columns), BF16),
            pltpu.VMEM((others, local, columns), BF16),
            pltpu.VMEM((others,) + gains.shape, F32),
            dma((2,)),
            dma((chips,)),
            dma((others, chips // shards)),
            dma((others,)),
            dma((others,)),
        ],
        compiler_params=remote_params(call, 48),
    )(y, w, gains, h_all)


def whole_of(part, axis, shards):
    shape = list(part.shape)
    shape[axis] *= shards
    return jax.ShapeDtypeStruct(tuple(shape), part.dtype)


def product_scattered(y, w, dims, cargo, axes, wholes, count, shards, call, cuts=2):
    block = y.shape[0] // count
    columns = w.shape[1 - dims[0][1][0]]
    return pl.pallas_call(
        functools.partial(product_kernel, count, shards, cuts, dims, axes),
        out_shape=[jax.ShapeDtypeStruct((block, columns), F32)]
        + list(wholes),
        in_specs=[VMEM, VMEM] + [ANY] * len(cargo),
        out_specs=[VMEM] + [ANY] * len(cargo),
        scratch_shapes=scatter_scratch(count, cuts, block, columns)
        + (crossing_scratch(shards, len(cargo)) if cargo else []),
        compiler_params=remote_params(call, 48),
    )(y, w, *cargo)


def one_hot_of(slot_ref, first, second, capacity):
    a = slot_ref[pl.ds(first, 1), :]
    b = slot_ref[pl.ds(second, 1), :]
    wanted = jnp.concatenate([a, jnp.where(b >= 0, b + capacity, -1)], axis=1)
    row = lax.broadcasted_iota(jnp.int32, (2 * capacity, wanted.shape[1]), 0)
    return jnp.where(row == wanted, 1.0, 0.0).astype(BF16)


def parts_of_own(i, shards, size, unit):
    place = (lax.axis_index("fsdp") + i) % shards
    return pl.ds(pl.multiple_of(place * (size // shards), unit), size // shards)


def gate_up_parts(i, shards, whole, own, wgu):
    rows = parts_of_own(i, shards, wgu.shape[0], 16)
    ffe = wgu.shape[1] // 2
    return [
        (whole[n].at[rows] if i else own[n], wgu.at[rows, pl.ds(n * ffe, ffe)]) for n in range(2)
    ]


def down_parts(i, shards, pieces, own, wd):
    columns = parts_of_own(i, shards, wd.shape[1], 128)
    parts = []
    first = 0
    for piece in pieces:
        rows = pl.ds(first, piece.shape[0])
        first += piece.shape[0]
        parts.append((piece.at[:, columns] if i else own.at[rows], wd.at[rows, columns]))
    return parts


def expert_kernel(
    count,
    shards,
    cuts,
    capacity,
    h_ref,
    slot_ref,
    chosen_ref,
    router_ref,
    dy_ref,
    wg_ref,
    wu_ref,
    wd1_ref,
    wd2_ref,
    wd3_ref,
    wg_own,
    wu_own,
    wd_own,
    xs_out,
    de_out,
    dx_ref,
    dl_out,
    ce_out,
    hid_out,
    dgu_out,
    land,
    ring_out,
    ring_in,
    side_out,
    side_in,
    wgu,
    wd,
    dyb,
    xs,
    de,
    dl,
    ce,
    hid,
    dgu,
    w_sem,
    dy_sem,
    out_sem,
):
    block, dim = h_ref.shape
    ffe = wd.shape[0]
    wd_refs = (wd1_ref, wd2_ref, wd3_ref)
    me = lax.axis_index("seq")
    chips = count // 2
    weights = [
        pltpu.make_async_copy(src, dst, w_sem.at[i, n])
        for i in range(shards)
        for n, (src, dst) in enumerate(
            gate_up_parts(i, shards, (wg_ref, wu_ref), (wg_own, wu_own), wgu)
            + down_parts(i, shards, wd_refs, wd_own, wd)
        )
    ]
    staged = (
        (xs, xs_out),
        (de, de_out),
        (dl, dl_out),
        (ce, ce_out),
        (hid, hid_out),
        (dgu, dgu_out),
    )

    def dy_copies(s):
        first, second = pair_owners(count, s)
        return [
            pltpu.make_async_copy(
                dy_ref.at[at_block(owner, block)], dyb.at[s % 2, pl.ds(half * block, block)], dy_sem.at[s % 2, half]
            )
            for half, owner in ((0, first), (1, second))
        ]

    for copy in weights + dy_copies(0):
        copy.start()

    def use(s, first, second, pump):
        @pl.when(s < chips - 1)
        def _():
            for copy in dy_copies(s + 1):
                copy.start()

        rows = pl.ds(pl.multiple_of(s * 2 * capacity, 16), 2 * capacity)
        pick = one_hot_of(slot_ref, first, second, capacity)
        x = mm(pick, land[s]).astype(BF16)
        xs[rows, :] = x
        chosen = mm(
            pick,
            jnp.concatenate(
                [
                    chosen_ref[pl.ds(pl.multiple_of(first * block, block), block), :],
                    chosen_ref[pl.ds(pl.multiple_of(second * block, block), block), :],
                ],
                axis=0,
            ),
        )
        logits = jnp.where(chosen > 0.5, mm(x, router_ref[...], NT), -1e30)
        weight = jnp.exp(logits - jnp.max(logits, axis=1, keepdims=True)) * chosen
        mass = jnp.sum(weight, axis=1, keepdims=True)
        expert_lane = lax.broadcasted_iota(jnp.int32, weight.shape, 1)
        wide_lane = lax.broadcasted_iota(jnp.int32, (2 * capacity, dl.shape[1]), 1)
        gate = jnp.sum(jnp.where(expert_lane == me, weight, 0.0), axis=1, keepdims=True)
        gate = gate / jnp.where(mass > 0.0, mass, 1.0)

        @pl.when(s == 0)
        def _():
            for copy in weights:
                copy.wait()

        gu = mm(x, wgu[...])
        pump(0)
        g, u = gu[:, :ffe], gu[:, ffe:]
        sig = jax.nn.sigmoid(g)
        silu = g * sig
        h = (silu * u).astype(BF16)
        hid[rows, :] = h
        e = mm(h, wd[...])
        ce[rows, :] = (gate * e).astype(BF16)
        pump(1)
        for copy in dy_copies(s):
            copy.wait()
        dys = mm(pick, dyb[s % 2])
        dgate = jnp.sum(dys * e, axis=1, keepdims=True)
        d = (gate * dys).astype(BF16)
        de[rows, :] = d
        pump(2)
        dh = mm(d, wd[...], NT)
        for c in range(3, cuts):
            pump(c)
        dg = (dh * u * (sig + silu * (1.0 - sig))).astype(BF16)
        du = (dh * silu).astype(BF16)
        dgu[rows, :ffe] = dg
        dgu[rows, ffe:] = du

        @pl.when(s == 1)
        def _():
            dx_ref[...] = mm(dgu[rows, :], wgu[...], NT).astype(BF16)

        high = dgate.astype(BF16).astype(F32)
        dl[rows, :] = jnp.where(
            wide_lane == me, high, jnp.where(wide_lane == me + 64, dgate - high, 0.0)
        ).astype(BF16)
        for i, (src, dst) in enumerate(staged):
            pltpu.make_async_copy(src.at[rows], dst.at[rows], out_sem.at[i]).start()

    gather_steps(count, cuts, h_ref, land, (ring_out, ring_in, side_out, side_in), use)
    for i, (src, dst) in enumerate(staged):
        pltpu.make_async_copy(src, dst, out_sem.at[i]).wait()


def expert_gathered(h2, slot, chosen, router, dy_all, weights, capacity, count, shards, call, cuts=4):
    block, dim = h2.shape
    ffe = weights[0].shape[1]
    total = count * capacity
    widths = (dim, dim, 128, dim, ffe, 2 * ffe)
    dma = pltpu.SemaphoreType.DMA
    return pl.pallas_call(
        functools.partial(expert_kernel, count, shards, cuts, capacity),
        out_shape=[
            jax.ShapeDtypeStruct((2 * capacity if i == 2 else total, n), BF16)
            for i, n in enumerate(widths[:2] + (dim,) + widths[2:])
        ],
        in_specs=[VMEM] * 4 + [ANY] * 9,
        out_specs=[ANY] * 2 + [VMEM] + [ANY] * 4,
        scratch_shapes=gather_scratch(count, cuts, block, dim)
        + [
            pltpu.VMEM((dim, 2 * ffe), BF16),
            pltpu.VMEM((ffe, dim), BF16),
            pltpu.VMEM((2, 2 * block, dim), BF16),
        ]
        + [pltpu.VMEM((total, n), BF16) for n in widths]
        + [dma((shards, 5)), dma((2, 2)), dma((6,))],
        compiler_params=remote_params(call, 60),
    )(h2, slot, chosen, router, dy_all, *weights)


def slots_back_kernel(
    count,
    shards,
    cuts,
    capacity,
    slot_ref,
    dl,
    dx0_ref,
    xs_ref,
    dgu_ref,
    wg_ref,
    wu_ref,
    wg_own,
    wu_own,
    o_ref,
    gate_out,
    *rest,
):
    bufs, sems = rest[:5], rest[5:9]
    dx, xs, dgu, wgu, gate, sem, w_sem, gate_sem = rest[9:]
    chips = count // 2
    block = o_ref.shape[0]
    ffe = gate.shape[1]
    load_dgu = pltpu.make_async_copy(dgu_ref, dgu, sem.at[0])
    load_xs = pltpu.make_async_copy(xs_ref, xs, sem.at[1])
    weights = [
        pltpu.make_async_copy(src, dst, w_sem.at[i, n])
        for i in range(shards)
        for n, (src, dst) in enumerate(
            gate_up_parts(i, shards, (wg_ref, wu_ref), (wg_own, wu_own), wgu)
        )
    ]
    part = xs.shape[1] // chips

    def begin():
        for load in [load_dgu] + weights + [load_xs]:
            load.start()

    def produce(k, first, second):
        rows = pl.ds(pl.multiple_of((k + 1) % chips * 2 * capacity, 16), 2 * capacity)

        @pl.when(k == 0)
        def _():
            dx[...] = dx0_ref[...]

        @pl.when(k == 1)
        def _():
            for load in [load_dgu] + weights:
                load.wait()

        @pl.when(k > 0)
        def _():
            dx[...] = mm(dgu[rows, :], wgu[...], NT).astype(BF16)

        pick = one_hot_of(slot_ref, first, second, capacity)
        both = jnp.concatenate([mm(pick, dx[...], TN), mm(pick, dl[rows, :], TN)], axis=1)
        return both[:block], both[block:]

    def extra(k):
        @pl.when(k == 0)
        def _():
            load_xs.wait()

        columns = pl.ds(pl.multiple_of(k * part, 128), part)
        rows = pl.ds(pl.multiple_of(k * part, 16), part)
        gate[rows, :] = mm(xs[:, columns], dgu[:, :ffe], TN).astype(BF16)
        pltpu.make_async_copy(gate.at[rows], gate_out.at[rows], gate_sem).start()

    scatter_steps(count, cuts, o_ref, bufs, sems, produce, extra, 1, begin)
    pltpu.make_async_copy(gate, gate_out, gate_sem).wait()


def slots_back(slot, dl, dx0, xs, dgu, weights, capacity, count, shards, call, cuts=2):
    block = slot.shape[1]
    dim, ffe = xs.shape[1], dgu.shape[1] // 2
    columns = dim + dl.shape[1]
    dma = pltpu.SemaphoreType.DMA
    return pl.pallas_call(
        functools.partial(slots_back_kernel, count, shards, cuts, capacity),
        out_shape=(
            jax.ShapeDtypeStruct((block, columns), F32),
            jax.ShapeDtypeStruct((dim, ffe), BF16),
        ),
        in_specs=[VMEM] * 3 + [ANY] * 6,
        out_specs=[VMEM, ANY],
        scratch_shapes=scatter_scratch(count, cuts, block, columns)
        + [pltpu.VMEM(a.shape, BF16) for a in (dx0, xs, dgu)]
        + [pltpu.VMEM((dim, 2 * ffe), BF16), pltpu.VMEM((dim, ffe), BF16)]
        + [dma((2,)), dma((shards, 2)), dma],
        compiler_params=remote_params(call, 60),
    )(slot, dl, dx0, xs, dgu, *weights)


def split3(x):
    first = x.astype(BF16)
    rest = x - first.astype(F32)
    second = rest.astype(BF16)
    return first, second, (rest - second.astype(F32)).astype(BF16)


def in_lanes(x):
    lane = lax.broadcasted_iota(jnp.int32, x.shape, 1)
    first = x.astype(BF16).astype(F32)
    second = (x - first).astype(BF16).astype(F32)
    third = x - first - second
    spread = jnp.where(lane == 0, first, jnp.where(lane == 1, second, third))
    return jnp.where(lane < 3, spread, 0.0).astype(BF16)


def swap_halves(x):
    half = x.shape[1] // 2
    return jnp.concatenate([x[:, half:], x[:, :half]], axis=1)


def rope_tables(cos_ref, sin_ref, i, tile):
    rows, width = cos_ref.shape
    late = i * tile // rows
    part = pl.ds(i * tile - late * rows, tile)
    lanes = slice(late * (width // 2), (late + 1) * (width // 2))
    cos = cos_ref[part, :][:, lanes]
    sin = sin_ref[part, :][:, lanes]
    return jnp.concatenate([cos, cos], axis=1), jnp.concatenate([-sin, sin], axis=1)


def unit_rows(u):
    r = lax.rsqrt(jnp.mean(u * u, axis=1, keepdims=True) + EPSILON)
    return r, u * r


def attend_kernel(
    count,
    shards,
    cuts,
    heads,
    tile,
    dy_ref,
    routes_ref,
    qkv_ref,
    gq_ref,
    gk_ref,
    cos_ref,
    sin_ref,
    start_ref,
    wg_ref,
    wd_ref,
    dy_all,
    routes_all,
    o_ref,
    qx_ref,
    kn_ref,
    wg_all,
    wd_all,
    land,
    ring_out,
    ring_in,
    side_out,
    side_in,
    x_out,
    x_in,
    tag,
    vx_ref,
    dy_sem,
):
    span = qkv_ref.shape[0]
    width = kn_ref.shape[1]
    block = dy_ref.shape[0]
    scale = width**-0.5 * LOG2E
    down = wd_all.shape[0]
    items = [(wg_ref, wg_all, 0), (wd_ref.at[pl.ds(down, down)], wd_all, 1)]
    start_item, wait_item = crossing(shards, items, x_out, x_in)

    def prepare(i):
        rows = pl.ds(i * tile, tile)
        cos, sin = rope_tables(cos_ref, sin_ref, i, tile)
        for h in range(heads + 1):
            _, unit = unit_rows(qkv_ref[rows, pl.ds(h * width, width)].astype(F32))
            u = unit * (gk_ref[...] if h == heads else gq_ref[...])
            u = u * cos + swap_halves(u) * sin
            if h == heads:
                kn_ref[rows, :] = u.astype(BF16)
            else:
                qx_ref[rows, pl.ds(2 * h * width, width)] = (u * scale).astype(BF16)
        vx_ref[rows, :width] = qkv_ref[rows, pl.ds((heads + 1) * width, width)]
        vx_ref[rows, width:] = jnp.ones((tile, width), BF16)

    def attend_rows(i, h):
        rows = pl.ds(i * tile, tile)
        start = start_ref[rows, :]
        row = i * tile + lax.broadcasted_iota(jnp.int32, (tile, tile), 0)
        q = qx_ref[rows, pl.ds(2 * h * width, width)]
        total = jnp.zeros((tile, 2 * width), F32)
        for j in range(i + 1):
            keys = pl.ds(j * tile, tile)
            s = mm(q, kn_ref[keys, :], NT)
            col = j * tile + lax.broadcasted_iota(jnp.int32, (tile, tile), 1)
            keep = col >= start
            if i == j:
                keep = keep & (col <= row)
            p = jnp.where(keep, jnp.exp2(s), 0.0).astype(BF16)
            total = total + mm(p, vx_ref[keys, :])
        weight = total[:, width:]
        o_ref[rows, pl.ds(h * width, width)] = (total[:, :width] / weight).astype(BF16)
        qx_ref[rows, pl.ds((2 * h + 1) * width, width)] = in_lanes(-jnp.log2(weight))

    units = []
    for i in range(span // tile):
        units.append((1.0, functools.partial(prepare, i)))
        units += [(0.7 * (i + 1), functools.partial(attend_rows, i, h)) for h in range(heads)]
    plan = spread_units(units, count // 2 - 1)

    def begin():
        for n in range(len(items)):
            start_item(n)

    tag[0, 0] = routes_ref[...]

    def use(s, first, second, pump):
        for half, owner in ((0, first), (1, second)):
            pltpu.make_async_copy(
                land.at[s, pl.ds(half * block, block)],
                dy_all.at[at_block(owner, block)],
                dy_sem.at[half],
            ).start()
            routes_all[owner] = tag[s, half]
        run_units(plan, s)
        for c in range(cuts + 1):
            pump(c)

    gather_steps(
        count, cuts, dy_ref, land, (ring_out, ring_in, side_out, side_in), use, shards, begin, tag
    )
    for n in range(len(items)):
        wait_item(n)
    half_rows = count * block // 2
    for half in range(2):
        pltpu.make_async_copy(
            dy_all.at[pl.ds(0, half_rows)], dy_all.at[pl.ds(0, half_rows)], dy_sem.at[half]
        ).wait()


def attend(dy, routes, qkv, gq, gk, cos, sin, start, w_gate, w_down, down_rows, count, shards, call, tile=512, cuts=4):
    span = qkv.shape[0]
    width = gq.shape[0]
    heads = qkv.shape[1] // width - 2
    block, dim = dy.shape
    chips = count // 2
    return pl.pallas_call(
        functools.partial(attend_kernel, count, shards, cuts, heads, min(tile, span // 2)),
        out_shape=(
            jax.ShapeDtypeStruct((count * block, dim), BF16),
            jax.ShapeDtypeStruct((count,) + routes.shape, BF16),
            jax.ShapeDtypeStruct((span, heads * width), BF16),
            jax.ShapeDtypeStruct((span, 2 * heads * width), BF16),
            jax.ShapeDtypeStruct((span, width), BF16),
            whole_of(w_gate, 0, shards),
            jax.ShapeDtypeStruct((down_rows, dim), BF16),
        ),
        in_specs=[VMEM] * 8 + [ANY] * 2,
        out_specs=[ANY] + [VMEM] * 4 + [ANY] * 2,
        scratch_shapes=gather_scratch(count, cuts + 1, block, dim)
        + crossing_scratch(shards, 2)
        + [
            pltpu.VMEM((chips, 2) + routes.shape, BF16),
            pltpu.VMEM((span, 2 * width), BF16),
            pltpu.SemaphoreType.DMA((2,)),
        ],
        compiler_params=remote_params(call, 56),
    )(dy, routes, qkv, gq[None, :], gk[None, :], cos, sin, start[:, None], w_gate, w_down)


def attend_back_kernel(
    count,
    shards,
    cuts,
    capacity,
    heads,
    tile,
    qx_ref,
    kn_ref,
    qkv_ref,
    o_ref,
    do_ref,
    gq_ref,
    gk_ref,
    cos_ref,
    sin_ref,
    start_ref,
    slot_ref,
    part_ref,
    ce_ref,
    dqkv_ref,
    gains_ref,
    mixed_ref,
    half_ref,
    *rest,
):
    bufs, sems = rest[:5], rest[5:9]
    gx_ref, dq_ref, dk_ref, dv_ref, held, held_sem, pair, pair_own, pair_out, pair_in = rest[9:]
    span = qx_ref.shape[0]
    width = kn_ref.shape[1]
    scale = width**-0.5
    chips = count // 2
    block = mixed_ref.shape[0]
    load = pltpu.make_async_copy(ce_ref, held, held_sem)
    load.start()

    mine = lax.axis_index("fsdp")
    me = lax.axis_index("seq")
    lane = me % 2
    chip_first = me - lane
    half_rows = half_ref.shape[0]

    def give_half(c):
        return pltpu.make_async_remote_copy(
            src_ref=part_ref.at[pl.ds(c * half_rows, half_rows)],
            dst_ref=pair.at[(mine + lane) % 2],
            send_sem=pair_out.at[c],
            recv_sem=pair_in.at[(mine + lane) % 2],
            device_id={"fsdp": lane, "seq": chip_first + c},
            device_id_type=MESH,
        )

    def take_half(n):
        return pltpu.make_async_remote_copy(
            src_ref=part_ref.at[pl.ds(0, half_rows)],
            dst_ref=pair.at[n],
            send_sem=pair_out.at[0],
            recv_sem=pair_in.at[n],
            device_id={"fsdp": 1 - mine, "seq": chip_first + mine},
            device_id_type=MESH,
        )

    keep_half = pltpu.make_async_copy(
        part_ref.at[pl.ds(pl.multiple_of(lane * half_rows, 16), half_rows)], pair.at[0], pair_own
    )

    def meet():
        barrier = pltpu.get_barrier_semaphore()
        pl.semaphore_signal(
            barrier,
            inc=1,
            device_id={"fsdp": 1 - mine, "seq": chip_first + mine},
            device_id_type=MESH,
        )

        @pl.when(lane != mine)
        def _():
            pl.semaphore_signal(
                barrier, inc=1, device_id={"seq": chip_first + mine}, device_id_type=MESH
            )

    def begin():
        for c in range(2):

            @pl.when((mine != lane) | (lane != c))
            def _(c=c):
                give_half(c).start()

        @pl.when(mine == lane)
        def _():
            keep_half.start()

    def end():
        for c in range(2):

            @pl.when((mine != lane) | (lane != c))
            def _(c=c):
                give_half(c).wait_send()

        @pl.when(mine == lane)
        def _():
            keep_half.wait()

        @pl.when(mine != lane)
        def _():
            take_half(0).wait_recv()

        take_half(1).wait_recv()
        half_ref[...] = (pair[0].astype(F32) + pair[1].astype(F32)).astype(BF16)

    summing = shards == 2
    partners = 1 + (mine != lane).astype(jnp.int32)

    def produce(k, first, second):
        @pl.when(k == 0)
        def _():
            load.wait()

        pair = pl.multiple_of((k + 1) % chips * 2 * capacity, 16)
        pick = one_hot_of(slot_ref, first, second, capacity)
        both = mm(pick, held[pl.ds(pair, 2 * capacity), :], TN)
        return both[:block], both[block:]

    def to_raw(d, h, i, gain, row):
        rows = pl.ds(i * tile, tile)
        cos, sin = rope_tables(cos_ref, sin_ref, i, tile)
        r, unit = unit_rows(qkv_ref[rows, pl.ds(h * width, width)].astype(F32))
        d = d * cos + swap_halves(d * sin)
        dg = d * gain
        raw = r * (dg - unit * jnp.mean(dg * unit, axis=1, keepdims=True))
        dqkv_ref[rows, pl.ds(h * width, width)] = raw.astype(BF16)
        gains_ref[row : row + 1, :] += jnp.sum(d * unit, axis=0, keepdims=True)

    def prepare(i):
        rows = pl.ds(i * tile, tile)
        for h in range(heads):
            cols = pl.ds(h * width, width)
            do = do_ref[rows, cols]
            inner = jnp.sum(do.astype(F32) * o_ref[rows, cols].astype(F32), axis=1, keepdims=True)
            gx_ref[rows, pl.ds(2 * h * width, width)] = do
            gx_ref[rows, pl.ds((2 * h + 1) * width, width)] = in_lanes(
                jnp.broadcast_to(-inner, (tile, width))
            )

    def tile_back(j, i):
        keys = pl.ds(j * tile, tile)
        rows = pl.ds(i * tile, tile)
        ones = jnp.ones((tile, width), BF16)
        kn = kn_ref[keys, :]
        kx = jnp.concatenate([kn, ones], axis=1)
        vx = jnp.concatenate([qkv_ref[keys, pl.ds((heads + 1) * width, width)], ones], axis=1)
        key = j * tile + lax.broadcasted_iota(jnp.int32, (tile, tile), 0)
        keep = key >= start_ref[:, rows]
        if i == j:
            row = i * tile + lax.broadcasted_iota(jnp.int32, (tile, tile), 1)
            keep = keep & (key <= row)
        for h in range(heads):
            qx = qx_ref[rows, pl.ds(2 * h * width, 2 * width)]
            gx = gx_ref[rows, pl.ds(2 * h * width, 2 * width)]
            p = jnp.where(keep, jnp.exp2(mm(kx, qx, NT)), 0.0)
            ds = (p * mm(vx, gx, NT)).astype(BF16)
            dv_ref[keys, :] += mm(p.astype(BF16), gx[:, :width])
            dk_ref[keys, :] += mm(ds, qx[:, :width])
            dq_ref[rows, pl.ds(h * width, width)] += mm(ds, kn, TN)

    def finish_keys(j):
        keys = pl.ds(j * tile, tile)
        dqkv_ref[keys, pl.ds((heads + 1) * width, width)] = dv_ref[keys, :].astype(BF16)
        to_raw(dk_ref[keys, :] * (1.0 / LOG2E), heads, j, gk_ref[...], 1)

    def finish_rows(i):
        rows = pl.ds(i * tile, tile)
        for h in range(heads):
            to_raw(dq_ref[rows, pl.ds(h * width, width)] * scale, h, i, gq_ref[...], 0)

    tiles = span // tile
    units = [(0.3, functools.partial(prepare, i)) for i in range(tiles)]
    for j in range(tiles):
        units += [(2.0, functools.partial(tile_back, j, i)) for i in range(j, tiles)]
        units.append((0.3, functools.partial(finish_keys, j)))
        units.append((0.6, functools.partial(finish_rows, j)))
    plan = spread_units(units, chips - 1)
    for ref in (dq_ref, dk_ref, dv_ref, gains_ref):
        ref[...] = jnp.zeros_like(ref)

    def extra(k):
        run_units(plan, k)

    if summing:
        scatter_steps(
            count, cuts, mixed_ref, bufs, sems, produce, extra, 1, begin, (meet, partners)
        )
        end()
    else:
        scatter_steps(count, cuts, mixed_ref, bufs, sems, produce, extra)
        half_ref[...] = jnp.zeros_like(half_ref)


def attend_back(qx, kn, qkv, o, do, gq, gk, cos, sin, start, slot, part, ce, capacity, count, shards, call, tile=512, cuts=2):
    span, width = kn.shape
    heads = o.shape[1] // width
    block = slot.shape[1]
    dim = ce.shape[1]
    return pl.pallas_call(
        functools.partial(
            attend_back_kernel, count, shards, cuts, capacity, heads, min(tile, span // 2)
        ),
        out_shape=(
            jax.ShapeDtypeStruct(qkv.shape, BF16),
            jax.ShapeDtypeStruct((8, width), F32),
            jax.ShapeDtypeStruct((block, dim), F32),
            jax.ShapeDtypeStruct((part.shape[0] // 2, dim), BF16),
        ),
        in_specs=[VMEM] * 12 + [ANY],
        out_specs=[VMEM] * 4,
        scratch_shapes=scatter_scratch(count, cuts, block, dim)
        + [
            pltpu.VMEM((span, 2 * heads * width), BF16),
            pltpu.VMEM((span, heads * width), F32),
            pltpu.VMEM((span, width), F32),
            pltpu.VMEM((span, width), F32),
            pltpu.VMEM(ce.shape, BF16),
            pltpu.SemaphoreType.DMA,
            pltpu.VMEM((2, part.shape[0] // 2, dim), BF16),
            pltpu.SemaphoreType.DMA,
            pltpu.SemaphoreType.DMA((2,)),
            pltpu.SemaphoreType.DMA((2,)),
        ],
        compiler_params=remote_params(call, 60),
    )(qx, kn, qkv, o, do, gq[None, :], gk[None, :], cos, sin, start[None, :], slot, part, ce)


def last_gather_kernel(count, members, cuts, extras, qkv_ref, *refs):
    x_refs, (q_all, kv_all) = refs[:extras], refs[extras : extras + 2]
    x_alls = refs[extras + 2 : 2 * extras + 2]
    heap, kv_sum, own_sem, mo, mi, ro, ri, so, si = refs[2 * extras + 2 :]
    me, chips, lane, position, step, following, previous, sibling = places(count)
    chip = me // 2
    place = chip % members
    first = chip - place
    rows = kv_sum.shape[0]
    gcols = q_all.shape[2]
    q_ref = qkv_ref.at[:, pl.ds(0, gcols)]
    kv_ref = qkv_ref.at[pl.ds(0, rows * members), pl.ds(gcols, kv_sum.shape[1])]

    def member(i):
        return (first + (place + i) % members) * 2 + lane

    greet([previous, sibling] + [member(i) for i in range(1, members)])

    def give(i):
        target = (place + i) % members
        return pltpu.make_async_remote_copy(
            src_ref=kv_ref.at[pl.ds(target * rows, rows)],
            dst_ref=heap.at[i - 1],
            send_sem=mo.at[i - 1],
            recv_sem=mi.at[i - 1],
            device_id={"seq": member(i)},
            device_id_type=MESH,
        )

    pieces = []
    for x_ref, x_all in zip(x_refs, x_alls):
        parts = row_parts(x_ref.shape[0], cuts if x_ref.shape[0] >= 64 else 1)
        pieces += [(x_ref, x_all, part) for part in parts]
    pieces += [(q_ref, q_all, part) for part in row_parts(q_ref.shape[0], cuts)]
    last = len(pieces)
    pieces.append((kv_sum, kv_all, pl.ds(0, rows)))

    def hop(c, owner, s, device, out_sem, in_sem, first_hop):
        x_ref, o_ref, part = pieces[c]
        return pltpu.make_async_remote_copy(
            src_ref=x_ref.at[part] if first_hop else o_ref.at[owner, part],
            dst_ref=o_ref.at[owner, part],
            send_sem=out_sem.at[s, c],
            recv_sem=in_sem.at[s, c],
            device_id={"seq": device},
            device_id_type=MESH,
        )

    def ring(c, owner, s, first_hop=False):
        return hop(c, owner, s, following, ro, ri, first_hop)

    def side(c, owner, s, first_hop=False):
        return hop(c, owner, s, sibling, so, si, first_hop)

    for i in range(1, members):
        give(i).start()
    mine = pltpu.make_async_copy(kv_ref.at[pl.ds(place * rows, rows)], kv_sum, own_sem.at[0])
    mine.start()
    own = [
        pltpu.make_async_copy(src, dst.at[me], own_sem.at[n + 2])
        for n, (src, dst) in enumerate(zip((q_ref,) + x_refs, (q_all,) + x_alls))
    ]
    for c in range(last):
        ring(c, me, 0, True).start()
        side(c, me, 0, True).start()
    for copy in own:
        copy.start()
    mine.wait()
    total = kv_sum[...].astype(F32)
    for i in range(1, members):
        give(i).wait_recv()
        total = total + heap[i - 1].astype(F32)
    kv_sum[...] = total.astype(BF16)
    own_kv = pltpu.make_async_copy(kv_sum, kv_all.at[me], own_sem.at[1])
    own_kv.start()
    ring(last, me, 0, True).start()
    side(last, me, 0, True).start()
    for s in range(1, chips):
        owner = chip_of((position - s * step + chips) % chips, chips) * 2 + lane
        for c in range(last + 1):
            ring(c, owner, s - 1).wait_recv()
            if s < chips - 1:
                ring(c, owner, s).start()
            side(c, owner, s).start()
    for i in range(1, members):
        give(i).wait_send()
    for s in range(chips):
        for c in range(last + 1):
            side(c, me, s).wait()
            if s < chips - 1:
                ring(c, me, s).wait_send()
    for copy in own + [own_kv]:
        copy.wait()


def last_gather(qkv, extras, gcols, local, count, members, call, cuts=4):
    chips = count // 2
    rows = local // members
    columns = qkv.shape[1] - gcols
    pieces = cuts + 1 + sum(cuts if x.shape[0] >= 64 else 1 for x in extras)
    dma = pltpu.SemaphoreType.DMA
    return pl.pallas_call(
        functools.partial(last_gather_kernel, count, members, cuts, len(extras)),
        out_shape=[
            jax.ShapeDtypeStruct((count, qkv.shape[0], gcols), BF16),
            jax.ShapeDtypeStruct((count, rows, columns), BF16),
        ]
        + [jax.ShapeDtypeStruct((count,) + x.shape, BF16) for x in extras],
        in_specs=[VMEM] * (1 + len(extras)),
        out_specs=[ANY] * (2 + len(extras)),
        scratch_shapes=[
            pltpu.VMEM((members - 1, rows, columns), BF16),
            pltpu.VMEM((rows, columns), BF16),
            dma((3 + len(extras),)),
            dma((members - 1,)),
            dma((members - 1,)),
        ]
        + [dma((chips, pieces))] * 4,
        compiler_params=pltpu.CompilerParams(collective_id=call, has_side_effects=True),
    )(qkv, *extras)


def finish_kernel(
    count,
    kv_heads,
    tile,
    q_ref,
    kv_ref,
    wq_ref,
    wk_ref,
    wv_ref,
    gain_ref,
    out_ref,
    gate_ref,
    up_ref,
    down_ref,
    dq_ref,
    dk_ref,
    dv_ref,
    dg_ref,
    dout_ref,
    dgate_ref,
    dup_ref,
    ddown_ref,
):
    dout_ref[...] = out_ref[...].astype(F32)
    dgate_ref[...] = gate_ref[...].astype(F32)
    dup_ref[...] = up_ref[...].astype(F32)
    ddown_ref[...] = down_ref[...].astype(F32)
    chips = count // 2
    members = count // kv_heads
    width = q_ref.shape[2]
    hd = kv_ref.shape[2] // 2
    member = pl.program_id(0) * members // pl.num_programs(0)

    def place(group):
        return (group % chips) * 2 + group // chips

    total = jnp.zeros((tile, 1), F32)
    for g in range(count):
        cols = pl.ds(g * width, width)
        grad = q_ref[place(g)].astype(F32)
        dq_ref[:, cols] = grad
        total += jnp.sum(grad * wq_ref[:, cols].astype(F32), axis=1, keepdims=True)
    for j in range(kv_heads):
        cols = pl.ds(j * hd, hd)
        pair = kv_ref[place(j * members + member)].astype(F32)
        dk_ref[:, cols] = pair[:, :hd]
        dv_ref[:, cols] = pair[:, hd:]
        total += jnp.sum(pair[:, :hd] * wk_ref[:, cols].astype(F32), axis=1, keepdims=True)
        total += jnp.sum(pair[:, hd:] * wv_ref[:, cols].astype(F32), axis=1, keepdims=True)
    dg_ref[...] = total / gain_ref[...].astype(F32)


def finish(q_all, kv_all, w_query, key_weight, value_weight, gain, others, kv_heads):
    count = q_all.shape[0]
    local, columns = w_query.shape
    rows = kv_all.shape[1]
    tile = min(128, rows)
    per = rows // tile
    kv_columns = key_weight.shape[1]

    steps = local // tile

    def row_block(n, rows=tile):
        return pl.BlockSpec((rows, n), lambda r: (r, 0))

    other_blocks = [row_block(a.shape[1], a.shape[0] // steps) for a in others]

    return pl.pallas_call(
        functools.partial(finish_kernel, count, kv_heads, tile),
        grid=(local // tile,),
        out_shape=(
            jax.ShapeDtypeStruct((local, columns), F32),
            jax.ShapeDtypeStruct((local, kv_columns), F32),
            jax.ShapeDtypeStruct((local, kv_columns), F32),
            jax.ShapeDtypeStruct((local, 1), F32),
        )
        + tuple(jax.ShapeDtypeStruct(a.shape, F32) for a in others),
        in_specs=[
            pl.BlockSpec((count, tile, q_all.shape[2]), lambda r: (0, r, 0)),
            pl.BlockSpec((count, tile, kv_all.shape[2]), lambda r: (0, r % per, 0)),
            row_block(columns),
            row_block(kv_columns),
            row_block(kv_columns),
            row_block(1),
        ]
        + other_blocks,
        out_specs=[row_block(columns), row_block(kv_columns), row_block(kv_columns), row_block(1)]
        + other_blocks,
        compiler_params=pltpu.CompilerParams(vmem_limit_bytes=48 * MIB),
    )(q_all, kv_all, w_query, key_weight, value_weight, gain[:, None], *others)


def run_starts(segment):
    position = jnp.arange(segment.shape[0], dtype=jnp.int32)
    fresh = jnp.concatenate([jnp.ones((1,), dtype=bool), segment[1:] != segment[:-1]])
    return position, lax.cummax(jnp.where(fresh, position, jnp.zeros_like(position)), axis=0)


def angles(offset, head_size):
    half = head_size // 2
    lane = jnp.arange(head_size, dtype=jnp.int32)
    frequency = jnp.exp((lane % half).astype(F32) * (-2.0 * math.log(THETA) / head_size))
    early, late = offset.reshape(2, -1)
    phases = jnp.where(lane[None, :] < half, early[:, None], late[:, None]) * frequency[None, :]
    return jnp.cos(phases), jnp.sin(phases)


def per_device(
    activations,
    cotangent,
    segments,
    routing,
    attn_gain,
    mlp_gain,
    query_gain,
    key_gain,
    w_query,
    key_weight,
    value_weight,
    w_out,
    w_router,
    w_gate,
    w_up,
    w_down,
):
    count = lax.axis_size("seq")
    shards = lax.axis_size("fsdp")
    me = lax.axis_index("seq")
    chips = count // 2
    x = activations[0].astype(F32)
    dy = cotangent[0]
    segment = segments[0]
    routes = routing[0]
    tok, dim = x.shape
    span = segment.shape[0]
    top = routes.shape[1]
    hd = query_gain.shape[0] * shards
    heads = w_query.shape[1] // hd
    kv_heads = key_weight.shape[1] // hd
    share = heads // count
    experts = w_router.shape[1]
    local_rows = w_out.shape[0]
    capacity = tok * top * 9 // (8 * experts)
    gcols = share * hd

    local_dim = attn_gain.shape[0]
    local_hd = query_gain.shape[0]
    head_gains = jnp.concatenate([query_gain, key_gain], axis=0)
    head_gains = jnp.pad(head_gains, (0, -head_gains.shape[0] % 128))
    small = jnp.concatenate(
        [v.astype(F32).reshape(-1, 128) for v in (attn_gain, mlp_gain, head_gains)], axis=0
    )
    small = jnp.pad(small, ((0, -small.shape[0] % 8), (0, 0)))
    ffe = w_down.shape[1]
    down_rows = ffe // 3 // 16 * 16
    h1_all, qkv, w_qkv, w_o, small, router, wd1 = front(
        activations[0],
        small,
        w_router.T,
        w_query,
        key_weight,
        value_weight,
        w_out,
        w_down[0],
        down_rows,
        hd,
        count,
        shards,
        1,
    )
    gain_rows = local_dim // 128
    g_attn = small[:, :gain_rows].reshape(-1)
    g_mlp = small[:, gain_rows : 2 * gain_rows].reshape(-1)
    g_query = small[:, 2 * gain_rows, :local_hd].reshape(-1)
    g_key = small[:, 2 * gain_rows, local_hd : 2 * local_hd].reshape(-1)
    r1 = lax.rsqrt(jnp.mean(x * x, axis=-1, keepdims=True) + EPSILON)
    position, doc_start = run_starts(segment)
    cos_full, sin_full = angles((position - doc_start).astype(F32), hd)
    start = jnp.where(segment > 0, doc_start, position)

    routes_sent = jnp.pad(routes.T, ((0, -top % 16), (0, 0))).astype(BF16)
    dy_all, routes_all, o, qx, kn, wg, wd2 = attend(
        dy,
        routes_sent,
        qkv,
        g_query,
        g_key,
        cos_full,
        sin_full,
        start,
        w_gate[0],
        w_down[0],
        down_rows,
        count,
        shards,
        4,
    )
    wholes = (
        whole_of(w_up[0], 0, shards),
        jax.ShapeDtypeStruct((ffe - 2 * down_rows, dim), BF16),
    )
    x2, wu, wd3 = product_scattered(
        o, w_o, NN, [w_up[0], w_down[0]], (0, 1), wholes, count, shards, 2
    )
    x2 = x + x2

    r2 = lax.rsqrt(jnp.mean(x2 * x2, axis=-1, keepdims=True) + EPSILON)
    h2 = (x2 * r2 * g_mlp).astype(BF16)
    def gates_of(hidden, chosen):
        logits = mm(hidden, router, NT)
        return jax.nn.softmax(jnp.where(chosen, logits, -1e30), axis=-1) * chosen

    def chosen_of(named):
        names = jnp.arange(experts, dtype=jnp.int32)
        return jnp.any(named[..., :, None] == names, axis=-2)

    routes_all = jnp.swapaxes(routes_all[:, :top].astype(jnp.int32), 1, 2)
    hit = jnp.any(routes_all == me, axis=-1)
    rank = jnp.cumsum(hit.astype(jnp.int32), axis=1) - hit
    slot = jnp.where(hit & (rank < capacity), rank, -1)
    chosen_all = chosen_of(routes_all.reshape(span, top)).astype(BF16)
    xs, de, dx0, dl, ce, hid, dgu = expert_gathered(
        h2,
        slot,
        chosen_all,
        router,
        dy_all,
        (wg, wu, wd1, wd2, wd3, w_gate[0], w_up[0], w_down[0]),
        capacity,
        count,
        shards,
        3,
    )
    dh2_wide, w_gate_part = slots_back(
        slot, dl, dx0, xs, dgu, (wg, wu, w_gate[0], w_up[0]), capacity, count, shards, 6
    )
    dgate = dh2_wide[:, dim : dim + experts] + dh2_wide[:, dim + 64 : dim + 64 + experts]
    gates = gates_of(h2, chosen_of(routes))
    dlogits = (gates * (dgate - jnp.sum(gates * dgate, axis=-1, keepdims=True))).astype(BF16)
    dh2 = dh2_wide[:, :dim] + mm(dlogits, router)
    router_part = mm(dlogits, h2, TN)
    xh = x2 * r2
    mlp_gain_part = jnp.sum(dh2 * xh, axis=0)
    dn = dh2 * g_mlp
    dx2 = dy.astype(F32) + r2 * (dn - xh * jnp.mean(dn * xh, axis=-1, keepdims=True))

    do, w_out_part, w_down_part, w_up_part = out_back(
        dx2.astype(BF16), w_o, o, hid, de, xs, dgu, count, 7
    )
    dqkv, head_gains, mixed, out_half = attend_back(
        qx,
        kn,
        qkv,
        o,
        do,
        g_query,
        g_key,
        cos_full,
        sin_full,
        start,
        slot,
        w_out_part,
        ce,
        capacity,
        count,
        shards,
        5,
    )
    mixed = x2 + mixed
    dh1, qkv_sum = token_back(dqkv, w_qkv, head_gains, h1_all, count, shards, 8)
    xh1 = x * r1
    dn1 = dh1 * g_attn
    input_grad = dx2 + r1 * (dn1 - xh1 * jnp.mean(dn1 * xh1, axis=-1, keepdims=True))

    def sum_fsdp(part, axis):
        return lax.psum_scatter(part.astype(BF16), "fsdp", scatter_dimension=axis, tiled=True)

    w_gate_sum = sum_fsdp(w_gate_part, 0)
    w_up_later, w_down_later, _ = lax.optimization_barrier((w_up_part, w_down_part, qkv_sum))
    w_up_sum = sum_fsdp(w_up_later, 0)
    w_down_sum = sum_fsdp(w_down_later, 1)

    small_part = jnp.concatenate([router_part, mlp_gain_part[None]], axis=0)
    small_part = jnp.pad(small_part, ((0, -small_part.shape[0] % 16), (0, 0)))
    small_sum = sum_fsdp(small_part, 1)
    extras = [out_half, small_sum] if shards == 2 else []
    q_all, kv_all, *rows_all = last_gather(
        qkv_sum, extras, gcols, local_dim, count, count // kv_heads, 10
    )
    if shards == 2:
        out_all, small_all = rows_all
        out_all = out_all.reshape(local_rows, dim)
    else:
        out_all, small_all = out_rows(w_out_part, small_sum, count)
    small_total = jnp.sum(small_all.astype(F32), axis=0)
    router_grad = small_total[:experts].T
    mlp_gain_grad = small_total[experts]
    (
        w_query_grad,
        w_key_grad,
        w_value_grad,
        attn_gain_grad,
        w_out_grad,
        w_gate_grad,
        w_up_grad,
        w_down_grad,
    ) = finish(
        q_all,
        kv_all,
        w_query,
        key_weight,
        value_weight,
        attn_gain,
        (out_all, w_gate_sum, w_up_sum, w_down_sum),
        kv_heads,
    )
    attn_gain_grad = attn_gain_grad[:, 0]
    head_gain_grads = jnp.sum(q_all[:, local_dim, : 2 * hd].astype(F32), axis=0)
    own_half = lax.axis_index("fsdp") * local_hd
    query_gain_grad = lax.dynamic_slice_in_dim(head_gain_grads[:hd], own_half, local_hd)
    key_gain_grad = lax.dynamic_slice_in_dim(head_gain_grads[hd:], own_half, local_hd)
    return (
        mixed.astype(BF16)[None],
        input_grad[None],
        attn_gain_grad,
        mlp_gain_grad,
        query_gain_grad,
        key_gain_grad,
        w_query_grad,
        w_key_grad,
        w_value_grad,
        w_out_grad,
        router_grad,
        w_gate_grad[None],
        w_up_grad[None],
        w_down_grad[None],
    )


def out_rows(part, small_sum, count):
    chips = count // 2
    gcols, dim = part.shape
    me = lax.axis_index("seq")
    group = (me % 2) * chips + me // 2
    blank = jnp.zeros((count * gcols, dim), BF16)
    placed = lax.dynamic_update_slice(blank, part, (group * gcols, 0))
    mine = lax.psum_scatter(placed, "fsdp", scatter_dimension=0, tiled=True)
    return lax.psum(mine, "seq"), lax.all_gather(small_sum, "seq", axis=0, tiled=False)


def solution(mesh):
    tokens = P("fsdp", "seq", None)
    rows = P("fsdp", None)
    vector = P("fsdp")
    expert_rows = P("seq", "fsdp", None)
    expert_columns = P("seq", None, "fsdp")
    return jax.shard_map(
        per_device,
        mesh=mesh,
        in_specs=(tokens, tokens, rows, tokens)
        + (vector,) * 4
        + (rows,) * 5
        + (expert_rows, expert_rows, expert_columns),
        out_specs=(tokens, tokens)
        + (vector,) * 4
        + (rows,) * 5
        + (expert_rows, expert_rows, expert_columns),
        check_vma=False,
    )
```
